32 devices in a mesh: dp: 16 (over z, y, x), tensor: 2 (over core).
Axes of the slice: x: 2, y: 2, z: 4, core: 2. Of those that a mesh axis runs over, the one named last changes fastest.
Arguments:
- tokens: bfloat16 [128, 197, 384], P(('dp', 'tensor')), may hold values from -6 to 6
- norm1_gain: float32 [384], replicated, may hold values from 0.5 to 1.5
- norm1_bias: float32 [384], replicated, may hold values from -3 to 3
- qkv_weight: bfloat16 [384, 1152], P('dp', 'tensor'), may hold values from -0.3125 to 0.3125
- mix_pre: float32 [6, 6], replicated, may hold values from -3 to 3
- mix_post: float32 [6, 6], replicated, may hold values from -3 to 3
- proj_weight: bfloat16 [384, 384], P('dp', 'tensor'), may hold values from -1.25 to 1.25
- proj_bias: float32 [384], replicated, may hold values from -3 to 3
- norm2_gain: float32 [384], replicated, may hold values from 0.5 to 1.5
- norm2_bias: float32 [384], replicated, may hold values from -3 to 3
- fc1_weight: bfloat16 [384, 1536], P(None, 'tensor'), may hold values from -0.3125 to 0.3125
- fc1_bias: bfloat16 [1536], P('tensor'), may hold values from -3 to 3
- conv_weight: bfloat16 [49, 1536], P(None, 'tensor'), may hold values from -0.875 to 0.875
- fc2_weight: bfloat16 [1536, 384], P('tensor'), may hold values from -0.15625 to 0.15625
- fc2_bias: float32 [384], replicated, may hold values from -3 to 3
- cotangent: bfloat16 [128, 197, 384], P(('dp', 'tensor')), may hold values from -6 to 6
Outputs:
- block_out: bfloat16 [128, 197, 384], P(('dp', 'tensor'))
- grad_tokens: float32 [128, 197, 384], P(('dp', 'tensor'))
- grad_norm1_gain: float32 [384], replicated
- grad_norm1_bias: float32 [384], replicated
- grad_qkv: float32 [384, 1152], P('dp', 'tensor')
- grad_mix_pre: float32 [6, 6], replicated
- grad_mix_post: float32 [6, 6], replicated
- grad_proj: float32 [384, 384], P('dp', 'tensor')
- grad_proj_bias: float32 [384], replicated
- grad_norm2_gain: float32 [384], replicated
- grad_norm2_bias: float32 [384], replicated
- grad_fc1: float32 [384, 1536], P(None, 'tensor')
- grad_fc1_bias: float32 [1536], P('tensor')
- grad_conv: float32 [49, 1536], P(None, 'tensor')
- grad_fc2: float32 [1536, 384], P('tensor')
- grad_fc2_bias: float32 [384], replicated
The draws below stay inside these ranges and needn't reach their ends.
All inputs are finite; a program needn't handle non-finite values.
Results may differ from the reference program's by a relative error of at most 0.014.
The reference program's roundings to bfloat16 on the way count: a program that leaves them out, or rounds other values in their place, can miss the bound.
Values may be sent and summed in bfloat16 or wider, within the bound.
A program may use at most 448 MiB of HBM per device.

```python
import jax
import jax.numpy as jnp
from jax import lax

D = 384
HEADS = 6
HEAD_DIM = 64
FF = 1536
KS = 7
GRID = 14
SEQ = 197
IMAGES = 128
N_DP = 16


def level_of(key, shape, split, smallest, top_value):
    def one(position, shards_of):
        heights = jax.random.uniform(jax.random.fold_in(jax.random.fold_in(key, 6), position), (shards_of,), jnp.float32, smallest / len(split), top_value / len(split))
        return jnp.repeat(jnp.exp(heights), shape[position] // shards_of).reshape((-1,) + (1,) * (len(shape) - position - 1))

    gain = one(*split[0])
    for cut in split[1:]:
        gain = gain * one(*cut)
    return gain


def scatter_about(stream_key, dims, scale, reach, cuts=(), dtype=jnp.bfloat16):
    entries = scale * jax.random.normal(stream_key, dims, jnp.float32)
    if cuts:
        entries = entries * level_of(stream_key, dims, cuts, -0.22, 0.18)
    return jnp.clip(entries, -reach, reach).astype(dtype)


def setup_inputs(seed: int = 0) -> dict:
    arg_keys = jax.random.split(jax.random.key(seed), 17)
    tokens = scatter_about(arg_keys[0], (IMAGES, SEQ, D), 1.0, 6.0, ((0, 32),))
    norm1_gain = jnp.clip(1.0 + 0.1 * jax.random.normal(arg_keys[1], (D,), jnp.float32), 0.5, 1.5)
    norm1_bias = scatter_about(arg_keys[2], (D,), 0.5, 3.0, (), jnp.float32)
    qkv_weight = scatter_about(arg_keys[3], (D, 3 * D), D ** -0.5, 0.3125, ((0, 16), (1, 2)))
    mix_pre = scatter_about(arg_keys[4], (HEADS, HEADS), 0.5, 3.0, (), jnp.float32)
    mix_post = scatter_about(arg_keys[5], (HEADS, HEADS), 0.5, 3.0, (), jnp.float32)
    proj_weight = scatter_about(arg_keys[6], (D, D), (D // 16) ** -0.5, 1.25, ((0, 16), (1, 2)))
    proj_bias = scatter_about(arg_keys[7], (D,), 0.5, 3.0, (), jnp.float32)
    norm2_gain = jnp.clip(1.0 + 0.1 * jax.random.normal(arg_keys[8], (D,), jnp.float32), 0.5, 1.5)
    norm2_bias = scatter_about(arg_keys[9], (D,), 0.5, 3.0, (), jnp.float32)
    fc1_weight = scatter_about(arg_keys[10], (D, FF), D ** -0.5, 0.3125, ((1, 2),))
    fc1_bias = scatter_about(arg_keys[11], (FF,), 0.5, 3.0, ((0, 2),))
    conv_weight = scatter_about(arg_keys[12], (KS * KS, FF), (KS * KS) ** -0.5, 0.875, ((1, 2),))
    fc2_weight = scatter_about(arg_keys[13], (FF, D), FF ** -0.5, 0.15625, ((0, 2),))
    fc2_bias = scatter_about(arg_keys[14], (D,), 0.5, 3.0, (), jnp.float32)
    cotangent = scatter_about(arg_keys[15], (IMAGES, SEQ, D), 1.0, 6.0, ((0, 32),))
    return {"tokens": tokens, "norm1_gain": norm1_gain, "norm1_bias": norm1_bias, "qkv_weight": qkv_weight, "mix_pre": mix_pre, "mix_post": mix_post, "proj_weight": proj_weight, "proj_bias": proj_bias, "norm2_gain": norm2_gain, "norm2_bias": norm2_bias, "fc1_weight": fc1_weight, "fc1_bias": fc1_bias, "conv_weight": conv_weight, "fc2_weight": fc2_weight, "fc2_bias": fc2_bias, "cotangent": cotangent}


highest = lax.Precision.HIGHEST

@jax.custom_vjp
def low(v):
    return lax.optimization_barrier(v.astype(jnp.bfloat16)).astype(jnp.float32)

@jax.custom_vjp
def low_back(v):
    return v

def low_keep(v):
    return (low(v), None)

def low_pass(kept, grad):
    return (grad,)

def back_keep(v):
    return (v, None)

def back_low(kept, grad):
    return (low(grad),)
low.defvjp(low_keep, low_pass)
low_back.defvjp(back_keep, back_low)

def layer_norm(values, norm_gain, norm_bias):
    centred = values - lax.optimization_barrier(jnp.mean(values, axis=-1, keepdims=True))
    spread = lax.optimization_barrier(jnp.mean(centred * centred, axis=-1, keepdims=True))
    return centred * lax.rsqrt(spread + 1e-05) * norm_gain + norm_bias

def depthwise(hidden, kernel):
    images = hidden.shape[0]
    width = hidden.shape[2]
    patches = hidden[:, 1:].reshape(images, GRID, GRID, width)
    radius = KS // 2
    padded = jnp.pad(patches, ((0, 0), (radius, radius), (radius, radius), (0, 0)))
    summed = jnp.zeros_like(patches)
    for tap_row in range(KS):
        for tap_col in range(KS):
            summed = summed + kernel[tap_row * KS + tap_col] * padded[:, tap_row:tap_row + GRID, tap_col:tap_col + GRID]
    return jnp.concatenate([hidden[:, :1], summed.reshape(images, GRID * GRID, width)], axis=1)

def forward(tokens, norm1_gain, norm1_bias, qkv_weight, mix_pre, mix_post, proj_weight, proj_bias, norm2_gain, norm2_bias, fc1_weight, fc1_bias, conv_weight, fc2_weight, fc2_bias):
    images = tokens.shape[0]
    normed = low(layer_norm(tokens, norm1_gain, norm1_bias))
    packed = low_back(low(jnp.einsum('bsd,dc->bsc', normed, qkv_weight, precision=highest)))
    packed = packed.reshape(images, SEQ, 3, HEADS, HEAD_DIM)
    query_rows = packed[:, :, 0]
    key_rows = packed[:, :, 1]
    value_rows = packed[:, :, 2]
    scores = low_back(jnp.einsum('bqhe,bkhe->bhqk', query_rows, key_rows, precision=highest) * HEAD_DIM ** (-0.5))
    mixed_scores = jnp.einsum('gh,bhqk->bgqk', mix_pre, scores, precision=highest)
    probabilities = jax.nn.softmax(mixed_scores, axis=-1)
    attn_weights = low(jnp.einsum('gh,bhqk->bgqk', mix_post, probabilities, precision=highest))
    attended = low_back(low(jnp.einsum('bhqk,bkhe->bqhe', attn_weights, value_rows, precision=highest)))
    attended = attended.reshape(images, SEQ, D)
    branch = low_back(jnp.einsum('bsd,de->bse', attended, proj_weight, precision=highest) + proj_bias)
    middle = tokens + branch
    normed_two = low(layer_norm(middle, norm2_gain, norm2_bias))
    hidden = low_back(jnp.einsum('bsd,df->bsf', normed_two, fc1_weight, precision=highest) + fc1_bias)
    convolved = low(depthwise(jax.nn.gelu(hidden, approximate=False), conv_weight))
    output = low_back(jnp.einsum('bsf,fd->bsd', convolved, fc2_weight, precision=highest) + fc2_bias)
    return middle + output

def reference(tokens, norm1_gain, norm1_bias, qkv_weight, mix_pre, mix_post, proj_weight, proj_bias, norm2_gain, norm2_bias, fc1_weight, fc1_bias, conv_weight, fc2_weight, fc2_bias, cotangent):
    params = tuple((argument.astype(jnp.float32) for argument in (norm1_gain, norm1_bias, qkv_weight, mix_pre, mix_post, proj_weight, proj_bias, norm2_gain, norm2_bias, fc1_weight, fc1_bias, conv_weight, fc2_weight, fc2_bias)))
    group_size = IMAGES // N_DP
    blocks = tokens.astype(jnp.float32).reshape(N_DP, group_size, SEQ, D)
    cotangents = cotangent.astype(jnp.float32).reshape(N_DP, group_size, SEQ, D)

    def accumulate(running, inputs_pair):
        inputs, grad_output = inputs_pair
        result, pullback = jax.vjp(forward, inputs, *params)
        gradients = pullback(grad_output)
        running = tuple((before + after for before, after in zip(running, gradients[1:])))
        return (running, (result.astype(jnp.bfloat16), gradients[0]))
    initial = tuple((jnp.zeros(argument.shape, jnp.float32) for argument in params))
    totals, (results, input_grads) = lax.scan(accumulate, initial, (blocks, cotangents))
    block_out = results.reshape(IMAGES, SEQ, D)
    grad_tokens = input_grads.reshape(IMAGES, SEQ, D)
    return (block_out, grad_tokens, totals[0], totals[1], totals[2], totals[3], totals[4], totals[5], totals[6], totals[7], totals[8], totals[9], totals[10], totals[11], totals[12], totals[13])
```

```python
import functools

import jax
import jax.numpy as jnp
import numpy as np
from jax import lax
from jax.experimental import pallas as pl
from jax.experimental.pallas import tpu as pltpu
from jax.sharding import PartitionSpec as P

HEADS = 6
HEAD_DIM = 64
KS = 7
GRID = 14
POINTS = 17
SEQ = 197
ROWS = 208
KEYS = 256
WIDTH = 384
HALF = 152
COEFS = 2 * HALF
CLASS_ROW = 145
CHUNK = 256
VMEM = 60 * 1024 * 1024

f32 = jnp.float32
bf16 = jnp.bfloat16


def fourier():
    pairs = [(0, 0)]
    for k in range(POINTS):
        for m in range(POINTS):
            other = ((-k) % POINTS, (-m) % POINTS)
            if (k, m) != (0, 0) and (k, m) < other:
                pairs.append((k, m))
    freq = np.array(pairs, np.float64)
    unit = 2.0 * np.pi / POINTS
    spots = np.array([(y, x) for y in range(GRID) for x in range(GRID)], np.float64)
    taps = np.array([(a - 3, c - 3) for a in range(KS) for c in range(KS)], np.float64)
    count = len(pairs)
    angle = unit * freq @ spots.T
    forward = np.zeros((COEFS, ROWS))
    forward[:count, 1:SEQ] = np.cos(angle)
    forward[HALF : HALF + count, 1:SEQ] = -np.sin(angle)
    forward[CLASS_ROW, 0] = 1.0
    weight = np.full((count, 1), 2.0)
    weight[0] = 1.0
    weight = weight / POINTS**2
    inverse = np.zeros((COEFS, ROWS))
    inverse[:count, 1:SEQ] = weight * np.cos(angle)
    inverse[HALF : HALF + count, 1:SEQ] = -weight * np.sin(angle)
    inverse[CLASS_ROW, 0] = 1.0
    turn = unit * freq @ taps.T
    kernel = np.zeros((COEFS, KS * KS))
    kernel[:count] = np.cos(turn)
    kernel[HALF : HALF + count] = np.sin(turn)
    back = np.zeros((COEFS, KS * KS))
    back[:count] = weight * np.cos(turn)
    back[HALF : HALF + count] = -weight * np.sin(turn)
    one = np.zeros((COEFS, 1))
    one[CLASS_ROW] = 1.0
    return forward, inverse.T, kernel, back.T, one


def split(matrix):
    high = np.asarray(matrix, np.float32).astype(bf16)
    low = (np.asarray(matrix, np.float32) - high.astype(np.float32)).astype(bf16)
    return high, low


def dot(a, b):
    return lax.dot_general(a, b, (((1,), (0,)), ((), ())), preferred_element_type=f32)


def dot_t(a, b):
    return lax.dot_general(a, b, (((1,), (1,)), ((), ())), preferred_element_type=f32)


def t_dot(a, b):
    return lax.dot_general(a, b, (((0,), (0,)), ((), ())), preferred_element_type=f32)


def centre(values):
    centred = values - jnp.mean(values, axis=-1, keepdims=True)
    spread = jnp.mean(centred * centred, axis=-1, keepdims=True)
    return centred, lax.rsqrt(spread + 1e-05)


def norm_back(centred, r, gain, grad):
    scaled = grad * gain
    moment = jnp.mean(scaled * centred, axis=-1, keepdims=True)
    back = r * (scaled - jnp.mean(scaled, axis=-1, keepdims=True) - centred * (r * r * moment))
    return back, grad * (centred * r)


def add_rows(values):
    return jnp.sum(values, axis=0, keepdims=True)


def row_mask(shape):
    return lax.broadcasted_iota(jnp.int32, shape, 0) < SEQ


def attention_forward(
    pre, post, tok, wqkv, wproj, gain1, bias1, pbias, gain2, bias2,
    n1_out, packed_out, probs_out, attn_out, att_out, mid_out, n2_out, pad, score, keys,
):
    pad[SEQ - 5 :] = jnp.zeros((ROWS - SEQ + 5, WIDTH), f32)
    pad[:SEQ] = tok[0].astype(f32)
    inputs = pad[...]
    centred, r = centre(inputs)
    inside = row_mask((ROWS, WIDTH))
    n1 = jnp.where(inside, centred * r * gain1[...] + bias1[...], 0.0).astype(bf16)
    n1_out[0] = n1
    packed = dot(n1, wqkv[...]).astype(bf16)
    packed_out[0, :ROWS] = packed
    packed_out[0, ROWS:] = jnp.zeros((KEYS - ROWS, 3 * WIDTH), bf16)
    low_half = lax.broadcasted_iota(jnp.int32, (ROWS, 128), 1) < HEAD_DIM
    zero = jnp.zeros((ROWS, 128), bf16)
    for p in range(HEADS // 2):
        query = packed_out[0, :ROWS, 128 * p : 128 * p + 128]
        key = packed_out[0, :, WIDTH + 128 * p : WIDTH + 128 * p + 128]
        score[2 * p] = dot_t(jnp.where(low_half, query, zero), key)
        score[2 * p + 1] = dot_t(jnp.where(low_half, zero, query), key)
    valid = lax.broadcasted_iota(jnp.int32, (16, KEYS), 1) < SEQ

    def rows_step(step, carry):
        rows = pl.ds(pl.multiple_of(step * 16, 16), 16)
        scores = [score[h, rows, :] for h in range(HEADS)]
        probs = []
        for g in range(HEADS):
            mixed = scores[0] * (pre[g, 0] * 0.125)
            for h in range(1, HEADS):
                mixed = mixed + scores[h] * (pre[g, h] * 0.125)
            mixed = jnp.where(valid, mixed, -1e30)
            top = jnp.max(mixed, axis=-1, keepdims=True)
            raised = jnp.exp(mixed - top)
            prob = raised * (1.0 / jnp.sum(raised, axis=-1, keepdims=True))
            probs_out[0, g, rows, :] = prob
            probs.append(prob)
        for g in range(HEADS):
            mixed = probs[0] * post[g, 0]
            for h in range(1, HEADS):
                mixed = mixed + probs[h] * post[g, h]
            attn_out[0, g, rows, :] = mixed.astype(bf16)
        return carry

    lax.fori_loop(0, ROWS // 16, rows_step, 0)
    pieces = []
    for p in range(HEADS // 2):
        value = packed_out[0, :, 2 * WIDTH + 128 * p : 2 * WIDTH + 128 * p + 128]
        pieces.append(
            jnp.where(low_half, dot(attn_out[0, 2 * p], value), dot(attn_out[0, 2 * p + 1], value))
        )
    attended = jnp.concatenate(pieces, axis=1).astype(bf16)
    att_out[0] = attended
    middle = inputs + (dot(attended, wproj[...]) + pbias[...])
    mid_out[0] = middle
    centred, r = centre(middle)
    n2_out[0] = jnp.where(inside, centred * r * gain2[...] + bias2[...], 0.0).astype(bf16)


def gelu_parts(hidden):
    size = jnp.abs(hidden) * np.float32(np.sqrt(0.5))
    t = 1.0 / (1.0 + 0.3275911 * size)
    raised = jnp.exp(-(size * size))
    series = t * (
        0.254829592
        + t * (-0.284496736 + t * (1.421413741 + t * (-1.453152027 + t * 1.061405429)))
    )
    tail = 0.5 * series * raised
    cdf = jnp.where(hidden < 0.0, tail, 1.0 - tail)
    return hidden * cdf, cdf + hidden * (raised * np.float32(1.0 / np.sqrt(2.0 * np.pi)))


def mlp(
    n2, cot, mid, fc1, fc1b, conv, fc2, fc2b, fwd, inv, kh, kl, bh, bl, one,
    block_out, gn2_out, gfc1_out, gb1_out, gconv_out, gfc2_out, gb2_out,
    cot_pad, pad, hid, grad, out_acc, conv_low, ghid_low,
):
    step = pl.program_id(0)
    images = n2.shape[0]

    @pl.when(step == 0)
    def _():
        total = jnp.zeros((1, WIDTH), f32)
        for b in range(images):
            pad[SEQ - 5 :] = jnp.zeros((ROWS - SEQ + 5, WIDTH), f32)
            pad[:SEQ] = cot[b].astype(f32)
            values = pad[...]
            total = total + add_rows(values)
            cot_pad[b * ROWS : (b + 1) * ROWS] = values.astype(bf16)
        gb2_out[...] = total

    w1 = fc1[...]
    w2 = fc2[...]
    taps = conv[...]
    turned = dot(kh[...], taps) + dot(kl[...], taps) + one[...]
    kr, ki = turned[:HALF], turned[HALF:]
    rows_all = n2[...].reshape(images * ROWS, WIDTH)
    hid[...] = dot(rows_all, w1) + fc1b[...].astype(f32)
    grad[...] = dot_t(cot_pad[...], w2)
    cross_r = jnp.zeros((HALF, CHUNK), f32)
    cross_i = jnp.zeros((HALF, CHUNK), f32)
    bias_sum = jnp.zeros((1, CHUNK), f32)
    for b in range(images):
        span = slice(b * ROWS, (b + 1) * ROWS)
        act, slope = gelu_parts(hid[span, :])
        x = dot(fwd[...], act.astype(bf16))
        y = dot(fwd[...], grad[span, :].astype(bf16))
        xr, xi = x[:HALF], x[HALF:]
        yr, yi = y[:HALF], y[HALF:]
        made = jnp.concatenate([xr * kr - xi * ki, xr * ki + xi * kr], axis=0).astype(bf16)
        back = jnp.concatenate([yr * kr + yi * ki, yi * kr - yr * ki], axis=0).astype(bf16)
        cross_r = cross_r + (xr * yr + xi * yi)
        cross_i = cross_i + (xi * yr - xr * yi)
        conv_low[span, :] = dot(inv[...], made).astype(bf16)
        ghid = (dot(inv[...], back) * slope).astype(bf16)
        bias_sum = bias_sum + add_rows(ghid.astype(f32))
        ghid_low[span, :] = ghid
    gb1_out[...] = bias_sum
    cross = jnp.concatenate([cross_r, cross_i], axis=0)
    high = cross.astype(bf16)
    low = (cross - high.astype(f32)).astype(bf16)
    gconv_out[...] = dot(bh[...], high) + dot(bl[...], high) + dot(bh[...], low)
    convolved = conv_low[...]
    ghid_all = ghid_low[...]
    part = dot(convolved, w2).reshape(images, ROWS, WIDTH)
    part_grad = dot_t(ghid_all, w1).reshape(images, ROWS, WIDTH)
    gfc2_out[...] = t_dot(convolved, cot_pad[...])
    gfc1_out[...] = t_dot(rows_all, ghid_all)

    @pl.when(step == 0)
    def _():
        out_acc[...] = part
        gn2_out[...] = part_grad

    @pl.when(step > 0)
    def _():
        out_acc[...] += part
        gn2_out[...] += part_grad

    @pl.when(step == pl.num_programs(0) - 1)
    def _():
        for b in range(images):
            result = mid[b] + (out_acc[b] + fc2b[...])
            block_out[b] = result[:SEQ].astype(bf16)


def attention_backward(
    pre, post, tok, cot, n1, packed, probs, attn, att, mid, gn2, wqkv, wproj, gain1, gain2,
    gtok_out, gqkv_out, gproj_out, rows_out, mix_out,
    pad, score, weight, low, mix,
):
    step = pl.program_id(0)

    @pl.when(step == 0)
    def _():
        gqkv_out[...] = jnp.zeros_like(gqkv_out)
        gproj_out[...] = jnp.zeros_like(gproj_out)
        rows_out[...] = jnp.zeros_like(rows_out)
        mix[...] = jnp.zeros_like(mix)

    pad[SEQ - 5 :] = jnp.zeros((ROWS - SEQ + 5, WIDTH), f32)
    pad[:SEQ] = cot[0].astype(f32)
    centred, r = centre(mid[0])
    grad = gn2[0]
    back, gain_rows = norm_back(centred, r, gain2[...], grad)
    rows_out[3:4] += add_rows(gain_rows)
    rows_out[4:5] += add_rows(grad)
    gmid = pad[...] + back
    gmid_low = gmid.astype(bf16)
    rows_out[2:3] += add_rows(gmid_low.astype(f32))
    gproj_out[...] += t_dot(att[0], gmid_low)
    gatt = dot_t(gmid_low, wproj[...]).astype(bf16)
    low_half = lax.broadcasted_iota(jnp.int32, (ROWS, 128), 1) < HEAD_DIM
    key_half = lax.broadcasted_iota(jnp.int32, (KEYS, 128), 1) < HEAD_DIM
    zero = jnp.zeros((ROWS, 128), bf16)
    for p in range(HEADS // 2):
        query = packed[0, :ROWS, 128 * p : 128 * p + 128]
        key = packed[0, :, WIDTH + 128 * p : WIDTH + 128 * p + 128]
        value = packed[0, :, 2 * WIDTH + 128 * p : 2 * WIDTH + 128 * p + 128]
        ahead = gatt[:, 128 * p : 128 * p + 128]
        score[2 * p] = dot_t(jnp.where(low_half, query, zero), key)
        score[2 * p + 1] = dot_t(jnp.where(low_half, zero, query), key)
        weight[2 * p] = dot_t(jnp.where(low_half, ahead, zero), value)
        weight[2 * p + 1] = dot_t(jnp.where(low_half, zero, ahead), value)

    def fold(values):
        values = values[:, :128] + values[:, 128:]
        return values[:8] + values[8:]

    def rows_step(index, carry):
        rows = pl.ds(pl.multiple_of(index * 16, 16), 16)
        weights = [weight[g, rows, :] for g in range(HEADS)]
        mixed = []
        for h in range(HEADS):
            prob = probs[0, h, rows, :]
            ahead = weights[0] * post[0, h]
            for g in range(1, HEADS):
                ahead = ahead + weights[g] * post[g, h]
            for g in range(HEADS):
                mix[HEADS * HEADS + g * HEADS + h] += fold(weights[g] * prob)
            inner = jnp.sum(prob * ahead, axis=-1, keepdims=True)
            mixed.append(prob * (ahead - inner))
        for h in range(HEADS):
            scores = score[h, rows, :]
            total = mixed[0] * pre[0, h]
            for g in range(1, HEADS):
                total = total + mixed[g] * pre[g, h]
            low[h, rows, :] = total.astype(bf16)
            for g in range(HEADS):
                mix[g * HEADS + h] += fold(mixed[g] * scores)
        return carry

    lax.fori_loop(0, ROWS // 16, rows_step, 0)
    queries, keys, values = [], [], []
    for p in range(HEADS // 2):
        query = packed[0, :ROWS, 128 * p : 128 * p + 128]
        key = packed[0, :, WIDTH + 128 * p : WIDTH + 128 * p + 128]
        ahead = gatt[:, 128 * p : 128 * p + 128]
        even, odd = low[2 * p], low[2 * p + 1]
        queries.append(jnp.where(low_half, dot(even, key), dot(odd, key)) * 0.125)
        keys.append(jnp.where(key_half, t_dot(even, query), t_dot(odd, query))[:ROWS] * 0.125)
        values.append(
            jnp.where(key_half, t_dot(attn[0, 2 * p], ahead), t_dot(attn[0, 2 * p + 1], ahead))[
                :ROWS
            ]
        )
    gpacked = jnp.concatenate(queries + keys + values, axis=1).astype(bf16)
    gqkv_out[...] += t_dot(n1[0], gpacked)
    gnormed = dot_t(gpacked, wqkv[...])
    pad[:SEQ] = tok[0].astype(f32)
    centred, r = centre(pad[...])
    back, gain_rows = norm_back(centred, r, gain1[...], gnormed)
    rows_out[0:1] += add_rows(gain_rows)
    rows_out[1:2] += add_rows(gnormed)
    gtok_out[0] = (gmid + back)[:SEQ]

    @pl.when(step == pl.num_programs(0) - 1)
    def _():
        mix_out[...] = jnp.sum(mix[...], axis=1)


def whole(shape):
    return pl.BlockSpec(shape, lambda *_: (0,) * len(shape))


def image(shape):
    return pl.BlockSpec((1,) + shape, lambda i: (i,) + (0,) * len(shape))


def params():
    return pltpu.CompilerParams(vmem_limit_bytes=VMEM, dimension_semantics=("arbitrary",))


def call_forward(tokens, wqkv, wproj, pre, post, gain1, bias1, pbias, gain2, bias2):
    images = tokens.shape[0]
    smem = pl.BlockSpec(memory_space=pltpu.SMEM)
    row = whole((1, WIDTH))
    return pl.pallas_call(
        attention_forward,
        grid=(images,),
        in_specs=[
            smem, smem, image((SEQ, WIDTH)), whole((WIDTH, 3 * WIDTH)), whole((WIDTH, WIDTH)),
            row, row, row, row, row,
        ],
        out_specs=[
            image((ROWS, WIDTH)), image((KEYS, 3 * WIDTH)), image((HEADS, ROWS, KEYS)),
            image((HEADS, ROWS, KEYS)), image((ROWS, WIDTH)), image((ROWS, WIDTH)),
            image((ROWS, WIDTH)),
        ],
        out_shape=[
            jax.ShapeDtypeStruct((images, ROWS, WIDTH), bf16),
            jax.ShapeDtypeStruct((images, KEYS, 3 * WIDTH), bf16),
            jax.ShapeDtypeStruct((images, HEADS, ROWS, KEYS), f32),
            jax.ShapeDtypeStruct((images, HEADS, ROWS, KEYS), bf16),
            jax.ShapeDtypeStruct((images, ROWS, WIDTH), bf16),
            jax.ShapeDtypeStruct((images, ROWS, WIDTH), f32),
            jax.ShapeDtypeStruct((images, ROWS, WIDTH), bf16),
        ],
        scratch_shapes=[
            pltpu.VMEM((ROWS, WIDTH), f32),
            pltpu.VMEM((HEADS, ROWS, KEYS), f32),
            pltpu.VMEM((8, 128), f32),
        ],
        compiler_params=params(),
        name="attention_forward",
    )(pre, post, tokens, wqkv, wproj, gain1, bias1, pbias, gain2, bias2)


def call_mlp(n2, cotangent, middle, fc1, fc1_bias, conv, fc2, fc2_bias):
    images = n2.shape[0]
    units = fc1.shape[1]
    steps = units // CHUNK
    forward, inverse, kernel, back, one = fourier()
    kernel_high, kernel_low = split(kernel)
    back_high, back_low = split(back)
    consts = [
        jnp.asarray(forward.astype(np.float32).astype(bf16)),
        jnp.asarray(inverse.astype(np.float32).astype(bf16)),
        jnp.asarray(kernel_high), jnp.asarray(kernel_low),
        jnp.asarray(back_high), jnp.asarray(back_low),
        jnp.asarray(one.astype(np.float32)),
    ]
    columns = lambda rows: pl.BlockSpec((rows, CHUNK), lambda i: (0, i))
    taps = KS * KS
    total = images * ROWS
    return pl.pallas_call(
        mlp,
        grid=(steps,),
        in_specs=[
            whole((images, ROWS, WIDTH)), whole((images, SEQ, WIDTH)), whole((images, ROWS, WIDTH)),
            columns(WIDTH), columns(1), columns(taps),
            pl.BlockSpec((CHUNK, WIDTH), lambda i: (i, 0)), whole((1, WIDTH)),
        ]
        + [whole(c.shape) for c in consts],
        out_specs=[
            whole((images, SEQ, WIDTH)), whole((images, ROWS, WIDTH)),
            columns(WIDTH), columns(1), columns(taps),
            pl.BlockSpec((CHUNK, WIDTH), lambda i: (i, 0)), whole((1, WIDTH)),
        ],
        out_shape=[
            jax.ShapeDtypeStruct((images, SEQ, WIDTH), bf16),
            jax.ShapeDtypeStruct((images, ROWS, WIDTH), f32),
            jax.ShapeDtypeStruct((WIDTH, units), f32),
            jax.ShapeDtypeStruct((1, units), f32),
            jax.ShapeDtypeStruct((taps, units), f32),
            jax.ShapeDtypeStruct((units, WIDTH), f32),
            jax.ShapeDtypeStruct((1, WIDTH), f32),
        ],
        scratch_shapes=[
            pltpu.VMEM((total, WIDTH), bf16),
            pltpu.VMEM((ROWS, WIDTH), f32),
            pltpu.VMEM((total, CHUNK), f32),
            pltpu.VMEM((total, CHUNK), f32),
            pltpu.VMEM((images, ROWS, WIDTH), f32),
            pltpu.VMEM((total, CHUNK), bf16),
            pltpu.VMEM((total, CHUNK), bf16),
        ],
        compiler_params=params(),
        name="mlp",
    )(n2, cotangent, middle, fc1, fc1_bias, conv, fc2, fc2_bias, *consts)


def call_backward(
    tokens, cotangent, n1, packed, probs, attn, att, mid, gn2, wqkv, wproj, pre, post, gain1, gain2
):
    images = tokens.shape[0]
    smem = pl.BlockSpec(memory_space=pltpu.SMEM)
    row = whole((1, WIDTH))
    return pl.pallas_call(
        attention_backward,
        grid=(images,),
        in_specs=[
            smem, smem, image((SEQ, WIDTH)), image((SEQ, WIDTH)), image((ROWS, WIDTH)),
            image((KEYS, 3 * WIDTH)), image((HEADS, ROWS, KEYS)), image((HEADS, ROWS, KEYS)),
            image((ROWS, WIDTH)), image((ROWS, WIDTH)), image((ROWS, WIDTH)),
            whole((WIDTH, 3 * WIDTH)), whole((WIDTH, WIDTH)), row, row,
        ],
        out_specs=[
            image((SEQ, WIDTH)), whole((WIDTH, 3 * WIDTH)), whole((WIDTH, WIDTH)),
            whole((8, WIDTH)), whole((2 * HEADS * HEADS, 128)),
        ],
        out_shape=[
            jax.ShapeDtypeStruct((images, SEQ, WIDTH), f32),
            jax.ShapeDtypeStruct((WIDTH, 3 * WIDTH), f32),
            jax.ShapeDtypeStruct((WIDTH, WIDTH), f32),
            jax.ShapeDtypeStruct((8, WIDTH), f32),
            jax.ShapeDtypeStruct((2 * HEADS * HEADS, 128), f32),
        ],
        scratch_shapes=[
            pltpu.VMEM((ROWS, WIDTH), f32),
            pltpu.VMEM((HEADS, ROWS, KEYS), f32),
            pltpu.VMEM((HEADS, ROWS, KEYS), f32),
            pltpu.VMEM((HEADS, ROWS, KEYS), bf16),
            pltpu.VMEM((2 * HEADS * HEADS, 8, 128), f32),
        ],
        compiler_params=params(),
        name="attention_backward",
    )(
        pre, post, tokens, cotangent, n1, packed, probs, attn, att, mid, gn2, wqkv, wproj,
        gain1, gain2,
    )


def local_block(
    tokens, norm1_gain, norm1_bias, wqkv, mix_pre, mix_post, wproj, proj_bias, norm2_gain,
    norm2_bias, fc1, fc1_bias, conv, fc2, fc2_bias, cotangent,
):
    row = lambda v: v.reshape(1, -1)
    gain1, gain2 = row(norm1_gain), row(norm2_gain)
    n1, packed, probs, attn, att, mid, n2 = call_forward(
        tokens, wqkv, wproj, mix_pre, mix_post, gain1, row(norm1_bias), row(proj_bias), gain2,
        row(norm2_bias),
    )
    block_out, gn2, gfc1, gb1, gconv, gfc2, gb2 = call_mlp(
        n2, cotangent, mid, fc1, row(fc1_bias), conv, fc2, row(fc2_bias)
    )
    gtok, gqkv, gproj, rows, mix = call_backward(
        tokens, cotangent, n1, packed, probs, attn, att, mid, gn2, wqkv, wproj, mix_pre, mix_post,
        gain1, gain2,
    )
    return block_out, gtok, gqkv, gproj, gfc1, gb1, gconv, gfc2, gb2, rows, mix


def shards(
    tokens, norm1_gain, norm1_bias, qkv_weight, mix_pre, mix_post, proj_weight, proj_bias,
    norm2_gain, norm2_bias, fc1_weight, fc1_bias, conv_weight, fc2_weight, fc2_bias, cotangent,
):
    gather = lambda v, axis, dim: lax.all_gather(v, axis, axis=dim, tiled=True)
    both = jnp.concatenate([qkv_weight, proj_weight], axis=1)
    rows = gather(both, "dp", 0)
    pair = lax.all_gather(rows, "tensor", axis=0)
    columns = qkv_weight.shape[1]
    wqkv = jnp.concatenate([pair[0, :, :columns], pair[1, :, :columns]], axis=1)
    wproj = jnp.concatenate([pair[0, :, columns:], pair[1, :, columns:]], axis=1)
    fc1 = gather(fc1_weight, "tensor", 1)
    fc1b = gather(fc1_bias, "tensor", 0)
    conv = gather(conv_weight, "tensor", 1)
    fc2 = gather(fc2_weight, "tensor", 0)
    block_out, gtok, gqkv, gproj, gfc1, gb1, gconv, gfc2, gb2, rows, mix = local_block(
        tokens, norm1_gain, norm1_bias, wqkv, mix_pre, mix_post, wproj, proj_bias, norm2_gain,
        norm2_bias, fc1, fc1b, conv, fc2, fc2_bias, cotangent,
    )
    scatter = lambda v, axis, dim: lax.psum_scatter(v, axis, scatter_dimension=dim, tiled=True)
    gqkv = scatter(scatter(gqkv.astype(bf16), "tensor", 1).astype(f32), "dp", 0)
    gproj = scatter(scatter(gproj.astype(bf16), "tensor", 1).astype(f32), "dp", 0)
    gfc1 = lax.psum(scatter(gfc1.astype(bf16), "tensor", 1).astype(f32), "dp")
    gfc2 = lax.psum(scatter(gfc2.astype(bf16), "tensor", 0).astype(f32), "dp")
    gconv = lax.psum(scatter(gconv, "tensor", 1), "dp")
    gb1 = lax.psum(scatter(gb1[0], "tensor", 0), "dp")
    mixes = jnp.sum(mix, axis=1).reshape(2, HEADS, HEADS)
    rows, gb2, mixes = lax.psum((rows, gb2, mixes), ("dp", "tensor"))
    return (
        block_out, gtok, rows[0], rows[1], gqkv, mixes[0] * 0.125, mixes[1], gproj, rows[2],
        rows[3], rows[4], gfc1, gb1, gconv, gfc2, gb2[0],
    )


def solution(mesh):
    spec = P(("dp", "tensor"), None, None)
    in_specs = (
        spec, P(), P(), P("dp", "tensor"), P(), P(), P("dp", "tensor"), P(), P(), P(),
        P(None, "tensor"), P("tensor"), P(None, "tensor"), P("tensor", None), P(), spec,
    )
    out_specs = (
        spec, spec, P(), P(), P("dp", "tensor"), P(), P(), P("dp", "tensor"), P(), P(), P(),
        P(None, "tensor"), P("tensor"), P(None, "tensor"), P("tensor", None), P(),
    )
    return jax.shard_map(shards, mesh=mesh, in_specs=in_specs, out_specs=out_specs, check_vma=False)
```

```python
import functools

import jax
import jax.numpy as jnp
import numpy as np
from jax import lax
from jax.experimental import pallas as pl
from jax.experimental.pallas import tpu as pltpu
from jax.sharding import PartitionSpec as P

HEADS = 6
HEAD_DIM = 64
KS = 7
GRID = 14
POINTS = 17
SEQ = 197
ROWS = 208
TAPS = 64
KEYS = 256
WIDTH = 384
HALF = 152
COEFS = 2 * HALF
CLASS_ROW = 145
CHUNK = 256
SMALL = 32
VMEM = 60 * 1024 * 1024

f32 = jnp.float32
bf16 = jnp.bfloat16


def fourier():
    pairs = [(0, 0)]
    for k in range(POINTS):
        for m in range(POINTS):
            other = ((-k) % POINTS, (-m) % POINTS)
            if (k, m) != (0, 0) and (k, m) < other:
                pairs.append((k, m))
    freq = np.array(pairs, np.float64)
    unit = 2.0 * np.pi / POINTS
    spots = np.array([(y, x) for y in range(GRID) for x in range(GRID)], np.float64)
    taps = np.array([(a - 3, c - 3) for a in range(KS) for c in range(KS)], np.float64)
    count = len(pairs)
    angle = unit * freq @ spots.T
    forward = np.zeros((COEFS, ROWS))
    forward[:count, 1:SEQ] = np.cos(angle)
    forward[HALF : HALF + count, 1:SEQ] = -np.sin(angle)
    forward[CLASS_ROW, 0] = 1.0
    weight = np.full((count, 1), 2.0)
    weight[0] = 1.0
    weight = weight / POINTS**2
    inverse = np.zeros((COEFS, ROWS))
    inverse[:count, 1:SEQ] = weight * np.cos(angle)
    inverse[HALF : HALF + count, 1:SEQ] = -weight * np.sin(angle)
    inverse[CLASS_ROW, 0] = 1.0
    turn = unit * freq @ taps.T
    kernel = np.zeros((COEFS, TAPS))
    kernel[:count, : KS * KS] = np.cos(turn)
    kernel[HALF : HALF + count, : KS * KS] = np.sin(turn)
    back = np.zeros((COEFS, TAPS))
    back[:count, : KS * KS] = weight * np.cos(turn)
    back[HALF : HALF + count, : KS * KS] = -weight * np.sin(turn)
    one = np.zeros((COEFS, 1))
    one[CLASS_ROW] = 1.0
    return forward, inverse.T, kernel, back.T, one


def split(matrix):
    high = np.asarray(matrix, np.float32).astype(bf16)
    low = (np.asarray(matrix, np.float32) - high.astype(np.float32)).astype(bf16)
    return high, low


def dot(a, b):
    return lax.dot_general(a, b, (((1,), (0,)), ((), ())), preferred_element_type=f32)


def dot_t(a, b):
    return lax.dot_general(a, b, (((1,), (1,)), ((), ())), preferred_element_type=f32)


def t_dot(a, b):
    return lax.dot_general(a, b, (((0,), (0,)), ((), ())), preferred_element_type=f32)


def centre(values):
    centred = values - jnp.mean(values, axis=-1, keepdims=True)
    spread = jnp.mean(centred * centred, axis=-1, keepdims=True)
    return centred, lax.rsqrt(spread + 1e-05)


def norm_back(centred, r, gain, grad):
    scaled = grad * gain
    moment = jnp.mean(scaled * centred, axis=-1, keepdims=True)
    back = r * (scaled - jnp.mean(scaled, axis=-1, keepdims=True) - centred * (r * r * moment))
    return back, grad * (centred * r)


def row(ref):
    return ref[...].reshape(1, ref.shape[0])


def add_rows(values):
    return jnp.sum(values, axis=0, keepdims=True)


def row_mask(shape):
    return lax.broadcasted_iota(jnp.int32, shape, 0) < SEQ


def attention_forward(
    pre, post, tok, wqkv, wproj, gain1, bias1, pbias, gain2, bias2,
    n1_out, packed_out, probs_out, attn_out, att_out, mid_out, n2_out, pad, score, keys,
):
    pad[SEQ - 5 :] = jnp.zeros((ROWS - SEQ + 5, WIDTH), f32)
    pad[:SEQ] = tok[0].astype(f32)
    inputs = pad[...]
    centred, r = centre(inputs)
    inside = row_mask((ROWS, WIDTH))
    n1 = jnp.where(inside, centred * r * row(gain1) + row(bias1), 0.0).astype(bf16)
    n1_out[0] = n1
    packed = dot(n1, wqkv[...]).astype(bf16)
    packed_out[0, :ROWS] = packed
    packed_out[0, ROWS:] = jnp.zeros((KEYS - ROWS, 3 * WIDTH), bf16)
    low_half = lax.broadcasted_iota(jnp.int32, (ROWS, 128), 1) < HEAD_DIM
    zero = jnp.zeros((ROWS, 128), bf16)
    for p in range(HEADS // 2):
        query = packed_out[0, :ROWS, 128 * p : 128 * p + 128]
        key = packed_out[0, :, WIDTH + 128 * p : WIDTH + 128 * p + 128]
        score[2 * p] = dot_t(jnp.where(low_half, query, zero), key)
        score[2 * p + 1] = dot_t(jnp.where(low_half, zero, query), key)
    valid = lax.broadcasted_iota(jnp.int32, (16, KEYS), 1) < SEQ

    def rows_step(step, carry):
        rows = pl.ds(pl.multiple_of(step * 16, 16), 16)
        scores = [score[h, rows, :] for h in range(HEADS)]
        probs = []
        for g in range(HEADS):
            mixed = scores[0] * (pre[g, 0] * 0.125)
            for h in range(1, HEADS):
                mixed = mixed + scores[h] * (pre[g, h] * 0.125)
            mixed = jnp.where(valid, mixed, -1e30)
            top = jnp.max(mixed, axis=-1, keepdims=True)
            raised = jnp.exp(mixed - top)
            prob = raised * (1.0 / jnp.sum(raised, axis=-1, keepdims=True))
            probs_out[0, g, rows, :] = prob
            probs.append(prob)
        for g in range(HEADS):
            mixed = probs[0] * post[g, 0]
            for h in range(1, HEADS):
                mixed = mixed + probs[h] * post[g, h]
            attn_out[0, g, rows, :] = mixed.astype(bf16)
        return carry

    lax.fori_loop(0, ROWS // 16, rows_step, 0)
    pieces = []
    for p in range(HEADS // 2):
        value = packed_out[0, :, 2 * WIDTH + 128 * p : 2 * WIDTH + 128 * p + 128]
        pieces.append(
            jnp.where(low_half, dot(attn_out[0, 2 * p], value), dot(attn_out[0, 2 * p + 1], value))
        )
    attended = jnp.concatenate(pieces, axis=1).astype(bf16)
    att_out[0] = attended
    middle = inputs + (dot(attended, wproj[...]) + row(pbias))
    mid_out[0] = middle
    centred, r = centre(middle)
    n2_out[0] = jnp.where(inside, centred * r * row(gain2) + row(bias2), 0.0).astype(bf16)


def gelu_parts(hidden):
    size = jnp.abs(hidden) * np.float32(np.sqrt(0.5))
    t = 1.0 / (1.0 + 0.3275911 * size)
    raised = jnp.exp(-(size * size))
    series = t * (
        0.254829592
        + t * (-0.284496736 + t * (1.421413741 + t * (-1.453152027 + t * 1.061405429)))
    )
    tail = 0.5 * series * raised
    cdf = jnp.where(hidden < 0.0, tail, 1.0 - tail)
    return hidden * cdf, cdf + hidden * (raised * np.float32(1.0 / np.sqrt(2.0 * np.pi)))


def mlp(
    n2, cot, mid, fc1, conv, fc2, fc2b, fwd, inv, kh, kl, bh, bl, one,
    block_out, gn2_out, gfc1_out, gconv_out, gfc2_out, gb2_out,
    cot_pad, pad, hid, grad, out_acc, conv_low, ghid_low,
):
    step = pl.program_id(0)
    images = n2.shape[0]

    @pl.when(step == 0)
    def _():
        total = jnp.zeros((1, WIDTH), f32)
        for b in range(images):
            pad[SEQ - 5 :] = jnp.zeros((ROWS - SEQ + 5, WIDTH), f32)
            pad[:SEQ] = cot[b].astype(f32)
            values = pad[...]
            total = total + add_rows(values)
            cot_pad[b * ROWS : (b + 1) * ROWS] = values.astype(bf16)
        gb2_out[...] = total

    w1 = fc1[...]
    w2 = fc2[...]
    taps = conv[...]
    turned = dot(kh[...], taps) + dot(kl[...], taps) + one[...]
    kr, ki = turned[:HALF], turned[HALF:]
    rows_all = n2[...].reshape(images * ROWS, WIDTH)
    hid[...] = dot(rows_all, w1) + taps.astype(f32)[KS * KS : KS * KS + 1]
    grad[...] = dot_t(cot_pad[...], w2)
    cross_r = jnp.zeros((HALF, CHUNK), f32)
    cross_i = jnp.zeros((HALF, CHUNK), f32)
    bias_sum = jnp.zeros((1, CHUNK), f32)
    for b in range(images):
        span = slice(b * ROWS, (b + 1) * ROWS)
        act, slope = gelu_parts(hid[span, :])
        x = dot(fwd[...], act.astype(bf16))
        y = dot(fwd[...], grad[span, :].astype(bf16))
        xr, xi = x[:HALF], x[HALF:]
        yr, yi = y[:HALF], y[HALF:]
        made = jnp.concatenate([xr * kr - xi * ki, xr * ki + xi * kr], axis=0).astype(bf16)
        back = jnp.concatenate([yr * kr + yi * ki, yi * kr - yr * ki], axis=0).astype(bf16)
        cross_r = cross_r + (xr * yr + xi * yi)
        cross_i = cross_i + (xi * yr - xr * yi)
        conv_low[span, :] = dot(inv[...], made).astype(bf16)
        ghid = (dot(inv[...], back) * slope).astype(bf16)
        bias_sum = bias_sum + add_rows(ghid.astype(f32))
        ghid_low[span, :] = ghid
    cross = jnp.concatenate([cross_r, cross_i], axis=0)
    high = cross.astype(bf16)
    low = (cross - high.astype(f32)).astype(bf16)
    gconv_out[...] = dot(bh[...], high) + dot(bl[...], high) + dot(bh[...], low)
    gconv_out[KS * KS : KS * KS + 1] = bias_sum
    convolved = conv_low[...]
    ghid_all = ghid_low[...]
    part = dot(convolved, w2).reshape(images, ROWS, WIDTH)
    part_grad = dot_t(ghid_all, w1).reshape(images, ROWS, WIDTH)
    gfc2_out[...] = t_dot(convolved, cot_pad[...])
    gfc1_out[...] = t_dot(rows_all, ghid_all)

    @pl.when(step == 0)
    def _():
        out_acc[...] = part
        gn2_out[...] = part_grad

    @pl.when(step > 0)
    def _():
        out_acc[...] += part
        gn2_out[...] += part_grad

    @pl.when(step == pl.num_programs(0) - 1)
    def _():
        for b in range(images):
            result = mid[b] + (out_acc[b] + row(fc2b))
            block_out[b] = result[:SEQ].astype(bf16)


def attention_backward(
    pre, post, tok, cot, n1, packed, probs, attn, att, mid, gn2, wqkv, wproj, gain1, gain2, gb2,
    gtok_out, gqkv_out, gproj_out, small_out,
    pad, score, weight, low, mix, rows_out, square,
):
    step = pl.program_id(0)

    @pl.when(step == 0)
    def _():
        gqkv_out[...] = jnp.zeros_like(gqkv_out)
        gproj_out[...] = jnp.zeros_like(gproj_out)
        rows_out[...] = jnp.zeros_like(rows_out)
        mix[...] = jnp.zeros_like(mix)

    pad[SEQ - 5 :] = jnp.zeros((ROWS - SEQ + 5, WIDTH), f32)
    pad[:SEQ] = cot[0].astype(f32)
    centred, r = centre(mid[0])
    grad = gn2[0]
    back, gain_rows = norm_back(centred, r, row(gain2), grad)
    rows_out[3:4] += add_rows(gain_rows)
    rows_out[4:5] += add_rows(grad)
    gmid = pad[...] + back
    gmid_low = gmid.astype(bf16)
    rows_out[2:3] += add_rows(gmid_low.astype(f32))
    gproj_out[...] += t_dot(att[0], gmid_low)
    gatt = dot_t(gmid_low, wproj[...]).astype(bf16)
    low_half = lax.broadcasted_iota(jnp.int32, (ROWS, 128), 1) < HEAD_DIM
    key_half = lax.broadcasted_iota(jnp.int32, (KEYS, 128), 1) < HEAD_DIM
    zero = jnp.zeros((ROWS, 128), bf16)
    for p in range(HEADS // 2):
        query = packed[0, :ROWS, 128 * p : 128 * p + 128]
        key = packed[0, :, WIDTH + 128 * p : WIDTH + 128 * p + 128]
        value = packed[0, :, 2 * WIDTH + 128 * p : 2 * WIDTH + 128 * p + 128]
        ahead = gatt[:, 128 * p : 128 * p + 128]
        score[2 * p] = dot_t(jnp.where(low_half, query, zero), key)
        score[2 * p + 1] = dot_t(jnp.where(low_half, zero, query), key)
        weight[2 * p] = dot_t(jnp.where(low_half, ahead, zero), value)
        weight[2 * p + 1] = dot_t(jnp.where(low_half, zero, ahead), value)

    def fold(values):
        values = values[:, :128] + values[:, 128:]
        return values[:8] + values[8:]

    def rows_step(index, carry):
        rows = pl.ds(pl.multiple_of(index * 16, 16), 16)
        weights = [weight[g, rows, :] for g in range(HEADS)]
        mixed = []
        for h in range(HEADS):
            prob = probs[0, h, rows, :]
            ahead = weights[0] * post[0, h]
            for g in range(1, HEADS):
                ahead = ahead + weights[g] * post[g, h]
            for g in range(HEADS):
                mix[HEADS * HEADS + g * HEADS + h] += fold(weights[g] * prob)
            inner = jnp.sum(prob * ahead, axis=-1, keepdims=True)
            mixed.append(prob * (ahead - inner))
        for h in range(HEADS):
            scores = score[h, rows, :]
            total = mixed[0] * pre[0, h]
            for g in range(1, HEADS):
                total = total + mixed[g] * pre[g, h]
            low[h, rows, :] = total.astype(bf16)
            for g in range(HEADS):
                mix[g * HEADS + h] += fold(mixed[g] * scores)
        return carry

    lax.fori_loop(0, ROWS // 16, rows_step, 0)
    queries, keys, values = [], [], []
    for p in range(HEADS // 2):
        query = packed[0, :ROWS, 128 * p : 128 * p + 128]
        key = packed[0, :, WIDTH + 128 * p : WIDTH + 128 * p + 128]
        ahead = gatt[:, 128 * p : 128 * p + 128]
        even, odd = low[2 * p], low[2 * p + 1]
        queries.append(jnp.where(low_half, dot(even, key), dot(odd, key)) * 0.125)
        keys.append(jnp.where(key_half, t_dot(even, query), t_dot(odd, query))[:ROWS] * 0.125)
        values.append(
            jnp.where(key_half, t_dot(attn[0, 2 * p], ahead), t_dot(attn[0, 2 * p + 1], ahead))[
                :ROWS
            ]
        )
    gpacked = jnp.concatenate(queries + keys + values, axis=1).astype(bf16)
    gqkv_out[...] += t_dot(n1[0], gpacked)
    gnormed = dot_t(gpacked, wqkv[...])
    pad[:SEQ] = tok[0].astype(f32)
    centred, r = centre(pad[...])
    back, gain_rows = norm_back(centred, r, row(gain1), gnormed)
    rows_out[0:1] += add_rows(gain_rows)
    rows_out[1:2] += add_rows(gnormed)
    gtok_out[0] = (gmid + back)[:SEQ]

    @pl.when(step == pl.num_programs(0) - 1)
    def _():
        rows_out[5:6] = gb2[...]
        for t in range(WIDTH // 128):
            small_out[8 * t : 8 * t + 8] = rows_out[:, 128 * t : 128 * t + 128]
        square[...] = jnp.zeros_like(square)
        square[: 2 * HEADS * HEADS] = jnp.sum(mix[...], axis=1)
        sums = add_rows(square[...].T)
        small_out[24:] = jnp.concatenate([sums, jnp.zeros((SMALL - 25, 128), f32)], axis=0)


def whole(shape):
    return pl.BlockSpec(shape, lambda *_: (0,) * len(shape))


def image(shape):
    return pl.BlockSpec((1,) + shape, lambda i: (i,) + (0,) * len(shape))


def params():
    return pltpu.CompilerParams(vmem_limit_bytes=VMEM, dimension_semantics=("arbitrary",))


def call_forward(tokens, wqkv, wproj, pre, post, gain1, bias1, pbias, gain2, bias2):
    images = tokens.shape[0]
    smem = pl.BlockSpec(memory_space=pltpu.SMEM)
    vector = whole((WIDTH,))
    return pl.pallas_call(
        attention_forward,
        grid=(images,),
        in_specs=[
            smem, smem, image((SEQ, WIDTH)), whole((WIDTH, 3 * WIDTH)), whole((WIDTH, WIDTH)),
            vector, vector, vector, vector, vector,
        ],
        out_specs=[
            image((ROWS, WIDTH)), image((KEYS, 3 * WIDTH)), image((HEADS, ROWS, KEYS)),
            image((HEADS, ROWS, KEYS)), image((ROWS, WIDTH)), image((ROWS, WIDTH)),
            image((ROWS, WIDTH)),
        ],
        out_shape=[
            jax.ShapeDtypeStruct((images, ROWS, WIDTH), bf16),
            jax.ShapeDtypeStruct((images, KEYS, 3 * WIDTH), bf16),
            jax.ShapeDtypeStruct((images, HEADS, ROWS, KEYS), f32),
            jax.ShapeDtypeStruct((images, HEADS, ROWS, KEYS), bf16),
            jax.ShapeDtypeStruct((images, ROWS, WIDTH), bf16),
            jax.ShapeDtypeStruct((images, ROWS, WIDTH), f32),
            jax.ShapeDtypeStruct((images, ROWS, WIDTH), bf16),
        ],
        scratch_shapes=[
            pltpu.VMEM((ROWS, WIDTH), f32),
            pltpu.VMEM((HEADS, ROWS, KEYS), f32),
            pltpu.VMEM((8, 128), f32),
        ],
        compiler_params=params(),
        name="attention_forward",
    )(pre, post, tokens, wqkv, wproj, gain1, bias1, pbias, gain2, bias2)


def call_mlp(n2, cotangent, middle, fc1, conv, fc2, fc2_bias):
    images = n2.shape[0]
    units = fc1.shape[1]
    steps = units // CHUNK
    forward, inverse, kernel, back, one = fourier()
    kernel_high, kernel_low = split(kernel)
    back_high, back_low = split(back)
    consts = [
        jnp.asarray(forward.astype(np.float32).astype(bf16)),
        jnp.asarray(inverse.astype(np.float32).astype(bf16)),
        jnp.asarray(kernel_high), jnp.asarray(kernel_low),
        jnp.asarray(back_high), jnp.asarray(back_low),
        jnp.asarray(one.astype(np.float32)),
    ]
    columns = lambda rows: pl.BlockSpec((rows, CHUNK), lambda i: (0, i))
    total = images * ROWS
    return pl.pallas_call(
        mlp,
        grid=(steps,),
        in_specs=[
            whole((images, ROWS, WIDTH)), whole((images, SEQ, WIDTH)), whole((images, ROWS, WIDTH)),
            columns(WIDTH), columns(TAPS),
            pl.BlockSpec((CHUNK, WIDTH), lambda i: (i, 0)), whole((WIDTH,)),
        ]
        + [whole(c.shape) for c in consts],
        out_specs=[
            whole((images, SEQ, WIDTH)), whole((images, ROWS, WIDTH)),
            columns(WIDTH), columns(TAPS),
            pl.BlockSpec((CHUNK, WIDTH), lambda i: (i, 0)), whole((1, WIDTH)),
        ],
        out_shape=[
            jax.ShapeDtypeStruct((images, SEQ, WIDTH), bf16),
            jax.ShapeDtypeStruct((images, ROWS, WIDTH), f32),
            jax.ShapeDtypeStruct((WIDTH, units), f32),
            jax.ShapeDtypeStruct((TAPS, units), f32),
            jax.ShapeDtypeStruct((units, WIDTH), f32),
            jax.ShapeDtypeStruct((1, WIDTH), f32),
        ],
        scratch_shapes=[
            pltpu.VMEM((total, WIDTH), bf16),
            pltpu.VMEM((ROWS, WIDTH), f32),
            pltpu.VMEM((total, CHUNK), f32),
            pltpu.VMEM((total, CHUNK), f32),
            pltpu.VMEM((images, ROWS, WIDTH), f32),
            pltpu.VMEM((total, CHUNK), bf16),
            pltpu.VMEM((total, CHUNK), bf16),
        ],
        compiler_params=params(),
        name="mlp",
    )(n2, cotangent, middle, fc1, conv, fc2, fc2_bias, *consts)


def call_backward(
    tokens, cotangent, n1, packed, probs, attn, att, mid, gn2, wqkv, wproj, pre, post, gain1, gain2, gb2
):
    images = tokens.shape[0]
    smem = pl.BlockSpec(memory_space=pltpu.SMEM)
    vector = whole((WIDTH,))
    return pl.pallas_call(
        attention_backward,
        grid=(images,),
        in_specs=[
            smem, smem, image((SEQ, WIDTH)), image((SEQ, WIDTH)), image((ROWS, WIDTH)),
            image((KEYS, 3 * WIDTH)), image((HEADS, ROWS, KEYS)), image((HEADS, ROWS, KEYS)),
            image((ROWS, WIDTH)), image((ROWS, WIDTH)), image((ROWS, WIDTH)),
            whole((WIDTH, 3 * WIDTH)), whole((WIDTH, WIDTH)), vector, vector,
            whole((1, WIDTH)),
        ],
        out_specs=[
            image((SEQ, WIDTH)), whole((WIDTH, 3 * WIDTH)), whole((WIDTH, WIDTH)),
            whole((SMALL, 128)),
        ],
        out_shape=[
            jax.ShapeDtypeStruct((images, SEQ, WIDTH), f32),
            jax.ShapeDtypeStruct((WIDTH, 3 * WIDTH), f32),
            jax.ShapeDtypeStruct((WIDTH, WIDTH), f32),
            jax.ShapeDtypeStruct((SMALL, 128), f32),
        ],
        scratch_shapes=[
            pltpu.VMEM((ROWS, WIDTH), f32),
            pltpu.VMEM((HEADS, ROWS, KEYS), f32),
            pltpu.VMEM((HEADS, ROWS, KEYS), f32),
            pltpu.VMEM((HEADS, ROWS, KEYS), bf16),
            pltpu.VMEM((2 * HEADS * HEADS, 8, 128), f32),
            pltpu.VMEM((8, WIDTH), f32),
            pltpu.VMEM((128, 128), f32),
        ],
        compiler_params=params(),
        name="attention_backward",
    )(
        pre, post, tokens, cotangent, n1, packed, probs, attn, att, mid, gn2, wqkv, wproj,
        gain1, gain2, gb2,
    )


def local_block(
    tokens, norm1_gain, norm1_bias, wqkv, mix_pre, mix_post, wproj, proj_bias, norm2_gain,
    norm2_bias, fc1, taps, fc2, fc2_bias, cotangent,
):
    n1, packed, probs, attn, att, mid, n2 = call_forward(
        tokens, wqkv, wproj, mix_pre, mix_post, norm1_gain, norm1_bias, proj_bias, norm2_gain,
        norm2_bias,
    )
    block_out, gn2, gfc1, gconv, gfc2, gb2 = call_mlp(n2, cotangent, mid, fc1, taps, fc2, fc2_bias)
    gtok, gqkv, gproj, small = call_backward(
        tokens, cotangent, n1, packed, probs, attn, att, mid, gn2, wqkv, wproj, mix_pre, mix_post,
        norm1_gain, norm2_gain, gb2,
    )
    return block_out, gtok, gqkv, gproj, gfc1, gconv, gfc2, small


SIDES = (8, 4, 2, 1)
ORDERS = ((3, 2, 1, 0), (2, 1, 0, 3), (1, 0, 3, 2))
MESH_IDS = pl.DeviceIdType.MESH
PIECE = 144
BLOCK = 320


def place():
    dp, core = lax.axis_index("dp"), lax.axis_index("tensor")
    bits = [lax.rem(dp // stride, 2) for stride in SIDES]
    partners = [(dp + (1 - 2 * bit) * stride, core) for bit, stride in zip(bits, SIDES)]
    return bits, partners, (dp, 1 - core), core


def meet(partners):
    barrier = pltpu.get_barrier_semaphore()
    for partner in partners:
        pl.semaphore_signal(barrier, inc=1, device_id=partner, device_id_type=MESH_IDS)
    pl.semaphore_wait(barrier, len(partners))


def send(src, dst, sems, index, device):
    copy = pltpu.make_async_remote_copy(
        src_ref=src, dst_ref=dst, send_sem=sems.at[0, index], recv_sem=sems.at[1, index],
        device_id=device, device_id_type=MESH_IDS,
    )
    copy.start()
    return copy


def region(fixed, rows):
    return tuple(fixed.get(axis, slice(None)) for axis in range(4)) + (rows,)


def combos(count):
    return [tuple((i >> (count - 1 - j)) & 1 for j in range(count)) for i in range(2**count)]


class Halving:
    def __init__(self, acc, landing, sems, first, parts, bits, partners):
        self.acc, self.landing, self.sems, self.first = acc, landing, sems, first
        self.parts, self.bits, self.partners = parts, bits, partners
        self.copies = {}

    def start(self, part, step):
        order, rows = ORDERS[part], pl.ds(*self.parts[part])
        axis = order[step]
        fixed = {a: self.bits[a] for a in order[:step]}
        fixed[axis] = 1 - self.bits[axis]
        dst = self.landing[step].at[(slice(None),) * (3 - step) + (rows,)]
        self.copies[part, step] = send(
            self.acc.at[region(fixed, rows)], dst, self.sems,
            self.first + step * len(self.parts) + part, self.partners[axis],
        )

    def add(self, part, step):
        order, rows = ORDERS[part], pl.ds(*self.parts[part])
        self.copies[part, step].wait_recv()
        fixed = {a: self.bits[a] for a in order[: step + 1]}
        free = [a for a in range(4) if a not in fixed]
        for combo in combos(len(free)):
            where = region({**fixed, **dict(zip(free, combo))}, rows)
            came = self.landing[step][combo + (rows,)]
            self.acc[where] = (self.acc[where].astype(f32) + came.astype(f32)).astype(bf16)

    def finish(self):
        for copy in self.copies.values():
            copy.wait_send()


class Doubling:
    def __init__(self, full, sems, first, parts, bits, partners):
        self.full, self.sems, self.first = full, sems, first
        self.parts, self.bits, self.partners = parts, bits, partners
        self.copies = {}

    def held(self, part, step):
        order, rows = ORDERS[part][::-1], pl.ds(*self.parts[part])
        return region({a: self.bits[a] for a in order[step:]}, rows)

    def come(self, part, step):
        order, rows = ORDERS[part][::-1], pl.ds(*self.parts[part])
        fixed = {a: self.bits[a] for a in order[step + 1 :]}
        fixed[order[step]] = 1 - self.bits[order[step]]
        return region(fixed, rows)

    def start(self, part, step):
        axis = ORDERS[part][::-1][step]
        where = self.held(part, step)
        self.copies[part, step] = send(
            self.full.at[where], self.full.at[where], self.sems,
            self.first + step * len(self.parts) + part, self.partners[axis],
        )

    def wait(self, part, step):
        self.copies[part, step].wait_recv()

    def finish(self):
        for copy in self.copies.values():
            copy.wait_send()


def tiles(values):
    return jnp.concatenate(
        [values[:, 128 * t : 128 * t + 128] for t in range(values.shape[1] // 128)], axis=0
    )


def untiles(values, count):
    rows = values.shape[0] // count
    return jnp.concatenate([values[t * rows : (t + 1) * rows] for t in range(count)], axis=1)


GATHER_PARTS = ((0, 48), (48, 48), (96, 48))


def gather_kernel(
    qkv, proj, fc1, conv, bias, fc2, wqkv, wproj, fc1_full, conv_full, fc2_full,
    full, other, taps, sems, pair_sems, local_sems,
):
    bits, partners, pair, core = place()
    half = fc1.shape[1]
    mine = tuple(bits)
    cols = pl.ds(pl.multiple_of(core * half, 128), half)
    both = jnp.concatenate([qkv[...].astype(f32), proj[...].astype(f32)], axis=1)
    full[mine] = tiles(both).astype(bf16)
    taps[...] = jnp.zeros(taps.shape, f32)
    taps[: KS * KS] = conv[...].astype(f32)
    taps[KS * KS : KS * KS + 1] = bias[...].astype(f32).reshape(1, half)
    conv_full[:, cols] = taps[...].astype(bf16)
    meet(partners + [pair])
    rows = pl.ds(pl.multiple_of(core * half, 128), half)
    pair_copies = [
        send(full.at[mine], other.at[mine], pair_sems, 0, pair),
        send(conv_full.at[:, cols], conv_full.at[:, cols], pair_sems, 1, pair),
        send(fc1, fc1_full.at[:, cols], pair_sems, 2, pair),
        send(fc2, fc2_full.at[rows], pair_sems, 3, pair),
    ]
    local = [
        pltpu.make_async_copy(fc1, fc1_full.at[:, cols], local_sems.at[0]),
        pltpu.make_async_copy(fc2, fc2_full.at[rows], local_sems.at[1]),
    ]
    gather = Doubling(full, sems, 0, GATHER_PARTS, bits, partners)
    parts = range(len(GATHER_PARTS))
    for part in parts:
        gather.start(part, 0)
    for copy in local:
        copy.start()
    for step in range(4):
        for part in parts:
            gather.wait(part, step)
            if step < 3:
                gather.start(part, step + 1)
            where = gather.come(part, step)
            pair_copies.append(
                send(full.at[where], other.at[where], pair_sems, 4 + 3 * step + part, pair)
            )
    for copy in pair_copies:
        copy.wait_recv()
    width = qkv.shape[1]
    for d in range(0, 16, 2):
        blocks = []
        for ref in (full, other):
            pair_rows = []
            for e in (d, d + 1):
                index = tuple((e // stride) % 2 for stride in SIDES)
                pair_rows.append(untiles(ref[index].astype(f32), 6))
            blocks.append(jnp.concatenate(pair_rows, axis=0))
        flip = core == 1
        first = jnp.where(flip, blocks[1], blocks[0])
        second = jnp.where(flip, blocks[0], blocks[1])
        rows = slice(24 * d, 24 * d + 48)
        wqkv[rows, :] = jnp.concatenate([first[:, :width], second[:, :width]], axis=1).astype(bf16)
        wproj[rows, :] = jnp.concatenate([first[:, width:], second[:, width:]], axis=1).astype(bf16)
    for copy in local:
        copy.wait()
    for copy in pair_copies:
        copy.wait_send()
    gather.finish()


def call_gather(qkv, proj, fc1, conv, bias, fc2):
    vmem = pl.BlockSpec(memory_space=pltpu.VMEM)
    half = fc1.shape[1]
    return pl.pallas_call(
        gather_kernel,
        in_specs=[vmem] * 6,
        out_specs=[vmem] * 5,
        out_shape=[
            jax.ShapeDtypeStruct((WIDTH, 3 * WIDTH), bf16),
            jax.ShapeDtypeStruct((WIDTH, WIDTH), bf16),
            jax.ShapeDtypeStruct((WIDTH, 2 * half), bf16),
            jax.ShapeDtypeStruct((64, 2 * half), bf16),
            jax.ShapeDtypeStruct((2 * half, WIDTH), bf16),
        ],
        scratch_shapes=[
            pltpu.VMEM((2, 2, 2, 2, PIECE, 128), bf16),
            pltpu.VMEM((2, 2, 2, 2, PIECE, 128), bf16),
            pltpu.VMEM((64, half), f32),
            pltpu.SemaphoreType.DMA((2, 12)),
            pltpu.SemaphoreType.DMA((2, 16)),
            pltpu.SemaphoreType.DMA((2,)),
        ],
        compiler_params=pltpu.CompilerParams(
            vmem_limit_bytes=VMEM, collective_id=0, has_side_effects=True
        ),
        name="gather_weights",
    )(qkv, proj, fc1, conv, bias, fc2)


MLP_PARTS = ((0, 112), (112, 112), (224, 96))


def reduce_mlp_kernel(gfc1, gconv, gfc2, total, acc, out, came, l0, l1, l2, l3, full, sems, psems):
    bits, partners, pair, core = place()
    half = gfc1.shape[1] // 2
    mine = tuple(bits)

    def pack(side):
        start = pl.multiple_of(side * half, 128)
        taps = tiles(gconv[:, pl.ds(start, half)])
        for d in range(16):
            one = tiles(gfc1[24 * d : 24 * d + 24, pl.ds(start, half)])
            two = tiles(gfc2[pl.ds(pl.multiple_of(start + 48 * d, 16), 48), :])
            three = taps[24 * d : 24 * d + 24]
            empty = jnp.zeros((BLOCK - 312, 128), f32)
            index = tuple((d // stride) % 2 for stride in SIDES)
            yield index, jnp.concatenate([one, two, three, empty], axis=0)

    for index, values in pack(1 - core):
        out[index] = values.astype(bf16)
    meet(partners + [pair])
    copy = send(out, came, psems, 0, pair)
    copy.wait_recv()
    for index, values in pack(core):
        acc[index] = (values + came[index].astype(f32)).astype(bf16)
    landing = [l0, l1, l2, l3]
    halving = Halving(acc, landing, sems, 0, MLP_PARTS, bits, partners)
    parts = range(3)
    for part in parts:
        halving.start(part, 0)
    for step in range(4):
        for part in parts:
            halving.add(part, step)
            if step < 3:
                halving.start(part, step + 1)
    full[mine] = acc[mine]
    doubling = Doubling(full, sems, 12, MLP_PARTS, bits, partners)
    for part in parts:
        doubling.start(part, 0)
    for step in range(4):
        for part in parts:
            doubling.wait(part, step)
            if step < 3:
                doubling.start(part, step + 1)
    total[...] = full[...]
    copy.wait_send()
    halving.finish()
    doubling.finish()


def call_reduce_mlp(gfc1, gconv, gfc2):
    vmem = pl.BlockSpec(memory_space=pltpu.VMEM)
    buffer = lambda free: pltpu.VMEM((2,) * free + (BLOCK, 128), bf16)
    return pl.pallas_call(
        reduce_mlp_kernel,
        in_specs=[vmem] * 3,
        out_specs=vmem,
        out_shape=jax.ShapeDtypeStruct((2, 2, 2, 2, BLOCK, 128), bf16),
        scratch_shapes=[
            buffer(4), buffer(4), buffer(4), buffer(3), buffer(2), buffer(1), buffer(0), buffer(4),
            pltpu.SemaphoreType.DMA((2, 24)),
            pltpu.SemaphoreType.DMA((2, 1)),
        ],
        compiler_params=pltpu.CompilerParams(
            vmem_limit_bytes=VMEM, collective_id=1, has_side_effects=True
        ),
        name="reduce_mlp",
    )(gfc1, gconv, gfc2)


def reduce_attention_kernel(
    gqkv, gproj, small, total, small_total, acc, own, out, came, l0, l1, l2, l3, sums, landed,
    sems, psems,
):
    bits, partners, pair, core = place()
    width, proj_width = gqkv.shape[1] // 2, gproj.shape[1] // 2
    mine = tuple(bits)
    for side in range(2):

        @pl.when(core == side)
        def _():
            for d in range(16):
                rows = slice(24 * d, 24 * d + 24)
                index = tuple((d // stride) % 2 for stride in SIDES)
                for half, ref in ((side, own), (1 - side, out)):
                    both = jnp.concatenate(
                        [
                            gqkv[rows, half * width : (half + 1) * width],
                            gproj[rows, half * proj_width : (half + 1) * proj_width],
                        ],
                        axis=1,
                    )
                    ref[index] = tiles(both).astype(ref.dtype)

    sums[0] = small[...]
    meet(partners + [pair])
    copy = send(out, came, psems, 0, pair)
    copies = [send(sums.at[0], landed.at[0], psems, 1, pair)]
    copy.wait_recv()
    for d in range(16):
        index = tuple((d // stride) % 2 for stride in SIDES)
        acc[index] = (own[index] + came[index].astype(f32)).astype(bf16)
    halving = Halving(acc, [l0, l1, l2, l3], sems, 0, GATHER_PARTS, bits, partners)
    parts = range(3)
    for part in parts:
        halving.start(part, 0)
    for step in range(4):
        copies[step].wait_recv()
        sums[step + 1] = sums[step] + landed[step]
        copies.append(
            send(sums.at[step + 1], landed.at[step + 1], psems, 2 + step, partners[3 - step])
        )
        for part in parts:
            halving.add(part, step)
            if step < 3:
                halving.start(part, step + 1)
    copies[4].wait_recv()
    small_total[...] = sums[4] + landed[4]
    total[...] = acc[mine]
    copy.wait_send()
    for copy in copies:
        copy.wait_send()
    halving.finish()


def call_reduce_attention(gqkv, gproj, small):
    vmem = pl.BlockSpec(memory_space=pltpu.VMEM)
    buffer = lambda free, dtype=bf16: pltpu.VMEM((2,) * free + (PIECE, 128), dtype)
    return pl.pallas_call(
        reduce_attention_kernel,
        in_specs=[vmem] * 3,
        out_specs=[vmem] * 2,
        out_shape=[
            jax.ShapeDtypeStruct((PIECE, 128), bf16),
            jax.ShapeDtypeStruct((SMALL, 128), f32),
        ],
        scratch_shapes=[
            buffer(4), buffer(4, f32), buffer(4), buffer(4), buffer(3), buffer(2), buffer(1),
            buffer(0), pltpu.VMEM((5, SMALL, 128), f32), pltpu.VMEM((5, SMALL, 128), f32),
            pltpu.SemaphoreType.DMA((2, 12)),
            pltpu.SemaphoreType.DMA((2, 6)),
        ],
        compiler_params=pltpu.CompilerParams(
            vmem_limit_bytes=VMEM, collective_id=2, has_side_effects=True
        ),
        name="reduce_attention",
    )(gqkv, gproj, small)


def finish_kernel(
    total, piece, small, gfc1, gb1, gconv, gfc2, gqkv, gproj, g1, b1, pb, g2, b2, fb, pre, post,
    taps, mixes,
):
    for d in range(16):
        index = tuple((d // stride) % 2 for stride in SIDES)
        block = total[index].astype(f32)
        gfc1[24 * d : 24 * d + 24, :] = untiles(block[:144], 6)
        gfc2[48 * d : 48 * d + 48, :] = untiles(block[144:288], 3)
        taps[24 * d : 24 * d + 24, :] = block[288:312]
    filters = untiles(taps[...], 6)
    gconv[...] = filters[: KS * KS]
    gb1[...] = filters[KS * KS].reshape(gb1.shape)
    both = untiles(piece[...].astype(f32), 6)
    width = gqkv.shape[1]
    gqkv[...] = both[:, :width]
    gproj[...] = both[:, width:]
    rows = untiles(small[:24], 3)
    for index, ref in enumerate((g1, b1, pb, g2, b2, fb)):
        ref[...] = rows[index].reshape(ref.shape)
    line = small[24:25]
    for index, ref in enumerate((pre, post)):
        for g in range(HEADS):
            start = HEADS * HEADS * index + HEADS * g
            mixes[index, g : g + 1, :HEADS] = line[:, start : start + HEADS]
    pre[...] = mixes[0, :HEADS, :HEADS] * 0.125
    post[...] = mixes[1, :HEADS, :HEADS]


def call_finish(total, piece, small, half):
    vmem = pl.BlockSpec(memory_space=pltpu.VMEM)
    shape = lambda *dims: jax.ShapeDtypeStruct(dims, f32)
    return pl.pallas_call(
        finish_kernel,
        in_specs=[vmem] * 3,
        out_specs=[vmem] * 14,
        out_shape=[
            shape(WIDTH, half), shape(half), shape(KS * KS, half), shape(half, WIDTH),
            shape(24, 3 * WIDTH // 2), shape(24, WIDTH // 2),
        ]
        + [shape(WIDTH)] * 6
        + [shape(HEADS, HEADS)] * 2,
        scratch_shapes=[pltpu.VMEM((WIDTH, 128), f32), pltpu.VMEM((2, 8, 128), f32)],
        compiler_params=pltpu.CompilerParams(vmem_limit_bytes=VMEM),
        name="finish",
    )(total, piece, small)


def shards_any(
    tokens, norm1_gain, norm1_bias, qkv_weight, mix_pre, mix_post, proj_weight, proj_bias,
    norm2_gain, norm2_bias, fc1_weight, fc1_bias, conv_weight, fc2_weight, fc2_bias, cotangent,
):
    gather = lambda v, axis, dim: lax.all_gather(v, axis, axis=dim, tiled=True)
    both = jnp.concatenate([qkv_weight, proj_weight], axis=1)
    pair = lax.all_gather(gather(both, "dp", 0), "tensor", axis=0)
    columns = qkv_weight.shape[1]
    wqkv = jnp.concatenate([pair[0, :, :columns], pair[1, :, :columns]], axis=1)
    wproj = jnp.concatenate([pair[0, :, columns:], pair[1, :, columns:]], axis=1)
    fc1 = gather(fc1_weight, "tensor", 1)
    taps = jnp.concatenate([conv_weight, fc1_bias[None]], axis=0)
    taps = jnp.pad(gather(taps, "tensor", 1), ((0, TAPS - KS * KS - 1), (0, 0)))
    fc2 = gather(fc2_weight, "tensor", 0)
    block_out, gtok, gqkv, gproj, gfc1, gconv, gfc2, small = local_block(
        tokens, norm1_gain, norm1_bias, wqkv, mix_pre, mix_post, wproj, proj_bias, norm2_gain,
        norm2_bias, fc1, taps, fc2, fc2_bias, cotangent,
    )
    scatter = lambda v, axis, dim: lax.psum_scatter(v, axis, scatter_dimension=dim, tiled=True)
    gqkv = scatter(scatter(gqkv, "tensor", 1), "dp", 0)
    gproj = scatter(scatter(gproj, "tensor", 1), "dp", 0)
    gfc1 = lax.psum(scatter(gfc1, "tensor", 1), "dp")
    gfc2 = lax.psum(scatter(gfc2, "tensor", 0), "dp")
    gconv = lax.psum(scatter(gconv, "tensor", 1), "dp")
    small = lax.psum(small, ("dp", "tensor"))
    rows = jnp.concatenate([small[0:8], small[8:16], small[16:24]], axis=1)
    mixes = small[24, : 2 * HEADS * HEADS].reshape(2, HEADS, HEADS)
    return (
        block_out, gtok, rows[0], rows[1], gqkv, mixes[0] * 0.125, mixes[1], gproj, rows[2],
        rows[3], rows[4], gfc1, gconv[KS * KS], gconv[: KS * KS], gfc2, rows[5],
    )


def shards_sixteen(
    tokens, norm1_gain, norm1_bias, qkv_weight, mix_pre, mix_post, proj_weight, proj_bias,
    norm2_gain, norm2_bias, fc1_weight, fc1_bias, conv_weight, fc2_weight, fc2_bias, cotangent,
):
    wqkv, wproj, fc1, taps, fc2 = call_gather(
        qkv_weight, proj_weight, fc1_weight, conv_weight, fc1_bias, fc2_weight
    )
    block_out, gtok, gqkv, gproj, gfc1, gconv, gfc2, small = local_block(
        tokens, norm1_gain, norm1_bias, wqkv, mix_pre, mix_post, wproj, proj_bias, norm2_gain,
        norm2_bias, fc1, taps, fc2, fc2_bias, cotangent,
    )
    total = call_reduce_mlp(gfc1, gconv, gfc2)
    piece, small = call_reduce_attention(gqkv, gproj, small)
    gfc1, gb1, gconv, gfc2, gqkv, gproj, g1, b1, pb, g2, b2, fb, pre, post = call_finish(
        total, piece, small, fc1_weight.shape[1]
    )
    return (
        block_out, gtok, g1, b1, gqkv, pre, post, gproj, pb, g2, b2, gfc1, gb1, gconv, gfc2, fb
    )


def solution(mesh):
    spec = P(("dp", "tensor"), None, None)
    in_specs = (
        spec, P(), P(), P("dp", "tensor"), P(), P(), P("dp", "tensor"), P(), P(), P(),
        P(None, "tensor"), P("tensor"), P(None, "tensor"), P("tensor", None), P(), spec,
    )
    out_specs = (
        spec, spec, P(), P(), P("dp", "tensor"), P(), P(), P("dp", "tensor"), P(), P(), P(),
        P(None, "tensor"), P("tensor"), P(None, "tensor"), P("tensor", None), P(),
    )
    sixteen = mesh.shape["dp"] == 16 and mesh.shape["tensor"] == 2
    body = shards_sixteen if sixteen else shards_any
    return jax.shard_map(body, mesh=mesh, in_specs=in_specs, out_specs=out_specs, check_vma=False)
```

```python
import functools

import jax
import jax.numpy as jnp
import numpy as np
from jax import lax
from jax.experimental import pallas as pl
from jax.experimental.pallas import tpu as pltpu
from jax.sharding import PartitionSpec as P

HEADS = 6
HEAD_DIM = 64
KS = 7
GRID = 14
POINTS = 17
SEQ = 197
ROWS = 208
TAPS = 64
KEYS = 256
WIDTH = 384
HALF = 152
COEFS = 2 * HALF
CLASS_ROW = 145
CHUNK = 512
STREAM = 256
SMALL = 32
VMEM = 62 * 1024 * 1024

f32 = jnp.float32
bf16 = jnp.bfloat16


def fourier():
    pairs = [(0, 0)]
    for k in range(POINTS):
        for m in range(POINTS):
            other = ((-k) % POINTS, (-m) % POINTS)
            if (k, m) != (0, 0) and (k, m) < other:
                pairs.append((k, m))
    freq = np.array(pairs, np.float64)
    unit = 2.0 * np.pi / POINTS
    spots = np.array([(y, x) for y in range(GRID) for x in range(GRID)], np.float64)
    taps = np.array([(a - 3, c - 3) for a in range(KS) for c in range(KS)], np.float64)
    count = len(pairs)
    angle = unit * freq @ spots.T
    forward = np.zeros((COEFS, ROWS))
    forward[:count, 1:SEQ] = np.cos(angle)
    forward[HALF : HALF + count, 1:SEQ] = -np.sin(angle)
    forward[CLASS_ROW, 0] = 1.0
    weight = np.full((count, 1), 2.0)
    weight[0] = 1.0
    weight = weight / POINTS**2
    inverse = np.zeros((COEFS, ROWS))
    inverse[:count, 1:SEQ] = weight * np.cos(angle)
    inverse[HALF : HALF + count, 1:SEQ] = -weight * np.sin(angle)
    inverse[CLASS_ROW, 0] = 1.0
    turn = unit * freq @ taps.T
    kernel = np.zeros((COEFS, TAPS))
    kernel[:count, : KS * KS] = np.cos(turn)
    kernel[HALF : HALF + count, : KS * KS] = np.sin(turn)
    back = np.zeros((COEFS, TAPS))
    back[:count, : KS * KS] = weight * np.cos(turn)
    back[HALF : HALF + count, : KS * KS] = -weight * np.sin(turn)
    one = np.zeros((COEFS, 1))
    one[CLASS_ROW] = 1.0
    return forward, inverse.T, kernel, back.T, one


def split(matrix):
    high = np.asarray(matrix, np.float32).astype(bf16)
    low = (np.asarray(matrix, np.float32) - high.astype(np.float32)).astype(bf16)
    return high, low


def dot(a, b):
    return lax.dot_general(a, b, (((1,), (0,)), ((), ())), preferred_element_type=f32)


def dot_t(a, b):
    return lax.dot_general(a, b, (((1,), (1,)), ((), ())), preferred_element_type=f32)


def t_dot(a, b):
    return lax.dot_general(a, b, (((0,), (0,)), ((), ())), preferred_element_type=f32)


def centre(values):
    centred = values - jnp.mean(values, axis=-1, keepdims=True)
    spread = jnp.mean(centred * centred, axis=-1, keepdims=True)
    return centred, lax.rsqrt(spread + 1e-05)


def norm_back(centred, r, gain, grad):
    scaled = grad * gain
    moment = jnp.mean(scaled * centred, axis=-1, keepdims=True)
    back = r * (scaled - jnp.mean(scaled, axis=-1, keepdims=True) - centred * (r * r * moment))
    return back, grad * (centred * r)


def row(ref):
    return ref[...].reshape(1, ref.shape[0])


def add_rows(values):
    return jnp.sum(values, axis=0, keepdims=True)


def row_mask(shape):
    return lax.broadcasted_iota(jnp.int32, shape, 0) < SEQ


def attention_forward(
    pre, post, tok, wqkv, wproj, gain1, bias1, pbias, gain2, bias2,
    n1_out, packed_out, probs_out, attn_out, att_out, mid_out, n2_out, pad, score, keys,
):
    pad[SEQ - 5 :] = jnp.zeros((ROWS - SEQ + 5, WIDTH), f32)
    pad[:SEQ] = tok[0].astype(f32)
    inputs = pad[...]
    centred, r = centre(inputs)
    inside = row_mask((ROWS, WIDTH))
    n1 = jnp.where(inside, centred * r * row(gain1) + row(bias1), 0.0).astype(bf16)
    n1_out[0] = n1
    packed = dot(n1, wqkv[...]).astype(bf16)
    packed_out[0, :ROWS] = packed
    packed_out[0, ROWS:] = jnp.zeros((KEYS - ROWS, 3 * WIDTH), bf16)
    low_half = lax.broadcasted_iota(jnp.int32, (ROWS, 128), 1) < HEAD_DIM
    zero = jnp.zeros((ROWS, 128), bf16)
    for p in range(HEADS // 2):
        query = packed_out[0, :ROWS, 128 * p : 128 * p + 128]
        key = packed_out[0, :, WIDTH + 128 * p : WIDTH + 128 * p + 128]
        score[2 * p] = dot_t(jnp.where(low_half, query, zero), key)
        score[2 * p + 1] = dot_t(jnp.where(low_half, zero, query), key)
    valid = lax.broadcasted_iota(jnp.int32, (16, KEYS), 1) < SEQ

    def rows_step(step, carry):
        rows = pl.ds(pl.multiple_of(step * 16, 16), 16)
        scores = [score[h, rows, :] for h in range(HEADS)]
        probs = []
        for g in range(HEADS):
            mixed = scores[0] * (pre[g, 0] * 0.125)
            for h in range(1, HEADS):
                mixed = mixed + scores[h] * (pre[g, h] * 0.125)
            mixed = jnp.where(valid, mixed, -1e30)
            top = jnp.max(mixed, axis=-1, keepdims=True)
            raised = jnp.exp(mixed - top)
            prob = raised * (1.0 / jnp.sum(raised, axis=-1, keepdims=True))
            probs_out[0, g, rows, :] = prob
            probs.append(prob)
        for g in range(HEADS):
            mixed = probs[0] * post[g, 0]
            for h in range(1, HEADS):
                mixed = mixed + probs[h] * post[g, h]
            attn_out[0, g, rows, :] = mixed.astype(bf16)
        return carry

    lax.fori_loop(0, ROWS // 16, rows_step, 0)
    pieces = []
    for p in range(HEADS // 2):
        value = packed_out[0, :, 2 * WIDTH + 128 * p : 2 * WIDTH + 128 * p + 128]
        pieces.append(
            jnp.where(low_half, dot(attn_out[0, 2 * p], value), dot(attn_out[0, 2 * p + 1], value))
        )
    attended = jnp.concatenate(pieces, axis=1).astype(bf16)
    att_out[0] = attended
    middle = inputs + (dot(attended, wproj[...]) + row(pbias))
    mid_out[0] = middle
    centred, r = centre(middle)
    n2_out[0] = jnp.where(inside, centred * r * row(gain2) + row(bias2), 0.0).astype(bf16)


def gelu_parts(hidden):
    size = jnp.abs(hidden) * np.float32(np.sqrt(0.5))
    t = 1.0 / (1.0 + 0.3275911 * size)
    raised = jnp.exp(-(size * size))
    series = t * (
        0.254829592
        + t * (-0.284496736 + t * (1.421413741 + t * (-1.453152027 + t * 1.061405429)))
    )
    tail = 0.5 * series * raised
    cdf = jnp.where(hidden < 0.0, tail, 1.0 - tail)
    return hidden * cdf, cdf + hidden * (raised * np.float32(1.0 / np.sqrt(2.0 * np.pi)))


def mlp(
    n2, cot, mid, fc1, conv, fc2, fc2b, fwd, inv, kh, kl, bh, bl, one,
    block_out, gn2_out, gfc1_out, gconv_out, gfc2_out, gb2_out,
    cot_pad, pad, hid, grad, out_acc, conv_low, ghid_low,
):
    step = pl.program_id(0)
    images = n2.shape[0]

    @pl.when(step == 0)
    def _():
        total = jnp.zeros((1, WIDTH), f32)
        for b in range(images):
            pad[SEQ - 5 :] = jnp.zeros((ROWS - SEQ + 5, WIDTH), f32)
            pad[:SEQ] = cot[b].astype(f32)
            values = pad[...]
            total = total + add_rows(values)
            cot_pad[b * ROWS : (b + 1) * ROWS] = values.astype(bf16)
        gb2_out[...] = total

    w1 = fc1[...]
    w2 = fc2[...]
    taps = conv[...]
    turned = dot(kh[...], taps) + dot(kl[...], taps) + one[...]
    kr, ki = turned[:HALF], turned[HALF:]
    rows_all = n2[...].reshape(images * ROWS, WIDTH)
    hid[...] = dot(rows_all, w1) + taps.astype(f32)[KS * KS : KS * KS + 1]
    grad[...] = dot_t(cot_pad[...], w2)
    cross_r = jnp.zeros((HALF, CHUNK), f32)
    cross_i = jnp.zeros((HALF, CHUNK), f32)
    bias_sum = jnp.zeros((1, CHUNK), f32)
    for b in range(images):
        span = slice(b * ROWS, (b + 1) * ROWS)
        act, slope = gelu_parts(hid[span, :])
        x = dot(fwd[...], act.astype(bf16))
        y = dot(fwd[...], grad[span, :].astype(bf16))
        xr, xi = x[:HALF], x[HALF:]
        yr, yi = y[:HALF], y[HALF:]
        made = jnp.concatenate([xr * kr - xi * ki, xr * ki + xi * kr], axis=0).astype(bf16)
        back = jnp.concatenate([yr * kr + yi * ki, yi * kr - yr * ki], axis=0).astype(bf16)
        cross_r = cross_r + (xr * yr + xi * yi)
        cross_i = cross_i + (xi * yr - xr * yi)
        conv_low[span, :] = dot(inv[...], made).astype(bf16)
        ghid = (dot(inv[...], back) * slope).astype(bf16)
        bias_sum = bias_sum + add_rows(ghid.astype(f32))
        ghid_low[span, :] = ghid
    cross = jnp.concatenate([cross_r, cross_i], axis=0)
    high = cross.astype(bf16)
    low = (cross - high.astype(f32)).astype(bf16)
    gconv_out[...] = dot(bh[...], high) + dot(bl[...], high) + dot(bh[...], low)
    gconv_out[KS * KS : KS * KS + 1] = bias_sum
    convolved = conv_low[...]
    ghid_all = ghid_low[...]
    part = dot(convolved, w2).reshape(images, ROWS, WIDTH)
    part_grad = dot_t(ghid_all, w1).reshape(images, ROWS, WIDTH)
    gfc2_out[...] = t_dot(convolved, cot_pad[...])
    gfc1_out[...] = t_dot(rows_all, ghid_all)

    @pl.when(step == 0)
    def _():
        out_acc[...] = part
        gn2_out[...] = part_grad

    @pl.when(step > 0)
    def _():
        out_acc[...] += part
        gn2_out[...] += part_grad

    @pl.when(step == pl.num_programs(0) - 1)
    def _():
        for b in range(images):
            result = mid[b] + (out_acc[b] + row(fc2b))
            block_out[b] = result[:SEQ].astype(bf16)


def attention_backward(
    pre, post, tok, cot, n1, packed, probs, attn, att, mid, gn2, wqkv, wproj, gain1, gain2, gb2,
    gtok_out, gqkv_out, gproj_out, small_out,
    pad, score, weight, low, mix, rows_out, square,
):
    step = pl.program_id(0)

    @pl.when(step == 0)
    def _():
        gqkv_out[...] = jnp.zeros_like(gqkv_out)
        gproj_out[...] = jnp.zeros_like(gproj_out)
        rows_out[...] = jnp.zeros_like(rows_out)
        mix[...] = jnp.zeros_like(mix)

    pad[SEQ - 5 :] = jnp.zeros((ROWS - SEQ + 5, WIDTH), f32)
    pad[:SEQ] = cot[0].astype(f32)
    centred, r = centre(mid[0])
    grad = gn2[0]
    back, gain_rows = norm_back(centred, r, row(gain2), grad)
    rows_out[3:4] += add_rows(gain_rows)
    rows_out[4:5] += add_rows(grad)
    gmid = pad[...] + back
    gmid_low = gmid.astype(bf16)
    rows_out[2:3] += add_rows(gmid_low.astype(f32))
    gproj_out[...] += t_dot(att[0], gmid_low)
    gatt = dot_t(gmid_low, wproj[...]).astype(bf16)
    low_half = lax.broadcasted_iota(jnp.int32, (ROWS, 128), 1) < HEAD_DIM
    key_half = lax.broadcasted_iota(jnp.int32, (KEYS, 128), 1) < HEAD_DIM
    zero = jnp.zeros((ROWS, 128), bf16)
    for p in range(HEADS // 2):
        query = packed[0, :ROWS, 128 * p : 128 * p + 128]
        key = packed[0, :, WIDTH + 128 * p : WIDTH + 128 * p + 128]
        value = packed[0, :, 2 * WIDTH + 128 * p : 2 * WIDTH + 128 * p + 128]
        ahead = gatt[:, 128 * p : 128 * p + 128]
        score[2 * p] = dot_t(jnp.where(low_half, query, zero), key)
        score[2 * p + 1] = dot_t(jnp.where(low_half, zero, query), key)
        weight[2 * p] = dot_t(jnp.where(low_half, ahead, zero), value)
        weight[2 * p + 1] = dot_t(jnp.where(low_half, zero, ahead), value)

    def fold(values):
        values = values[:, :128] + values[:, 128:]
        return values[:8] + values[8:]

    def rows_step(index, carry):
        rows = pl.ds(pl.multiple_of(index * 16, 16), 16)
        weights = [weight[g, rows, :] for g in range(HEADS)]
        mixed = []
        for h in range(HEADS):
            prob = probs[0, h, rows, :]
            ahead = weights[0] * post[0, h]
            for g in range(1, HEADS):
                ahead = ahead + weights[g] * post[g, h]
            for g in range(HEADS):
                mix[HEADS * HEADS + g * HEADS + h] += fold(weights[g] * prob)
            inner = jnp.sum(prob * ahead, axis=-1, keepdims=True)
            mixed.append(prob * (ahead - inner))
        for h in range(HEADS):
            scores = score[h, rows, :]
            total = mixed[0] * pre[0, h]
            for g in range(1, HEADS):
                total = total + mixed[g] * pre[g, h]
            low[h, rows, :] = total.astype(bf16)
            for g in range(HEADS):
                mix[g * HEADS + h] += fold(mixed[g] * scores)
        return carry

    lax.fori_loop(0, ROWS // 16, rows_step, 0)
    queries, keys, values = [], [], []
    for p in range(HEADS // 2):
        query = packed[0, :ROWS, 128 * p : 128 * p + 128]
        key = packed[0, :, WIDTH + 128 * p : WIDTH + 128 * p + 128]
        ahead = gatt[:, 128 * p : 128 * p + 128]
        even, odd = low[2 * p], low[2 * p + 1]
        queries.append(jnp.where(low_half, dot(even, key), dot(odd, key)) * 0.125)
        keys.append(jnp.where(key_half, t_dot(even, query), t_dot(odd, query))[:ROWS] * 0.125)
        values.append(
            jnp.where(key_half, t_dot(attn[0, 2 * p], ahead), t_dot(attn[0, 2 * p + 1], ahead))[
                :ROWS
            ]
        )
    gpacked = jnp.concatenate(queries + keys + values, axis=1).astype(bf16)
    gqkv_out[...] += t_dot(n1[0], gpacked)
    gnormed = dot_t(gpacked, wqkv[...])
    pad[:SEQ] = tok[0].astype(f32)
    centred, r = centre(pad[...])
    back, gain_rows = norm_back(centred, r, row(gain1), gnormed)
    rows_out[0:1] += add_rows(gain_rows)
    rows_out[1:2] += add_rows(gnormed)
    gtok_out[0] = (gmid + back)[:SEQ]

    @pl.when(step == pl.num_programs(0) - 1)
    def _():
        rows_out[5:6] = gb2[...]
        for t in range(WIDTH // 128):
            small_out[8 * t : 8 * t + 8] = rows_out[:, 128 * t : 128 * t + 128]
        square[...] = jnp.zeros_like(square)
        square[: 2 * HEADS * HEADS] = jnp.sum(mix[...], axis=1)
        sums = add_rows(square[...].T)
        small_out[24:] = jnp.concatenate([sums, jnp.zeros((SMALL - 25, 128), f32)], axis=0)


def whole(shape):
    return pl.BlockSpec(shape, lambda *_: (0,) * len(shape))


def image(shape):
    return pl.BlockSpec((1,) + shape, lambda i: (i,) + (0,) * len(shape))


def params():
    return pltpu.CompilerParams(vmem_limit_bytes=VMEM, dimension_semantics=("arbitrary",))


def call_forward(tokens, wqkv, wproj, pre, post, gain1, bias1, pbias, gain2, bias2):
    images = tokens.shape[0]
    smem = pl.BlockSpec(memory_space=pltpu.SMEM)
    vector = whole((WIDTH,))
    return pl.pallas_call(
        attention_forward,
        grid=(images,),
        in_specs=[
            smem, smem, image((SEQ, WIDTH)), whole((WIDTH, 3 * WIDTH)), whole((WIDTH, WIDTH)),
            vector, vector, vector, vector, vector,
        ],
        out_specs=[
            image((ROWS, WIDTH)), image((KEYS, 3 * WIDTH)), image((HEADS, ROWS, KEYS)),
            image((HEADS, ROWS, KEYS)), image((ROWS, WIDTH)), image((ROWS, WIDTH)),
            image((ROWS, WIDTH)),
        ],
        out_shape=[
            jax.ShapeDtypeStruct((images, ROWS, WIDTH), bf16),
            jax.ShapeDtypeStruct((images, KEYS, 3 * WIDTH), bf16),
            jax.ShapeDtypeStruct((images, HEADS, ROWS, KEYS), f32),
            jax.ShapeDtypeStruct((images, HEADS, ROWS, KEYS), bf16),
            jax.ShapeDtypeStruct((images, ROWS, WIDTH), bf16),
            jax.ShapeDtypeStruct((images, ROWS, WIDTH), f32),
            jax.ShapeDtypeStruct((images, ROWS, WIDTH), bf16),
        ],
        scratch_shapes=[
            pltpu.VMEM((ROWS, WIDTH), f32),
            pltpu.VMEM((HEADS, ROWS, KEYS), f32),
            pltpu.VMEM((8, 128), f32),
        ],
        compiler_params=params(),
        name="attention_forward",
    )(pre, post, tokens, wqkv, wproj, gain1, bias1, pbias, gain2, bias2)


def call_mlp(n2, cotangent, middle, fc1, conv, fc2, fc2_bias):
    images = n2.shape[0]
    units = fc1.shape[1]
    steps = units // CHUNK
    forward, inverse, kernel, back, one = fourier()
    kernel_high, kernel_low = split(kernel)
    back_high, back_low = split(back)
    consts = [
        jnp.asarray(forward.astype(np.float32).astype(bf16)),
        jnp.asarray(inverse.astype(np.float32).astype(bf16)),
        jnp.asarray(kernel_high), jnp.asarray(kernel_low),
        jnp.asarray(back_high), jnp.asarray(back_low),
        jnp.asarray(one.astype(np.float32)),
    ]
    columns = lambda rows: pl.BlockSpec((rows, CHUNK), lambda i: (0, i))
    total = images * ROWS
    return pl.pallas_call(
        mlp,
        grid=(steps,),
        in_specs=[
            whole((images, ROWS, WIDTH)), whole((images, SEQ, WIDTH)), whole((images, ROWS, WIDTH)),
            columns(WIDTH), columns(TAPS),
            pl.BlockSpec((CHUNK, WIDTH), lambda i: (i, 0)), whole((WIDTH,)),
        ]
        + [whole(c.shape) for c in consts],
        out_specs=[
            whole((images, SEQ, WIDTH)), whole((images, ROWS, WIDTH)),
            columns(WIDTH), columns(TAPS),
            pl.BlockSpec((CHUNK, WIDTH), lambda i: (i, 0)), whole((1, WIDTH)),
        ],
        out_shape=[
            jax.ShapeDtypeStruct((images, SEQ, WIDTH), bf16),
            jax.ShapeDtypeStruct((images, ROWS, WIDTH), f32),
            jax.ShapeDtypeStruct((WIDTH, units), f32),
            jax.ShapeDtypeStruct((TAPS, units), f32),
            jax.ShapeDtypeStruct((units, WIDTH), f32),
            jax.ShapeDtypeStruct((1, WIDTH), f32),
        ],
        scratch_shapes=[
            pltpu.VMEM((total, WIDTH), bf16),
            pltpu.VMEM((ROWS, WIDTH), f32),
            pltpu.VMEM((total, CHUNK), f32),
            pltpu.VMEM((total, CHUNK), f32),
            pltpu.VMEM((images, ROWS, WIDTH), f32),
            pltpu.VMEM((total, CHUNK), bf16),
            pltpu.VMEM((total, CHUNK), bf16),
        ],
        compiler_params=params(),
        name="mlp",
    )(n2, cotangent, middle, fc1, conv, fc2, fc2_bias, *consts)


def call_backward(
    tokens, cotangent, n1, packed, probs, attn, att, mid, gn2, wqkv, wproj, pre, post, gain1, gain2, gb2
):
    images = tokens.shape[0]
    smem = pl.BlockSpec(memory_space=pltpu.SMEM)
    vector = whole((WIDTH,))
    return pl.pallas_call(
        attention_backward,
        grid=(images,),
        in_specs=[
            smem, smem, image((SEQ, WIDTH)), image((SEQ, WIDTH)), image((ROWS, WIDTH)),
            image((KEYS, 3 * WIDTH)), image((HEADS, ROWS, KEYS)), image((HEADS, ROWS, KEYS)),
            image((ROWS, WIDTH)), image((ROWS, WIDTH)), image((ROWS, WIDTH)),
            whole((WIDTH, 3 * WIDTH)), whole((WIDTH, WIDTH)), vector, vector,
            whole((1, WIDTH)),
        ],
        out_specs=[
            image((SEQ, WIDTH)), whole((WIDTH, 3 * WIDTH)), whole((WIDTH, WIDTH)),
            whole((SMALL, 128)),
        ],
        out_shape=[
            jax.ShapeDtypeStruct((images, SEQ, WIDTH), f32),
            jax.ShapeDtypeStruct((WIDTH, 3 * WIDTH), f32),
            jax.ShapeDtypeStruct((WIDTH, WIDTH), f32),
            jax.ShapeDtypeStruct((SMALL, 128), f32),
        ],
        scratch_shapes=[
            pltpu.VMEM((ROWS, WIDTH), f32),
            pltpu.VMEM((HEADS, ROWS, KEYS), f32),
            pltpu.VMEM((HEADS, ROWS, KEYS), f32),
            pltpu.VMEM((HEADS, ROWS, KEYS), bf16),
            pltpu.VMEM((2 * HEADS * HEADS, 8, 128), f32),
            pltpu.VMEM((8, WIDTH), f32),
            pltpu.VMEM((128, 128), f32),
        ],
        compiler_params=params(),
        name="attention_backward",
    )(
        pre, post, tokens, cotangent, n1, packed, probs, attn, att, mid, gn2, wqkv, wproj,
        gain1, gain2, gb2,
    )


def local_block(
    tokens, norm1_gain, norm1_bias, wqkv, mix_pre, mix_post, wproj, proj_bias, norm2_gain,
    norm2_bias, fc1, taps, fc2, fc2_bias, cotangent,
):
    n1, packed, probs, attn, att, mid, n2 = call_forward(
        tokens, wqkv, wproj, mix_pre, mix_post, norm1_gain, norm1_bias, proj_bias, norm2_gain,
        norm2_bias,
    )
    block_out, gn2, gfc1, gconv, gfc2, gb2 = call_mlp(n2, cotangent, mid, fc1, taps, fc2, fc2_bias)
    gtok, gqkv, gproj, small = call_backward(
        tokens, cotangent, n1, packed, probs, attn, att, mid, gn2, wqkv, wproj, mix_pre, mix_post,
        norm1_gain, norm2_gain, gb2,
    )
    return block_out, gtok, gqkv, gproj, gfc1, gconv, gfc2, small


SIDES = (8, 4, 2, 1)
ORDERS = ((3, 2, 1, 0), (2, 1, 0, 3), (1, 0, 3, 2))
MESH_IDS = pl.DeviceIdType.MESH
PIECE = 144
PIECE_PARTS = ((0, 48), (48, 48), (96, 48))
BLOCK = 112
BLOCK_PARTS = ((0, 48), (48, 32), (80, 32))
STREAMS = 3


def place():
    dp, core = lax.axis_index("dp"), lax.axis_index("tensor")
    bits = [lax.rem(dp // stride, 2) for stride in SIDES]
    partners = [(dp + (1 - 2 * bit) * stride, core) for bit, stride in zip(bits, SIDES)]
    return bits, partners, (dp, 1 - core), core


def meet(partners):
    barrier = pltpu.get_barrier_semaphore()
    for partner in partners:
        pl.semaphore_signal(barrier, inc=1, device_id=partner, device_id_type=MESH_IDS)
    pl.semaphore_wait(barrier, len(partners))


def remote(src, dst, sems, index, device):
    return pltpu.make_async_remote_copy(
        src_ref=src, dst_ref=dst, send_sem=sems.at[(0,) + index], recv_sem=sems.at[(1,) + index],
        device_id=device, device_id_type=MESH_IDS,
    )


def region(fixed, rows):
    return tuple(fixed.get(axis, slice(None)) for axis in range(4)) + (rows,)


def combos(count):
    return [tuple((i >> (count - 1 - j)) & 1 for j in range(count)) for i in range(2**count)]


def index_of(d):
    return tuple((d // stride) % 2 for stride in SIDES)


class Halving:
    def __init__(self, acc, landing, sems, parts, turn, bits, partners):
        self.acc, self.landing, self.sems = acc, landing, sems
        self.parts, self.turn, self.bits, self.partners = parts, turn, bits, partners

    def copy(self, part, step):
        order, rows = ORDERS[(part + self.turn) % 3], pl.ds(*self.parts[part])
        axis = order[step]
        fixed = {a: self.bits[a] for a in order[:step]}
        fixed[axis] = 1 - self.bits[axis]
        dst = self.landing[step].at[(slice(None),) * (3 - step) + (rows,)]
        return remote(
            self.acc.at[region(fixed, rows)], dst, self.sems, (part, step), self.partners[axis]
        )

    def start(self, step):
        for part in range(3):
            self.copy(part, step).start()

    def act(self, step):
        for part in range(3):
            order, rows = ORDERS[(part + self.turn) % 3], pl.ds(*self.parts[part])
            self.copy(part, step).wait_recv()
            fixed = {a: self.bits[a] for a in order[: step + 1]}
            free = [a for a in range(4) if a not in fixed]
            for combo in combos(len(free)):
                where = region({**fixed, **dict(zip(free, combo))}, rows)
                came = self.landing[step][combo + (rows,)]
                self.acc[where] = (self.acc[where].astype(f32) + came.astype(f32)).astype(bf16)
            if step < 3:
                self.copy(part, step + 1).start()

    def finish(self):
        for step in range(4):
            for part in range(3):
                self.copy(part, step).wait_send()


class Doubling:
    def __init__(self, full, sems, parts, turn, bits, partners):
        self.full, self.sems = full, sems
        self.parts, self.turn, self.bits, self.partners = parts, turn, bits, partners

    def come(self, part, step):
        order, rows = ORDERS[(part + self.turn) % 3][::-1], pl.ds(*self.parts[part])
        fixed = {a: self.bits[a] for a in order[step + 1 :]}
        fixed[order[step]] = 1 - self.bits[order[step]]
        return region(fixed, rows)

    def copy(self, part, step):
        order, rows = ORDERS[(part + self.turn) % 3][::-1], pl.ds(*self.parts[part])
        held = region({a: self.bits[a] for a in order[step:]}, rows)
        return remote(
            self.full.at[held], self.full.at[held], self.sems, (part, step),
            self.partners[order[step]],
        )

    def start(self):
        for part in range(3):
            self.copy(part, 0).start()

    def act(self, step, then=None):
        for part in range(3):
            self.copy(part, step).wait_recv()
            if step < 3:
                self.copy(part, step + 1).start()
            if then is not None:
                then(part, step)

    def finish(self):
        for step in range(4):
            for part in range(3):
                self.copy(part, step).wait_send()


def tiles(values):
    return jnp.concatenate(
        [values[:, 128 * t : 128 * t + 128] for t in range(values.shape[1] // 128)], axis=0
    )


def untiles(values, count):
    rows = values.shape[0] // count
    return jnp.concatenate([values[t * rows : (t + 1) * rows] for t in range(count)], axis=1)


def block_kernel(
    pre, post, tok, cot, gain1, bias1, pbias, gain2, bias2, fc2b,
    qkv, proj, fc1, conv, bias, fc2, fwd, inv, kh, kl, bh, bl, one,
    block_out, gtok_out, *rest,
):
    fulls, (piece_out, small_out), rest = rest[:STREAMS], rest[STREAMS : STREAMS + 2], rest[STREAMS + 2 :]
    (
        piece_full, piece_other, taps_pad, wqkv, wproj, fc1_full, fc2_full, conv_full,
        inputs, cot_pad, n1, packed, score, probs, attn, att, mid, n2,
        turned, ghat, hid, conv_low, ghid_low, gmid, gmid_low, gatt, low, gpacked, mix,
        rows_out, square, gqkv, gproj, small_sums, small_landed,
        streams_out, streams_came, streams_acc, streams_landing, gconv, att_bufs,
        local_sems, gather_sems, gather_pair_sems, stream_pair_sems, stream_sems, att_sems, att_pair_sems,
    ) = rest
    images = tok.shape[0]
    total = images * ROWS
    half = fc1.shape[1]
    bits, partners, pair, core = place()
    mine = tuple(bits)
    mine_start = pl.multiple_of(core * half, 128)
    other_start = pl.multiple_of((1 - core) * half, 128)
    cols, rows_of = pl.ds(mine_start, half), pl.ds(mine_start, half)
    span = lambda b: slice(b * ROWS, (b + 1) * ROWS)
    spans = [span(b) for b in range(images)]
    inside = row_mask((ROWS, WIDTH))

    both = jnp.concatenate([qkv[...].astype(f32), proj[...].astype(f32)], axis=1)
    piece_full[mine] = tiles(both).astype(bf16)
    taps_pad[...] = jnp.zeros(taps_pad.shape, f32)
    taps_pad[: KS * KS] = conv[...].astype(f32)
    taps_pad[KS * KS : KS * KS + 1] = bias[...].astype(f32).reshape(1, half)
    conv_full[:, cols] = taps_pad[...].astype(bf16)
    meet(partners + [pair])
    gather = Doubling(piece_full, gather_sems, PIECE_PARTS, 0, bits, partners)
    gather.start()
    weights_come = [
        remote(conv_full.at[:, cols], conv_full.at[:, cols], gather_pair_sems, (0,), pair),
        remote(fc2, fc2_full.at[rows_of], gather_pair_sems, (1,), pair),
        remote(fc1, fc1_full.at[:, cols], gather_pair_sems, (2,), pair),
    ]
    forwards = [
        remote(piece_full.at[mine], piece_other.at[mine], gather_pair_sems, (3,), pair)
    ]
    local = [
        pltpu.make_async_copy(fc2, fc2_full.at[rows_of], local_sems.at[0]),
        pltpu.make_async_copy(fc1, fc1_full.at[:, cols], local_sems.at[1]),
    ]
    for copy in weights_come + forwards + local:
        copy.start()

    def forward(part, step):
        where = gather.come(part, step)
        copy = remote(
            piece_full.at[where], piece_other.at[where], gather_pair_sems,
            (4 + 3 * step + part,), pair,
        )
        copy.start()
        forwards.append(copy)

    cot_sum = jnp.zeros((1, WIDTH), f32)
    for b in range(images):
        for source, ref in ((tok, inputs), (cot, gmid)):
            ref[b * ROWS + SEQ - 5 : (b + 1) * ROWS] = jnp.zeros((ROWS - SEQ + 5, WIDTH), f32)
            ref[b * ROWS : b * ROWS + SEQ] = source[b].astype(f32)
        grads = gmid[spans[b], :]
        cot_sum = cot_sum + add_rows(grads)
        cot_pad[spans[b], :] = grads.astype(bf16)
    gather.act(0, forward)
    for b in range(images):
        centred, r = centre(inputs[spans[b], :])
        n1[spans[b], :] = jnp.where(inside, centred * r * row(gain1) + row(bias1), 0.0).astype(bf16)

    def prepare(start):
        units = pl.ds(start, half)
        taps = conv_full[:, units]
        turned[:, units] = dot(kh[...], taps) + dot(kl[...], taps) + one[...]
        hid[...] = dot_t(cot_pad[...], fc2_full[units, :])
        for b in range(images):
            ghat[b, :, units] = dot(fwd[...], hid[spans[b], :].astype(bf16))

    gather.act(1, forward)
    for copy in local:
        copy.wait()
    prepare(mine_start)
    gather.act(2, forward)
    for copy in weights_come:
        copy.wait_recv()
    prepare(other_start)
    gather.act(3, forward)
    for copy in forwards:
        copy.wait_recv()
    width = qkv.shape[1]
    flip = core == 1
    for d in range(0, 16, 2):
        blocks = [
            jnp.concatenate([untiles(ref[index_of(e)].astype(f32), 6) for e in (d, d + 1)], axis=0)
            for ref in (piece_full, piece_other)
        ]
        first = jnp.where(flip, blocks[1], blocks[0])
        second = jnp.where(flip, blocks[0], blocks[1])
        rows = slice(24 * d, 24 * d + 48)
        wqkv[rows, :] = jnp.concatenate([first[:, :width], second[:, :width]], axis=1).astype(bf16)
        wproj[rows, :] = jnp.concatenate([first[:, width:], second[:, width:]], axis=1).astype(bf16)

    for n in range(0, 3 * WIDTH, WIDTH):
        gpacked[:, n : n + WIDTH] = dot(n1[...], wqkv[:, n : n + WIDTH]).astype(bf16)
    for b in range(images):
        packed[b, :ROWS] = gpacked[spans[b], :]
        packed[b, ROWS:] = jnp.zeros((KEYS - ROWS, 3 * WIDTH), bf16)
    low_half = lax.broadcasted_iota(jnp.int32, (ROWS, 128), 1) < HEAD_DIM
    key_half = lax.broadcasted_iota(jnp.int32, (KEYS, 128), 1) < HEAD_DIM
    zero = jnp.zeros((ROWS, 128), bf16)
    valid = lax.broadcasted_iota(jnp.int32, (16, KEYS), 1) < SEQ

    def section(b, which, pair_of_heads, count=KEYS):
        start = which * WIDTH + 128 * pair_of_heads
        return packed[b, :count, start : start + 128]

    def find_scores(b):
        for p in range(HEADS // 2):
            query, key = section(b, 0, p, ROWS), section(b, 1, p)
            score[2 * p] = dot_t(jnp.where(low_half, query, zero), key)
            score[2 * p + 1] = dot_t(jnp.where(low_half, zero, query), key)

    def attend(b, carry):
        find_scores(b)

        def rows_step(step, carry):
            rows = pl.ds(pl.multiple_of(step * 16, 16), 16)
            scores = [score[h, rows, :] for h in range(HEADS)]
            found = []
            for g in range(HEADS):
                mixed = scores[0] * (pre[g, 0] * 0.125)
                for h in range(1, HEADS):
                    mixed = mixed + scores[h] * (pre[g, h] * 0.125)
                mixed = jnp.where(valid, mixed, -1e30)
                top = jnp.max(mixed, axis=-1, keepdims=True)
                raised = jnp.exp(mixed - top)
                prob = raised * (1.0 / jnp.sum(raised, axis=-1, keepdims=True))
                probs[b, g, rows, :] = prob
                found.append(prob)
            for g in range(HEADS):
                mixed = found[0] * post[g, 0]
                for h in range(1, HEADS):
                    mixed = mixed + found[h] * post[g, h]
                attn[b, g, rows, :] = mixed.astype(bf16)
            return carry

        lax.fori_loop(0, ROWS // 16, rows_step, 0, unroll=ROWS // 16)
        pieces = []
        for p in range(HEADS // 2):
            value = section(b, 2, p)
            pieces.append(
                jnp.where(low_half, dot(attn[b, 2 * p], value), dot(attn[b, 2 * p + 1], value))
            )
        rows = pl.ds(pl.multiple_of(b * ROWS, 16), ROWS)
        att[rows, :] = jnp.concatenate(pieces, axis=1).astype(bf16)
        return carry

    lax.fori_loop(0, images, attend, 0)
    branch = dot(att[...], wproj[...])
    for b in range(images):
        middle = inputs[spans[b], :] + (branch[spans[b]] + row(pbias))
        mid[spans[b], :] = middle
        centred, r = centre(middle)
        n2[spans[b], :] = jnp.where(inside, centred * r * row(gain2) + row(bias2), 0.0).astype(bf16)

    def exchange_copy(s):
        return remote(streams_out.at[s], streams_came.at[s], stream_pair_sems, (s,), pair)

    halvings = [
        Halving(
            streams_acc.at[s], [ref.at[s] for ref in streams_landing], stream_sems.at[s, 0],
            BLOCK_PARTS, s, bits, partners,
        )
        for s in range(STREAMS)
    ]
    doublings = [
        Doubling(fulls[s], stream_sems.at[s, 1], BLOCK_PARTS, s, bits, partners)
        for s in range(STREAMS)
    ]

    def act(s, step):
        if step < 0:
            halvings[s].start(0)
        elif step < 4:
            halvings[s].act(step)
            if step == 3:
                fulls[s][mine] = streams_acc[(s,) + mine]
                doublings[s].start()
        else:
            doublings[s].act(step - 4)

    def blocks():
        filters = tiles(gconv[...])
        empty = jnp.zeros((BLOCK - 104, 128), f32)
        for d in range(16):
            yield index_of(d), jnp.concatenate(
                [
                    tiles(gqkv[24 * d : 24 * d + 24, :STREAM]),
                    tiles(hid[16 * d : 16 * d + 16, :WIDTH]),
                    filters[8 * d : 8 * d + 8],
                    empty,
                ],
                axis=0,
            )

    def mlp(i, carry):
        units = pl.ds(
            pl.multiple_of(lax.rem((1 - core) * STREAMS + i, 2 * STREAMS) * STREAM, STREAM), STREAM
        )
        bias_row = conv_full[:, units].astype(f32)[KS * KS : KS * KS + 1]
        hid[:, :STREAM] = dot(n2[...], fc1_full[:, units]) + bias_row
        kr, ki = turned[:HALF, units], turned[HALF:, units]
        cross_r = jnp.zeros((HALF, STREAM), f32)
        cross_i = jnp.zeros((HALF, STREAM), f32)
        bias_sum = jnp.zeros((1, STREAM), f32)
        for b in range(images):
            activated, slope = gelu_parts(hid[spans[b], :STREAM])
            hid[spans[b], :STREAM] = slope
            x = dot(fwd[...], activated.astype(bf16))
            xr, xi = x[:HALF], x[HALF:]
            yr, yi = ghat[b, :HALF, units], ghat[b, HALF:, units]
            ahead = jnp.concatenate([xr * kr - xi * ki, xr * ki + xi * kr], axis=0).astype(bf16)
            back = jnp.concatenate([yr * kr + yi * ki, yi * kr - yr * ki], axis=0).astype(bf16)
            cross_r = cross_r + (xr * yr + xi * yi)
            cross_i = cross_i + (xi * yr - xr * yi)
            conv_low[spans[b], units] = dot(inv[...], ahead).astype(bf16)
            ghid = (dot(inv[...], back) * hid[spans[b], :STREAM]).astype(bf16)
            bias_sum = bias_sum + add_rows(ghid.astype(f32))
            ghid_low[spans[b], units] = ghid
        cross = jnp.concatenate([cross_r, cross_i], axis=0)
        high = cross.astype(bf16)
        low_part = (cross - high.astype(f32)).astype(bf16)
        last = lax.broadcasted_iota(jnp.int32, (TAPS, STREAM), 0) == KS * KS
        gconv[...] = jnp.where(
            last, bias_sum, dot(bh[...], high) + dot(bl[...], high) + dot(bh[...], low_part)
        )
        hid[:STREAM, :WIDTH] = t_dot(conv_low[:, units], cot_pad[...])
        gqkv[:, :STREAM] = t_dot(n2[...], ghid_low[:, units])

        @pl.when(i < STREAMS)
        def _():
            for index, values in blocks():
                streams_out[(i,) + index] = values.astype(bf16)
            exchange_copy(i).start()

        @pl.when(i >= STREAMS)
        def _():
            s = i - STREAMS
            exchange_copy(s).wait_recv()
            for index, values in blocks():
                came = streams_came[(s,) + index].astype(f32)
                streams_acc[(s,) + index] = (values + came).astype(bf16)

        for turn, items in enumerate((((0, -1),), ((0, 0), (1, -1)), ((0, 1), (1, 0), (2, -1)))):

            @pl.when(i == STREAMS + turn)
            def _():
                for item in items:
                    act(*item)

        return carry

    lax.fori_loop(0, 2 * STREAMS, mlp, 0)
    pending = [
        (2, 0), (1, 1), (0, 2), (2, 1), (1, 2), (0, 3), (2, 2), (1, 3), (0, 4), (2, 3), (1, 4),
        (0, 5), (2, 4), (1, 5), (0, 6), (2, 5), (1, 6), (0, 7), (2, 6), (1, 7), (2, 7),
    ]

    def poll(count=1):
        for _ in range(count):
            if pending:
                act(*pending.pop(0))

    hid[:, :WIDTH] = dot_t(ghid_low[...], fc1_full[...])
    hid[:, WIDTH:] = dot(conv_low[...], fc2_full[...])
    gain_sum = jnp.zeros((1, WIDTH), f32)
    bias_sum = jnp.zeros((1, WIDTH), f32)
    proj_sum = jnp.zeros((1, WIDTH), f32)
    for b in range(images):
        middle = mid[spans[b], :]
        block_out[b] = (middle + (hid[spans[b], WIDTH:] + row(fc2b)))[:SEQ].astype(bf16)
        centred, r = centre(middle)
        grad = hid[spans[b], :WIDTH]
        back, gain_rows = norm_back(centred, r, row(gain2), grad)
        gain_sum = gain_sum + add_rows(gain_rows)
        bias_sum = bias_sum + add_rows(grad)
        whole_grad = gmid[spans[b], :] + back
        gmid[spans[b], :] = whole_grad
        rounded = whole_grad.astype(bf16)
        proj_sum = proj_sum + add_rows(rounded.astype(f32))
        gmid_low[spans[b], :] = rounded
    poll()
    gatt[...] = dot_t(gmid_low[...], wproj[...]).astype(bf16)
    mix[...] = jnp.zeros_like(mix)

    def fold(values):
        values = values[:, :128] + values[:, 128:]
        return values[:8] + values[8:]

    places = 4
    plan = [[pending.pop(0)] for _ in range(images * places) if pending]

    def poll_at(b, spot):
        for image_index in range(images):
            index = image_index * places + spot
            if index < len(plan):

                @pl.when(b == image_index)
                def _():
                    for item in plan[index]:
                        act(*item)

    def put_weight(g, values):
        ghat[1, :ROWS, KEYS * g : KEYS * (g + 1)] = values

    def back_image(b, carry):
        rows_of_image = pl.ds(pl.multiple_of(b * ROWS, 16), ROWS)
        find_scores(b)
        for p in range(HEADS // 2):
            value = section(b, 2, p)
            ahead = gatt[rows_of_image, 128 * p : 128 * p + 128]
            put_weight(2 * p, dot_t(jnp.where(low_half, ahead, zero), value))
            put_weight(2 * p + 1, dot_t(jnp.where(low_half, zero, ahead), value))
        poll_at(b, 0)

        def back_step(step, carry):
            rows = pl.ds(pl.multiple_of(step * 16, 16), 16)
            weights = [ghat[1, rows, KEYS * g : KEYS * (g + 1)] for g in range(HEADS)]
            mixed = []
            for h in range(HEADS):
                prob = probs[b, h, rows, :]
                ahead = weights[0] * post[0, h]
                for g in range(1, HEADS):
                    ahead = ahead + weights[g] * post[g, h]
                for g in range(HEADS):
                    mix[HEADS * HEADS + g * HEADS + h] += fold(weights[g] * prob)
                inner = jnp.sum(prob * ahead, axis=-1, keepdims=True)
                mixed.append(prob * (ahead - inner))
            for h in range(HEADS):
                scores = score[h, rows, :]
                sums = mixed[0] * pre[0, h]
                for g in range(1, HEADS):
                    sums = sums + mixed[g] * pre[g, h]
                low[h, rows, :] = sums.astype(bf16)
                for g in range(HEADS):
                    mix[g * HEADS + h] += fold(mixed[g] * scores)
            return carry

        lax.fori_loop(0, 7, back_step, 0, unroll=7)
        poll_at(b, 1)
        lax.fori_loop(7, ROWS // 16, back_step, 0, unroll=6)
        poll_at(b, 2)
        queries, keys, values = [], [], []
        for p in range(HEADS // 2):
            query, key = section(b, 0, p, ROWS), section(b, 1, p)
            ahead = gatt[rows_of_image, 128 * p : 128 * p + 128]
            even, odd = low[2 * p], low[2 * p + 1]
            queries.append(jnp.where(low_half, dot(even, key), dot(odd, key)) * 0.125)
            keys.append(jnp.where(key_half, t_dot(even, query), t_dot(odd, query))[:ROWS] * 0.125)
            values.append(
                jnp.where(
                    key_half, t_dot(attn[b, 2 * p], ahead), t_dot(attn[b, 2 * p + 1], ahead)
                )[:ROWS]
            )
        gpacked[rows_of_image, :] = jnp.concatenate(queries + keys + values, axis=1).astype(bf16)
        poll_at(b, 3)
        return carry

    lax.fori_loop(0, images, back_image, 0)
    gproj[...] = t_dot(att[...], gmid_low[...])
    for n in range(0, 3 * WIDTH, WIDTH):
        gqkv[:, n : n + WIDTH] = t_dot(n1[...], gpacked[:, n : n + WIDTH])
    poll()

    width, proj_width = gqkv.shape[1] // 2, gproj.shape[1] // 2

    def pieces(side):
        for d in range(16):
            rows = slice(24 * d, 24 * d + 24)
            both = jnp.concatenate(
                [
                    gqkv[rows, side * width : (side + 1) * width],
                    gproj[rows, side * proj_width : (side + 1) * proj_width],
                ],
                axis=1,
            )
            yield index_of(d), tiles(both)

    for side in range(2):

        @pl.when(core == side)
        def _():
            for index, values in pieces(1 - side):
                att_bufs["out"][index] = values.astype(bf16)

    exchange = remote(att_bufs["out"], att_bufs["came"], att_pair_sems, (0,), pair)
    exchange.start()
    hid[:, :WIDTH] = dot_t(gpacked[...], wqkv[...])
    norm_gain = jnp.zeros((1, WIDTH), f32)
    norm_bias = jnp.zeros((1, WIDTH), f32)
    attention = Halving(
        att_bufs["acc"], att_bufs["landing"], att_sems, PIECE_PARTS, 0, bits, partners
    )
    for b in range(images):
        centred, r = centre(inputs[spans[b], :])
        grad = hid[spans[b], :WIDTH]
        back, gain_rows = norm_back(centred, r, row(gain1), grad)
        norm_gain = norm_gain + add_rows(gain_rows)
        norm_bias = norm_bias + add_rows(grad)
        gtok_out[b] = (gmid[spans[b], :] + back)[:SEQ]
        if b == 1:
            exchange.wait_recv()
            for side in range(2):

                @pl.when(core == side)
                def _():
                    for index, values in pieces(side):
                        came = att_bufs["came"][index].astype(f32)
                        att_bufs["acc"][index] = (values + came).astype(bf16)

            attention.start(0)
            poll()
    rows_out[...] = jnp.concatenate(
        [norm_gain, norm_bias, proj_sum, gain_sum, bias_sum, cot_sum, jnp.zeros((2, WIDTH), f32)],
        axis=0,
    )
    for t in range(WIDTH // 128):
        small_sums[0, 8 * t : 8 * t + 8] = rows_out[:, 128 * t : 128 * t + 128]
    square[...] = jnp.zeros_like(square)
    square[: 2 * HEADS * HEADS] = jnp.sum(mix[...], axis=1)
    sums = add_rows(square[...].T)
    small_sums[0, 24:] = jnp.concatenate([sums, jnp.zeros((SMALL - 25, 128), f32)], axis=0)

    def small_copy(step):
        device = pair if step == 0 else partners[4 - step]
        return remote(
            small_sums.at[step], small_landed.at[step], att_pair_sems, (1 + step,), device
        )

    small_copy(0).start()
    for step in range(4):
        small_copy(step).wait_recv()
        small_sums[step + 1] = small_sums[step] + small_landed[step]
        small_copy(step + 1).start()
        attention.act(step)
        poll(2)
    poll(len(pending))
    small_copy(4).wait_recv()
    small_out[...] = small_sums[4] + small_landed[4]
    piece_out[...] = att_bufs["acc"][mine]
    for copy in weights_come + forwards + [exchange]:
        copy.wait_send()
    for s in range(STREAMS):
        exchange_copy(s).wait_send()
    for step in range(5):
        small_copy(step).wait_send()
    gather.finish()
    attention.finish()
    for s in range(STREAMS):
        halvings[s].finish()
        doublings[s].finish()


def call_block(
    pre, post, tok, cot, gain1, bias1, pbias, gain2, bias2, fc2b, qkv, proj, fc1, conv, bias, fc2
):
    images, half = tok.shape[0], fc1.shape[1]
    units, total = 2 * half, images * ROWS
    forward, inverse, kernel, back, one = fourier()
    kernel_high, kernel_low = split(kernel)
    back_high, back_low = split(back)
    consts = [
        jnp.asarray(forward.astype(np.float32).astype(bf16)),
        jnp.asarray(inverse.astype(np.float32).astype(bf16)),
        jnp.asarray(kernel_high), jnp.asarray(kernel_low),
        jnp.asarray(back_high), jnp.asarray(back_low),
        jnp.asarray(one.astype(np.float32)),
    ]
    vmem = pl.BlockSpec(memory_space=pltpu.VMEM)
    smem = pl.BlockSpec(memory_space=pltpu.SMEM)
    hbm = pl.BlockSpec(memory_space=pl.ANY)

    def bufs(rows):
        buffer = lambda free: pltpu.VMEM((2,) * free + (rows, 128), bf16)
        return {
            "acc": buffer(4), "out": buffer(4), "came": buffer(4),
            "landing": [buffer(3), buffer(2), buffer(1), buffer(0)],
        }

    stacked = lambda free: pltpu.VMEM((STREAMS,) + (2,) * free + (BLOCK, 128), bf16)
    tall = lambda width, dtype: pltpu.VMEM((total, width), dtype)
    cube = lambda dtype: pltpu.VMEM((HEADS, ROWS, KEYS), dtype)
    scratch = dict(
        piece_full=pltpu.VMEM((2, 2, 2, 2, PIECE, 128), bf16),
        piece_other=pltpu.VMEM((2, 2, 2, 2, PIECE, 128), bf16),
        taps_pad=pltpu.VMEM((TAPS, half), f32),
        wqkv=pltpu.VMEM((WIDTH, 3 * WIDTH), bf16),
        wproj=pltpu.VMEM((WIDTH, WIDTH), bf16),
        fc1_full=pltpu.VMEM((WIDTH, units), bf16),
        fc2_full=pltpu.VMEM((units, WIDTH), bf16),
        conv_full=pltpu.VMEM((TAPS, units), bf16),
        inputs=tall(WIDTH, f32),
        cot_pad=tall(WIDTH, bf16),
        n1=tall(WIDTH, bf16),
        packed=pltpu.VMEM((images, KEYS, 3 * WIDTH), bf16),
        score=cube(f32),
        probs=pltpu.VMEM((images, HEADS, ROWS, KEYS), f32),
        attn=pltpu.VMEM((images, HEADS, ROWS, KEYS), bf16),
        att=tall(WIDTH, bf16),
        mid=tall(WIDTH, f32),
        n2=tall(WIDTH, bf16),
        turned=pltpu.VMEM((COEFS, units), f32),
        ghat=pltpu.VMEM((images, COEFS, units), f32),
        hid=tall(half, f32),
        conv_low=tall(units, bf16),
        ghid_low=tall(units, bf16),
        gmid=tall(WIDTH, f32),
        gmid_low=tall(WIDTH, bf16),
        gatt=tall(WIDTH, bf16),
        low=cube(bf16),
        gpacked=tall(3 * WIDTH, bf16),
        mix=pltpu.VMEM((2 * HEADS * HEADS, 8, 128), f32),
        rows_out=pltpu.VMEM((8, WIDTH), f32),
        square=pltpu.VMEM((128, 128), f32),
        gqkv=pltpu.VMEM((WIDTH, 3 * WIDTH), f32),
        gproj=pltpu.VMEM((WIDTH, WIDTH), f32),
        small_sums=pltpu.VMEM((5, SMALL, 128), f32),
        small_landed=pltpu.VMEM((5, SMALL, 128), f32),
        streams_out=stacked(4),
        streams_came=stacked(4),
        streams_acc=stacked(4),
        streams_landing=[stacked(free) for free in (3, 2, 1, 0)],
        gconv=pltpu.VMEM((TAPS, STREAM), f32),
        att_bufs=bufs(PIECE),
        local_sems=pltpu.SemaphoreType.DMA((2,)),
        gather_sems=pltpu.SemaphoreType.DMA((2, 3, 4)),
        gather_pair_sems=pltpu.SemaphoreType.DMA((2, 16)),
        stream_pair_sems=pltpu.SemaphoreType.DMA((2, STREAMS)),
        stream_sems=pltpu.SemaphoreType.DMA((STREAMS, 2, 2, 3, 4)),
        att_sems=pltpu.SemaphoreType.DMA((2, 3, 4)),
        att_pair_sems=pltpu.SemaphoreType.DMA((2, 6)),
    )
    return pl.pallas_call(
        block_kernel,
        in_specs=[smem] * 2 + [vmem] * 10 + [hbm] + [vmem] * 2 + [hbm] + [vmem] * len(consts),
        out_specs=[vmem] * (4 + STREAMS),
        out_shape=[
            jax.ShapeDtypeStruct(tok.shape, bf16),
            jax.ShapeDtypeStruct(tok.shape, f32),
        ]
        + [jax.ShapeDtypeStruct((2, 2, 2, 2, BLOCK, 128), bf16)] * STREAMS
        + [
            jax.ShapeDtypeStruct((PIECE, 128), bf16),
            jax.ShapeDtypeStruct((SMALL, 128), f32),
        ],
        scratch_shapes=list(scratch.values()),
        compiler_params=pltpu.CompilerParams(
            vmem_limit_bytes=VMEM, collective_id=0, has_side_effects=True
        ),
        name="block",
    )(
        pre, post, tok, cot, gain1, bias1, pbias, gain2, bias2, fc2b, qkv, proj, fc1, conv, bias,
        fc2, *consts,
    )


def finish_kernel(
    t0, t1, t2, piece, small, gfc1, gb1, gconv, gfc2, gqkv, gproj, g1, b1, pb, g2, b2, fb,
    pre, post, taps, mixes,
):
    for s, total in enumerate((t0, t1, t2)):
        side = slice(s * STREAM, (s + 1) * STREAM)
        for d in range(16):
            block = total[index_of(d)].astype(f32)
            gfc1[24 * d : 24 * d + 24, side] = untiles(block[:48], 2)
            gfc2[s * STREAM + 16 * d : s * STREAM + 16 * d + 16, :] = untiles(block[48:96], 3)
            taps[8 * d : 8 * d + 8, :] = block[96:104]
        filters = untiles(taps[...], 2)
        gconv[:, side] = filters[: KS * KS]
        gb1[side] = filters[KS * KS]
    both = untiles(piece[...].astype(f32), 6)
    width = gqkv.shape[1]
    gqkv[...] = both[:, :width]
    gproj[...] = both[:, width:]
    rows = untiles(small[:24], 3)
    for index, ref in enumerate((g1, b1, pb, g2, b2, fb)):
        ref[...] = rows[index].reshape(ref.shape)
    line = small[24:25]
    for index, ref in enumerate((pre, post)):
        for g in range(HEADS):
            start = HEADS * HEADS * index + HEADS * g
            mixes[index, g : g + 1, :HEADS] = line[:, start : start + HEADS]
    pre[...] = mixes[0, :HEADS, :HEADS] * 0.125
    post[...] = mixes[1, :HEADS, :HEADS]


def call_finish(totals, piece, small, half):
    vmem = pl.BlockSpec(memory_space=pltpu.VMEM)
    shape = lambda *dims: jax.ShapeDtypeStruct(dims, f32)
    return pl.pallas_call(
        finish_kernel,
        in_specs=[vmem] * (STREAMS + 2),
        out_specs=[vmem] * 14,
        out_shape=[
            shape(WIDTH, half), shape(half), shape(KS * KS, half), shape(half, WIDTH),
            shape(24, 3 * WIDTH // 2), shape(24, WIDTH // 2),
        ]
        + [shape(WIDTH)] * 6
        + [shape(HEADS, HEADS)] * 2,
        scratch_shapes=[pltpu.VMEM((128, 128), f32), pltpu.VMEM((2, 8, 128), f32)],
        compiler_params=pltpu.CompilerParams(vmem_limit_bytes=VMEM),
        name="finish",
    )(*totals, piece, small)


def shards_any(
    tokens, norm1_gain, norm1_bias, qkv_weight, mix_pre, mix_post, proj_weight, proj_bias,
    norm2_gain, norm2_bias, fc1_weight, fc1_bias, conv_weight, fc2_weight, fc2_bias, cotangent,
):
    gather = lambda v, axis, dim: lax.all_gather(v, axis, axis=dim, tiled=True)
    both = jnp.concatenate([qkv_weight, proj_weight], axis=1)
    pair = lax.all_gather(gather(both, "dp", 0), "tensor", axis=0)
    columns = qkv_weight.shape[1]
    wqkv = jnp.concatenate([pair[0, :, :columns], pair[1, :, :columns]], axis=1)
    wproj = jnp.concatenate([pair[0, :, columns:], pair[1, :, columns:]], axis=1)
    fc1 = gather(fc1_weight, "tensor", 1)
    taps = jnp.concatenate([conv_weight, fc1_bias[None]], axis=0)
    taps = jnp.pad(gather(taps, "tensor", 1), ((0, TAPS - KS * KS - 1), (0, 0)))
    fc2 = gather(fc2_weight, "tensor", 0)
    block_out, gtok, gqkv, gproj, gfc1, gconv, gfc2, small = local_block(
        tokens, norm1_gain, norm1_bias, wqkv, mix_pre, mix_post, wproj, proj_bias, norm2_gain,
        norm2_bias, fc1, taps, fc2, fc2_bias, cotangent,
    )
    scatter = lambda v, axis, dim: lax.psum_scatter(v, axis, scatter_dimension=dim, tiled=True)
    gqkv = scatter(scatter(gqkv, "tensor", 1), "dp", 0)
    gproj = scatter(scatter(gproj, "tensor", 1), "dp", 0)
    gfc1 = lax.psum(scatter(gfc1, "tensor", 1), "dp")
    gfc2 = lax.psum(scatter(gfc2, "tensor", 0), "dp")
    gconv = lax.psum(scatter(gconv, "tensor", 1), "dp")
    small = lax.psum(small, ("dp", "tensor"))
    rows = jnp.concatenate([small[0:8], small[8:16], small[16:24]], axis=1)
    mixes = small[24, : 2 * HEADS * HEADS].reshape(2, HEADS, HEADS)
    return (
        block_out, gtok, rows[0], rows[1], gqkv, mixes[0] * 0.125, mixes[1], gproj, rows[2],
        rows[3], rows[4], gfc1, gconv[KS * KS], gconv[: KS * KS], gfc2, rows[5],
    )


def shards_sixteen(
    tokens, norm1_gain, norm1_bias, qkv_weight, mix_pre, mix_post, proj_weight, proj_bias,
    norm2_gain, norm2_bias, fc1_weight, fc1_bias, conv_weight, fc2_weight, fc2_bias, cotangent,
):
    block_out, gtok, t0, t1, t2, piece, small = call_block(
        mix_pre, mix_post, tokens, cotangent, norm1_gain, norm1_bias, proj_bias, norm2_gain,
        norm2_bias, fc2_bias, qkv_weight, proj_weight, fc1_weight, conv_weight, fc1_bias,
        fc2_weight,
    )
    gfc1, gb1, gconv, gfc2, gqkv, gproj, g1, b1, pb, g2, b2, fb, pre, post = call_finish(
        (t0, t1, t2), piece, small, fc1_weight.shape[1]
    )
    return (
        block_out, gtok, g1, b1, gqkv, pre, post, gproj, pb, g2, b2, gfc1, gb1, gconv, gfc2, fb
    )


def solution(mesh):
    spec = P(("dp", "tensor"), None, None)
    in_specs = (
        spec, P(), P(), P("dp", "tensor"), P(), P(), P("dp", "tensor"), P(), P(), P(),
        P(None, "tensor"), P("tensor"), P(None, "tensor"), P("tensor", None), P(), spec,
    )
    out_specs = (
        spec, spec, P(), P(), P("dp", "tensor"), P(), P(), P("dp", "tensor"), P(), P(), P(),
        P(None, "tensor"), P("tensor"), P(None, "tensor"), P("tensor", None), P(),
    )
    sixteen = mesh.shape["dp"] == 16 and mesh.shape["tensor"] == 2
    body = shards_sixteen if sixteen else shards_any
    return jax.shard_map(body, mesh=mesh, in_specs=in_specs, out_specs=out_specs, check_vma=False)
```

```python
import functools

import jax
import jax.numpy as jnp
import numpy as np
from jax import lax
from jax.experimental import pallas as pl
from jax.experimental.pallas import tpu as pltpu
from jax.sharding import PartitionSpec as P

HEADS = 6
HEAD_DIM = 64
KS = 7
GRID = 14
POINTS = 17
SEQ = 197
ROWS = 208
TAPS = 64
KEYS = 256
WIDTH = 384
HALF = 152
COEFS = 2 * HALF
CLASS_ROW = 145
CHUNK = 512
STREAM = 256
SMALL = 32
VMEM = 62 * 1024 * 1024

f32 = jnp.float32
bf16 = jnp.bfloat16


def fourier():
    pairs = [(0, 0)]
    for k in range(POINTS):
        for m in range(POINTS):
            other = ((-k) % POINTS, (-m) % POINTS)
            if (k, m) != (0, 0) and (k, m) < other:
                pairs.append((k, m))
    freq = np.array(pairs, np.float64)
    unit = 2.0 * np.pi / POINTS
    spots = np.array([(y, x) for y in range(GRID) for x in range(GRID)], np.float64)
    taps = np.array([(a - 3, c - 3) for a in range(KS) for c in range(KS)], np.float64)
    count = len(pairs)
    angle = unit * freq @ spots.T
    forward = np.zeros((COEFS, ROWS))
    forward[:count, 1:SEQ] = np.cos(angle)
    forward[HALF : HALF + count, 1:SEQ] = -np.sin(angle)
    forward[CLASS_ROW, 0] = 1.0
    weight = np.full((count, 1), 2.0)
    weight[0] = 1.0
    weight = weight / POINTS**2
    inverse = np.zeros((COEFS, ROWS))
    inverse[:count, 1:SEQ] = weight * np.cos(angle)
    inverse[HALF : HALF + count, 1:SEQ] = -weight * np.sin(angle)
    inverse[CLASS_ROW, 0] = 1.0
    turn = unit * freq @ taps.T
    kernel = np.zeros((COEFS, TAPS))
    kernel[:count, : KS * KS] = np.cos(turn)
    kernel[HALF : HALF + count, : KS * KS] = np.sin(turn)
    back = np.zeros((COEFS, TAPS))
    back[:count, : KS * KS] = weight * np.cos(turn)
    back[HALF : HALF + count, : KS * KS] = -weight * np.sin(turn)
    one = np.zeros((COEFS, 1))
    one[CLASS_ROW] = 1.0
    return forward, inverse.T, kernel, back.T, one


def split(matrix):
    high = np.asarray(matrix, np.float32).astype(bf16)
    low = (np.asarray(matrix, np.float32) - high.astype(np.float32)).astype(bf16)
    return high, low


def dot(a, b):
    return lax.dot_general(a, b, (((1,), (0,)), ((), ())), preferred_element_type=f32)


def dot_t(a, b):
    return lax.dot_general(a, b, (((1,), (1,)), ((), ())), preferred_element_type=f32)


def t_dot(a, b):
    return lax.dot_general(a, b, (((0,), (0,)), ((), ())), preferred_element_type=f32)


def centre(values):
    centred = values - jnp.mean(values, axis=-1, keepdims=True)
    spread = jnp.mean(centred * centred, axis=-1, keepdims=True)
    return centred, lax.rsqrt(spread + 1e-05)


def norm_back(centred, r, gain, grad):
    scaled = grad * gain
    moment = jnp.mean(scaled * centred, axis=-1, keepdims=True)
    back = r * (scaled - jnp.mean(scaled, axis=-1, keepdims=True) - centred * (r * r * moment))
    return back, grad * (centred * r)


def row(ref):
    return ref[...].reshape(1, ref.shape[0])


def add_rows(values):
    return jnp.sum(values, axis=0, keepdims=True)


def row_mask(shape):
    return lax.broadcasted_iota(jnp.int32, shape, 0) < SEQ


def attention_forward(
    pre, post, tok, wqkv, wproj, gain1, bias1, pbias, gain2, bias2,
    n1_out, packed_out, probs_out, attn_out, att_out, mid_out, n2_out, pad, score, keys,
):
    pad[SEQ - 5 :] = jnp.zeros((ROWS - SEQ + 5, WIDTH), f32)
    pad[:SEQ] = tok[0].astype(f32)
    inputs = pad[...]
    centred, r = centre(inputs)
    inside = row_mask((ROWS, WIDTH))
    n1 = jnp.where(inside, centred * r * row(gain1) + row(bias1), 0.0).astype(bf16)
    n1_out[0] = n1
    packed = dot(n1, wqkv[...]).astype(bf16)
    packed_out[0, :ROWS] = packed
    packed_out[0, ROWS:] = jnp.zeros((KEYS - ROWS, 3 * WIDTH), bf16)
    low_half = lax.broadcasted_iota(jnp.int32, (ROWS, 128), 1) < HEAD_DIM
    zero = jnp.zeros((ROWS, 128), bf16)
    for p in range(HEADS // 2):
        query = packed_out[0, :ROWS, 128 * p : 128 * p + 128]
        key = packed_out[0, :, WIDTH + 128 * p : WIDTH + 128 * p + 128]
        score[2 * p] = dot_t(jnp.where(low_half, query, zero), key)
        score[2 * p + 1] = dot_t(jnp.where(low_half, zero, query), key)
    valid = lax.broadcasted_iota(jnp.int32, (16, KEYS), 1) < SEQ

    def rows_step(step, carry):
        rows = pl.ds(pl.multiple_of(step * 16, 16), 16)
        scores = [score[h, rows, :] for h in range(HEADS)]
        probs = []
        for g in range(HEADS):
            mixed = scores[0] * (pre[g, 0] * 0.125)
            for h in range(1, HEADS):
                mixed = mixed + scores[h] * (pre[g, h] * 0.125)
            mixed = jnp.where(valid, mixed, -1e30)
            top = jnp.max(mixed, axis=-1, keepdims=True)
            raised = jnp.exp(mixed - top)
            prob = raised * (1.0 / jnp.sum(raised, axis=-1, keepdims=True))
            probs_out[0, g, rows, :] = prob
            probs.append(prob)
        for g in range(HEADS):
            mixed = probs[0] * post[g, 0]
            for h in range(1, HEADS):
                mixed = mixed + probs[h] * post[g, h]
            attn_out[0, g, rows, :] = mixed.astype(bf16)
        return carry

    lax.fori_loop(0, ROWS // 16, rows_step, 0)
    pieces = []
    for p in range(HEADS // 2):
        value = packed_out[0, :, 2 * WIDTH + 128 * p : 2 * WIDTH + 128 * p + 128]
        pieces.append(
            jnp.where(low_half, dot(attn_out[0, 2 * p], value), dot(attn_out[0, 2 * p + 1], value))
        )
    attended = jnp.concatenate(pieces, axis=1).astype(bf16)
    att_out[0] = attended
    middle = inputs + (dot(attended, wproj[...]) + row(pbias))
    mid_out[0] = middle
    centred, r = centre(middle)
    n2_out[0] = jnp.where(inside, centred * r * row(gain2) + row(bias2), 0.0).astype(bf16)


def gelu_parts(hidden):
    size = jnp.abs(hidden) * np.float32(np.sqrt(0.5))
    t = 1.0 / (1.0 + 0.3275911 * size)
    raised = jnp.exp(-(size * size))
    series = t * (
        0.254829592
        + t * (-0.284496736 + t * (1.421413741 + t * (-1.453152027 + t * 1.061405429)))
    )
    tail = 0.5 * series * raised
    cdf = jnp.where(hidden < 0.0, tail, 1.0 - tail)
    return hidden * cdf, cdf + hidden * (raised * np.float32(1.0 / np.sqrt(2.0 * np.pi)))


def mlp(
    n2, cot, mid, fc1, conv, fc2, fc2b, fwd, inv, kh, kl, bh, bl, one,
    block_out, gn2_out, gfc1_out, gconv_out, gfc2_out, gb2_out,
    cot_pad, pad, hid, grad, out_acc, conv_low, ghid_low,
):
    step = pl.program_id(0)
    images = n2.shape[0]

    @pl.when(step == 0)
    def _():
        total = jnp.zeros((1, WIDTH), f32)
        for b in range(images):
            pad[SEQ - 5 :] = jnp.zeros((ROWS - SEQ + 5, WIDTH), f32)
            pad[:SEQ] = cot[b].astype(f32)
            values = pad[...]
            total = total + add_rows(values)
            cot_pad[b * ROWS : (b + 1) * ROWS] = values.astype(bf16)
        gb2_out[...] = total

    w1 = fc1[...]
    w2 = fc2[...]
    taps = conv[...]
    turned = dot(kh[...], taps) + dot(kl[...], taps) + one[...]
    kr, ki = turned[:HALF], turned[HALF:]
    rows_all = n2[...].reshape(images * ROWS, WIDTH)
    hid[...] = dot(rows_all, w1) + taps.astype(f32)[KS * KS : KS * KS + 1]
    grad[...] = dot_t(cot_pad[...], w2)
    cross_r = jnp.zeros((HALF, CHUNK), f32)
    cross_i = jnp.zeros((HALF, CHUNK), f32)
    bias_sum = jnp.zeros((1, CHUNK), f32)
    for b in range(images):
        span = slice(b * ROWS, (b + 1) * ROWS)
        act, slope = gelu_parts(hid[span, :])
        x = dot(fwd[...], act.astype(bf16))
        y = dot(fwd[...], grad[span, :].astype(bf16))
        xr, xi = x[:HALF], x[HALF:]
        yr, yi = y[:HALF], y[HALF:]
        made = jnp.concatenate([xr * kr - xi * ki, xr * ki + xi * kr], axis=0).astype(bf16)
        back = jnp.concatenate([yr * kr + yi * ki, yi * kr - yr * ki], axis=0).astype(bf16)
        cross_r = cross_r + (xr * yr + xi * yi)
        cross_i = cross_i + (xi * yr - xr * yi)
        conv_low[span, :] = dot(inv[...], made).astype(bf16)
        ghid = (dot(inv[...], back) * slope).astype(bf16)
        bias_sum = bias_sum + add_rows(ghid.astype(f32))
        ghid_low[span, :] = ghid
    cross = jnp.concatenate([cross_r, cross_i], axis=0)
    high = cross.astype(bf16)
    low = (cross - high.astype(f32)).astype(bf16)
    gconv_out[...] = dot(bh[...], high) + dot(bl[...], high) + dot(bh[...], low)
    gconv_out[KS * KS : KS * KS + 1] = bias_sum
    convolved = conv_low[...]
    ghid_all = ghid_low[...]
    part = dot(convolved, w2).reshape(images, ROWS, WIDTH)
    part_grad = dot_t(ghid_all, w1).reshape(images, ROWS, WIDTH)
    gfc2_out[...] = t_dot(convolved, cot_pad[...])
    gfc1_out[...] = t_dot(rows_all, ghid_all)

    @pl.when(step == 0)
    def _():
        out_acc[...] = part
        gn2_out[...] = part_grad

    @pl.when(step > 0)
    def _():
        out_acc[...] += part
        gn2_out[...] += part_grad

    @pl.when(step == pl.num_programs(0) - 1)
    def _():
        for b in range(images):
            result = mid[b] + (out_acc[b] + row(fc2b))
            block_out[b] = result[:SEQ].astype(bf16)


def attention_backward(
    pre, post, tok, cot, n1, packed, probs, attn, att, mid, gn2, wqkv, wproj, gain1, gain2, gb2,
    gtok_out, gqkv_out, gproj_out, small_out,
    pad, score, weight, low, mix, rows_out, square,
):
    step = pl.program_id(0)

    @pl.when(step == 0)
    def _():
        gqkv_out[...] = jnp.zeros_like(gqkv_out)
        gproj_out[...] = jnp.zeros_like(gproj_out)
        rows_out[...] = jnp.zeros_like(rows_out)
        mix[...] = jnp.zeros_like(mix)

    pad[SEQ - 5 :] = jnp.zeros((ROWS - SEQ + 5, WIDTH), f32)
    pad[:SEQ] = cot[0].astype(f32)
    centred, r = centre(mid[0])
    grad = gn2[0]
    back, gain_rows = norm_back(centred, r, row(gain2), grad)
    rows_out[3:4] += add_rows(gain_rows)
    rows_out[4:5] += add_rows(grad)
    gmid = pad[...] + back
    gmid_low = gmid.astype(bf16)
    rows_out[2:3] += add_rows(gmid_low.astype(f32))
    gproj_out[...] += t_dot(att[0], gmid_low)
    gatt = dot_t(gmid_low, wproj[...]).astype(bf16)
    low_half = lax.broadcasted_iota(jnp.int32, (ROWS, 128), 1) < HEAD_DIM
    key_half = lax.broadcasted_iota(jnp.int32, (KEYS, 128), 1) < HEAD_DIM
    zero = jnp.zeros((ROWS, 128), bf16)
    for p in range(HEADS // 2):
        query = packed[0, :ROWS, 128 * p : 128 * p + 128]
        key = packed[0, :, WIDTH + 128 * p : WIDTH + 128 * p + 128]
        value = packed[0, :, 2 * WIDTH + 128 * p : 2 * WIDTH + 128 * p + 128]
        ahead = gatt[:, 128 * p : 128 * p + 128]
        score[2 * p] = dot_t(jnp.where(low_half, query, zero), key)
        score[2 * p + 1] = dot_t(jnp.where(low_half, zero, query), key)
        weight[2 * p] = dot_t(jnp.where(low_half, ahead, zero), value)
        weight[2 * p + 1] = dot_t(jnp.where(low_half, zero, ahead), value)

    def fold(values):
        values = values[:, :128] + values[:, 128:]
        return values[:8] + values[8:]

    def rows_step(index, carry):
        rows = pl.ds(pl.multiple_of(index * 16, 16), 16)
        weights = [weight[g, rows, :] for g in range(HEADS)]
        mixed = []
        for h in range(HEADS):
            prob = probs[0, h, rows, :]
            ahead = weights[0] * post[0, h]
            for g in range(1, HEADS):
                ahead = ahead + weights[g] * post[g, h]
            for g in range(HEADS):
                mix[HEADS * HEADS + g * HEADS + h] += fold(weights[g] * prob)
            inner = jnp.sum(prob * ahead, axis=-1, keepdims=True)
            mixed.append(prob * (ahead - inner))
        for h in range(HEADS):
            scores = score[h, rows, :]
            total = mixed[0] * pre[0, h]
            for g in range(1, HEADS):
                total = total + mixed[g] * pre[g, h]
            low[h, rows, :] = total.astype(bf16)
            for g in range(HEADS):
                mix[g * HEADS + h] += fold(mixed[g] * scores)
        return carry

    lax.fori_loop(0, ROWS // 16, rows_step, 0)
    queries, keys, values = [], [], []
    for p in range(HEADS // 2):
        query = packed[0, :ROWS, 128 * p : 128 * p + 128]
        key = packed[0, :, WIDTH + 128 * p : WIDTH + 128 * p + 128]
        ahead = gatt[:, 128 * p : 128 * p + 128]
        even, odd = low[2 * p], low[2 * p + 1]
        queries.append(jnp.where(low_half, dot(even, key), dot(odd, key)) * 0.125)
        keys.append(jnp.where(key_half, t_dot(even, query), t_dot(odd, query))[:ROWS] * 0.125)
        values.append(
            jnp.where(key_half, t_dot(attn[0, 2 * p], ahead), t_dot(attn[0, 2 * p + 1], ahead))[
                :ROWS
            ]
        )
    gpacked = jnp.concatenate(queries + keys + values, axis=1).astype(bf16)
    gqkv_out[...] += t_dot(n1[0], gpacked)
    gnormed = dot_t(gpacked, wqkv[...])
    pad[:SEQ] = tok[0].astype(f32)
    centred, r = centre(pad[...])
    back, gain_rows = norm_back(centred, r, row(gain1), gnormed)
    rows_out[0:1] += add_rows(gain_rows)
    rows_out[1:2] += add_rows(gnormed)
    gtok_out[0] = (gmid + back)[:SEQ]

    @pl.when(step == pl.num_programs(0) - 1)
    def _():
        rows_out[5:6] = gb2[...]
        for t in range(WIDTH // 128):
            small_out[8 * t : 8 * t + 8] = rows_out[:, 128 * t : 128 * t + 128]
        square[...] = jnp.zeros_like(square)
        square[: 2 * HEADS * HEADS] = jnp.sum(mix[...], axis=1)
        sums = add_rows(square[...].T)
        small_out[24:] = jnp.concatenate([sums, jnp.zeros((SMALL - 25, 128), f32)], axis=0)


def whole(shape):
    return pl.BlockSpec(shape, lambda *_: (0,) * len(shape))


def image(shape):
    return pl.BlockSpec((1,) + shape, lambda i: (i,) + (0,) * len(shape))


def params():
    return pltpu.CompilerParams(vmem_limit_bytes=VMEM, dimension_semantics=("arbitrary",))


def call_forward(tokens, wqkv, wproj, pre, post, gain1, bias1, pbias, gain2, bias2):
    images = tokens.shape[0]
    smem = pl.BlockSpec(memory_space=pltpu.SMEM)
    vector = whole((WIDTH,))
    return pl.pallas_call(
        attention_forward,
        grid=(images,),
        in_specs=[
            smem, smem, image((SEQ, WIDTH)), whole((WIDTH, 3 * WIDTH)), whole((WIDTH, WIDTH)),
            vector, vector, vector, vector, vector,
        ],
        out_specs=[
            image((ROWS, WIDTH)), image((KEYS, 3 * WIDTH)), image((HEADS, ROWS, KEYS)),
            image((HEADS, ROWS, KEYS)), image((ROWS, WIDTH)), image((ROWS, WIDTH)),
            image((ROWS, WIDTH)),
        ],
        out_shape=[
            jax.ShapeDtypeStruct((images, ROWS, WIDTH), bf16),
            jax.ShapeDtypeStruct((images, KEYS, 3 * WIDTH), bf16),
            jax.ShapeDtypeStruct((images, HEADS, ROWS, KEYS), f32),
            jax.ShapeDtypeStruct((images, HEADS, ROWS, KEYS), bf16),
            jax.ShapeDtypeStruct((images, ROWS, WIDTH), bf16),
            jax.ShapeDtypeStruct((images, ROWS, WIDTH), f32),
            jax.ShapeDtypeStruct((images, ROWS, WIDTH), bf16),
        ],
        scratch_shapes=[
            pltpu.VMEM((ROWS, WIDTH), f32),
            pltpu.VMEM((HEADS, ROWS, KEYS), f32),
            pltpu.VMEM((8, 128), f32),
        ],
        compiler_params=params(),
        name="attention_forward",
    )(pre, post, tokens, wqkv, wproj, gain1, bias1, pbias, gain2, bias2)


def call_mlp(n2, cotangent, middle, fc1, conv, fc2, fc2_bias):
    images = n2.shape[0]
    units = fc1.shape[1]
    steps = units // CHUNK
    forward, inverse, kernel, back, one = fourier()
    kernel_high, kernel_low = split(kernel)
    back_high, back_low = split(back)
    consts = [
        jnp.asarray(forward.astype(np.float32).astype(bf16)),
        jnp.asarray(inverse.astype(np.float32).astype(bf16)),
        jnp.asarray(kernel_high), jnp.asarray(kernel_low),
        jnp.asarray(back_high), jnp.asarray(back_low),
        jnp.asarray(one.astype(np.float32)),
    ]
    columns = lambda rows: pl.BlockSpec((rows, CHUNK), lambda i: (0, i))
    total = images * ROWS
    return pl.pallas_call(
        mlp,
        grid=(steps,),
        in_specs=[
            whole((images, ROWS, WIDTH)), whole((images, SEQ, WIDTH)), whole((images, ROWS, WIDTH)),
            columns(WIDTH), columns(TAPS),
            pl.BlockSpec((CHUNK, WIDTH), lambda i: (i, 0)), whole((WIDTH,)),
        ]
        + [whole(c.shape) for c in consts],
        out_specs=[
            whole((images, SEQ, WIDTH)), whole((images, ROWS, WIDTH)),
            columns(WIDTH), columns(TAPS),
            pl.BlockSpec((CHUNK, WIDTH), lambda i: (i, 0)), whole((1, WIDTH)),
        ],
        out_shape=[
            jax.ShapeDtypeStruct((images, SEQ, WIDTH), bf16),
            jax.ShapeDtypeStruct((images, ROWS, WIDTH), f32),
            jax.ShapeDtypeStruct((WIDTH, units), f32),
            jax.ShapeDtypeStruct((TAPS, units), f32),
            jax.ShapeDtypeStruct((units, WIDTH), f32),
            jax.ShapeDtypeStruct((1, WIDTH), f32),
        ],
        scratch_shapes=[
            pltpu.VMEM((total, WIDTH), bf16),
            pltpu.VMEM((ROWS, WIDTH), f32),
            pltpu.VMEM((total, CHUNK), f32),
            pltpu.VMEM((total, CHUNK), f32),
            pltpu.VMEM((images, ROWS, WIDTH), f32),
            pltpu.VMEM((total, CHUNK), bf16),
            pltpu.VMEM((total, CHUNK), bf16),
        ],
        compiler_params=params(),
        name="mlp",
    )(n2, cotangent, middle, fc1, conv, fc2, fc2_bias, *consts)


def call_backward(
    tokens, cotangent, n1, packed, probs, attn, att, mid, gn2, wqkv, wproj, pre, post, gain1, gain2, gb2
):
    images = tokens.shape[0]
    smem = pl.BlockSpec(memory_space=pltpu.SMEM)
    vector = whole((WIDTH,))
    return pl.pallas_call(
        attention_backward,
        grid=(images,),
        in_specs=[
            smem, smem, image((SEQ, WIDTH)), image((SEQ, WIDTH)), image((ROWS, WIDTH)),
            image((KEYS, 3 * WIDTH)), image((HEADS, ROWS, KEYS)), image((HEADS, ROWS, KEYS)),
            image((ROWS, WIDTH)), image((ROWS, WIDTH)), image((ROWS, WIDTH)),
            whole((WIDTH, 3 * WIDTH)), whole((WIDTH, WIDTH)), vector, vector,
            whole((1, WIDTH)),
        ],
        out_specs=[
            image((SEQ, WIDTH)), whole((WIDTH, 3 * WIDTH)), whole((WIDTH, WIDTH)),
            whole((SMALL, 128)),
        ],
        out_shape=[
            jax.ShapeDtypeStruct((images, SEQ, WIDTH), f32),
            jax.ShapeDtypeStruct((WIDTH, 3 * WIDTH), f32),
            jax.ShapeDtypeStruct((WIDTH, WIDTH), f32),
            jax.ShapeDtypeStruct((SMALL, 128), f32),
        ],
        scratch_shapes=[
            pltpu.VMEM((ROWS, WIDTH), f32),
            pltpu.VMEM((HEADS, ROWS, KEYS), f32),
            pltpu.VMEM((HEADS, ROWS, KEYS), f32),
            pltpu.VMEM((HEADS, ROWS, KEYS), bf16),
            pltpu.VMEM((2 * HEADS * HEADS, 8, 128), f32),
            pltpu.VMEM((8, WIDTH), f32),
            pltpu.VMEM((128, 128), f32),
        ],
        compiler_params=params(),
        name="attention_backward",
    )(
        pre, post, tokens, cotangent, n1, packed, probs, attn, att, mid, gn2, wqkv, wproj,
        gain1, gain2, gb2,
    )


def local_block(
    tokens, norm1_gain, norm1_bias, wqkv, mix_pre, mix_post, wproj, proj_bias, norm2_gain,
    norm2_bias, fc1, taps, fc2, fc2_bias, cotangent,
):
    n1, packed, probs, attn, att, mid, n2 = call_forward(
        tokens, wqkv, wproj, mix_pre, mix_post, norm1_gain, norm1_bias, proj_bias, norm2_gain,
        norm2_bias,
    )
    block_out, gn2, gfc1, gconv, gfc2, gb2 = call_mlp(n2, cotangent, mid, fc1, taps, fc2, fc2_bias)
    gtok, gqkv, gproj, small = call_backward(
        tokens, cotangent, n1, packed, probs, attn, att, mid, gn2, wqkv, wproj, mix_pre, mix_post,
        norm1_gain, norm2_gain, gb2,
    )
    return block_out, gtok, gqkv, gproj, gfc1, gconv, gfc2, small


SIDES = (8, 4, 2, 1)
DEPTH, PLANE = (0, 1), (2, 3)
ROUNDS = ((PLANE, DEPTH), (DEPTH, PLANE))
FLIPS = ((0, 1), (1, 0), (1, 1))
MESH_IDS = pl.DeviceIdType.MESH
PIECE = 144
PIECE_PARTS = ((0, 96), (96, 48))
BLOCK = 112
BLOCK_PARTS = ((0, 80), (80, 32))
STREAMS = 3


class Place:
    def __init__(self):
        self.dp, self.core = lax.axis_index("dp"), lax.axis_index("tensor")
        self.bits = tuple(lax.rem(self.dp // stride, 2) for stride in SIDES)
        self.pair = (self.dp, 1 - self.core)

    def peer(self, axes, flip):
        dp = self.dp
        for axis, turn in zip(axes, flip):
            if turn:
                dp = dp + (1 - 2 * self.bits[axis]) * SIDES[axis]
        return dp, self.core

    def mine(self, axes):
        return {axis: self.bits[axis] for axis in axes}

    def theirs(self, axes, flip):
        return {
            axis: 1 - self.bits[axis] if turn else self.bits[axis] for axis, turn in zip(axes, flip)
        }

    def everyone(self):
        peers = [self.peer(axes, flip) for axes in (PLANE, DEPTH) for flip in FLIPS]
        return peers + [self.pair]


def meet(partners):
    barrier = pltpu.get_barrier_semaphore()
    for partner in partners:
        pl.semaphore_signal(barrier, inc=1, device_id=partner, device_id_type=MESH_IDS)
    pl.semaphore_wait(barrier, len(partners))


def remote(src, dst, sems, index, device):
    return pltpu.make_async_remote_copy(
        src_ref=src, dst_ref=dst, send_sem=sems.at[(0,) + index], recv_sem=sems.at[(1,) + index],
        device_id=device, device_id_type=MESH_IDS,
    )


def region(fixed, rows):
    return tuple(fixed.get(axis, slice(None)) for axis in range(4)) + (rows,)


def index_of(d):
    return tuple((d // stride) % 2 for stride in SIDES)


class Sum:
    def __init__(self, acc, landing, sems, parts, where):
        self.acc, self.landing, self.sems = acc, landing, sems
        self.parts, self.where = parts, where

    def copy(self, part, turn, peer):
        rows, axes, flip = pl.ds(*self.parts[part]), ROUNDS[part][turn], FLIPS[peer]
        fixed = self.where.theirs(axes, flip)
        if turn == 0:
            dst = self.landing[0].at[peer, :, :, rows]
        else:
            fixed.update(self.where.mine(ROUNDS[part][0]))
            dst = self.landing[1].at[peer, rows]
        return remote(
            self.acc.at[region(fixed, rows)], dst, self.sems, (part, turn, peer),
            self.where.peer(axes, flip),
        )

    def start(self):
        for part in range(2):
            for peer in range(3):
                self.copy(part, 0, peer).start()

    def act(self, turn):
        for part in range(2):
            rows = pl.ds(*self.parts[part])
            first, second = ROUNDS[part]
            for peer in range(3):
                self.copy(part, turn, peer).wait_recv()
            for near in (0, 1) if turn == 0 else (None,):
                for far in (0, 1) if turn == 0 else (None,):
                    fixed = self.where.mine(first)
                    if turn == 0:
                        fixed.update({second[0]: near, second[1]: far})
                        came = [self.landing[0][peer, near, far, rows] for peer in range(3)]
                    else:
                        fixed.update(self.where.mine(second))
                        came = [self.landing[1][peer, rows] for peer in range(3)]
                    spot = region(fixed, rows)
                    total = self.acc[spot].astype(f32)
                    for values in came:
                        total = total + values.astype(f32)
                    self.acc[spot] = total.astype(bf16)
            if turn == 0:
                for peer in range(3):
                    self.copy(part, 1, peer).start()

    def finish(self):
        for part in range(2):
            for turn in range(2):
                for peer in range(3):
                    self.copy(part, turn, peer).wait_send()


class Gather:
    def __init__(self, full, sems, parts, where):
        self.full, self.sems, self.parts, self.where = full, sems, parts, where

    def spot(self, part, turn, flip):
        first, second = ROUNDS[part][::-1]
        if turn == 0:
            fixed = {**self.where.mine(second), **self.where.theirs(first, flip)}
        else:
            fixed = self.where.theirs(second, flip)
        return region(fixed, pl.ds(*self.parts[part]))

    def copy(self, part, turn, peer):
        axes, held = ROUNDS[part][::-1][turn], self.spot(part, turn, (0, 0))
        return remote(
            self.full.at[held], self.full.at[held], self.sems, (part, turn, peer),
            self.where.peer(axes, FLIPS[peer]),
        )

    def start(self):
        for part in range(2):
            for peer in range(3):
                self.copy(part, 0, peer).start()

    def act(self, turn, then=None):
        for part in range(2):
            for peer in range(3):
                self.copy(part, turn, peer).wait_recv()
            if turn == 0:
                for peer in range(3):
                    self.copy(part, 1, peer).start()
            if then is not None:
                for peer in range(3):
                    then(part, turn, peer)

    def finish(self):
        for part in range(2):
            for turn in range(2):
                for peer in range(3):
                    self.copy(part, turn, peer).wait_send()


def tiles(values):
    return jnp.concatenate(
        [values[:, 128 * t : 128 * t + 128] for t in range(values.shape[1] // 128)], axis=0
    )


def untiles(values, count):
    rows = values.shape[0] // count
    return jnp.concatenate([values[t * rows : (t + 1) * rows] for t in range(count)], axis=1)


def block_kernel(
    pre, post, tok, cot, gain1, bias1, pbias, gain2, bias2, fc2b,
    qkv, proj, fc1, conv, bias, fc2, fwd, inv, kh, kl, bh, bl, one,
    block_out, gtok_out, *rest,
):
    fulls, (piece_out, small_out), rest = rest[:STREAMS], rest[STREAMS : STREAMS + 2], rest[STREAMS + 2 :]
    (
        piece_full, piece_other, taps_pad, wqkv, wproj, fc1_full, fc2_full, conv_full,
        inputs, cot_pad, n1, packed, score, probs, attn, att, mid, n2,
        turned, ghat, hid, conv_low, ghid_low, gmid, gmid_low, gatt, low, gpacked, mix,
        rows_out, square, gqkv, gproj, small_sums, small_landed,
        streams_out, streams_came, streams_acc, streams_landing, gconv, att_bufs,
        local_sems, gather_sems, gather_pair_sems, stream_pair_sems, stream_sems, att_sems, att_pair_sems,
    ) = rest
    images = tok.shape[0]
    total = images * ROWS
    half = fc1.shape[1]
    where = Place()
    pair, core, mine = where.pair, where.core, where.bits
    mine_start = pl.multiple_of(core * half, 128)
    other_start = pl.multiple_of((1 - core) * half, 128)
    cols, rows_of = pl.ds(mine_start, half), pl.ds(mine_start, half)
    span = lambda b: slice(b * ROWS, (b + 1) * ROWS)
    spans = [span(b) for b in range(images)]
    inside = row_mask((ROWS, WIDTH))

    both = jnp.concatenate([qkv[...].astype(f32), proj[...].astype(f32)], axis=1)
    piece_full[mine] = tiles(both).astype(bf16)
    taps_pad[...] = jnp.zeros(taps_pad.shape, f32)
    taps_pad[: KS * KS] = conv[...].astype(f32)
    taps_pad[KS * KS : KS * KS + 1] = bias[...].astype(f32).reshape(1, half)
    conv_full[:, cols] = taps_pad[...].astype(bf16)
    meet(where.everyone())
    gather = Gather(piece_full, gather_sems, PIECE_PARTS, where)
    gather.start()
    weights_come = [
        remote(conv_full.at[:, cols], conv_full.at[:, cols], gather_pair_sems, (0,), pair),
        remote(fc2, fc2_full.at[rows_of], gather_pair_sems, (1,), pair),
        remote(fc1, fc1_full.at[:, cols], gather_pair_sems, (2,), pair),
    ]
    forwards = [
        remote(piece_full.at[mine], piece_other.at[mine], gather_pair_sems, (3,), pair)
    ]
    local = [
        pltpu.make_async_copy(fc2, fc2_full.at[rows_of], local_sems.at[0]),
        pltpu.make_async_copy(fc1, fc1_full.at[:, cols], local_sems.at[1]),
    ]
    for copy in weights_come + forwards + local:
        copy.start()

    def forward(part, turn, peer):
        spot = gather.spot(part, turn, FLIPS[peer])
        copy = remote(
            piece_full.at[spot], piece_other.at[spot], gather_pair_sems,
            (4 + 6 * part + 3 * turn + peer,), pair,
        )
        copy.start()
        forwards.append(copy)

    cot_sum = jnp.zeros((1, WIDTH), f32)
    for b in range(images):
        for source, ref in ((tok, inputs), (cot, gmid)):
            ref[b * ROWS + SEQ - 5 : (b + 1) * ROWS] = jnp.zeros((ROWS - SEQ + 5, WIDTH), f32)
            ref[b * ROWS : b * ROWS + SEQ] = source[b].astype(f32)
        grads = gmid[spans[b], :]
        cot_sum = cot_sum + add_rows(grads)
        cot_pad[spans[b], :] = grads.astype(bf16)
    for b in range(images):
        centred, r = centre(inputs[spans[b], :])
        n1[spans[b], :] = jnp.where(inside, centred * r * row(gain1) + row(bias1), 0.0).astype(bf16)

    def prepare(start):
        units = pl.ds(start, half)
        taps = conv_full[:, units]
        turned[:, units] = dot(kh[...], taps) + dot(kl[...], taps) + one[...]
        hid[...] = dot_t(cot_pad[...], fc2_full[units, :])
        for b in range(images):
            ghat[b, :, units] = dot(fwd[...], hid[spans[b], :].astype(bf16))

    gather.act(0, forward)
    for copy in local:
        copy.wait()
    prepare(mine_start)
    for copy in weights_come:
        copy.wait_recv()
    prepare(other_start)
    gather.act(1, forward)
    for copy in forwards:
        copy.wait_recv()
    width = qkv.shape[1]
    flip = core == 1
    for d in range(0, 16, 2):
        blocks = [
            jnp.concatenate([untiles(ref[index_of(e)].astype(f32), 6) for e in (d, d + 1)], axis=0)
            for ref in (piece_full, piece_other)
        ]
        first = jnp.where(flip, blocks[1], blocks[0])
        second = jnp.where(flip, blocks[0], blocks[1])
        rows = slice(24 * d, 24 * d + 48)
        wqkv[rows, :] = jnp.concatenate([first[:, :width], second[:, :width]], axis=1).astype(bf16)
        wproj[rows, :] = jnp.concatenate([first[:, width:], second[:, width:]], axis=1).astype(bf16)

    for n in range(0, 3 * WIDTH, WIDTH):
        gpacked[:, n : n + WIDTH] = dot(n1[...], wqkv[:, n : n + WIDTH]).astype(bf16)
    for b in range(images):
        packed[b, :ROWS] = gpacked[spans[b], :]
        packed[b, ROWS:] = jnp.zeros((KEYS - ROWS, 3 * WIDTH), bf16)
    low_half = lax.broadcasted_iota(jnp.int32, (ROWS, 128), 1) < HEAD_DIM
    key_half = lax.broadcasted_iota(jnp.int32, (KEYS, 128), 1) < HEAD_DIM
    zero = jnp.zeros((ROWS, 128), bf16)
    valid = lax.broadcasted_iota(jnp.int32, (16, KEYS), 1) < SEQ

    def section(b, which, pair_of_heads, count=KEYS):
        start = which * WIDTH + 128 * pair_of_heads
        return packed[b, :count, start : start + 128]

    def find_scores(b):
        for p in range(HEADS // 2):
            query, key = section(b, 0, p, ROWS), section(b, 1, p)
            score[2 * p] = dot_t(jnp.where(low_half, query, zero), key)
            score[2 * p + 1] = dot_t(jnp.where(low_half, zero, query), key)

    def attend(b, carry):
        find_scores(b)

        def rows_step(step, carry):
            rows = pl.ds(pl.multiple_of(step * 16, 16), 16)
            scores = [score[h, rows, :] for h in range(HEADS)]
            found = []
            for g in range(HEADS):
                mixed = scores[0] * (pre[g, 0] * 0.125)
                for h in range(1, HEADS):
                    mixed = mixed + scores[h] * (pre[g, h] * 0.125)
                mixed = jnp.where(valid, mixed, -1e30)
                top = jnp.max(mixed, axis=-1, keepdims=True)
                raised = jnp.exp(mixed - top)
                prob = raised * (1.0 / jnp.sum(raised, axis=-1, keepdims=True))
                probs[b, g, rows, :] = prob
                found.append(prob)
            for g in range(HEADS):
                mixed = found[0] * post[g, 0]
                for h in range(1, HEADS):
                    mixed = mixed + found[h] * post[g, h]
                attn[b, g, rows, :] = mixed.astype(bf16)
            return carry

        lax.fori_loop(0, ROWS // 16, rows_step, 0, unroll=ROWS // 16)
        pieces = []
        for p in range(HEADS // 2):
            value = section(b, 2, p)
            pieces.append(
                jnp.where(low_half, dot(attn[b, 2 * p], value), dot(attn[b, 2 * p + 1], value))
            )
        rows = pl.ds(pl.multiple_of(b * ROWS, 16), ROWS)
        att[rows, :] = jnp.concatenate(pieces, axis=1).astype(bf16)
        return carry

    lax.fori_loop(0, images, attend, 0)
    branch = dot(att[...], wproj[...])
    for b in range(images):
        middle = inputs[spans[b], :] + (branch[spans[b]] + row(pbias))
        mid[spans[b], :] = middle
        centred, r = centre(middle)
        n2[spans[b], :] = jnp.where(inside, centred * r * row(gain2) + row(bias2), 0.0).astype(bf16)

    def exchange_copy(s):
        return remote(streams_out.at[s], streams_came.at[s], stream_pair_sems, (s,), pair)

    sums = [
        Sum(
            streams_acc.at[s], [ref.at[s] for ref in streams_landing], stream_sems.at[s, 0],
            BLOCK_PARTS, where,
        )
        for s in range(STREAMS)
    ]
    gathers = [Gather(fulls[s], stream_sems.at[s, 1], BLOCK_PARTS, where) for s in range(STREAMS)]

    def act(s, step):
        if step < 0:
            sums[s].start()
        elif step < 2:
            sums[s].act(step)
            if step == 1:
                fulls[s][mine] = streams_acc[(s,) + mine]
                gathers[s].start()
        else:
            gathers[s].act(step - 2)

    def blocks():
        filters = tiles(gconv[...])
        empty = jnp.zeros((BLOCK - 104, 128), f32)
        for d in range(16):
            yield index_of(d), jnp.concatenate(
                [
                    tiles(gqkv[24 * d : 24 * d + 24, :STREAM]),
                    tiles(hid[16 * d : 16 * d + 16, :WIDTH]),
                    filters[8 * d : 8 * d + 8],
                    empty,
                ],
                axis=0,
            )

    def mlp(i, carry):
        s, own = i // 2, lax.rem(i, 2)
        owner = (1 - core) * (1 - own) + core * own
        units = pl.ds(pl.multiple_of((owner * STREAMS + s) * STREAM, STREAM), STREAM)
        bias_row = conv_full[:, units].astype(f32)[KS * KS : KS * KS + 1]
        hid[:, :STREAM] = dot(n2[...], fc1_full[:, units]) + bias_row
        kr, ki = turned[:HALF, units], turned[HALF:, units]
        cross_r = jnp.zeros((HALF, STREAM), f32)
        cross_i = jnp.zeros((HALF, STREAM), f32)
        bias_sum = jnp.zeros((1, STREAM), f32)
        for b in range(images):
            activated, slope = gelu_parts(hid[spans[b], :STREAM])
            hid[spans[b], :STREAM] = slope
            x = dot(fwd[...], activated.astype(bf16))
            xr, xi = x[:HALF], x[HALF:]
            yr, yi = ghat[b, :HALF, units], ghat[b, HALF:, units]
            ahead = jnp.concatenate([xr * kr - xi * ki, xr * ki + xi * kr], axis=0).astype(bf16)
            back = jnp.concatenate([yr * kr + yi * ki, yi * kr - yr * ki], axis=0).astype(bf16)
            cross_r = cross_r + (xr * yr + xi * yi)
            cross_i = cross_i + (xi * yr - xr * yi)
            conv_low[spans[b], units] = dot(inv[...], ahead).astype(bf16)
            ghid = (dot(inv[...], back) * hid[spans[b], :STREAM]).astype(bf16)
            bias_sum = bias_sum + add_rows(ghid.astype(f32))
            ghid_low[spans[b], units] = ghid
        cross = jnp.concatenate([cross_r, cross_i], axis=0)
        high = cross.astype(bf16)
        low_part = (cross - high.astype(f32)).astype(bf16)
        last = lax.broadcasted_iota(jnp.int32, (TAPS, STREAM), 0) == KS * KS
        gconv[...] = jnp.where(
            last, bias_sum, dot(bh[...], high) + dot(bl[...], high) + dot(bh[...], low_part)
        )
        hid[:STREAM, :WIDTH] = t_dot(conv_low[:, units], cot_pad[...])
        gqkv[:, :STREAM] = t_dot(n2[...], ghid_low[:, units])

        @pl.when(own == 0)
        def _():
            for index, values in blocks():
                streams_out[(s,) + index] = values.astype(bf16)
            exchange_copy(s).start()

        @pl.when(own == 1)
        def _():
            exchange_copy(s).wait_recv()
            for index, values in blocks():
                came = streams_came[(s,) + index].astype(f32)
                streams_acc[(s,) + index] = (values + came).astype(bf16)

        plan = {1: ((0, -1),), 3: ((0, 0), (1, -1)), 4: ((0, 1),), 5: ((2, -1), (1, 0), (0, 2))}
        for turn, items in plan.items():

            @pl.when(i == turn)
            def _():
                for item in items:
                    act(*item)

        return carry

    lax.fori_loop(0, 2 * STREAMS, mlp, 0)

    hid[:, :WIDTH] = dot_t(ghid_low[...], fc1_full[...])
    hid[:, WIDTH:] = dot(conv_low[...], fc2_full[...])
    gain_sum = jnp.zeros((1, WIDTH), f32)
    bias_sum = jnp.zeros((1, WIDTH), f32)
    proj_sum = jnp.zeros((1, WIDTH), f32)
    for b in range(images):
        middle = mid[spans[b], :]
        block_out[b] = (middle + (hid[spans[b], WIDTH:] + row(fc2b)))[:SEQ].astype(bf16)
        centred, r = centre(middle)
        grad = hid[spans[b], :WIDTH]
        back, gain_rows = norm_back(centred, r, row(gain2), grad)
        gain_sum = gain_sum + add_rows(gain_rows)
        bias_sum = bias_sum + add_rows(grad)
        whole_grad = gmid[spans[b], :] + back
        gmid[spans[b], :] = whole_grad
        rounded = whole_grad.astype(bf16)
        proj_sum = proj_sum + add_rows(rounded.astype(f32))
        gmid_low[spans[b], :] = rounded
    act(1, 1)
    gatt[...] = dot_t(gmid_low[...], wproj[...]).astype(bf16)
    mix[...] = jnp.zeros_like(mix)

    def fold(values):
        values = values[:, :128] + values[:, 128:]
        return values[:8] + values[8:]

    plan = {(0, 3): ((1, 2), (2, 0)), (1, 3): ((2, 1),), (2, 3): ((2, 2),)}

    def poll_at(b, spot):
        for (image_index, at), items in plan.items():
            if at == spot:

                @pl.when(b == image_index)
                def _():
                    for item in items:
                        act(*item)

    def put_weight(g, values):
        ghat[1, :ROWS, KEYS * g : KEYS * (g + 1)] = values

    def back_image(b, carry):
        rows_of_image = pl.ds(pl.multiple_of(b * ROWS, 16), ROWS)
        find_scores(b)
        for p in range(HEADS // 2):
            value = section(b, 2, p)
            ahead = gatt[rows_of_image, 128 * p : 128 * p + 128]
            put_weight(2 * p, dot_t(jnp.where(low_half, ahead, zero), value))
            put_weight(2 * p + 1, dot_t(jnp.where(low_half, zero, ahead), value))
        poll_at(b, 0)

        def back_step(step, carry):
            rows = pl.ds(pl.multiple_of(step * 16, 16), 16)
            weights = [ghat[1, rows, KEYS * g : KEYS * (g + 1)] for g in range(HEADS)]
            mixed = []
            for h in range(HEADS):
                prob = probs[b, h, rows, :]
                ahead = weights[0] * post[0, h]
                for g in range(1, HEADS):
                    ahead = ahead + weights[g] * post[g, h]
                for g in range(HEADS):
                    mix[HEADS * HEADS + g * HEADS + h] += fold(weights[g] * prob)
                inner = jnp.sum(prob * ahead, axis=-1, keepdims=True)
                mixed.append(prob * (ahead - inner))
            for h in range(HEADS):
                scores = score[h, rows, :]
                sums = mixed[0] * pre[0, h]
                for g in range(1, HEADS):
                    sums = sums + mixed[g] * pre[g, h]
                low[h, rows, :] = sums.astype(bf16)
                for g in range(HEADS):
                    mix[g * HEADS + h] += fold(mixed[g] * scores)
            return carry

        lax.fori_loop(0, 7, back_step, 0, unroll=7)
        poll_at(b, 1)
        lax.fori_loop(7, ROWS // 16, back_step, 0, unroll=6)
        poll_at(b, 2)
        queries, keys, values = [], [], []
        for p in range(HEADS // 2):
            query, key = section(b, 0, p, ROWS), section(b, 1, p)
            ahead = gatt[rows_of_image, 128 * p : 128 * p + 128]
            even, odd = low[2 * p], low[2 * p + 1]
            queries.append(jnp.where(low_half, dot(even, key), dot(odd, key)) * 0.125)
            keys.append(jnp.where(key_half, t_dot(even, query), t_dot(odd, query))[:ROWS] * 0.125)
            values.append(
                jnp.where(
                    key_half, t_dot(attn[b, 2 * p], ahead), t_dot(attn[b, 2 * p + 1], ahead)
                )[:ROWS]
            )
        gpacked[rows_of_image, :] = jnp.concatenate(queries + keys + values, axis=1).astype(bf16)
        poll_at(b, 3)
        return carry

    lax.fori_loop(0, images, back_image, 0)
    gproj[...] = t_dot(att[...], gmid_low[...])
    for n in range(0, 3 * WIDTH, WIDTH):
        gqkv[:, n : n + WIDTH] = t_dot(n1[...], gpacked[:, n : n + WIDTH])

    width, proj_width = gqkv.shape[1] // 2, gproj.shape[1] // 2

    def pieces(side):
        for d in range(16):
            rows = slice(24 * d, 24 * d + 24)
            both = jnp.concatenate(
                [
                    gqkv[rows, side * width : (side + 1) * width],
                    gproj[rows, side * proj_width : (side + 1) * proj_width],
                ],
                axis=1,
            )
            yield index_of(d), tiles(both)

    for side in range(2):

        @pl.when(core == side)
        def _():
            for index, values in pieces(1 - side):
                att_bufs["out"][index] = values.astype(bf16)

    exchange = remote(att_bufs["out"], att_bufs["came"], att_pair_sems, (0,), pair)
    exchange.start()
    hid[:, :WIDTH] = dot_t(gpacked[...], wqkv[...])
    attention = Sum(att_bufs["acc"], att_bufs["landing"], att_sems, PIECE_PARTS, where)
    exchange.wait_recv()
    for side in range(2):

        @pl.when(core == side)
        def _():
            for index, values in pieces(side):
                came = att_bufs["came"][index].astype(f32)
                att_bufs["acc"][index] = (values + came).astype(bf16)

    attention.start()
    norm_gain = jnp.zeros((1, WIDTH), f32)
    norm_bias = jnp.zeros((1, WIDTH), f32)
    for b in range(images):
        centred, r = centre(inputs[spans[b], :])
        grad = hid[spans[b], :WIDTH]
        back, gain_rows = norm_back(centred, r, row(gain1), grad)
        norm_gain = norm_gain + add_rows(gain_rows)
        norm_bias = norm_bias + add_rows(grad)
        gtok_out[b] = (gmid[spans[b], :] + back)[:SEQ]
    rows_out[...] = jnp.concatenate(
        [norm_gain, norm_bias, proj_sum, gain_sum, bias_sum, cot_sum, jnp.zeros((2, WIDTH), f32)],
        axis=0,
    )
    for t in range(WIDTH // 128):
        small_sums[0, 8 * t : 8 * t + 8] = rows_out[:, 128 * t : 128 * t + 128]
    square[...] = jnp.zeros_like(square)
    square[: 2 * HEADS * HEADS] = jnp.sum(mix[...], axis=1)
    line = add_rows(square[...].T)
    small_sums[0, 24:] = jnp.concatenate([line, jnp.zeros((SMALL - 25, 128), f32)], axis=0)

    def small_copy(turn, peer):
        if turn == 0:
            device = pair
        else:
            device = where.peer((PLANE, DEPTH)[turn - 1], FLIPS[peer])
        index = 0 if turn == 0 else 3 * turn - 2 + peer
        return remote(
            small_sums.at[turn], small_landed.at[index], att_pair_sems, (1 + index,), device
        )

    small_counts = (1, 3, 3)

    def small_start(turn):
        for peer in range(small_counts[turn]):
            small_copy(turn, peer).start()

    def small_take(turn):
        total = small_sums[turn]
        for peer in range(small_counts[turn]):
            small_copy(turn, peer).wait_recv()
            total = total + small_landed[0 if turn == 0 else 3 * turn - 2 + peer]
        return total

    small_start(0)
    small_sums[1] = small_take(0)
    small_start(1)
    attention.act(0)
    small_sums[2] = small_take(1)
    small_start(2)
    for s in range(STREAMS):
        act(s, 3)
    small_out[...] = small_take(2)
    attention.act(1)
    piece_out[...] = att_bufs["acc"][mine]
    for copy in weights_come + forwards + [exchange]:
        copy.wait_send()
    for turn in range(3):
        for peer in range(small_counts[turn]):
            small_copy(turn, peer).wait_send()
    for s in range(STREAMS):
        exchange_copy(s).wait_send()
    gather.finish()
    attention.finish()
    for s in range(STREAMS):
        sums[s].finish()
        gathers[s].finish()


def call_block(
    pre, post, tok, cot, gain1, bias1, pbias, gain2, bias2, fc2b, qkv, proj, fc1, conv, bias, fc2
):
    images, half = tok.shape[0], fc1.shape[1]
    units, total = 2 * half, images * ROWS
    forward, inverse, kernel, back, one = fourier()
    kernel_high, kernel_low = split(kernel)
    back_high, back_low = split(back)
    consts = [
        jnp.asarray(forward.astype(np.float32).astype(bf16)),
        jnp.asarray(inverse.astype(np.float32).astype(bf16)),
        jnp.asarray(kernel_high), jnp.asarray(kernel_low),
        jnp.asarray(back_high), jnp.asarray(back_low),
        jnp.asarray(one.astype(np.float32)),
    ]
    vmem = pl.BlockSpec(memory_space=pltpu.VMEM)
    smem = pl.BlockSpec(memory_space=pltpu.SMEM)
    hbm = pl.BlockSpec(memory_space=pl.ANY)

    def bufs(rows):
        buffer = lambda free: pltpu.VMEM((2,) * free + (rows, 128), bf16)
        return {
            "acc": buffer(4), "out": buffer(4), "came": buffer(4),
            "landing": [
                pltpu.VMEM((3, 2, 2, rows, 128), bf16), pltpu.VMEM((3, rows, 128), bf16),
            ],
        }

    stacked = lambda free: pltpu.VMEM((STREAMS,) + (2,) * free + (BLOCK, 128), bf16)
    tall = lambda width, dtype: pltpu.VMEM((total, width), dtype)
    cube = lambda dtype: pltpu.VMEM((HEADS, ROWS, KEYS), dtype)
    scratch = dict(
        piece_full=pltpu.VMEM((2, 2, 2, 2, PIECE, 128), bf16),
        piece_other=pltpu.VMEM((2, 2, 2, 2, PIECE, 128), bf16),
        taps_pad=pltpu.VMEM((TAPS, half), f32),
        wqkv=pltpu.VMEM((WIDTH, 3 * WIDTH), bf16),
        wproj=pltpu.VMEM((WIDTH, WIDTH), bf16),
        fc1_full=pltpu.VMEM((WIDTH, units), bf16),
        fc2_full=pltpu.VMEM((units, WIDTH), bf16),
        conv_full=pltpu.VMEM((TAPS, units), bf16),
        inputs=tall(WIDTH, f32),
        cot_pad=tall(WIDTH, bf16),
        n1=tall(WIDTH, bf16),
        packed=pltpu.VMEM((images, KEYS, 3 * WIDTH), bf16),
        score=cube(f32),
        probs=pltpu.VMEM((images, HEADS, ROWS, KEYS), f32),
        attn=pltpu.VMEM((images, HEADS, ROWS, KEYS), bf16),
        att=tall(WIDTH, bf16),
        mid=tall(WIDTH, f32),
        n2=tall(WIDTH, bf16),
        turned=pltpu.VMEM((COEFS, units), f32),
        ghat=pltpu.VMEM((images, COEFS, units), f32),
        hid=tall(half, f32),
        conv_low=tall(units, bf16),
        ghid_low=tall(units, bf16),
        gmid=tall(WIDTH, f32),
        gmid_low=tall(WIDTH, bf16),
        gatt=tall(WIDTH, bf16),
        low=cube(bf16),
        gpacked=tall(3 * WIDTH, bf16),
        mix=pltpu.VMEM((2 * HEADS * HEADS, 8, 128), f32),
        rows_out=pltpu.VMEM((8, WIDTH), f32),
        square=pltpu.VMEM((128, 128), f32),
        gqkv=pltpu.VMEM((WIDTH, 3 * WIDTH), f32),
        gproj=pltpu.VMEM((WIDTH, WIDTH), f32),
        small_sums=pltpu.VMEM((3, SMALL, 128), f32),
        small_landed=pltpu.VMEM((7, SMALL, 128), f32),
        streams_out=stacked(4),
        streams_came=stacked(4),
        streams_acc=stacked(4),
        streams_landing=[
            pltpu.VMEM((STREAMS, 3, 2, 2, BLOCK, 128), bf16),
            pltpu.VMEM((STREAMS, 3, BLOCK, 128), bf16),
        ],
        gconv=pltpu.VMEM((TAPS, STREAM), f32),
        att_bufs=bufs(PIECE),
        local_sems=pltpu.SemaphoreType.DMA((2,)),
        gather_sems=pltpu.SemaphoreType.DMA((2, 2, 2, 3)),
        gather_pair_sems=pltpu.SemaphoreType.DMA((2, 16)),
        stream_pair_sems=pltpu.SemaphoreType.DMA((2, STREAMS)),
        stream_sems=pltpu.SemaphoreType.DMA((STREAMS, 2, 2, 2, 2, 3)),
        att_sems=pltpu.SemaphoreType.DMA((2, 2, 2, 3)),
        att_pair_sems=pltpu.SemaphoreType.DMA((2, 8)),
    )
    return pl.pallas_call(
        block_kernel,
        in_specs=[smem] * 2 + [vmem] * 10 + [hbm] + [vmem] * 2 + [hbm] + [vmem] * len(consts),
        out_specs=[vmem] * (4 + STREAMS),
        out_shape=[
            jax.ShapeDtypeStruct(tok.shape, bf16),
            jax.ShapeDtypeStruct(tok.shape, f32),
        ]
        + [jax.ShapeDtypeStruct((2, 2, 2, 2, BLOCK, 128), bf16)] * STREAMS
        + [
            jax.ShapeDtypeStruct((PIECE, 128), bf16),
            jax.ShapeDtypeStruct((SMALL, 128), f32),
        ],
        scratch_shapes=list(scratch.values()),
        compiler_params=pltpu.CompilerParams(
            vmem_limit_bytes=VMEM, collective_id=0, has_side_effects=True
        ),
        name="block",
    )(
        pre, post, tok, cot, gain1, bias1, pbias, gain2, bias2, fc2b, qkv, proj, fc1, conv, bias,
        fc2, *consts,
    )


def finish_kernel(
    t0, t1, t2, piece, small, gfc1, gb1, gconv, gfc2, gqkv, gproj, g1, b1, pb, g2, b2, fb,
    pre, post, taps, mixes,
):
    for s, total in enumerate((t0, t1, t2)):
        side = slice(s * STREAM, (s + 1) * STREAM)
        for d in range(16):
            block = total[index_of(d)].astype(f32)
            gfc1[24 * d : 24 * d + 24, side] = untiles(block[:48], 2)
            gfc2[s * STREAM + 16 * d : s * STREAM + 16 * d + 16, :] = untiles(block[48:96], 3)
            taps[8 * d : 8 * d + 8, :] = block[96:104]
        filters = untiles(taps[...], 2)
        gconv[:, side] = filters[: KS * KS]
        gb1[side] = filters[KS * KS]
    both = untiles(piece[...].astype(f32), 6)
    width = gqkv.shape[1]
    gqkv[...] = both[:, :width]
    gproj[...] = both[:, width:]
    rows = untiles(small[:24], 3)
    for index, ref in enumerate((g1, b1, pb, g2, b2, fb)):
        ref[...] = rows[index].reshape(ref.shape)
    line = small[24:25]
    for index, ref in enumerate((pre, post)):
        for g in range(HEADS):
            start = HEADS * HEADS * index + HEADS * g
            mixes[index, g : g + 1, :HEADS] = line[:, start : start + HEADS]
    pre[...] = mixes[0, :HEADS, :HEADS] * 0.125
    post[...] = mixes[1, :HEADS, :HEADS]


def call_finish(totals, piece, small, half):
    vmem = pl.BlockSpec(memory_space=pltpu.VMEM)
    shape = lambda *dims: jax.ShapeDtypeStruct(dims, f32)
    return pl.pallas_call(
        finish_kernel,
        in_specs=[vmem] * (STREAMS + 2),
        out_specs=[vmem] * 14,
        out_shape=[
            shape(WIDTH, half), shape(half), shape(KS * KS, half), shape(half, WIDTH),
            shape(24, 3 * WIDTH // 2), shape(24, WIDTH // 2),
        ]
        + [shape(WIDTH)] * 6
        + [shape(HEADS, HEADS)] * 2,
        scratch_shapes=[pltpu.VMEM((128, 128), f32), pltpu.VMEM((2, 8, 128), f32)],
        compiler_params=pltpu.CompilerParams(vmem_limit_bytes=VMEM),
        name="finish",
    )(*totals, piece, small)


def shards_any(
    tokens, norm1_gain, norm1_bias, qkv_weight, mix_pre, mix_post, proj_weight, proj_bias,
    norm2_gain, norm2_bias, fc1_weight, fc1_bias, conv_weight, fc2_weight, fc2_bias, cotangent,
):
    gather = lambda v, axis, dim: lax.all_gather(v, axis, axis=dim, tiled=True)
    both = jnp.concatenate([qkv_weight, proj_weight], axis=1)
    pair = lax.all_gather(gather(both, "dp", 0), "tensor", axis=0)
    columns = qkv_weight.shape[1]
    wqkv = jnp.concatenate([pair[0, :, :columns], pair[1, :, :columns]], axis=1)
    wproj = jnp.concatenate([pair[0, :, columns:], pair[1, :, columns:]], axis=1)
    fc1 = gather(fc1_weight, "tensor", 1)
    taps = jnp.concatenate([conv_weight, fc1_bias[None]], axis=0)
    taps = jnp.pad(gather(taps, "tensor", 1), ((0, TAPS - KS * KS - 1), (0, 0)))
    fc2 = gather(fc2_weight, "tensor", 0)
    block_out, gtok, gqkv, gproj, gfc1, gconv, gfc2, small = local_block(
        tokens, norm1_gain, norm1_bias, wqkv, mix_pre, mix_post, wproj, proj_bias, norm2_gain,
        norm2_bias, fc1, taps, fc2, fc2_bias, cotangent,
    )
    scatter = lambda v, axis, dim: lax.psum_scatter(v, axis, scatter_dimension=dim, tiled=True)
    gqkv = scatter(scatter(gqkv, "tensor", 1), "dp", 0)
    gproj = scatter(scatter(gproj, "tensor", 1), "dp", 0)
    gfc1 = lax.psum(scatter(gfc1, "tensor", 1), "dp")
    gfc2 = lax.psum(scatter(gfc2, "tensor", 0), "dp")
    gconv = lax.psum(scatter(gconv, "tensor", 1), "dp")
    small = lax.psum(small, ("dp", "tensor"))
    rows = jnp.concatenate([small[0:8], small[8:16], small[16:24]], axis=1)
    mixes = small[24, : 2 * HEADS * HEADS].reshape(2, HEADS, HEADS)
    return (
        block_out, gtok, rows[0], rows[1], gqkv, mixes[0] * 0.125, mixes[1], gproj, rows[2],
        rows[3], rows[4], gfc1, gconv[KS * KS], gconv[: KS * KS], gfc2, rows[5],
    )


def shards_sixteen(
    tokens, norm1_gain, norm1_bias, qkv_weight, mix_pre, mix_post, proj_weight, proj_bias,
    norm2_gain, norm2_bias, fc1_weight, fc1_bias, conv_weight, fc2_weight, fc2_bias, cotangent,
):
    block_out, gtok, t0, t1, t2, piece, small = call_block(
        mix_pre, mix_post, tokens, cotangent, norm1_gain, norm1_bias, proj_bias, norm2_gain,
        norm2_bias, fc2_bias, qkv_weight, proj_weight, fc1_weight, conv_weight, fc1_bias,
        fc2_weight,
    )
    gfc1, gb1, gconv, gfc2, gqkv, gproj, g1, b1, pb, g2, b2, fb, pre, post = call_finish(
        (t0, t1, t2), piece, small, fc1_weight.shape[1]
    )
    return (
        block_out, gtok, g1, b1, gqkv, pre, post, gproj, pb, g2, b2, gfc1, gb1, gconv, gfc2, fb
    )


def solution(mesh):
    spec = P(("dp", "tensor"), None, None)
    in_specs = (
        spec, P(), P(), P("dp", "tensor"), P(), P(), P("dp", "tensor"), P(), P(), P(),
        P(None, "tensor"), P("tensor"), P(None, "tensor"), P("tensor", None), P(), spec,
    )
    out_specs = (
        spec, spec, P(), P(), P("dp", "tensor"), P(), P(), P("dp", "tensor"), P(), P(), P(),
        P(None, "tensor"), P("tensor"), P(None, "tensor"), P("tensor", None), P(),
    )
    sixteen = mesh.shape["dp"] == 16 and mesh.shape["tensor"] == 2
    body = shards_sixteen if sixteen else shards_any
    return jax.shard_map(body, mesh=mesh, in_specs=in_specs, out_specs=out_specs, check_vma=False)
```

```python
import functools

import jax
import jax.numpy as jnp
import numpy as np
from jax import lax
from jax.experimental import pallas as pl
from jax.experimental.pallas import tpu as pltpu
from jax.sharding import PartitionSpec as P

HEADS = 6
HEAD_DIM = 64
KS = 7
GRID = 14
POINTS = 17
SEQ = 197
ROWS = 208
TAPS = 64
KEYS = 256
WIDTH = 384
HALF = 152
COEFS = 2 * HALF
CLASS_ROW = 145
CHUNK = 512
STREAM = 256
SMALL = 32
VMEM = 62 * 1024 * 1024

f32 = jnp.float32
bf16 = jnp.bfloat16


def fourier():
    pairs = [(0, 0)]
    for k in range(POINTS):
        for m in range(POINTS):
            other = ((-k) % POINTS, (-m) % POINTS)
            if (k, m) != (0, 0) and (k, m) < other:
                pairs.append((k, m))
    freq = np.array(pairs, np.float64)
    unit = 2.0 * np.pi / POINTS
    spots = np.array([(y, x) for y in range(GRID) for x in range(GRID)], np.float64)
    taps = np.array([(a - 3, c - 3) for a in range(KS) for c in range(KS)], np.float64)
    count = len(pairs)
    angle = unit * freq @ spots.T
    forward = np.zeros((COEFS, ROWS))
    forward[:count, 1:SEQ] = np.cos(angle)
    forward[HALF : HALF + count, 1:SEQ] = -np.sin(angle)
    forward[CLASS_ROW, 0] = 1.0
    weight = np.full((count, 1), 2.0)
    weight[0] = 1.0
    weight = weight / POINTS**2
    inverse = np.zeros((COEFS, ROWS))
    inverse[:count, 1:SEQ] = weight * np.cos(angle)
    inverse[HALF : HALF + count, 1:SEQ] = -weight * np.sin(angle)
    inverse[CLASS_ROW, 0] = 1.0
    turn = unit * freq @ taps.T
    kernel = np.zeros((COEFS, TAPS))
    kernel[:count, : KS * KS] = np.cos(turn)
    kernel[HALF : HALF + count, : KS * KS] = np.sin(turn)
    back = np.zeros((COEFS, TAPS))
    back[:count, : KS * KS] = weight * np.cos(turn)
    back[HALF : HALF + count, : KS * KS] = -weight * np.sin(turn)
    one = np.zeros((COEFS, 1))
    one[CLASS_ROW] = 1.0
    return forward, inverse.T, kernel, back.T, one


def split(matrix):
    high = np.asarray(matrix, np.float32).astype(bf16)
    low = (np.asarray(matrix, np.float32) - high.astype(np.float32)).astype(bf16)
    return high, low


def dot(a, b):
    return lax.dot_general(a, b, (((1,), (0,)), ((), ())), preferred_element_type=f32)


def dot_t(a, b):
    return lax.dot_general(a, b, (((1,), (1,)), ((), ())), preferred_element_type=f32)


def t_dot(a, b):
    return lax.dot_general(a, b, (((0,), (0,)), ((), ())), preferred_element_type=f32)


def centre(values):
    centred = values - jnp.mean(values, axis=-1, keepdims=True)
    spread = jnp.mean(centred * centred, axis=-1, keepdims=True)
    return centred, lax.rsqrt(spread + 1e-05)


def norm_back(centred, r, gain, grad):
    scaled = grad * gain
    moment = jnp.mean(scaled * centred, axis=-1, keepdims=True)
    back = r * (scaled - jnp.mean(scaled, axis=-1, keepdims=True) - centred * (r * r * moment))
    return back, grad * (centred * r)


def row(ref):
    return ref[...].reshape(1, ref.shape[0])


def add_rows(values):
    return jnp.sum(values, axis=0, keepdims=True)


def row_mask(shape):
    return lax.broadcasted_iota(jnp.int32, shape, 0) < SEQ


def attention_forward(
    pre, post, tok, wqkv, wproj, gain1, bias1, pbias, gain2, bias2,
    n1_out, packed_out, probs_out, attn_out, att_out, mid_out, n2_out, pad, score, keys,
):
    pad[SEQ - 5 :] = jnp.zeros((ROWS - SEQ + 5, WIDTH), f32)
    pad[:SEQ] = tok[0].astype(f32)
    inputs = pad[...]
    centred, r = centre(inputs)
    inside = row_mask((ROWS, WIDTH))
    n1 = jnp.where(inside, centred * r * row(gain1) + row(bias1), 0.0).astype(bf16)
    n1_out[0] = n1
    packed = dot(n1, wqkv[...]).astype(bf16)
    packed_out[0, :ROWS] = packed
    packed_out[0, ROWS:] = jnp.zeros((KEYS - ROWS, 3 * WIDTH), bf16)
    low_half = lax.broadcasted_iota(jnp.int32, (ROWS, 128), 1) < HEAD_DIM
    zero = jnp.zeros((ROWS, 128), bf16)
    for p in range(HEADS // 2):
        query = packed_out[0, :ROWS, 128 * p : 128 * p + 128]
        key = packed_out[0, :, WIDTH + 128 * p : WIDTH + 128 * p + 128]
        score[2 * p] = dot_t(jnp.where(low_half, query, zero), key)
        score[2 * p + 1] = dot_t(jnp.where(low_half, zero, query), key)
    valid = lax.broadcasted_iota(jnp.int32, (16, KEYS), 1) < SEQ

    def rows_step(step, carry):
        rows = pl.ds(pl.multiple_of(step * 16, 16), 16)
        scores = [score[h, rows, :] for h in range(HEADS)]
        probs = []
        for g in range(HEADS):
            mixed = scores[0] * (pre[g, 0] * 0.125)
            for h in range(1, HEADS):
                mixed = mixed + scores[h] * (pre[g, h] * 0.125)
            mixed = jnp.where(valid, mixed, -1e30)
            top = jnp.max(mixed, axis=-1, keepdims=True)
            raised = jnp.exp(mixed - top)
            prob = raised * (1.0 / jnp.sum(raised, axis=-1, keepdims=True))
            probs_out[0, g, rows, :] = prob
            probs.append(prob)
        for g in range(HEADS):
            mixed = probs[0] * post[g, 0]
            for h in range(1, HEADS):
                mixed = mixed + probs[h] * post[g, h]
            attn_out[0, g, rows, :] = mixed.astype(bf16)
        return carry

    lax.fori_loop(0, ROWS // 16, rows_step, 0)
    pieces = []
    for p in range(HEADS // 2):
        value = packed_out[0, :, 2 * WIDTH + 128 * p : 2 * WIDTH + 128 * p + 128]
        pieces.append(
            jnp.where(low_half, dot(attn_out[0, 2 * p], value), dot(attn_out[0, 2 * p + 1], value))
        )
    attended = jnp.concatenate(pieces, axis=1).astype(bf16)
    att_out[0] = attended
    middle = inputs + (dot(attended, wproj[...]) + row(pbias))
    mid_out[0] = middle
    centred, r = centre(middle)
    n2_out[0] = jnp.where(inside, centred * r * row(gain2) + row(bias2), 0.0).astype(bf16)


def gelu_parts(hidden):
    size = jnp.abs(hidden) * np.float32(np.sqrt(0.5))
    t = 1.0 / (1.0 + 0.3275911 * size)
    raised = jnp.exp(-(size * size))
    series = t * (
        0.254829592
        + t * (-0.284496736 + t * (1.421413741 + t * (-1.453152027 + t * 1.061405429)))
    )
    tail = 0.5 * series * raised
    cdf = jnp.where(hidden < 0.0, tail, 1.0 - tail)
    return hidden * cdf, cdf + hidden * (raised * np.float32(1.0 / np.sqrt(2.0 * np.pi)))


def mlp(
    n2, cot, mid, fc1, conv, fc2, fc2b, fwd, inv, kh, kl, bh, bl, one,
    block_out, gn2_out, gfc1_out, gconv_out, gfc2_out, gb2_out,
    cot_pad, pad, hid, grad, out_acc, conv_low, ghid_low,
):
    step = pl.program_id(0)
    images = n2.shape[0]

    @pl.when(step == 0)
    def _():
        total = jnp.zeros((1, WIDTH), f32)
        for b in range(images):
            pad[SEQ - 5 :] = jnp.zeros((ROWS - SEQ + 5, WIDTH), f32)
            pad[:SEQ] = cot[b].astype(f32)
            values = pad[...]
            total = total + add_rows(values)
            cot_pad[b * ROWS : (b + 1) * ROWS] = values.astype(bf16)
        gb2_out[...] = total

    w1 = fc1[...]
    w2 = fc2[...]
    taps = conv[...]
    turned = dot(kh[...], taps) + dot(kl[...], taps) + one[...]
    kr, ki = turned[:HALF], turned[HALF:]
    rows_all = n2[...].reshape(images * ROWS, WIDTH)
    hid[...] = dot(rows_all, w1) + taps.astype(f32)[KS * KS : KS * KS + 1]
    grad[...] = dot_t(cot_pad[...], w2)
    cross_r = jnp.zeros((HALF, CHUNK), f32)
    cross_i = jnp.zeros((HALF, CHUNK), f32)
    bias_sum = jnp.zeros((1, CHUNK), f32)
    for b in range(images):
        span = slice(b * ROWS, (b + 1) * ROWS)
        act, slope = gelu_parts(hid[span, :])
        x = dot(fwd[...], act.astype(bf16))
        y = dot(fwd[...], grad[span, :].astype(bf16))
        xr, xi = x[:HALF], x[HALF:]
        yr, yi = y[:HALF], y[HALF:]
        made = jnp.concatenate([xr * kr - xi * ki, xr * ki + xi * kr], axis=0).astype(bf16)
        back = jnp.concatenate([yr * kr + yi * ki, yi * kr - yr * ki], axis=0).astype(bf16)
        cross_r = cross_r + (xr * yr + xi * yi)
        cross_i = cross_i + (xi * yr - xr * yi)
        conv_low[span, :] = dot(inv[...], made).astype(bf16)
        ghid = (dot(inv[...], back) * slope).astype(bf16)
        bias_sum = bias_sum + add_rows(ghid.astype(f32))
        ghid_low[span, :] = ghid
    cross = jnp.concatenate([cross_r, cross_i], axis=0)
    high = cross.astype(bf16)
    low = (cross - high.astype(f32)).astype(bf16)
    gconv_out[...] = dot(bh[...], high) + dot(bl[...], high) + dot(bh[...], low)
    gconv_out[KS * KS : KS * KS + 1] = bias_sum
    convolved = conv_low[...]
    ghid_all = ghid_low[...]
    part = dot(convolved, w2).reshape(images, ROWS, WIDTH)
    part_grad = dot_t(ghid_all, w1).reshape(images, ROWS, WIDTH)
    gfc2_out[...] = t_dot(convolved, cot_pad[...])
    gfc1_out[...] = t_dot(rows_all, ghid_all)

    @pl.when(step == 0)
    def _():
        out_acc[...] = part
        gn2_out[...] = part_grad

    @pl.when(step > 0)
    def _():
        out_acc[...] += part
        gn2_out[...] += part_grad

    @pl.when(step == pl.num_programs(0) - 1)
    def _():
        for b in range(images):
            result = mid[b] + (out_acc[b] + row(fc2b))
            block_out[b] = result[:SEQ].astype(bf16)


def attention_backward(
    pre, post, tok, cot, n1, packed, probs, attn, att, mid, gn2, wqkv, wproj, gain1, gain2, gb2,
    gtok_out, gqkv_out, gproj_out, small_out,
    pad, score, weight, low, mix, rows_out, square,
):
    step = pl.program_id(0)

    @pl.when(step == 0)
    def _():
        gqkv_out[...] = jnp.zeros_like(gqkv_out)
        gproj_out[...] = jnp.zeros_like(gproj_out)
        rows_out[...] = jnp.zeros_like(rows_out)
        mix[...] = jnp.zeros_like(mix)

    pad[SEQ - 5 :] = jnp.zeros((ROWS - SEQ + 5, WIDTH), f32)
    pad[:SEQ] = cot[0].astype(f32)
    centred, r = centre(mid[0])
    grad = gn2[0]
    back, gain_rows = norm_back(centred, r, row(gain2), grad)
    rows_out[3:4] += add_rows(gain_rows)
    rows_out[4:5] += add_rows(grad)
    gmid = pad[...] + back
    gmid_low = gmid.astype(bf16)
    rows_out[2:3] += add_rows(gmid_low.astype(f32))
    gproj_out[...] += t_dot(att[0], gmid_low)
    gatt = dot_t(gmid_low, wproj[...]).astype(bf16)
    low_half = lax.broadcasted_iota(jnp.int32, (ROWS, 128), 1) < HEAD_DIM
    key_half = lax.broadcasted_iota(jnp.int32, (KEYS, 128), 1) < HEAD_DIM
    zero = jnp.zeros((ROWS, 128), bf16)
    for p in range(HEADS // 2):
        query = packed[0, :ROWS, 128 * p : 128 * p + 128]
        key = packed[0, :, WIDTH + 128 * p : WIDTH + 128 * p + 128]
        value = packed[0, :, 2 * WIDTH + 128 * p : 2 * WIDTH + 128 * p + 128]
        ahead = gatt[:, 128 * p : 128 * p + 128]
        score[2 * p] = dot_t(jnp.where(low_half, query, zero), key)
        score[2 * p + 1] = dot_t(jnp.where(low_half, zero, query), key)
        weight[2 * p] = dot_t(jnp.where(low_half, ahead, zero), value)
        weight[2 * p + 1] = dot_t(jnp.where(low_half, zero, ahead), value)

    def fold(values):
        values = values[:, :128] + values[:, 128:]
        return values[:8] + values[8:]

    def rows_step(index, carry):
        rows = pl.ds(pl.multiple_of(index * 16, 16), 16)
        weights = [weight[g, rows, :] for g in range(HEADS)]
        mixed = []
        for h in range(HEADS):
            prob = probs[0, h, rows, :]
            ahead = weights[0] * post[0, h]
            for g in range(1, HEADS):
                ahead = ahead + weights[g] * post[g, h]
            for g in range(HEADS):
                mix[HEADS * HEADS + g * HEADS + h] += fold(weights[g] * prob)
            inner = jnp.sum(prob * ahead, axis=-1, keepdims=True)
            mixed.append(prob * (ahead - inner))
        for h in range(HEADS):
            scores = score[h, rows, :]
            total = mixed[0] * pre[0, h]
            for g in range(1, HEADS):
                total = total + mixed[g] * pre[g, h]
            low[h, rows, :] = total.astype(bf16)
            for g in range(HEADS):
                mix[g * HEADS + h] += fold(mixed[g] * scores)
        return carry

    lax.fori_loop(0, ROWS // 16, rows_step, 0)
    queries, keys, values = [], [], []
    for p in range(HEADS // 2):
        query = packed[0, :ROWS, 128 * p : 128 * p + 128]
        key = packed[0, :, WIDTH + 128 * p : WIDTH + 128 * p + 128]
        ahead = gatt[:, 128 * p : 128 * p + 128]
        even, odd = low[2 * p], low[2 * p + 1]
        queries.append(jnp.where(low_half, dot(even, key), dot(odd, key)) * 0.125)
        keys.append(jnp.where(key_half, t_dot(even, query), t_dot(odd, query))[:ROWS] * 0.125)
        values.append(
            jnp.where(key_half, t_dot(attn[0, 2 * p], ahead), t_dot(attn[0, 2 * p + 1], ahead))[
                :ROWS
            ]
        )
    gpacked = jnp.concatenate(queries + keys + values, axis=1).astype(bf16)
    gqkv_out[...] += t_dot(n1[0], gpacked)
    gnormed = dot_t(gpacked, wqkv[...])
    pad[:SEQ] = tok[0].astype(f32)
    centred, r = centre(pad[...])
    back, gain_rows = norm_back(centred, r, row(gain1), gnormed)
    rows_out[0:1] += add_rows(gain_rows)
    rows_out[1:2] += add_rows(gnormed)
    gtok_out[0] = (gmid + back)[:SEQ]

    @pl.when(step == pl.num_programs(0) - 1)
    def _():
        rows_out[5:6] = gb2[...]
        for t in range(WIDTH // 128):
            small_out[8 * t : 8 * t + 8] = rows_out[:, 128 * t : 128 * t + 128]
        square[...] = jnp.zeros_like(square)
        square[: 2 * HEADS * HEADS] = jnp.sum(mix[...], axis=1)
        sums = add_rows(square[...].T)
        small_out[24:] = jnp.concatenate([sums, jnp.zeros((SMALL - 25, 128), f32)], axis=0)


def whole(shape):
    return pl.BlockSpec(shape, lambda *_: (0,) * len(shape))


def image(shape):
    return pl.BlockSpec((1,) + shape, lambda i: (i,) + (0,) * len(shape))


def params():
    return pltpu.CompilerParams(vmem_limit_bytes=VMEM, dimension_semantics=("arbitrary",))


def call_forward(tokens, wqkv, wproj, pre, post, gain1, bias1, pbias, gain2, bias2):
    images = tokens.shape[0]
    smem = pl.BlockSpec(memory_space=pltpu.SMEM)
    vector = whole((WIDTH,))
    return pl.pallas_call(
        attention_forward,
        grid=(images,),
        in_specs=[
            smem, smem, image((SEQ, WIDTH)), whole((WIDTH, 3 * WIDTH)), whole((WIDTH, WIDTH)),
            vector, vector, vector, vector, vector,
        ],
        out_specs=[
            image((ROWS, WIDTH)), image((KEYS, 3 * WIDTH)), image((HEADS, ROWS, KEYS)),
            image((HEADS, ROWS, KEYS)), image((ROWS, WIDTH)), image((ROWS, WIDTH)),
            image((ROWS, WIDTH)),
        ],
        out_shape=[
            jax.ShapeDtypeStruct((images, ROWS, WIDTH), bf16),
            jax.ShapeDtypeStruct((images, KEYS, 3 * WIDTH), bf16),
            jax.ShapeDtypeStruct((images, HEADS, ROWS, KEYS), f32),
            jax.ShapeDtypeStruct((images, HEADS, ROWS, KEYS), bf16),
            jax.ShapeDtypeStruct((images, ROWS, WIDTH), bf16),
            jax.ShapeDtypeStruct((images, ROWS, WIDTH), f32),
            jax.ShapeDtypeStruct((images, ROWS, WIDTH), bf16),
        ],
        scratch_shapes=[
            pltpu.VMEM((ROWS, WIDTH), f32),
            pltpu.VMEM((HEADS, ROWS, KEYS), f32),
            pltpu.VMEM((8, 128), f32),
        ],
        compiler_params=params(),
        name="attention_forward",
    )(pre, post, tokens, wqkv, wproj, gain1, bias1, pbias, gain2, bias2)


def call_mlp(n2, cotangent, middle, fc1, conv, fc2, fc2_bias):
    images = n2.shape[0]
    units = fc1.shape[1]
    steps = units // CHUNK
    forward, inverse, kernel, back, one = fourier()
    kernel_high, kernel_low = split(kernel)
    back_high, back_low = split(back)
    consts = [
        jnp.asarray(forward.astype(np.float32).astype(bf16)),
        jnp.asarray(inverse.astype(np.float32).astype(bf16)),
        jnp.asarray(kernel_high), jnp.asarray(kernel_low),
        jnp.asarray(back_high), jnp.asarray(back_low),
        jnp.asarray(one.astype(np.float32)),
    ]
    columns = lambda rows: pl.BlockSpec((rows, CHUNK), lambda i: (0, i))
    total = images * ROWS
    return pl.pallas_call(
        mlp,
        grid=(steps,),
        in_specs=[
            whole((images, ROWS, WIDTH)), whole((images, SEQ, WIDTH)), whole((images, ROWS, WIDTH)),
            columns(WIDTH), columns(TAPS),
            pl.BlockSpec((CHUNK, WIDTH), lambda i: (i, 0)), whole((WIDTH,)),
        ]
        + [whole(c.shape) for c in consts],
        out_specs=[
            whole((images, SEQ, WIDTH)), whole((images, ROWS, WIDTH)),
            columns(WIDTH), columns(TAPS),
            pl.BlockSpec((CHUNK, WIDTH), lambda i: (i, 0)), whole((1, WIDTH)),
        ],
        out_shape=[
            jax.ShapeDtypeStruct((images, SEQ, WIDTH), bf16),
            jax.ShapeDtypeStruct((images, ROWS, WIDTH), f32),
            jax.ShapeDtypeStruct((WIDTH, units), f32),
            jax.ShapeDtypeStruct((TAPS, units), f32),
            jax.ShapeDtypeStruct((units, WIDTH), f32),
            jax.ShapeDtypeStruct((1, WIDTH), f32),
        ],
        scratch_shapes=[
            pltpu.VMEM((total, WIDTH), bf16),
            pltpu.VMEM((ROWS, WIDTH), f32),
            pltpu.VMEM((total, CHUNK), f32),
            pltpu.VMEM((total, CHUNK), f32),
            pltpu.VMEM((images, ROWS, WIDTH), f32),
            pltpu.VMEM((total, CHUNK), bf16),
            pltpu.VMEM((total, CHUNK), bf16),
        ],
        compiler_params=params(),
        name="mlp",
    )(n2, cotangent, middle, fc1, conv, fc2, fc2_bias, *consts)


def call_backward(
    tokens, cotangent, n1, packed, probs, attn, att, mid, gn2, wqkv, wproj, pre, post, gain1, gain2, gb2
):
    images = tokens.shape[0]
    smem = pl.BlockSpec(memory_space=pltpu.SMEM)
    vector = whole((WIDTH,))
    return pl.pallas_call(
        attention_backward,
        grid=(images,),
        in_specs=[
            smem, smem, image((SEQ, WIDTH)), image((SEQ, WIDTH)), image((ROWS, WIDTH)),
            image((KEYS, 3 * WIDTH)), image((HEADS, ROWS, KEYS)), image((HEADS, ROWS, KEYS)),
            image((ROWS, WIDTH)), image((ROWS, WIDTH)), image((ROWS, WIDTH)),
            whole((WIDTH, 3 * WIDTH)), whole((WIDTH, WIDTH)), vector, vector,
            whole((1, WIDTH)),
        ],
        out_specs=[
            image((SEQ, WIDTH)), whole((WIDTH, 3 * WIDTH)), whole((WIDTH, WIDTH)),
            whole((SMALL, 128)),
        ],
        out_shape=[
            jax.ShapeDtypeStruct((images, SEQ, WIDTH), f32),
            jax.ShapeDtypeStruct((WIDTH, 3 * WIDTH), f32),
            jax.ShapeDtypeStruct((WIDTH, WIDTH), f32),
            jax.ShapeDtypeStruct((SMALL, 128), f32),
        ],
        scratch_shapes=[
            pltpu.VMEM((ROWS, WIDTH), f32),
            pltpu.VMEM((HEADS, ROWS, KEYS), f32),
            pltpu.VMEM((HEADS, ROWS, KEYS), f32),
            pltpu.VMEM((HEADS, ROWS, KEYS), bf16),
            pltpu.VMEM((2 * HEADS * HEADS, 8, 128), f32),
            pltpu.VMEM((8, WIDTH), f32),
            pltpu.VMEM((128, 128), f32),
        ],
        compiler_params=params(),
        name="attention_backward",
    )(
        pre, post, tokens, cotangent, n1, packed, probs, attn, att, mid, gn2, wqkv, wproj,
        gain1, gain2, gb2,
    )


def local_block(
    tokens, norm1_gain, norm1_bias, wqkv, mix_pre, mix_post, wproj, proj_bias, norm2_gain,
    norm2_bias, fc1, taps, fc2, fc2_bias, cotangent,
):
    n1, packed, probs, attn, att, mid, n2 = call_forward(
        tokens, wqkv, wproj, mix_pre, mix_post, norm1_gain, norm1_bias, proj_bias, norm2_gain,
        norm2_bias,
    )
    block_out, gn2, gfc1, gconv, gfc2, gb2 = call_mlp(n2, cotangent, mid, fc1, taps, fc2, fc2_bias)
    gtok, gqkv, gproj, small = call_backward(
        tokens, cotangent, n1, packed, probs, attn, att, mid, gn2, wqkv, wproj, mix_pre, mix_post,
        norm1_gain, norm2_gain, gb2,
    )
    return block_out, gtok, gqkv, gproj, gfc1, gconv, gfc2, small


SIDES = (8, 4, 2, 1)
DEPTH, PLANE = (0, 1), (2, 3)
ROUNDS = ((PLANE, DEPTH), (DEPTH, PLANE))
FLIPS = ((0, 1), (1, 0), (1, 1))
MESH_IDS = pl.DeviceIdType.MESH
PIECE = 144
PIECE_PARTS = ((0, 96), (96, 48))
BLOCK = 112
BLOCK_PARTS = ((0, 80), (80, 32))
STREAMS = 3
MLP_PLAN = {(1, 4): ((0, -1),), (3, 4): ((1, -1), (0, 0)), (5, 4): ((2, -1), (0, 1), (1, 0))}
BACK_PLAN = {
    (0, 3): ((0, 2), (1, 1)), (1, 3): ((2, 0),), (2, 0): ((1, 2),), (2, 3): ((2, 1),),
    (3, 3): ((2, 2),),
}


class Place:
    def __init__(self):
        self.dp, self.core = lax.axis_index("dp"), lax.axis_index("tensor")
        self.bits = tuple(lax.rem(self.dp // stride, 2) for stride in SIDES)
        self.pair = (self.dp, 1 - self.core)

    def peer(self, axes, flip):
        dp = self.dp
        for axis, turn in zip(axes, flip):
            if turn:
                dp = dp + (1 - 2 * self.bits[axis]) * SIDES[axis]
        return dp, self.core

    def mine(self, axes):
        return {axis: self.bits[axis] for axis in axes}

    def theirs(self, axes, flip):
        return {
            axis: 1 - self.bits[axis] if turn else self.bits[axis] for axis, turn in zip(axes, flip)
        }

    def everyone(self):
        peers = [self.peer(axes, flip) for axes in (PLANE, DEPTH) for flip in FLIPS]
        return peers + [self.pair]


def meet(partners):
    barrier = pltpu.get_barrier_semaphore()
    for partner in partners:
        pl.semaphore_signal(barrier, inc=1, device_id=partner, device_id_type=MESH_IDS)
    pl.semaphore_wait(barrier, len(partners))


def remote(src, dst, sems, index, device):
    return pltpu.make_async_remote_copy(
        src_ref=src, dst_ref=dst, send_sem=sems.at[(0,) + index], recv_sem=sems.at[(1,) + index],
        device_id=device, device_id_type=MESH_IDS,
    )


def region(fixed, rows):
    return tuple(fixed.get(axis, slice(None)) for axis in range(4)) + (rows,)


def index_of(d):
    return tuple((d // stride) % 2 for stride in SIDES)


class Sum:
    def __init__(self, acc, landing, sems, parts, where):
        self.acc, self.landing, self.sems = acc, landing, sems
        self.parts, self.where = parts, where

    def copy(self, part, turn, peer):
        rows, axes, flip = pl.ds(*self.parts[part]), ROUNDS[part][turn], FLIPS[peer]
        fixed = self.where.theirs(axes, flip)
        if turn == 0:
            dst = self.landing[0].at[peer, :, :, rows]
        else:
            fixed.update(self.where.mine(ROUNDS[part][0]))
            dst = self.landing[1].at[peer, rows]
        return remote(
            self.acc.at[region(fixed, rows)], dst, self.sems, (part, turn, peer),
            self.where.peer(axes, flip),
        )

    def start(self):
        for part in range(2):
            for peer in range(3):
                self.copy(part, 0, peer).start()

    def act(self, turn):
        for part in range(2):
            rows = pl.ds(*self.parts[part])
            first, second = ROUNDS[part]
            for peer in range(3):
                self.copy(part, turn, peer).wait_recv()
            for near in (0, 1) if turn == 0 else (None,):
                for far in (0, 1) if turn == 0 else (None,):
                    fixed = self.where.mine(first)
                    if turn == 0:
                        fixed.update({second[0]: near, second[1]: far})
                        came = [self.landing[0][peer, near, far, rows] for peer in range(3)]
                    else:
                        fixed.update(self.where.mine(second))
                        came = [self.landing[1][peer, rows] for peer in range(3)]
                    spot = region(fixed, rows)
                    total = self.acc[spot].astype(f32)
                    for values in came:
                        total = total + values.astype(f32)
                    self.acc[spot] = total.astype(bf16)
            if turn == 0:
                for peer in range(3):
                    self.copy(part, 1, peer).start()

    def finish(self):
        for part in range(2):
            for turn in range(2):
                for peer in range(3):
                    self.copy(part, turn, peer).wait_send()


class Gather:
    def __init__(self, full, sems, parts, where):
        self.full, self.sems, self.parts, self.where = full, sems, parts, where

    def spot(self, part, turn, flip):
        first, second = ROUNDS[part][::-1]
        if turn == 0:
            fixed = {**self.where.mine(second), **self.where.theirs(first, flip)}
        else:
            fixed = self.where.theirs(second, flip)
        return region(fixed, pl.ds(*self.parts[part]))

    def copy(self, part, turn, peer):
        axes, held = ROUNDS[part][::-1][turn], self.spot(part, turn, (0, 0))
        return remote(
            self.full.at[held], self.full.at[held], self.sems, (part, turn, peer),
            self.where.peer(axes, FLIPS[peer]),
        )

    def start(self):
        for part in range(2):
            for peer in range(3):
                self.copy(part, 0, peer).start()

    def act(self, turn, then=None):
        for part in range(2):
            for peer in range(3):
                self.copy(part, turn, peer).wait_recv()
            if turn == 0:
                for peer in range(3):
                    self.copy(part, 1, peer).start()
            if then is not None:
                for peer in range(3):
                    then(part, turn, peer)

    def finish(self):
        for part in range(2):
            for turn in range(2):
                for peer in range(3):
                    self.copy(part, turn, peer).wait_send()


def tiles(values):
    return jnp.concatenate(
        [values[:, 128 * t : 128 * t + 128] for t in range(values.shape[1] // 128)], axis=0
    )


def untiles(values, count):
    rows = values.shape[0] // count
    return jnp.concatenate([values[t * rows : (t + 1) * rows] for t in range(count)], axis=1)


def block_kernel(
    pre, post, tok, cot, gain1, bias1, pbias, gain2, bias2, fc2b,
    qkv, proj, fc1, conv, bias, fc2, fwd, inv, kh, kl, bh, bl, one,
    block_out, gtok_out, fulls_out, piece_out, small_out, *rest,
):
    (
        tok_held, cot_held, out_held, gtok_held, fulls_held,
        piece_full, piece_other, taps_pad, wqkv, wproj, fc1_full, fc2_full, conv_full,
        inputs, cot_pad, n1, packed, score, probs, attn, att, mid, n2,
        turned, ghat, hid, conv_low, ghid_low, gmid, gmid_low, gatt, low, gpacked, mix,
        rows_out, square, gqkv, gproj, small_sums, small_landed,
        streams_out, streams_came, streams_acc, streams_landing, gconv, att_bufs,
        local_sems, leave_sems, gather_sems, gather_pair_sems, stream_pair_sems, stream_sems, att_sems, att_pair_sems,
    ) = rest
    images = tok.shape[1]
    total = images * ROWS
    half = fc1.shape[1]
    where = Place()
    pair, core, mine = where.pair, where.core, where.bits
    mine_start = pl.multiple_of(core * half, 128)
    other_start = pl.multiple_of((1 - core) * half, 128)
    cols, rows_of = pl.ds(mine_start, half), pl.ds(mine_start, half)
    span = lambda b: slice(b * ROWS, (b + 1) * ROWS)
    spans = [span(b) for b in range(images)]
    inside = row_mask((ROWS, WIDTH))
    fulls = [fulls_held.at[s] for s in range(STREAMS)]
    local = [
        pltpu.make_async_copy(src, dst, local_sems.at[index])
        for index, (src, dst) in enumerate(
            (
                (tok, tok_held), (cot, cot_held), (fc2, fc2_full.at[rows_of]),
                (fc1, fc1_full.at[:, cols]),
            )
        )
    ]
    for copy in local:
        copy.start()

    both = jnp.concatenate([qkv[...].astype(f32), proj[...].astype(f32)], axis=1)
    piece_full[mine] = tiles(both).astype(bf16)
    taps_pad[...] = jnp.zeros(taps_pad.shape, f32)
    taps_pad[: KS * KS] = conv[...].astype(f32)
    taps_pad[KS * KS : KS * KS + 1] = bias[...].astype(f32).reshape(1, half)
    conv_full[:, cols] = taps_pad[...].astype(bf16)
    meet(where.everyone())
    gather = Gather(piece_full, gather_sems, PIECE_PARTS, where)
    gather.start()
    weights_come = [
        remote(conv_full.at[:, cols], conv_full.at[:, cols], gather_pair_sems, (0,), pair),
        remote(fc2, fc2_full.at[rows_of], gather_pair_sems, (1,), pair),
        remote(fc1, fc1_full.at[:, cols], gather_pair_sems, (2,), pair),
    ]
    forwards = [
        remote(piece_full.at[mine], piece_other.at[mine], gather_pair_sems, (3,), pair)
    ]
    for copy in weights_come + forwards:
        copy.start()

    def forward(part, turn, peer):
        spot = gather.spot(part, turn, FLIPS[peer])
        copy = remote(
            piece_full.at[spot], piece_other.at[spot], gather_pair_sems,
            (4 + 6 * part + 3 * turn + peer,), pair,
        )
        copy.start()
        forwards.append(copy)

    cot_sum = jnp.zeros((1, WIDTH), f32)
    local[0].wait()
    local[1].wait()
    for source, ref in ((tok_held, inputs), (cot_held, gmid)):
        flat = source[...].reshape(SEQ, images * WIDTH)
        for b in range(images):
            ref[b * ROWS + SEQ - 5 : (b + 1) * ROWS] = jnp.zeros((ROWS - SEQ + 5, WIDTH), f32)
            ref[b * ROWS : b * ROWS + SEQ] = flat[:, b * WIDTH : (b + 1) * WIDTH].astype(f32)
    for b in range(images):
        grads = gmid[spans[b], :]
        cot_sum = cot_sum + add_rows(grads)
        cot_pad[spans[b], :] = grads.astype(bf16)
    for b in range(images):
        centred, r = centre(inputs[spans[b], :])
        n1[spans[b], :] = jnp.where(inside, centred * r * row(gain1) + row(bias1), 0.0).astype(bf16)

    def prepare(start):
        units = pl.ds(start, half)
        taps = conv_full[:, units]
        turned[:, units] = dot(kh[...], taps) + dot(kl[...], taps) + one[...]
        hid[...] = dot_t(cot_pad[...], fc2_full[units, :])
        for b in range(images):
            ghat[b, :, units] = dot(fwd[...], hid[spans[b], :].astype(bf16))

    gather.act(0, forward)
    for copy in local[2:]:
        copy.wait()
    prepare(mine_start)
    for copy in weights_come:
        copy.wait_recv()
    prepare(other_start)
    gather.act(1, forward)
    for copy in forwards:
        copy.wait_recv()
    width = qkv.shape[1]
    flip = core == 1
    for d in range(0, 16, 2):
        blocks = [
            jnp.concatenate([untiles(ref[index_of(e)].astype(f32), 6) for e in (d, d + 1)], axis=0)
            for ref in (piece_full, piece_other)
        ]
        first = jnp.where(flip, blocks[1], blocks[0])
        second = jnp.where(flip, blocks[0], blocks[1])
        rows = slice(24 * d, 24 * d + 48)
        wqkv[rows, :] = jnp.concatenate([first[:, :width], second[:, :width]], axis=1).astype(bf16)
        wproj[rows, :] = jnp.concatenate([first[:, width:], second[:, width:]], axis=1).astype(bf16)

    for n in range(0, 3 * WIDTH, WIDTH):
        gpacked[:, n : n + WIDTH] = dot(n1[...], wqkv[:, n : n + WIDTH]).astype(bf16)
    for b in range(images):
        packed[b, :ROWS] = gpacked[spans[b], :]
        packed[b, ROWS:] = jnp.zeros((KEYS - ROWS, 3 * WIDTH), bf16)
    low_half = lax.broadcasted_iota(jnp.int32, (ROWS, 128), 1) < HEAD_DIM
    key_half = lax.broadcasted_iota(jnp.int32, (KEYS, 128), 1) < HEAD_DIM
    zero = jnp.zeros((ROWS, 128), bf16)
    valid = lax.broadcasted_iota(jnp.int32, (16, KEYS), 1) < SEQ

    def section(b, which, pair_of_heads, count=KEYS):
        start = which * WIDTH + 128 * pair_of_heads
        return packed[b, :count, start : start + 128]

    def find_scores(b):
        for p in range(HEADS // 2):
            query, key = section(b, 0, p, ROWS), section(b, 1, p)
            score[2 * p] = dot_t(jnp.where(low_half, query, zero), key)
            score[2 * p + 1] = dot_t(jnp.where(low_half, zero, query), key)

    def attend(b, carry):
        find_scores(b)

        def rows_step(step, carry):
            rows = pl.ds(pl.multiple_of(step * 16, 16), 16)
            scores = [score[h, rows, :] for h in range(HEADS)]
            found = []
            for g in range(HEADS):
                mixed = scores[0] * (pre[g, 0] * 0.125)
                for h in range(1, HEADS):
                    mixed = mixed + scores[h] * (pre[g, h] * 0.125)
                mixed = jnp.where(valid, mixed, -1e30)
                top = jnp.max(mixed, axis=-1, keepdims=True)
                raised = jnp.exp(mixed - top)
                prob = raised * (1.0 / jnp.sum(raised, axis=-1, keepdims=True))
                probs[b, g, rows, :] = prob
                found.append(prob)
            for g in range(HEADS):
                mixed = found[0] * post[g, 0]
                for h in range(1, HEADS):
                    mixed = mixed + found[h] * post[g, h]
                attn[b, g, rows, :] = mixed.astype(bf16)
            return carry

        lax.fori_loop(0, ROWS // 16, rows_step, 0, unroll=ROWS // 16)
        pieces = []
        for p in range(HEADS // 2):
            value = section(b, 2, p)
            pieces.append(
                jnp.where(low_half, dot(attn[b, 2 * p], value), dot(attn[b, 2 * p + 1], value))
            )
        rows = pl.ds(pl.multiple_of(b * ROWS, 16), ROWS)
        att[rows, :] = jnp.concatenate(pieces, axis=1).astype(bf16)
        return carry

    lax.fori_loop(0, images, attend, 0)
    branch = dot(att[...], wproj[...])
    for b in range(images):
        middle = inputs[spans[b], :] + (branch[spans[b]] + row(pbias))
        mid[spans[b], :] = middle
        centred, r = centre(middle)
        n2[spans[b], :] = jnp.where(inside, centred * r * row(gain2) + row(bias2), 0.0).astype(bf16)

    def exchange_copy(s):
        return remote(streams_out.at[s], streams_came.at[s], stream_pair_sems, (s,), pair)

    sums = [
        Sum(
            streams_acc.at[s], [ref.at[s] for ref in streams_landing], stream_sems.at[s, 0],
            BLOCK_PARTS, where,
        )
        for s in range(STREAMS)
    ]
    gathers = [Gather(fulls[s], stream_sems.at[s, 1], BLOCK_PARTS, where) for s in range(STREAMS)]

    def act(s, step):
        if step < 0:
            sums[s].start()
        elif step < 2:
            sums[s].act(step)
            if step == 1:
                fulls[s][mine] = streams_acc[(s,) + mine]
                gathers[s].start()
        else:
            gathers[s].act(step - 2)

    def poll(plan, index, spot):
        for (turn, at), items in plan.items():
            if at == spot:

                @pl.when(index == turn)
                def _():
                    for item in items:
                        act(*item)

    def blocks():
        filters = tiles(gconv[...])
        empty = jnp.zeros((BLOCK - 104, 128), f32)
        for d in range(16):
            yield index_of(d), jnp.concatenate(
                [
                    tiles(gqkv[24 * d : 24 * d + 24, :STREAM]),
                    tiles(hid[16 * d : 16 * d + 16, :WIDTH]),
                    filters[8 * d : 8 * d + 8],
                    empty,
                ],
                axis=0,
            )

    def mlp(i, carry):
        s, own = i // 2, lax.rem(i, 2)
        owner = (1 - core) * (1 - own) + core * own
        units = pl.ds(pl.multiple_of((owner * STREAMS + s) * STREAM, STREAM), STREAM)
        bias_row = conv_full[:, units].astype(f32)[KS * KS : KS * KS + 1]
        hid[:, :STREAM] = dot(n2[...], fc1_full[:, units]) + bias_row
        kr, ki = turned[:HALF, units], turned[HALF:, units]
        cross_r = jnp.zeros((HALF, STREAM), f32)
        cross_i = jnp.zeros((HALF, STREAM), f32)
        bias_sum = jnp.zeros((1, STREAM), f32)
        held = {}

        def stage_act(b):
            activated, slope = gelu_parts(hid[spans[b], :STREAM])
            hid[spans[b], :STREAM] = slope
            held["act", b] = activated.astype(bf16)

        def stage_turn(b):
            held["x", b] = dot(fwd[...], held.pop(("act", b)))

        def stage_mix(b):
            x = held.pop(("x", b))
            xr, xi = x[:HALF], x[HALF:]
            yr, yi = ghat[b, :HALF, units], ghat[b, HALF:, units]
            ahead = jnp.concatenate([xr * kr - xi * ki, xr * ki + xi * kr], axis=0)
            back = jnp.concatenate([yr * kr + yi * ki, yi * kr - yr * ki], axis=0)
            held["r"] = held["r"] + (xr * yr + xi * yi)
            held["i"] = held["i"] + (xi * yr - xr * yi)
            held["mix", b] = (ahead.astype(bf16), back.astype(bf16))

        def stage_back(b):
            ahead, back = held.pop(("mix", b))
            conv_low[spans[b], units] = dot(inv[...], ahead).astype(bf16)
            ghid = (dot(inv[...], back) * hid[spans[b], :STREAM]).astype(bf16)
            held["bias"] = held["bias"] + add_rows(ghid.astype(f32))
            ghid_low[spans[b], units] = ghid

        held["r"], held["i"], held["bias"] = cross_r, cross_i, bias_sum
        stages = (stage_act, stage_turn, stage_mix, stage_back)
        for beat in range(images + len(stages) - 1):
            for depth in reversed(range(len(stages))):
                if 0 <= beat - depth < images:
                    stages[depth](beat - depth)
        cross_r, cross_i, bias_sum = held["r"], held["i"], held["bias"]
        cross = jnp.concatenate([cross_r, cross_i], axis=0)
        high = cross.astype(bf16)
        low_part = (cross - high.astype(f32)).astype(bf16)
        last = lax.broadcasted_iota(jnp.int32, (TAPS, STREAM), 0) == KS * KS
        gconv[...] = jnp.where(
            last, bias_sum, dot(bh[...], high) + dot(bl[...], high) + dot(bh[...], low_part)
        )
        hid[:STREAM, :WIDTH] = t_dot(conv_low[:, units], cot_pad[...])
        gqkv[:, :STREAM] = t_dot(n2[...], ghid_low[:, units])

        @pl.when(own == 0)
        def _():
            for index, values in blocks():
                streams_out[(s,) + index] = values.astype(bf16)
            exchange_copy(s).start()

        @pl.when(own == 1)
        def _():
            exchange_copy(s).wait_recv()
            for index, values in blocks():
                came = streams_came[(s,) + index].astype(f32)
                streams_acc[(s,) + index] = (values + came).astype(bf16)

        poll(MLP_PLAN, i, images)
        return carry

    lax.fori_loop(0, 2 * STREAMS, mlp, 0)

    hid[:, :WIDTH] = dot_t(ghid_low[...], fc1_full[...])
    gain_sum = jnp.zeros((1, WIDTH), f32)
    bias_sum = jnp.zeros((1, WIDTH), f32)
    proj_sum = jnp.zeros((1, WIDTH), f32)
    for b in range(images):
        middle = mid[spans[b], :]
        centred, r = centre(middle)
        grad = hid[spans[b], :WIDTH]
        back, gain_rows = norm_back(centred, r, row(gain2), grad)
        gain_sum = gain_sum + add_rows(gain_rows)
        bias_sum = bias_sum + add_rows(grad)
        whole_grad = gmid[spans[b], :] + back
        gmid[spans[b], :] = whole_grad
        rounded = whole_grad.astype(bf16)
        proj_sum = proj_sum + add_rows(rounded.astype(f32))
        gmid_low[spans[b], :] = rounded
    gatt[...] = dot_t(gmid_low[...], wproj[...]).astype(bf16)
    mix[...] = jnp.zeros_like(mix)

    def fold(values):
        values = values[:, :128] + values[:, 128:]
        return values[:8] + values[8:]

    def put_weight(g, values):
        ghat[1, :ROWS, KEYS * g : KEYS * (g + 1)] = values

    def back_image(b, carry):
        rows_of_image = pl.ds(pl.multiple_of(b * ROWS, 16), ROWS)
        find_scores(b)
        for p in range(HEADS // 2):
            value = section(b, 2, p)
            ahead = gatt[rows_of_image, 128 * p : 128 * p + 128]
            put_weight(2 * p, dot_t(jnp.where(low_half, ahead, zero), value))
            put_weight(2 * p + 1, dot_t(jnp.where(low_half, zero, ahead), value))
        poll(BACK_PLAN, b, 0)

        def back_step(step, carry):
            rows = pl.ds(pl.multiple_of(step * 16, 16), 16)
            weights = [ghat[1, rows, KEYS * g : KEYS * (g + 1)] for g in range(HEADS)]
            mixed = []
            for h in range(HEADS):
                prob = probs[b, h, rows, :]
                ahead = weights[0] * post[0, h]
                for g in range(1, HEADS):
                    ahead = ahead + weights[g] * post[g, h]
                for g in range(HEADS):
                    mix[HEADS * HEADS + g * HEADS + h] += fold(weights[g] * prob)
                inner = jnp.sum(prob * ahead, axis=-1, keepdims=True)
                mixed.append(prob * (ahead - inner))
            for h in range(HEADS):
                scores = score[h, rows, :]
                sums = mixed[0] * pre[0, h]
                for g in range(1, HEADS):
                    sums = sums + mixed[g] * pre[g, h]
                low[h, rows, :] = sums.astype(bf16)
                for g in range(HEADS):
                    mix[g * HEADS + h] += fold(mixed[g] * scores)
            return carry

        lax.fori_loop(0, 7, back_step, 0, unroll=7)
        poll(BACK_PLAN, b, 1)
        lax.fori_loop(7, ROWS // 16, back_step, 0, unroll=6)
        poll(BACK_PLAN, b, 2)
        queries, keys, values = [], [], []
        for p in range(HEADS // 2):
            query, key = section(b, 0, p, ROWS), section(b, 1, p)
            ahead = gatt[rows_of_image, 128 * p : 128 * p + 128]
            even, odd = low[2 * p], low[2 * p + 1]
            queries.append(jnp.where(low_half, dot(even, key), dot(odd, key)) * 0.125)
            keys.append(jnp.where(key_half, t_dot(even, query), t_dot(odd, query))[:ROWS] * 0.125)
            values.append(
                jnp.where(
                    key_half, t_dot(attn[b, 2 * p], ahead), t_dot(attn[b, 2 * p + 1], ahead)
                )[:ROWS]
            )
        gpacked[rows_of_image, :] = jnp.concatenate(queries + keys + values, axis=1).astype(bf16)
        poll(BACK_PLAN, b, 3)
        return carry

    lax.fori_loop(0, images, back_image, 0)
    gproj[...] = t_dot(att[...], gmid_low[...])
    for n in range(0, 3 * WIDTH, WIDTH):
        gqkv[:, n : n + WIDTH] = t_dot(n1[...], gpacked[:, n : n + WIDTH])

    width, proj_width = gqkv.shape[1] // 2, gproj.shape[1] // 2

    def pieces(side):
        for d in range(16):
            rows = slice(24 * d, 24 * d + 24)
            both = jnp.concatenate(
                [
                    gqkv[rows, side * width : (side + 1) * width],
                    gproj[rows, side * proj_width : (side + 1) * proj_width],
                ],
                axis=1,
            )
            yield index_of(d), tiles(both)

    for side in range(2):

        @pl.when(core == side)
        def _():
            for index, values in pieces(1 - side):
                att_bufs["out"][index] = values.astype(bf16)

    exchange = remote(att_bufs["out"], att_bufs["came"], att_pair_sems, (0,), pair)
    exchange.start()
    hid[:, :WIDTH] = dot_t(gpacked[...], wqkv[...])
    attention = Sum(att_bufs["acc"], att_bufs["landing"], att_sems, PIECE_PARTS, where)
    exchange.wait_recv()
    for side in range(2):

        @pl.when(core == side)
        def _():
            for index, values in pieces(side):
                came = att_bufs["came"][index].astype(f32)
                att_bufs["acc"][index] = (values + came).astype(bf16)

    attention.start()
    hid[:, WIDTH:] = dot(conv_low[...], fc2_full[...])
    for b in range(images):
        result = mid[spans[b], :] + (hid[spans[b], WIDTH:] + row(fc2b))
        gtok_held[:, b, :] = result[:SEQ]
    out_held[...] = gtok_held[...].astype(bf16)
    leaving = [pltpu.make_async_copy(out_held, block_out, leave_sems.at[0])]
    leaving[0].start()
    norm_gain = jnp.zeros((1, WIDTH), f32)
    norm_bias = jnp.zeros((1, WIDTH), f32)
    for b in range(images):
        centred, r = centre(inputs[spans[b], :])
        grad = hid[spans[b], :WIDTH]
        back, gain_rows = norm_back(centred, r, row(gain1), grad)
        norm_gain = norm_gain + add_rows(gain_rows)
        norm_bias = norm_bias + add_rows(grad)
        gtok_held[:, b, :] = (gmid[spans[b], :] + back)[:SEQ]
    leaving.append(pltpu.make_async_copy(gtok_held, gtok_out, leave_sems.at[1]))
    leaving[1].start()
    rows_out[...] = jnp.concatenate(
        [norm_gain, norm_bias, proj_sum, gain_sum, bias_sum, cot_sum, jnp.zeros((2, WIDTH), f32)],
        axis=0,
    )
    for t in range(WIDTH // 128):
        small_sums[0, 8 * t : 8 * t + 8] = rows_out[:, 128 * t : 128 * t + 128]
    square[...] = jnp.zeros_like(square)
    square[: 2 * HEADS * HEADS] = jnp.sum(mix[...], axis=1)
    line = add_rows(square[...].T)
    small_sums[0, 24:] = jnp.concatenate([line, jnp.zeros((SMALL - 25, 128), f32)], axis=0)

    def small_copy(turn, peer):
        if turn == 0:
            device = pair
        else:
            device = where.peer((PLANE, DEPTH)[turn - 1], FLIPS[peer])
        index = 0 if turn == 0 else 3 * turn - 2 + peer
        return remote(
            small_sums.at[turn], small_landed.at[index], att_pair_sems, (1 + index,), device
        )

    small_counts = (1, 3, 3)

    def small_start(turn):
        for peer in range(small_counts[turn]):
            small_copy(turn, peer).start()

    def small_take(turn):
        total = small_sums[turn]
        for peer in range(small_counts[turn]):
            small_copy(turn, peer).wait_recv()
            total = total + small_landed[0 if turn == 0 else 3 * turn - 2 + peer]
        return total

    small_start(0)
    small_sums[1] = small_take(0)
    small_start(1)
    attention.act(0)
    small_sums[2] = small_take(1)
    small_start(2)
    for s in range(STREAMS):
        act(s, 3)
    leaving.append(pltpu.make_async_copy(fulls_held, fulls_out, leave_sems.at[2]))
    leaving[2].start()
    small_out[...] = small_take(2)
    attention.act(1)
    piece_out[...] = att_bufs["acc"][mine]
    for copy in leaving:
        copy.wait()
    for copy in weights_come + forwards + [exchange]:
        copy.wait_send()
    for turn in range(3):
        for peer in range(small_counts[turn]):
            small_copy(turn, peer).wait_send()
    for s in range(STREAMS):
        exchange_copy(s).wait_send()
    gather.finish()
    attention.finish()
    for s in range(STREAMS):
        sums[s].finish()
        gathers[s].finish()


def call_block(
    pre, post, tok, cot, gain1, bias1, pbias, gain2, bias2, fc2b, qkv, proj, fc1, conv, bias, fc2
):
    images, half = tok.shape[1], fc1.shape[1]
    units, total = 2 * half, images * ROWS
    forward, inverse, kernel, back, one = fourier()
    kernel_high, kernel_low = split(kernel)
    back_high, back_low = split(back)
    consts = [
        jnp.asarray(forward.astype(np.float32).astype(bf16)),
        jnp.asarray(inverse.astype(np.float32).astype(bf16)),
        jnp.asarray(kernel_high), jnp.asarray(kernel_low),
        jnp.asarray(back_high), jnp.asarray(back_low),
        jnp.asarray(one.astype(np.float32)),
    ]
    vmem = pl.BlockSpec(memory_space=pltpu.VMEM)
    smem = pl.BlockSpec(memory_space=pltpu.SMEM)
    hbm = pl.BlockSpec(memory_space=pl.ANY)

    def bufs(rows):
        buffer = lambda free: pltpu.VMEM((2,) * free + (rows, 128), bf16)
        return {
            "acc": buffer(4), "out": buffer(4), "came": buffer(4),
            "landing": [
                pltpu.VMEM((3, 2, 2, rows, 128), bf16), pltpu.VMEM((3, rows, 128), bf16),
            ],
        }

    stacked = lambda free: pltpu.VMEM((STREAMS,) + (2,) * free + (BLOCK, 128), bf16)
    tall = lambda width, dtype: pltpu.VMEM((total, width), dtype)
    cube = lambda dtype: pltpu.VMEM((HEADS, ROWS, KEYS), dtype)
    scratch = dict(
        tok_held=pltpu.VMEM(tok.shape, bf16),
        cot_held=pltpu.VMEM(tok.shape, bf16),
        out_held=pltpu.VMEM(tok.shape, bf16),
        gtok_held=pltpu.VMEM(tok.shape, f32),
        fulls_held=stacked(4),
        piece_full=pltpu.VMEM((2, 2, 2, 2, PIECE, 128), bf16),
        piece_other=pltpu.VMEM((2, 2, 2, 2, PIECE, 128), bf16),
        taps_pad=pltpu.VMEM((TAPS, half), f32),
        wqkv=pltpu.VMEM((WIDTH, 3 * WIDTH), bf16),
        wproj=pltpu.VMEM((WIDTH, WIDTH), bf16),
        fc1_full=pltpu.VMEM((WIDTH, units), bf16),
        fc2_full=pltpu.VMEM((units, WIDTH), bf16),
        conv_full=pltpu.VMEM((TAPS, units), bf16),
        inputs=tall(WIDTH, f32),
        cot_pad=tall(WIDTH, bf16),
        n1=tall(WIDTH, bf16),
        packed=pltpu.VMEM((images, KEYS, 3 * WIDTH), bf16),
        score=cube(f32),
        probs=pltpu.VMEM((images, HEADS, ROWS, KEYS), f32),
        attn=pltpu.VMEM((images, HEADS, ROWS, KEYS), bf16),
        att=tall(WIDTH, bf16),
        mid=tall(WIDTH, f32),
        n2=tall(WIDTH, bf16),
        turned=pltpu.VMEM((COEFS, units), f32),
        ghat=pltpu.VMEM((images, COEFS, units), f32),
        hid=tall(half, f32),
        conv_low=tall(units, bf16),
        ghid_low=tall(units, bf16),
        gmid=tall(WIDTH, f32),
        gmid_low=tall(WIDTH, bf16),
        gatt=tall(WIDTH, bf16),
        low=cube(bf16),
        gpacked=tall(3 * WIDTH, bf16),
        mix=pltpu.VMEM((2 * HEADS * HEADS, 8, 128), f32),
        rows_out=pltpu.VMEM((8, WIDTH), f32),
        square=pltpu.VMEM((128, 128), f32),
        gqkv=pltpu.VMEM((WIDTH, 3 * WIDTH), f32),
        gproj=pltpu.VMEM((WIDTH, WIDTH), f32),
        small_sums=pltpu.VMEM((3, SMALL, 128), f32),
        small_landed=pltpu.VMEM((7, SMALL, 128), f32),
        streams_out=stacked(4),
        streams_came=stacked(4),
        streams_acc=stacked(4),
        streams_landing=[
            pltpu.VMEM((STREAMS, 3, 2, 2, BLOCK, 128), bf16),
            pltpu.VMEM((STREAMS, 3, BLOCK, 128), bf16),
        ],
        gconv=pltpu.VMEM((TAPS, STREAM), f32),
        att_bufs=bufs(PIECE),
        local_sems=pltpu.SemaphoreType.DMA((10,)),
        leave_sems=pltpu.SemaphoreType.DMA((3,)),
        gather_sems=pltpu.SemaphoreType.DMA((2, 2, 2, 3)),
        gather_pair_sems=pltpu.SemaphoreType.DMA((2, 16)),
        stream_pair_sems=pltpu.SemaphoreType.DMA((2, STREAMS)),
        stream_sems=pltpu.SemaphoreType.DMA((STREAMS, 2, 2, 2, 2, 3)),
        att_sems=pltpu.SemaphoreType.DMA((2, 2, 2, 3)),
        att_pair_sems=pltpu.SemaphoreType.DMA((2, 8)),
    )
    return pl.pallas_call(
        block_kernel,
        in_specs=[smem] * 2 + [hbm] * 2 + [vmem] * 8 + [hbm] + [vmem] * 2 + [hbm] + [vmem] * len(consts),
        out_specs=[hbm] * 3 + [vmem] * 2,
        out_shape=[
            jax.ShapeDtypeStruct(tok.shape, bf16),
            jax.ShapeDtypeStruct(tok.shape, f32),
        ]
        + [
            jax.ShapeDtypeStruct((STREAMS, 2, 2, 2, 2, BLOCK, 128), bf16),
            jax.ShapeDtypeStruct((PIECE, 128), bf16),
            jax.ShapeDtypeStruct((SMALL, 128), f32),
        ],
        scratch_shapes=list(scratch.values()),
        compiler_params=pltpu.CompilerParams(
            vmem_limit_bytes=VMEM, collective_id=0, has_side_effects=True
        ),
        name="block",
    )(
        pre, post, tok, cot, gain1, bias1, pbias, gain2, bias2, fc2b, qkv, proj, fc1, conv, bias,
        fc2, *consts,
    )


def finish_kernel(
    totals_in, piece, small, out_in, gtok_in, gfc1_out, gb1, gconv, gfc2_out, gqkv, gproj, g1, b1,
    pb, g2, b2, fb, pre, post, out, gtok, totals, out_held, gtok_held, gfc1, gfc2, taps, mixes,
    sems,
):
    coming = [
        pltpu.make_async_copy(totals_in.at[s], totals.at[s], sems.at[s]) for s in range(STREAMS)
    ]
    coming += [
        pltpu.make_async_copy(gtok_in, gtok_held, sems.at[STREAMS]),
        pltpu.make_async_copy(out_in, out_held, sems.at[STREAMS + 1]),
    ]
    for copy in coming:
        copy.start()
    leaving = []

    def leave(src, dst):
        copy = pltpu.make_async_copy(src, dst, sems.at[STREAMS + 2 + len(leaving)])
        copy.start()
        leaving.append(copy)

    both = untiles(piece[...].astype(f32), 6)
    width = gqkv.shape[1]
    gqkv[...] = both[:, :width]
    gproj[...] = both[:, width:]
    rows = untiles(small[:24], 3)
    for index, ref in enumerate((g1, b1, pb, g2, b2, fb)):
        ref[...] = rows[index].reshape(ref.shape)
    line = small[24:25]
    for index, ref in enumerate((pre, post)):
        for g in range(HEADS):
            start = HEADS * HEADS * index + HEADS * g
            mixes[index, g : g + 1, :HEADS] = line[:, start : start + HEADS]
    pre[...] = mixes[0, :HEADS, :HEADS] * 0.125
    post[...] = mixes[1, :HEADS, :HEADS]
    for s in range(STREAMS):
        side = slice(s * STREAM, (s + 1) * STREAM)
        coming[s].wait()
        for d in range(16):
            block = totals[(s,) + index_of(d)].astype(f32)
            gfc1[24 * d : 24 * d + 24, side] = untiles(block[:48], 2)
            gfc2[s * STREAM + 16 * d : s * STREAM + 16 * d + 16, :] = untiles(block[48:96], 3)
            taps[8 * d : 8 * d + 8, :] = block[96:104]
        leave(gfc2.at[side], gfc2_out.at[side])
        leave(gfc1.at[:, side], gfc1_out.at[:, side])
        filters = untiles(taps[...], 2)
        gconv[:, side] = filters[: KS * KS]
        gb1[side] = filters[KS * KS]
        if s == 0:
            coming[STREAMS].wait()
            leave(gtok_held, gtok)
            coming[STREAMS + 1].wait()
            leave(out_held, out)
    for copy in leaving:
        copy.wait()


def call_finish(totals, piece, small, block_out, gtok, half):
    hbm = pl.BlockSpec(memory_space=pl.ANY)
    vmem = pl.BlockSpec(memory_space=pltpu.VMEM)
    shape = lambda *dims: jax.ShapeDtypeStruct(dims, f32)
    return pl.pallas_call(
        finish_kernel,
        in_specs=[hbm] + [vmem] * 2 + [hbm] * 2,
        out_specs=[hbm] + [vmem] * 2 + [hbm] + [vmem] * 10 + [hbm] * 2,
        out_shape=[
            shape(WIDTH, half), shape(half), shape(KS * KS, half), shape(half, WIDTH),
            shape(24, 3 * WIDTH // 2), shape(24, WIDTH // 2),
        ]
        + [shape(WIDTH)] * 6
        + [shape(HEADS, HEADS)] * 2
        + [jax.ShapeDtypeStruct(v.shape, v.dtype) for v in (block_out, gtok)],
        scratch_shapes=[
            pltpu.VMEM(totals.shape, bf16),
            pltpu.VMEM(block_out.shape, bf16), pltpu.VMEM(gtok.shape, f32),
            pltpu.VMEM((WIDTH, half), f32), pltpu.VMEM((half, WIDTH), f32),
            pltpu.VMEM((128, 128), f32), pltpu.VMEM((2, 8, 128), f32),
            pltpu.SemaphoreType.DMA((STREAMS + 2 + 2 * STREAMS + 2,)),
        ],
        compiler_params=pltpu.CompilerParams(vmem_limit_bytes=VMEM),
        name="finish",
    )(totals, piece, small, block_out, gtok)


def shards_any(
    tokens, norm1_gain, norm1_bias, qkv_weight, mix_pre, mix_post, proj_weight, proj_bias,
    norm2_gain, norm2_bias, fc1_weight, fc1_bias, conv_weight, fc2_weight, fc2_bias, cotangent,
):
    gather = lambda v, axis, dim: lax.all_gather(v, axis, axis=dim, tiled=True)
    both = jnp.concatenate([qkv_weight, proj_weight], axis=1)
    pair = lax.all_gather(gather(both, "dp", 0), "tensor", axis=0)
    columns = qkv_weight.shape[1]
    wqkv = jnp.concatenate([pair[0, :, :columns], pair[1, :, :columns]], axis=1)
    wproj = jnp.concatenate([pair[0, :, columns:], pair[1, :, columns:]], axis=1)
    fc1 = gather(fc1_weight, "tensor", 1)
    taps = jnp.concatenate([conv_weight, fc1_bias[None]], axis=0)
    taps = jnp.pad(gather(taps, "tensor", 1), ((0, TAPS - KS * KS - 1), (0, 0)))
    fc2 = gather(fc2_weight, "tensor", 0)
    block_out, gtok, gqkv, gproj, gfc1, gconv, gfc2, small = local_block(
        tokens, norm1_gain, norm1_bias, wqkv, mix_pre, mix_post, wproj, proj_bias, norm2_gain,
        norm2_bias, fc1, taps, fc2, fc2_bias, cotangent,
    )
    scatter = lambda v, axis, dim: lax.psum_scatter(v, axis, scatter_dimension=dim, tiled=True)
    gqkv = scatter(scatter(gqkv, "tensor", 1), "dp", 0)
    gproj = scatter(scatter(gproj, "tensor", 1), "dp", 0)
    gfc1 = lax.psum(scatter(gfc1, "tensor", 1), "dp")
    gfc2 = lax.psum(scatter(gfc2, "tensor", 0), "dp")
    gconv = lax.psum(scatter(gconv, "tensor", 1), "dp")
    small = lax.psum(small, ("dp", "tensor"))
    rows = jnp.concatenate([small[0:8], small[8:16], small[16:24]], axis=1)
    mixes = small[24, : 2 * HEADS * HEADS].reshape(2, HEADS, HEADS)
    return (
        block_out, gtok, rows[0], rows[1], gqkv, mixes[0] * 0.125, mixes[1], gproj, rows[2],
        rows[3], rows[4], gfc1, gconv[KS * KS], gconv[: KS * KS], gfc2, rows[5],
    )


def shards_sixteen(
    tokens, norm1_gain, norm1_bias, qkv_weight, mix_pre, mix_post, proj_weight, proj_bias,
    norm2_gain, norm2_bias, fc1_weight, fc1_bias, conv_weight, fc2_weight, fc2_bias, cotangent,
):
    turn = lambda v: jnp.transpose(v, (1, 0, 2))
    block_out, gtok, totals, piece, small = call_block(
        mix_pre, mix_post, turn(tokens), turn(cotangent), norm1_gain, norm1_bias, proj_bias, norm2_gain,
        norm2_bias, fc2_bias, qkv_weight, proj_weight, fc1_weight, conv_weight, fc1_bias,
        fc2_weight,
    )
    (
        gfc1, gb1, gconv, gfc2, gqkv, gproj, g1, b1, pb, g2, b2, fb, pre, post, block_out, gtok
    ) = call_finish(totals, piece, small, block_out, gtok, fc1_weight.shape[1])
    block_out, gtok = turn(block_out), turn(gtok)
    return (
        block_out, gtok, g1, b1, gqkv, pre, post, gproj, pb, g2, b2, gfc1, gb1, gconv, gfc2, fb
    )


def solution(mesh):
    spec = P(("dp", "tensor"), None, None)
    in_specs = (
        spec, P(), P(), P("dp", "tensor"), P(), P(), P("dp", "tensor"), P(), P(), P(),
        P(None, "tensor"), P("tensor"), P(None, "tensor"), P("tensor", None), P(), spec,
    )
    out_specs = (
        spec, spec, P(), P(), P("dp", "tensor"), P(), P(), P("dp", "tensor"), P(), P(), P(),
        P(None, "tensor"), P("tensor"), P(None, "tensor"), P("tensor", None), P(),
    )
    sixteen = mesh.shape["dp"] == 16 and mesh.shape["tensor"] == 2
    body = shards_sixteen if sixteen else shards_any
    return jax.shard_map(body, mesh=mesh, in_specs=in_specs, out_specs=out_specs, check_vma=False)
```

```python
import functools

import jax
import jax.numpy as jnp
import numpy as np
from jax import lax
from jax.experimental import pallas as pl
from jax.experimental.pallas import tpu as pltpu
from jax.sharding import PartitionSpec as P

HEADS = 6
HEAD_DIM = 64
KS = 7
GRID = 14
POINTS = 17
SEQ = 197
ROWS = 208
TAPS = 64
KEYS = 256
WIDTH = 384
HALF = 160
COEFS = 2 * HALF
CLASS_ROW = 145
CHUNK = 512
STREAM = 256
SMALL = 32
VMEM = 62 * 1024 * 1024

f32 = jnp.float32
bf16 = jnp.bfloat16


def fourier():
    pairs = [(0, 0)]
    for k in range(POINTS):
        for m in range(POINTS):
            other = ((-k) % POINTS, (-m) % POINTS)
            if (k, m) != (0, 0) and (k, m) < other:
                pairs.append((k, m))
    freq = np.array(pairs, np.float64)
    unit = 2.0 * np.pi / POINTS
    spots = np.array([(y, x) for y in range(GRID) for x in range(GRID)], np.float64)
    taps = np.array([(a - 3, c - 3) for a in range(KS) for c in range(KS)], np.float64)
    count = len(pairs)
    angle = unit * freq @ spots.T
    forward = np.zeros((COEFS, ROWS))
    forward[:count, 1:SEQ] = np.cos(angle)
    forward[HALF : HALF + count, 1:SEQ] = -np.sin(angle)
    forward[CLASS_ROW, 0] = 1.0
    weight = np.full((count, 1), 2.0)
    weight[0] = 1.0
    weight = weight / POINTS**2
    inverse = np.zeros((COEFS, ROWS))
    inverse[:count, 1:SEQ] = weight * np.cos(angle)
    inverse[HALF : HALF + count, 1:SEQ] = -weight * np.sin(angle)
    inverse[CLASS_ROW, 0] = 1.0
    turn = unit * freq @ taps.T
    kernel = np.zeros((COEFS, TAPS))
    kernel[:count, : KS * KS] = np.cos(turn)
    kernel[HALF : HALF + count, : KS * KS] = np.sin(turn)
    back = np.zeros((COEFS, TAPS))
    back[:count, : KS * KS] = weight * np.cos(turn)
    back[HALF : HALF + count, : KS * KS] = -weight * np.sin(turn)
    one = np.zeros((COEFS, 1))
    one[CLASS_ROW] = 1.0
    return forward, inverse.T, kernel, back.T, one


def split(matrix):
    high = np.asarray(matrix, np.float32).astype(bf16)
    low = (np.asarray(matrix, np.float32) - high.astype(np.float32)).astype(bf16)
    return high, low


def dot(a, b):
    return lax.dot_general(a, b, (((1,), (0,)), ((), ())), preferred_element_type=f32)


def dot_t(a, b):
    return lax.dot_general(a, b, (((1,), (1,)), ((), ())), preferred_element_type=f32)


def t_dot(a, b):
    return lax.dot_general(a, b, (((0,), (0,)), ((), ())), preferred_element_type=f32)


def centre(values):
    centred = values - jnp.mean(values, axis=-1, keepdims=True)
    spread = jnp.mean(centred * centred, axis=-1, keepdims=True)
    return centred, lax.rsqrt(spread + 1e-05)


def norm_back(centred, r, gain, grad):
    scaled = grad * gain
    moment = jnp.mean(scaled * centred, axis=-1, keepdims=True)
    back = r * (scaled - jnp.mean(scaled, axis=-1, keepdims=True) - centred * (r * r * moment))
    return back, grad * (centred * r)


def row(ref):
    return ref[...].reshape(1, ref.shape[0])


def add_rows(values):
    return jnp.sum(values, axis=0, keepdims=True)


def row_mask(shape):
    return lax.broadcasted_iota(jnp.int32, shape, 0) < SEQ


def attention_forward(
    pre, post, tok, wqkv, wproj, gain1, bias1, pbias, gain2, bias2,
    n1_out, packed_out, probs_out, attn_out, att_out, mid_out, n2_out, pad, score, keys,
):
    pad[SEQ - 5 :] = jnp.zeros((ROWS - SEQ + 5, WIDTH), f32)
    pad[:SEQ] = tok[0].astype(f32)
    inputs = pad[...]
    centred, r = centre(inputs)
    inside = row_mask((ROWS, WIDTH))
    n1 = jnp.where(inside, centred * r * row(gain1) + row(bias1), 0.0).astype(bf16)
    n1_out[0] = n1
    packed = dot(n1, wqkv[...]).astype(bf16)
    packed_out[0, :ROWS] = packed
    packed_out[0, ROWS:] = jnp.zeros((KEYS - ROWS, 3 * WIDTH), bf16)
    low_half = lax.broadcasted_iota(jnp.int32, (ROWS, 128), 1) < HEAD_DIM
    zero = jnp.zeros((ROWS, 128), bf16)
    for p in range(HEADS // 2):
        query = packed_out[0, :ROWS, 128 * p : 128 * p + 128]
        key = packed_out[0, :, WIDTH + 128 * p : WIDTH + 128 * p + 128]
        score[2 * p] = dot_t(jnp.where(low_half, query, zero), key)
        score[2 * p + 1] = dot_t(jnp.where(low_half, zero, query), key)
    valid = lax.broadcasted_iota(jnp.int32, (16, KEYS), 1) < SEQ

    def rows_step(step, carry):
        rows = pl.ds(pl.multiple_of(step * 16, 16), 16)
        scores = [score[h, rows, :] for h in range(HEADS)]
        probs = []
        for g in range(HEADS):
            mixed = scores[0] * (pre[g, 0] * 0.125)
            for h in range(1, HEADS):
                mixed = mixed + scores[h] * (pre[g, h] * 0.125)
            mixed = jnp.where(valid, mixed, -1e30)
            top = jnp.max(mixed, axis=-1, keepdims=True)
            raised = jnp.exp(mixed - top)
            prob = raised * (1.0 / jnp.sum(raised, axis=-1, keepdims=True))
            probs_out[0, g, rows, :] = prob
            probs.append(prob)
        for g in range(HEADS):
            mixed = probs[0] * post[g, 0]
            for h in range(1, HEADS):
                mixed = mixed + probs[h] * post[g, h]
            attn_out[0, g, rows, :] = mixed.astype(bf16)
        return carry

    lax.fori_loop(0, ROWS // 16, rows_step, 0)
    pieces = []
    for p in range(HEADS // 2):
        value = packed_out[0, :, 2 * WIDTH + 128 * p : 2 * WIDTH + 128 * p + 128]
        pieces.append(
            jnp.where(low_half, dot(attn_out[0, 2 * p], value), dot(attn_out[0, 2 * p + 1], value))
        )
    attended = jnp.concatenate(pieces, axis=1).astype(bf16)
    att_out[0] = attended
    middle = inputs + (dot(attended, wproj[...]) + row(pbias))
    mid_out[0] = middle
    centred, r = centre(middle)
    n2_out[0] = jnp.where(inside, centred * r * row(gain2) + row(bias2), 0.0).astype(bf16)


def gelu_parts(hidden):
    size = jnp.abs(hidden) * np.float32(np.sqrt(0.5))
    t = 1.0 / (1.0 + 0.3275911 * size)
    raised = jnp.exp(-(size * size))
    series = t * (
        0.254829592
        + t * (-0.284496736 + t * (1.421413741 + t * (-1.453152027 + t * 1.061405429)))
    )
    tail = 0.5 * series * raised
    cdf = jnp.where(hidden < 0.0, tail, 1.0 - tail)
    return hidden * cdf, cdf + hidden * (raised * np.float32(1.0 / np.sqrt(2.0 * np.pi)))


def mlp(
    n2, cot, mid, fc1, conv, fc2, fc2b, fwd, inv, kh, kl, bh, bl, one,
    block_out, gn2_out, gfc1_out, gconv_out, gfc2_out, gb2_out,
    cot_pad, pad, hid, grad, out_acc, conv_low, ghid_low,
):
    step = pl.program_id(0)
    images = n2.shape[0]

    @pl.when(step == 0)
    def _():
        total = jnp.zeros((1, WIDTH), f32)
        for b in range(images):
            pad[SEQ - 5 :] = jnp.zeros((ROWS - SEQ + 5, WIDTH), f32)
            pad[:SEQ] = cot[b].astype(f32)
            values = pad[...]
            total = total + add_rows(values)
            cot_pad[b * ROWS : (b + 1) * ROWS] = values.astype(bf16)
        gb2_out[...] = total

    w1 = fc1[...]
    w2 = fc2[...]
    taps = conv[...]
    turned = dot(kh[...], taps) + dot(kl[...], taps) + one[...]
    kr, ki = turned[:HALF], turned[HALF:]
    rows_all = n2[...].reshape(images * ROWS, WIDTH)
    hid[...] = dot(rows_all, w1) + taps.astype(f32)[KS * KS : KS * KS + 1]
    grad[...] = dot_t(cot_pad[...], w2)
    cross_r = jnp.zeros((HALF, CHUNK), f32)
    cross_i = jnp.zeros((HALF, CHUNK), f32)
    bias_sum = jnp.zeros((1, CHUNK), f32)
    for b in range(images):
        span = slice(b * ROWS, (b + 1) * ROWS)
        act, slope = gelu_parts(hid[span, :])
        x = dot(fwd[...], act.astype(bf16))
        y = dot(fwd[...], grad[span, :].astype(bf16))
        xr, xi = x[:HALF], x[HALF:]
        yr, yi = y[:HALF], y[HALF:]
        made = jnp.concatenate([xr * kr - xi * ki, xr * ki + xi * kr], axis=0).astype(bf16)
        back = jnp.concatenate([yr * kr + yi * ki, yi * kr - yr * ki], axis=0).astype(bf16)
        cross_r = cross_r + (xr * yr + xi * yi)
        cross_i = cross_i + (xi * yr - xr * yi)
        conv_low[span, :] = dot(inv[...], made).astype(bf16)
        ghid = (dot(inv[...], back) * slope).astype(bf16)
        bias_sum = bias_sum + add_rows(ghid.astype(f32))
        ghid_low[span, :] = ghid
    cross = jnp.concatenate([cross_r, cross_i], axis=0)
    high = cross.astype(bf16)
    low = (cross - high.astype(f32)).astype(bf16)
    gconv_out[...] = dot(bh[...], high) + dot(bl[...], high) + dot(bh[...], low)
    gconv_out[KS * KS : KS * KS + 1] = bias_sum
    convolved = conv_low[...]
    ghid_all = ghid_low[...]
    part = dot(convolved, w2).reshape(images, ROWS, WIDTH)
    part_grad = dot_t(ghid_all, w1).reshape(images, ROWS, WIDTH)
    gfc2_out[...] = t_dot(convolved, cot_pad[...])
    gfc1_out[...] = t_dot(rows_all, ghid_all)

    @pl.when(step == 0)
    def _():
        out_acc[...] = part
        gn2_out[...] = part_grad

    @pl.when(step > 0)
    def _():
        out_acc[...] += part
        gn2_out[...] += part_grad

    @pl.when(step == pl.num_programs(0) - 1)
    def _():
        for b in range(images):
            result = mid[b] + (out_acc[b] + row(fc2b))
            block_out[b] = result[:SEQ].astype(bf16)


def attention_backward(
    pre, post, tok, cot, n1, packed, probs, attn, att, mid, gn2, wqkv, wproj, gain1, gain2, gb2,
    gtok_out, gqkv_out, gproj_out, small_out,
    pad, score, weight, low, mix, rows_out, square,
):
    step = pl.program_id(0)

    @pl.when(step == 0)
    def _():
        gqkv_out[...] = jnp.zeros_like(gqkv_out)
        gproj_out[...] = jnp.zeros_like(gproj_out)
        rows_out[...] = jnp.zeros_like(rows_out)
        mix[...] = jnp.zeros_like(mix)

    pad[SEQ - 5 :] = jnp.zeros((ROWS - SEQ + 5, WIDTH), f32)
    pad[:SEQ] = cot[0].astype(f32)
    centred, r = centre(mid[0])
    grad = gn2[0]
    back, gain_rows = norm_back(centred, r, row(gain2), grad)
    rows_out[3:4] += add_rows(gain_rows)
    rows_out[4:5] += add_rows(grad)
    gmid = pad[...] + back
    gmid_low = gmid.astype(bf16)
    rows_out[2:3] += add_rows(gmid_low.astype(f32))
    gproj_out[...] += t_dot(att[0], gmid_low)
    gatt = dot_t(gmid_low, wproj[...]).astype(bf16)
    low_half = lax.broadcasted_iota(jnp.int32, (ROWS, 128), 1) < HEAD_DIM
    key_half = lax.broadcasted_iota(jnp.int32, (KEYS, 128), 1) < HEAD_DIM
    zero = jnp.zeros((ROWS, 128), bf16)
    for p in range(HEADS // 2):
        query = packed[0, :ROWS, 128 * p : 128 * p + 128]
        key = packed[0, :, WIDTH + 128 * p : WIDTH + 128 * p + 128]
        value = packed[0, :, 2 * WIDTH + 128 * p : 2 * WIDTH + 128 * p + 128]
        ahead = gatt[:, 128 * p : 128 * p + 128]
        score[2 * p] = dot_t(jnp.where(low_half, query, zero), key)
        score[2 * p + 1] = dot_t(jnp.where(low_half, zero, query), key)
        weight[2 * p] = dot_t(jnp.where(low_half, ahead, zero), value)
        weight[2 * p + 1] = dot_t(jnp.where(low_half, zero, ahead), value)

    def fold(values):
        values = values[:, :128] + values[:, 128:]
        return values[:8] + values[8:]

    def rows_step(index, carry):
        rows = pl.ds(pl.multiple_of(index * 16, 16), 16)
        weights = [weight[g, rows, :] for g in range(HEADS)]
        mixed = []
        for h in range(HEADS):
            prob = probs[0, h, rows, :]
            ahead = weights[0] * post[0, h]
            for g in range(1, HEADS):
                ahead = ahead + weights[g] * post[g, h]
            for g in range(HEADS):
                mix[HEADS * HEADS + g * HEADS + h] += fold(weights[g] * prob)
            inner = jnp.sum(prob * ahead, axis=-1, keepdims=True)
            mixed.append(prob * (ahead - inner))
        for h in range(HEADS):
            scores = score[h, rows, :]
            total = mixed[0] * pre[0, h]
            for g in range(1, HEADS):
                total = total + mixed[g] * pre[g, h]
            low[h, rows, :] = total.astype(bf16)
            for g in range(HEADS):
                mix[g * HEADS + h] += fold(mixed[g] * scores)
        return carry

    lax.fori_loop(0, ROWS // 16, rows_step, 0)
    queries, keys, values = [], [], []
    for p in range(HEADS // 2):
        query = packed[0, :ROWS, 128 * p : 128 * p + 128]
        key = packed[0, :, WIDTH + 128 * p : WIDTH + 128 * p + 128]
        ahead = gatt[:, 128 * p : 128 * p + 128]
        even, odd = low[2 * p], low[2 * p + 1]
        queries.append(jnp.where(low_half, dot(even, key), dot(odd, key)) * 0.125)
        keys.append(jnp.where(key_half, t_dot(even, query), t_dot(odd, query))[:ROWS] * 0.125)
        values.append(
            jnp.where(key_half, t_dot(attn[0, 2 * p], ahead), t_dot(attn[0, 2 * p + 1], ahead))[
                :ROWS
            ]
        )
    gpacked = jnp.concatenate(queries + keys + values, axis=1).astype(bf16)
    gqkv_out[...] += t_dot(n1[0], gpacked)
    gnormed = dot_t(gpacked, wqkv[...])
    pad[:SEQ] = tok[0].astype(f32)
    centred, r = centre(pad[...])
    back, gain_rows = norm_back(centred, r, row(gain1), gnormed)
    rows_out[0:1] += add_rows(gain_rows)
    rows_out[1:2] += add_rows(gnormed)
    gtok_out[0] = (gmid + back)[:SEQ]

    @pl.when(step == pl.num_programs(0) - 1)
    def _():
        rows_out[5:6] = gb2[...]
        for t in range(WIDTH // 128):
            small_out[8 * t : 8 * t + 8] = rows_out[:, 128 * t : 128 * t + 128]
        square[...] = jnp.zeros_like(square)
        square[: 2 * HEADS * HEADS] = jnp.sum(mix[...], axis=1)
        sums = add_rows(square[...].T)
        small_out[24:] = jnp.concatenate([sums, jnp.zeros((SMALL - 25, 128), f32)], axis=0)


def whole(shape):
    return pl.BlockSpec(shape, lambda *_: (0,) * len(shape))


def image(shape):
    return pl.BlockSpec((1,) + shape, lambda i: (i,) + (0,) * len(shape))


def params():
    return pltpu.CompilerParams(vmem_limit_bytes=VMEM, dimension_semantics=("arbitrary",))


def call_forward(tokens, wqkv, wproj, pre, post, gain1, bias1, pbias, gain2, bias2):
    images = tokens.shape[0]
    smem = pl.BlockSpec(memory_space=pltpu.SMEM)
    vector = whole((WIDTH,))
    return pl.pallas_call(
        attention_forward,
        grid=(images,),
        in_specs=[
            smem, smem, image((SEQ, WIDTH)), whole((WIDTH, 3 * WIDTH)), whole((WIDTH, WIDTH)),
            vector, vector, vector, vector, vector,
        ],
        out_specs=[
            image((ROWS, WIDTH)), image((KEYS, 3 * WIDTH)), image((HEADS, ROWS, KEYS)),
            image((HEADS, ROWS, KEYS)), image((ROWS, WIDTH)), image((ROWS, WIDTH)),
            image((ROWS, WIDTH)),
        ],
        out_shape=[
            jax.ShapeDtypeStruct((images, ROWS, WIDTH), bf16),
            jax.ShapeDtypeStruct((images, KEYS, 3 * WIDTH), bf16),
            jax.ShapeDtypeStruct((images, HEADS, ROWS, KEYS), f32),
            jax.ShapeDtypeStruct((images, HEADS, ROWS, KEYS), bf16),
            jax.ShapeDtypeStruct((images, ROWS, WIDTH), bf16),
            jax.ShapeDtypeStruct((images, ROWS, WIDTH), f32),
            jax.ShapeDtypeStruct((images, ROWS, WIDTH), bf16),
        ],
        scratch_shapes=[
            pltpu.VMEM((ROWS, WIDTH), f32),
            pltpu.VMEM((HEADS, ROWS, KEYS), f32),
            pltpu.VMEM((8, 128), f32),
        ],
        compiler_params=params(),
        name="attention_forward",
    )(pre, post, tokens, wqkv, wproj, gain1, bias1, pbias, gain2, bias2)


def call_mlp(n2, cotangent, middle, fc1, conv, fc2, fc2_bias):
    images = n2.shape[0]
    units = fc1.shape[1]
    steps = units // CHUNK
    forward, inverse, kernel, back, one = fourier()
    kernel_high, kernel_low = split(kernel)
    back_high, back_low = split(back)
    consts = [
        jnp.asarray(forward.astype(np.float32).astype(bf16)),
        jnp.asarray(inverse.astype(np.float32).astype(bf16)),
        jnp.asarray(kernel_high), jnp.asarray(kernel_low),
        jnp.asarray(back_high), jnp.asarray(back_low),
        jnp.asarray(one.astype(np.float32)),
    ]
    columns = lambda rows: pl.BlockSpec((rows, CHUNK), lambda i: (0, i))
    total = images * ROWS
    return pl.pallas_call(
        mlp,
        grid=(steps,),
        in_specs=[
            whole((images, ROWS, WIDTH)), whole((images, SEQ, WIDTH)), whole((images, ROWS, WIDTH)),
            columns(WIDTH), columns(TAPS),
            pl.BlockSpec((CHUNK, WIDTH), lambda i: (i, 0)), whole((WIDTH,)),
        ]
        + [whole(c.shape) for c in consts],
        out_specs=[
            whole((images, SEQ, WIDTH)), whole((images, ROWS, WIDTH)),
            columns(WIDTH), columns(TAPS),
            pl.BlockSpec((CHUNK, WIDTH), lambda i: (i, 0)), whole((1, WIDTH)),
        ],
        out_shape=[
            jax.ShapeDtypeStruct((images, SEQ, WIDTH), bf16),
            jax.ShapeDtypeStruct((images, ROWS, WIDTH), f32),
            jax.ShapeDtypeStruct((WIDTH, units), f32),
            jax.ShapeDtypeStruct((TAPS, units), f32),
            jax.ShapeDtypeStruct((units, WIDTH), f32),
            jax.ShapeDtypeStruct((1, WIDTH), f32),
        ],
        scratch_shapes=[
            pltpu.VMEM((total, WIDTH), bf16),
            pltpu.VMEM((ROWS, WIDTH), f32),
            pltpu.VMEM((total, CHUNK), f32),
            pltpu.VMEM((total, CHUNK), f32),
            pltpu.VMEM((images, ROWS, WIDTH), f32),
            pltpu.VMEM((total, CHUNK), bf16),
            pltpu.VMEM((total, CHUNK), bf16),
        ],
        compiler_params=params(),
        name="mlp",
    )(n2, cotangent, middle, fc1, conv, fc2, fc2_bias, *consts)


def call_backward(
    tokens, cotangent, n1, packed, probs, attn, att, mid, gn2, wqkv, wproj, pre, post, gain1, gain2, gb2
):
    images = tokens.shape[0]
    smem = pl.BlockSpec(memory_space=pltpu.SMEM)
    vector = whole((WIDTH,))
    return pl.pallas_call(
        attention_backward,
        grid=(images,),
        in_specs=[
            smem, smem, image((SEQ, WIDTH)), image((SEQ, WIDTH)), image((ROWS, WIDTH)),
            image((KEYS, 3 * WIDTH)), image((HEADS, ROWS, KEYS)), image((HEADS, ROWS, KEYS)),
            image((ROWS, WIDTH)), image((ROWS, WIDTH)), image((ROWS, WIDTH)),
            whole((WIDTH, 3 * WIDTH)), whole((WIDTH, WIDTH)), vector, vector,
            whole((1, WIDTH)),
        ],
        out_specs=[
            image((SEQ, WIDTH)), whole((WIDTH, 3 * WIDTH)), whole((WIDTH, WIDTH)),
            whole((SMALL, 128)),
        ],
        out_shape=[
            jax.ShapeDtypeStruct((images, SEQ, WIDTH), f32),
            jax.ShapeDtypeStruct((WIDTH, 3 * WIDTH), f32),
            jax.ShapeDtypeStruct((WIDTH, WIDTH), f32),
            jax.ShapeDtypeStruct((SMALL, 128), f32),
        ],
        scratch_shapes=[
            pltpu.VMEM((ROWS, WIDTH), f32),
            pltpu.VMEM((HEADS, ROWS, KEYS), f32),
            pltpu.VMEM((HEADS, ROWS, KEYS), f32),
            pltpu.VMEM((HEADS, ROWS, KEYS), bf16),
            pltpu.VMEM((2 * HEADS * HEADS, 8, 128), f32),
            pltpu.VMEM((8, WIDTH), f32),
            pltpu.VMEM((128, 128), f32),
        ],
        compiler_params=params(),
        name="attention_backward",
    )(
        pre, post, tokens, cotangent, n1, packed, probs, attn, att, mid, gn2, wqkv, wproj,
        gain1, gain2, gb2,
    )


def local_block(
    tokens, norm1_gain, norm1_bias, wqkv, mix_pre, mix_post, wproj, proj_bias, norm2_gain,
    norm2_bias, fc1, taps, fc2, fc2_bias, cotangent,
):
    n1, packed, probs, attn, att, mid, n2 = call_forward(
        tokens, wqkv, wproj, mix_pre, mix_post, norm1_gain, norm1_bias, proj_bias, norm2_gain,
        norm2_bias,
    )
    block_out, gn2, gfc1, gconv, gfc2, gb2 = call_mlp(n2, cotangent, mid, fc1, taps, fc2, fc2_bias)
    gtok, gqkv, gproj, small = call_backward(
        tokens, cotangent, n1, packed, probs, attn, att, mid, gn2, wqkv, wproj, mix_pre, mix_post,
        norm1_gain, norm2_gain, gb2,
    )
    return block_out, gtok, gqkv, gproj, gfc1, gconv, gfc2, small


SIDES = (8, 4, 2, 1)
DEPTH, PLANE = (0, 1), (2, 3)
ROUNDS = ((PLANE, DEPTH), (DEPTH, PLANE))
FLIPS = ((0, 1), (1, 0), (1, 1))
MESH_IDS = pl.DeviceIdType.MESH
PIECE = 144
PIECE_PARTS = ((0, 96), (96, 48))
BLOCK = 112
BLOCK_PARTS = ((0, 80), (80, 32))
STREAMS = 3
MLP_PLAN = {(1, 4): ((0, -1),), (3, 4): ((1, -1), (0, 0)), (5, 4): ((2, -1), (0, 1), (1, 0))}
BACK_PLAN = {
    (0, 3): ((0, 2), (1, 1)), (1, 1): ((2, 0),), (1, 2): ((1, 2),), (1, 3): ((2, 1),),
}
TAIL_PLAN = ()


class Place:
    def __init__(self):
        self.dp, self.core = lax.axis_index("dp"), lax.axis_index("tensor")
        self.bits = tuple(lax.rem(self.dp // stride, 2) for stride in SIDES)
        self.pair = (self.dp, 1 - self.core)

    def peer(self, axes, flip):
        dp = self.dp
        for axis, turn in zip(axes, flip):
            if turn:
                dp = dp + (1 - 2 * self.bits[axis]) * SIDES[axis]
        return dp, self.core

    def mine(self, axes):
        return {axis: self.bits[axis] for axis in axes}

    def theirs(self, axes, flip):
        return {
            axis: 1 - self.bits[axis] if turn else self.bits[axis] for axis, turn in zip(axes, flip)
        }

    def everyone(self):
        peers = [self.peer(axes, flip) for axes in (PLANE, DEPTH) for flip in FLIPS]
        return peers + [self.pair]


def greet(partners):
    barrier = pltpu.get_barrier_semaphore()
    for partner in partners:
        pl.semaphore_signal(barrier, inc=1, device_id=partner, device_id_type=MESH_IDS)
    return lambda: pl.semaphore_wait(barrier, len(partners))


def remote(src, dst, sems, index, device):
    return pltpu.make_async_remote_copy(
        src_ref=src, dst_ref=dst, send_sem=sems.at[(0,) + index], recv_sem=sems.at[(1,) + index],
        device_id=device, device_id_type=MESH_IDS,
    )


def region(fixed, rows):
    return tuple(fixed.get(axis, slice(None)) for axis in range(4)) + (rows,)


def index_of(d):
    return tuple((d // stride) % 2 for stride in SIDES)


class Sum:
    def __init__(self, acc, landing, sems, parts, where):
        self.acc, self.landing, self.sems = acc, landing, sems
        self.parts, self.where = parts, where

    def copy(self, part, turn, peer):
        rows, axes, flip = pl.ds(*self.parts[part]), ROUNDS[part][turn], FLIPS[peer]
        fixed = self.where.theirs(axes, flip)
        if turn == 0:
            dst = self.landing[0].at[peer, :, :, rows]
        else:
            fixed.update(self.where.mine(ROUNDS[part][0]))
            dst = self.landing[1].at[peer, rows]
        return remote(
            self.acc.at[region(fixed, rows)], dst, self.sems, (part, turn, peer),
            self.where.peer(axes, flip),
        )

    def start(self):
        for part in range(2):
            for peer in range(3):
                self.copy(part, 0, peer).start()

    def act(self, turn):
        for part in range(2):
            rows = pl.ds(*self.parts[part])
            first, second = ROUNDS[part]
            for peer in range(3):
                self.copy(part, turn, peer).wait_recv()
            for near in (0, 1) if turn == 0 else (None,):
                for far in (0, 1) if turn == 0 else (None,):
                    fixed = self.where.mine(first)
                    if turn == 0:
                        fixed.update({second[0]: near, second[1]: far})
                        came = [self.landing[0][peer, near, far, rows] for peer in range(3)]
                    else:
                        fixed.update(self.where.mine(second))
                        came = [self.landing[1][peer, rows] for peer in range(3)]
                    spot = region(fixed, rows)
                    total = self.acc[spot].astype(f32)
                    for values in came:
                        total = total + values.astype(f32)
                    self.acc[spot] = total.astype(bf16)
            if turn == 0:
                for peer in range(3):
                    self.copy(part, 1, peer).start()

    def finish(self):
        for part in range(2):
            for turn in range(2):
                for peer in range(3):
                    self.copy(part, turn, peer).wait_send()


class Gather:
    def __init__(self, full, sems, parts, where):
        self.full, self.sems, self.parts, self.where = full, sems, parts, where

    def spot(self, part, turn, flip):
        first, second = ROUNDS[part][::-1]
        if turn == 0:
            fixed = {**self.where.mine(second), **self.where.theirs(first, flip)}
        else:
            fixed = self.where.theirs(second, flip)
        return region(fixed, pl.ds(*self.parts[part]))

    def copy(self, part, turn, peer):
        axes, held = ROUNDS[part][::-1][turn], self.spot(part, turn, (0, 0))
        return remote(
            self.full.at[held], self.full.at[held], self.sems, (part, turn, peer),
            self.where.peer(axes, FLIPS[peer]),
        )

    def start(self):
        for part in range(2):
            for peer in range(3):
                self.copy(part, 0, peer).start()

    def act(self, turn, then=None):
        for part in range(2):
            for peer in range(3):
                self.copy(part, turn, peer).wait_recv()
            if turn == 0:
                for peer in range(3):
                    self.copy(part, 1, peer).start()
            if then is not None:
                for peer in range(3):
                    then(part, turn, peer)

    def finish(self):
        for part in range(2):
            for turn in range(2):
                for peer in range(3):
                    self.copy(part, turn, peer).wait_send()


def tiles(values):
    return jnp.concatenate(
        [values[:, 128 * t : 128 * t + 128] for t in range(values.shape[1] // 128)], axis=0
    )


def weave(*lists):
    steps = [((k + 0.5) / len(one), step) for one in lists for k, step in enumerate(one)]
    for _, step in sorted(steps, key=lambda item: item[0]):
        step()


def untiles(values, count):
    rows = values.shape[0] // count
    return jnp.concatenate([values[t * rows : (t + 1) * rows] for t in range(count)], axis=1)


def block_kernel(
    pre, post, tok, cot, gain1, bias1, pbias, gain2, bias2, fc2b,
    qkv, proj, fc1, conv, bias, fc2, fwd_in, inv_in, kh_in, kl_in, bh_in, bl_in, one,
    block_out, gtok_out, fulls_out, piece_out, small_out, *rest,
):
    (
        tok_held, cot_held, out_held, gtok_held, out_wide, fwd, inv, kh, kl, bh, bl,
        piece_full, piece_other, taps_pad, wqkv, wproj, fc1_blocks, fc2_full, conv_full,
        cot_pad, n1, packed, score, weight, probs, attn, att, mid, n2,
        turned, ghat, hid, hidden, slope, acted, weights, conv_low, ghid_low, gmid, gmid_low, gatt, low, gpacked, mix,
        rows_out, square, gqkv, gproj, small_sums, small_landed,
        streams_out, streams_came, streams_acc, streams_landing, gconv, made, ahead, behind, cross, att_bufs,
        local_sems, leave_sems, gather_sems, gather_pair_sems, stream_pair_sems, stream_sems, att_sems, att_pair_sems,
    ) = rest
    images = tok.shape[1]
    total = images * ROWS
    half = fc1.shape[1]
    where = Place()
    pair, core, mine = where.pair, where.core, where.bits
    met = greet(where.everyone())
    mine_start = pl.multiple_of(core * half, 128)
    cols, rows_of = pl.ds(mine_start, half), pl.ds(mine_start, half)
    span = lambda b: slice(b * ROWS, (b + 1) * ROWS)
    spans = [span(b) for b in range(images)]
    inside = row_mask((ROWS, WIDTH))
    fulls = [streams_came.at[s] for s in range(STREAMS)]
    sides = [(s, pl.ds(s * STREAM, STREAM)) for s in range(STREAMS)]
    local = [
        pltpu.make_async_copy(src, dst, local_sems.at[index])
        for index, (src, dst) in enumerate(
            (
                (tok, tok_held), (cot, cot_held), (fc2, fc2_full.at[rows_of]),
                (fwd_in, fwd), (kh_in, kh), (kl_in, kl),
                *((fc1.at[:, side], fc1_blocks.at[core * STREAMS + s]) for s, side in sides),
                (inv_in, inv), (bh_in, bh), (bl_in, bl),
            )
        )
    ]
    for copy in local:
        copy.start()

    both = jnp.concatenate([qkv[...].astype(f32), proj[...].astype(f32)], axis=1)
    piece_full[mine] = tiles(both).astype(bf16)
    taps_pad[...] = jnp.zeros(taps_pad.shape, f32)
    taps_pad[: KS * KS] = conv[...].astype(f32)
    taps_pad[KS * KS : KS * KS + 1] = bias[...].astype(f32).reshape(1, half)
    conv_full[:, cols] = taps_pad[...].astype(bf16)
    met()
    gather = Gather(piece_full, gather_sems, PIECE_PARTS, where)
    gather.start()
    weights_come = [
        remote(conv_full.at[:, cols], conv_full.at[:, cols], gather_pair_sems, (0,), pair),
        remote(fc2, fc2_full.at[rows_of], gather_pair_sems, (1,), pair),
        *(
            remote(
                fc1.at[:, side], fc1_blocks.at[core * STREAMS + s], gather_pair_sems, (2 + s,), pair
            )
            for s, side in sides
        ),
    ]
    forwards = [
        remote(
            piece_full.at[mine], piece_other.at[mine], gather_pair_sems, (2 + STREAMS,), pair
        )
    ]
    for copy in weights_come + forwards:
        copy.start()

    def forward(part, turn, peer):
        spot = gather.spot(part, turn, FLIPS[peer])
        copy = remote(
            piece_full.at[spot], piece_other.at[spot], gather_pair_sems,
            (3 + STREAMS + 6 * part + 3 * turn + peer,), pair,
        )
        copy.start()
        forwards.append(copy)

    cot_sum = jnp.zeros((1, WIDTH), f32)
    local[0].wait()
    local[1].wait()
    for source, ref in ((tok_held, mid), (cot_held, gmid)):
        flat = source[...].reshape(SEQ, images * WIDTH)
        for b in range(images):
            ref[b * ROWS + SEQ - 5 : (b + 1) * ROWS] = jnp.zeros((ROWS - SEQ + 5, WIDTH), f32)
            ref[b * ROWS : b * ROWS + SEQ] = flat[:, b * WIDTH : (b + 1) * WIDTH].astype(f32)
    for b in range(images):
        grads = gmid[spans[b], :]
        cot_sum = cot_sum + add_rows(grads)
        cot_pad[spans[b], :] = grads.astype(bf16)
    for b in range(images):
        centred, r = centre(mid[spans[b], :])
        n1[spans[b], :] = jnp.where(inside, centred * r * row(gain1) + row(bias1), 0.0).astype(bf16)

    def prepare(side):
        def prepare_unit(s, carry):
            block = side * STREAMS + s
            units = pl.ds(pl.multiple_of(block * STREAM, STREAM), STREAM)
            taps = conv_full[:, units]
            turned[block] = dot(kh[...], taps) + dot(kl[...], taps) + one[...]
            grads = dot_t(cot_pad[...], fc2_full[units, :]).astype(bf16)
            for b in range(images):
                ghat[block, b] = dot(fwd[...], grads[spans[b]]).astype(bf16)
            return carry

        lax.fori_loop(0, STREAMS, prepare_unit, 0)

    gather.act(0, forward)
    for copy in local[2:]:
        copy.wait()
    prepare(core)
    for copy in weights_come:
        copy.wait_recv()
    prepare(1 - core)
    gather.act(1, forward)
    for copy in forwards:
        copy.wait_recv()
    width = qkv.shape[1]
    flip = core == 1
    for d in range(0, 16, 2):
        blocks = [
            jnp.concatenate([untiles(ref[index_of(e)].astype(f32), 6) for e in (d, d + 1)], axis=0)
            for ref in (piece_full, piece_other)
        ]
        first = jnp.where(flip, blocks[1], blocks[0])
        second = jnp.where(flip, blocks[0], blocks[1])
        rows = slice(24 * d, 24 * d + 48)
        wqkv[rows, :] = jnp.concatenate([first[:, :width], second[:, :width]], axis=1).astype(bf16)
        wproj[rows, :] = jnp.concatenate([first[:, width:], second[:, width:]], axis=1).astype(bf16)

    for n in range(0, 3 * WIDTH, WIDTH):
        gpacked[:, n : n + WIDTH] = dot(n1[...], wqkv[:, n : n + WIDTH]).astype(bf16)
    for b in range(images):
        packed[b % 2][b // 2, :ROWS] = gpacked[spans[b], :]
        packed[b % 2][b // 2, ROWS:] = jnp.zeros((KEYS - ROWS, 3 * WIDTH), bf16)
    low_half = lax.broadcasted_iota(jnp.int32, (ROWS, 128), 1) < HEAD_DIM
    key_half = lax.broadcasted_iota(jnp.int32, (KEYS, 128), 1) < HEAD_DIM
    zero = jnp.zeros((ROWS, 128), bf16)
    valid = lax.broadcasted_iota(jnp.int32, (16, KEYS), 1) < SEQ

    def section(q, side, which, pair_of_heads, count=KEYS):
        start = which * WIDTH + 128 * pair_of_heads
        return packed[side][q, :count, start : start + 128]

    def rows_at(q, side):
        return pl.ds(pl.multiple_of((2 * q + side) * ROWS, 16), ROWS)

    def skewed(q, stages, after=None):
        for beat in range(2 + max(depth for depth, _ in stages)):
            weave(
                *[
                    [functools.partial(step, q, beat - depth) for step in steps]
                    for depth, steps in stages
                    if 0 <= beat - depth < 2
                ]
            )
            if after is not None:
                after(beat)

    pairs = range(HEADS // 2)
    row_blocks = [slice(r, r + 16) for r in range(0, ROWS, 16)]

    def products(left, right, target, p):
        target[2 * p] = dot_t(jnp.where(low_half, left, zero), right)
        target[2 * p + 1] = dot_t(jnp.where(low_half, zero, left), right)

    def score_step(p, q, side):
        products(section(q, side, 0, p, ROWS), section(q, side, 1, p), score[side], p)

    def softmax_rows(rows, q, side):
        scores = [score[side][h, rows, :] for h in range(HEADS)]
        found = []
        for g in range(HEADS):
            mixed = scores[0] * (pre[g, 0] * 0.125)
            for h in range(1, HEADS):
                mixed = mixed + scores[h] * (pre[g, h] * 0.125)
            mixed = jnp.where(valid, mixed, -1e30)
            top = jnp.max(mixed, axis=-1, keepdims=True)
            raised = jnp.exp(mixed - top)
            prob = raised * (1.0 / jnp.sum(raised, axis=-1, keepdims=True))
            probs[side][q, g, rows, :] = prob
            found.append(prob)
        for g in range(HEADS):
            mixed = found[0] * post[g, 0]
            for h in range(1, HEADS):
                mixed = mixed + found[h] * post[g, h]
            attn[side][q, g, rows, :] = mixed.astype(bf16)

    def out_step(p, q, side):
        value = section(q, side, 2, p)
        even, odd = dot(attn[side][q, 2 * p], value), dot(attn[side][q, 2 * p + 1], value)
        att[rows_at(q, side), 128 * p : 128 * p + 128] = jnp.where(low_half, even, odd).astype(
            bf16
        )

    def each(function, items):
        return [functools.partial(function, item) for item in items]

    def attend(q, carry):
        skewed(
            q,
            (
                (0, each(score_step, pairs)), (1, each(softmax_rows, row_blocks)),
                (2, each(out_step, pairs)),
            ),
        )
        return carry

    lax.fori_loop(0, images // 2, attend, 0)
    hid[...] = dot(att[...], wproj[...])
    for b in range(images):
        middle = mid[spans[b], :] + (hid[spans[b], :] + row(pbias))
        mid[spans[b], :] = middle
        centred, r = centre(middle)
        n2[spans[b], :] = jnp.where(inside, centred * r * row(gain2) + row(bias2), 0.0).astype(bf16)

    def exchange_copy(s):
        return remote(streams_out.at[s], streams_came.at[s], stream_pair_sems, (s,), pair)

    sums = [
        Sum(
            streams_acc.at[s], [ref.at[s] for ref in streams_landing], stream_sems.at[s, 0],
            BLOCK_PARTS, where,
        )
        for s in range(STREAMS)
    ]
    gathers = [Gather(fulls[s], stream_sems.at[s, 1], BLOCK_PARTS, where) for s in range(STREAMS)]

    def act(s, step):
        if step < 0:
            sums[s].start()
        elif step < 2:
            sums[s].act(step)
            if step == 1:
                fulls[s][mine] = streams_acc[(s,) + mine]
                gathers[s].start()
        else:
            gathers[s].act(step - 2)

    def poll(plan, index, spot):
        for (turn, at), items in plan.items():
            if at == spot:

                @pl.when(index == turn)
                def _():
                    for item in items:
                        act(*item)

    def blocks():
        filters = tiles(gconv[...])
        empty = jnp.zeros((BLOCK - 104, 128), f32)
        for d in range(16):
            yield index_of(d), jnp.concatenate(
                [
                    tiles(gqkv[24 * d : 24 * d + 24, :STREAM]),
                    tiles(hid[16 * d : 16 * d + 16]),
                    filters[8 * d : 8 * d + 8],
                    empty,
                ],
                axis=0,
            )

    def mlp(i, carry):
        s, own = i // 2, lax.rem(i, 2)
        owner = (1 - core) * (1 - own) + core * own
        unit = owner * STREAMS + s
        units = pl.ds(pl.multiple_of(unit * STREAM, STREAM), STREAM)
        bias_row = conv_full[:, units].astype(f32)[KS * KS : KS * KS + 1]
        weights[...] = fc1_blocks[unit]
        sums_of = {"bias": jnp.zeros((8, STREAM), f32)}

        def first(b, start, count):
            rows = slice(b * ROWS + start, b * ROWS + start + count)
            hidden[b % 2][start : start + count] = dot(n2[rows, :], weights[...]) + bias_row

        def activate(b, start):
            rows = slice(start, start + 16)
            activated, slopes = gelu_parts(hidden[b % 2][rows])
            slope[b][rows] = slopes
            acted[b % 2][rows] = activated.astype(bf16)

        def transform(b, start, count):
            made[b % 2][start : start + count] = dot(
                fwd[start : start + count], acted[b % 2][...]
            )

        def multiply(b, start):
            real, imag = slice(start, start + 16), slice(HALF + start, HALF + start + 16)
            xr, xi = made[b % 2][real], made[b % 2][imag]
            yr, yi = ghat[unit, b, real].astype(f32), ghat[unit, b, imag].astype(f32)
            kr, ki = turned[unit, real], turned[unit, imag]
            ahead[b % 2][real] = (xr * kr - xi * ki).astype(bf16)
            ahead[b % 2][imag] = (xr * ki + xi * kr).astype(bf16)
            behind[b % 2][real] = (yr * kr + yi * ki).astype(bf16)
            behind[b % 2][imag] = (yi * kr - yr * ki).astype(bf16)
            cross_r, cross_i = xr * yr + xi * yi, xi * yr - xr * yi
            if b > 0:
                cross_r, cross_i = cross[real] + cross_r, cross[imag] + cross_i
            cross[real], cross[imag] = cross_r, cross_i

        def invert(b, start, count):
            near = slice(start, start + count)
            rows = slice(b * ROWS + start, b * ROWS + start + count)
            part = inv[near]
            conv_low[unit, rows] = dot(part, ahead[b % 2][...]).astype(bf16)
            ghid = (dot(part, behind[b % 2][...]) * slope[b][near]).astype(bf16)
            ghid_low[unit, rows] = ghid
            rounded = ghid.astype(f32)
            total = sums_of["bias"]
            for r in range(0, count, 8):
                total = total + rounded[r : r + 8]
            sums_of["bias"] = total

        stages = (
            lambda b: [functools.partial(first, b, 0, ROWS)],
            lambda b: [functools.partial(activate, b, start) for start in range(0, ROWS, 16)],
            lambda b: [
                functools.partial(transform, b, start, HALF) for start in (0, HALF)
            ],
            lambda b: [functools.partial(multiply, b, start) for start in range(0, HALF, 16)],
            lambda b: [functools.partial(invert, b, *block) for block in ((0, 112), (112, 96))],
        )
        for beat in range(images + len(stages) - 1):
            weave(
                *[
                    stage(beat - depth)
                    for depth, stage in enumerate(stages)
                    if 0 <= beat - depth < images
                ]
            )
        bias_sum = add_rows(sums_of["bias"])
        high = cross[...].astype(bf16)
        low_part = (cross[...] - high.astype(f32)).astype(bf16)
        last = lax.broadcasted_iota(jnp.int32, (TAPS, STREAM), 0) == KS * KS
        gconv[...] = jnp.where(
            last, bias_sum, dot(bh[...], high) + dot(bl[...], high) + dot(bh[...], low_part)
        )
        hid[:STREAM] = t_dot(conv_low[unit], cot_pad[...])
        gqkv[:, :STREAM] = t_dot(n2[...], ghid_low[unit])

        @pl.when(own == 0)
        def _():
            for index, values in blocks():
                streams_out[(s,) + index] = values.astype(bf16)
            exchange_copy(s).start()

        @pl.when(own == 1)
        def _():
            exchange_copy(s).wait_recv()
            for index, values in blocks():
                came = streams_came[(s,) + index].astype(f32)
                streams_acc[(s,) + index] = (values + came).astype(bf16)

        poll(MLP_PLAN, i, images)
        return carry

    lax.fori_loop(0, 2 * STREAMS, mlp, 0)

    every = range(2 * STREAMS)
    joined = lambda ref, *rows: jnp.concatenate([ref[(u,) + rows] for u in every], axis=1)
    for b in range(images):
        hid[spans[b], :] = dot_t(joined(ghid_low, spans[b]), joined(fc1_blocks))
    gain_sum = jnp.zeros((1, WIDTH), f32)
    bias_sum = jnp.zeros((1, WIDTH), f32)
    proj_sum = jnp.zeros((1, WIDTH), f32)
    for b in range(images):
        middle = mid[spans[b], :]
        centred, r = centre(middle)
        grad = hid[spans[b], :]
        back, gain_rows = norm_back(centred, r, row(gain2), grad)
        gain_sum = gain_sum + add_rows(gain_rows)
        bias_sum = bias_sum + add_rows(grad)
        whole_grad = gmid[spans[b], :] + back
        gmid[spans[b], :] = whole_grad
        rounded = whole_grad.astype(bf16)
        proj_sum = proj_sum + add_rows(rounded.astype(f32))
        gmid_low[spans[b], :] = rounded
    gatt[...] = dot_t(gmid_low[...], wproj[...]).astype(bf16)
    gproj[...] = t_dot(att[...], gmid_low[...])
    mix[...] = jnp.zeros_like(mix)

    def fold(values):
        values = values[:, :128] + values[:, 128:]
        return values[:8] + values[8:]

    def weight_step(p, q, side):
        ahead_p = gatt[rows_at(q, side), 128 * p : 128 * p + 128]
        products(ahead_p, section(q, side, 2, p), weight[side], p)

    def back_rows(rows, q, side):
        given = [weight[side][g, rows, :] for g in range(HEADS)]
        mixed = []
        for h in range(HEADS):
            prob = probs[side][q, h, rows, :]
            ahead_h = given[0] * post[0, h]
            for g in range(1, HEADS):
                ahead_h = ahead_h + given[g] * post[g, h]
            for g in range(HEADS):
                mix[HEADS * HEADS + g * HEADS + h] += fold(given[g] * prob)
            inner = jnp.sum(prob * ahead_h, axis=-1, keepdims=True)
            mixed.append(prob * (ahead_h - inner))
        for h in range(HEADS):
            scores = score[side][h, rows, :]
            total = mixed[0] * pre[0, h]
            for g in range(1, HEADS):
                total = total + mixed[g] * pre[g, h]
            low[side][h, rows, :] = total.astype(bf16)
            for g in range(HEADS):
                mix[g * HEADS + h] += fold(mixed[g] * scores)

    def value_step(p, q, side):
        rows, lanes = rows_at(q, side), 2 * WIDTH + 128 * p
        ahead_p = gatt[rows, 128 * p : 128 * p + 128]
        even, odd = t_dot(attn[side][q, 2 * p], ahead_p), t_dot(attn[side][q, 2 * p + 1], ahead_p)
        gpacked[rows, lanes : lanes + 128] = jnp.where(key_half, even, odd)[:ROWS].astype(bf16)

    def query_step(p, q, side):
        key = section(q, side, 1, p)
        even, odd = dot(low[side][2 * p], key), dot(low[side][2 * p + 1], key)
        gpacked[rows_at(q, side), 128 * p : 128 * p + 128] = (
            jnp.where(low_half, even, odd) * 0.125
        ).astype(bf16)

    def key_step(p, q, side):
        query, lanes = section(q, side, 0, p, ROWS), WIDTH + 128 * p
        even, odd = t_dot(low[side][2 * p], query), t_dot(low[side][2 * p + 1], query)
        gpacked[rows_at(q, side), lanes : lanes + 128] = (
            jnp.where(key_half, even, odd)[:ROWS] * 0.125
        ).astype(bf16)

    def back_couple(q, carry):
        skewed(
            q,
            (
                (0, each(score_step, pairs) + each(weight_step, pairs)),
                (1, each(back_rows, row_blocks)), (1, each(value_step, pairs)),
                (2, each(query_step, pairs) + each(key_step, pairs)),
            ),
            lambda beat: poll(BACK_PLAN, q, beat),
        )
        return carry

    lax.fori_loop(0, images // 2, back_couple, 0)
    for n in range(0, 3 * WIDTH, WIDTH):
        gqkv[:, n : n + WIDTH] = t_dot(n1[...], gpacked[:, n : n + WIDTH])

    width, proj_width = gqkv.shape[1] // 2, gproj.shape[1] // 2

    def pieces(side):
        for d in range(16):
            rows = slice(24 * d, 24 * d + 24)
            both = jnp.concatenate(
                [
                    gqkv[rows, side * width : (side + 1) * width],
                    gproj[rows, side * proj_width : (side + 1) * proj_width],
                ],
                axis=1,
            )
            yield index_of(d), tiles(both)

    gather.finish()
    for copy in forwards:
        copy.wait_send()
    for side in range(2):

        @pl.when(core == side)
        def _():
            for index, values in pieces(1 - side):
                piece_full[index] = values.astype(bf16)

    exchange = remote(piece_full, piece_other, att_pair_sems, (0,), pair)
    exchange.start()
    for b in range(images):
        hid[spans[b], :] = dot_t(gpacked[spans[b], :], wqkv[...])
    attention = Sum(att_bufs["acc"], att_bufs["landing"], att_sems, PIECE_PARTS, where)
    exchange.wait_recv()
    for side in range(2):

        @pl.when(core == side)
        def _():
            for index, values in pieces(side):
                came = piece_other[index].astype(f32)
                att_bufs["acc"][index] = (values + came).astype(bf16)

    attention.start()

    for item in TAIL_PLAN:
        act(*item)
    norm_gain = jnp.zeros((1, WIDTH), f32)
    norm_bias = jnp.zeros((1, WIDTH), f32)
    flat = tok_held[...].reshape(SEQ, images * WIDTH)
    for b in range(images):
        rows = slice(b * ROWS, b * ROWS + SEQ)
        centred, r = centre(flat[:, b * WIDTH : (b + 1) * WIDTH].astype(f32))
        grad = hid[rows, :]
        back, gain_rows = norm_back(centred, r, row(gain1), grad)
        norm_gain = norm_gain + add_rows(gain_rows)
        norm_bias = norm_bias + add_rows(grad)
        gtok_held[:, b, :] = gmid[rows, :] + back
    leaving = [pltpu.make_async_copy(gtok_held, gtok_out, leave_sems.at[1])]
    leaving[0].start()
    rows_out[...] = jnp.concatenate(
        [norm_gain, norm_bias, proj_sum, gain_sum, bias_sum, cot_sum, jnp.zeros((2, WIDTH), f32)],
        axis=0,
    )
    for t in range(WIDTH // 128):
        small_sums[0, 8 * t : 8 * t + 8] = rows_out[:, 128 * t : 128 * t + 128]
    square[...] = jnp.zeros_like(square)
    square[: 2 * HEADS * HEADS] = jnp.sum(mix[...], axis=1)
    line = add_rows(square[...].T)
    small_sums[0, 24:] = jnp.concatenate([line, jnp.zeros((SMALL - 25, 128), f32)], axis=0)

    def small_copy(turn, peer):
        if turn == 0:
            device = pair
        else:
            device = where.peer((PLANE, DEPTH)[turn - 1], FLIPS[peer])
        index = 0 if turn == 0 else 3 * turn - 2 + peer
        return remote(
            small_sums.at[turn], small_landed.at[index], att_pair_sems, (1 + index,), device
        )

    small_counts = (1, 3, 3)

    def small_start(turn):
        for peer in range(small_counts[turn]):
            small_copy(turn, peer).start()

    def small_take(turn):
        total = small_sums[turn]
        for peer in range(small_counts[turn]):
            small_copy(turn, peer).wait_recv()
            total = total + small_landed[0 if turn == 0 else 3 * turn - 2 + peer]
        return total

    def second_projection(b):
        second = dot(joined(conv_low, spans[b]), fc2_full[...])
        result = mid[spans[b], :] + (second + row(fc2b))
        out_wide[:, b, :] = result[:SEQ]

    small_start(0)
    for b in range(images // 2):
        second_projection(b)
    small_sums[1] = small_take(0)
    small_start(1)
    act(2, 2)
    attention.act(0)
    for b in range(images // 2, images):
        second_projection(b)
    out_held[...] = out_wide[...].astype(bf16)
    leaving.append(pltpu.make_async_copy(out_held, block_out, leave_sems.at[0]))
    leaving[1].start()
    small_sums[2] = small_take(1)
    small_start(2)
    for s in range(STREAMS):
        act(s, 3)
    leaving.append(pltpu.make_async_copy(streams_came, fulls_out, leave_sems.at[2]))
    leaving[2].start()
    small_out[...] = small_take(2)
    attention.act(1)
    piece_out[...] = att_bufs["acc"][mine]
    for copy in leaving:
        copy.wait()
    for copy in weights_come + [exchange]:
        copy.wait_send()
    for turn in range(3):
        for peer in range(small_counts[turn]):
            small_copy(turn, peer).wait_send()
    for s in range(STREAMS):
        exchange_copy(s).wait_send()
    attention.finish()
    for s in range(STREAMS):
        sums[s].finish()
        gathers[s].finish()


def call_block(
    pre, post, tok, cot, gain1, bias1, pbias, gain2, bias2, fc2b, qkv, proj, fc1, conv, bias, fc2
):
    images, half = tok.shape[1], fc1.shape[1]
    units, total = 2 * half, images * ROWS
    forward, inverse, kernel, back, one = fourier()
    kernel_high, kernel_low = split(kernel)
    back_high, back_low = split(back)
    consts = [
        jnp.asarray(forward.astype(np.float32).astype(bf16)),
        jnp.asarray(inverse.astype(np.float32).astype(bf16)),
        jnp.asarray(kernel_high), jnp.asarray(kernel_low),
        jnp.asarray(back_high), jnp.asarray(back_low),
        jnp.asarray(one.astype(np.float32)),
    ]
    vmem = pl.BlockSpec(memory_space=pltpu.VMEM)
    smem = pl.BlockSpec(memory_space=pltpu.SMEM)
    hbm = pl.BlockSpec(memory_space=pl.ANY)

    def bufs(rows):
        buffer = lambda free: pltpu.VMEM((2,) * free + (rows, 128), bf16)
        return {
            "acc": buffer(4),
            "landing": [
                pltpu.VMEM((3, 2, 2, rows, 128), bf16), pltpu.VMEM((3, rows, 128), bf16),
            ],
        }

    stacked = lambda free: pltpu.VMEM((STREAMS,) + (2,) * free + (BLOCK, 128), bf16)
    tall = lambda width, dtype: pltpu.VMEM((total, width), dtype)
    two = lambda shape, dtype, count=2: [pltpu.VMEM(shape, dtype) for _ in range(count)]
    scratch = dict(
        tok_held=pltpu.VMEM(tok.shape, bf16),
        cot_held=pltpu.VMEM(tok.shape, bf16),
        out_held=pltpu.VMEM(tok.shape, bf16),
        gtok_held=pltpu.VMEM(tok.shape, f32),
        out_wide=pltpu.VMEM(tok.shape, f32),
        **{
            name: pltpu.VMEM(value.shape, bf16)
            for name, value in zip(("fwd", "inv", "kh", "kl", "bh", "bl"), consts)
        },
        piece_full=pltpu.VMEM((2, 2, 2, 2, PIECE, 128), bf16),
        piece_other=pltpu.VMEM((2, 2, 2, 2, PIECE, 128), bf16),
        taps_pad=pltpu.VMEM((TAPS, half), f32),
        wqkv=pltpu.VMEM((WIDTH, 3 * WIDTH), bf16),
        wproj=pltpu.VMEM((WIDTH, WIDTH), bf16),
        fc1_blocks=pltpu.VMEM((2 * STREAMS, WIDTH, STREAM), bf16),
        fc2_full=pltpu.VMEM((units, WIDTH), bf16),
        conv_full=pltpu.VMEM((TAPS, units), bf16),
        cot_pad=tall(WIDTH, bf16),
        n1=tall(WIDTH, bf16),
        packed=two((images // 2, KEYS, 3 * WIDTH), bf16),
        score=two((HEADS, ROWS, KEYS), f32),
        weight=two((HEADS, ROWS, KEYS), f32),
        probs=two((images // 2, HEADS, ROWS, KEYS), f32),
        attn=two((images // 2, HEADS, ROWS, KEYS), bf16),
        att=tall(WIDTH, bf16),
        mid=tall(WIDTH, f32),
        n2=tall(WIDTH, bf16),
        turned=pltpu.VMEM((2 * STREAMS, COEFS, STREAM), f32),
        ghat=pltpu.VMEM((2 * STREAMS, images, COEFS, STREAM), bf16),
        hid=tall(WIDTH, f32),
        hidden=two((ROWS, STREAM), f32),
        slope=two((ROWS, STREAM), f32, images),
        acted=two((ROWS, STREAM), bf16),
        weights=pltpu.VMEM((WIDTH, STREAM), bf16),
        conv_low=pltpu.VMEM((2 * STREAMS, total, STREAM), bf16),
        ghid_low=pltpu.VMEM((2 * STREAMS, total, STREAM), bf16),
        gmid=tall(WIDTH, f32),
        gmid_low=tall(WIDTH, bf16),
        gatt=tall(WIDTH, bf16),
        low=two((HEADS, ROWS, KEYS), bf16),
        gpacked=tall(3 * WIDTH, bf16),
        mix=pltpu.VMEM((2 * HEADS * HEADS, 8, 128), f32),
        rows_out=pltpu.VMEM((8, WIDTH), f32),
        square=pltpu.VMEM((128, 128), f32),
        gqkv=pltpu.VMEM((WIDTH, 3 * WIDTH), f32),
        gproj=pltpu.VMEM((WIDTH, WIDTH), f32),
        small_sums=pltpu.VMEM((3, SMALL, 128), f32),
        small_landed=pltpu.VMEM((7, SMALL, 128), f32),
        streams_out=stacked(4),
        streams_came=stacked(4),
        streams_acc=stacked(4),
        streams_landing=[
            pltpu.VMEM((STREAMS, 3, 2, 2, BLOCK, 128), bf16),
            pltpu.VMEM((STREAMS, 3, BLOCK, 128), bf16),
        ],
        gconv=pltpu.VMEM((TAPS, STREAM), f32),
        made=two((COEFS, STREAM), f32),
        ahead=two((COEFS, STREAM), bf16),
        behind=two((COEFS, STREAM), bf16),
        cross=pltpu.VMEM((COEFS, STREAM), f32),
        att_bufs=bufs(PIECE),
        local_sems=pltpu.SemaphoreType.DMA((9 + STREAMS,)),
        leave_sems=pltpu.SemaphoreType.DMA((3,)),
        gather_sems=pltpu.SemaphoreType.DMA((2, 2, 2, 3)),
        gather_pair_sems=pltpu.SemaphoreType.DMA((2, 15 + STREAMS)),
        stream_pair_sems=pltpu.SemaphoreType.DMA((2, STREAMS)),
        stream_sems=pltpu.SemaphoreType.DMA((STREAMS, 2, 2, 2, 2, 3)),
        att_sems=pltpu.SemaphoreType.DMA((2, 2, 2, 3)),
        att_pair_sems=pltpu.SemaphoreType.DMA((2, 8)),
    )
    return pl.pallas_call(
        block_kernel,
        in_specs=[smem] * 2 + [hbm] * 2 + [vmem] * 8 + [hbm] + [vmem] * 2 + [hbm] * 7 + [vmem],
        out_specs=[hbm] * 3 + [vmem] * 2,
        out_shape=[
            jax.ShapeDtypeStruct(tok.shape, bf16),
            jax.ShapeDtypeStruct(tok.shape, f32),
        ]
        + [
            jax.ShapeDtypeStruct((STREAMS, 2, 2, 2, 2, BLOCK, 128), bf16),
            jax.ShapeDtypeStruct((PIECE, 128), bf16),
            jax.ShapeDtypeStruct((SMALL, 128), f32),
        ],
        scratch_shapes=list(scratch.values()),
        compiler_params=pltpu.CompilerParams(
            vmem_limit_bytes=VMEM, collective_id=0, has_side_effects=True
        ),
        name="block",
    )(
        pre, post, tok, cot, gain1, bias1, pbias, gain2, bias2, fc2b, qkv, proj, fc1, conv, bias,
        fc2, *consts,
    )


def finish_kernel(totals_in, piece, small, out_in, gtok_in, *rest):
    outs, rest = rest[:16], rest[16:]
    held, (totals, out_held, gtok_held, taps, mixes, sems) = rest[:14], rest[14:]
    gfc1, gb1, gconv, gfc2, gqkv, gproj, g1, b1, pb, g2, b2, fb, pre, post = held
    coming = [
        pltpu.make_async_copy(totals_in.at[s], totals.at[s], sems.at[s]) for s in range(STREAMS)
    ]
    coming += [
        pltpu.make_async_copy(gtok_in, gtok_held, sems.at[STREAMS]),
        pltpu.make_async_copy(out_in, out_held, sems.at[STREAMS + 1]),
    ]
    for copy in coming:
        copy.start()
    leaving = []

    def leave(src, dst):
        copy = pltpu.make_async_copy(src, dst, sems.at[STREAMS + 2 + len(leaving)])
        copy.start()
        leaving.append(copy)

    both = untiles(piece[...].astype(f32), 6)
    width = gqkv.shape[1]
    gqkv[...] = both[:, :width]
    gproj[...] = both[:, width:]
    rows = untiles(small[:24], 3)
    for index, ref in enumerate((g1, b1, pb, g2, b2, fb)):
        ref[...] = rows[index].reshape(ref.shape)
    line = small[24:25]
    for index, ref in enumerate((pre, post)):
        for g in range(HEADS):
            start = HEADS * HEADS * index + HEADS * g
            mixes[index, g : g + 1, :HEADS] = line[:, start : start + HEADS]
    pre[...] = mixes[0, :HEADS, :HEADS] * 0.125
    post[...] = mixes[1, :HEADS, :HEADS]
    for index in range(4, 14):
        leave(held[index], outs[index])
    for s in range(STREAMS):
        side = slice(s * STREAM, (s + 1) * STREAM)
        coming[s].wait()
        for d in range(16):
            block = totals[(s,) + index_of(d)].astype(f32)
            gfc1[24 * d : 24 * d + 24, side] = untiles(block[:48], 2)
            gfc2[s * STREAM + 16 * d : s * STREAM + 16 * d + 16, :] = untiles(block[48:96], 3)
            taps[8 * d : 8 * d + 8, :] = block[96:104]
        leave(gfc2.at[side], outs[3].at[side])
        leave(gfc1.at[:, side], outs[0].at[:, side])
        filters = untiles(taps[...], 2)
        gconv[:, side] = filters[: KS * KS]
        gb1[side] = filters[KS * KS]
        if s == 0:
            coming[STREAMS].wait()
            leave(gtok_held, outs[15])
            coming[STREAMS + 1].wait()
            leave(out_held, outs[14])
    leave(gconv, outs[2])
    leave(gb1, outs[1])
    for copy in leaving:
        copy.wait()


def call_finish(totals, piece, small, block_out, gtok, half):
    hbm = pl.BlockSpec(memory_space=pl.ANY)
    vmem = pl.BlockSpec(memory_space=pltpu.VMEM)
    shapes = [
        (WIDTH, half), (half,), (KS * KS, half), (half, WIDTH), (24, 3 * WIDTH // 2),
        (24, WIDTH // 2),
    ]
    shapes += [(WIDTH,)] * 6 + [(HEADS, HEADS)] * 2
    return pl.pallas_call(
        finish_kernel,
        in_specs=[hbm] + [vmem] * 2 + [hbm] * 2,
        out_specs=[hbm] * 16,
        out_shape=[jax.ShapeDtypeStruct(shape, f32) for shape in shapes]
        + [jax.ShapeDtypeStruct(v.shape, v.dtype) for v in (block_out, gtok)],
        scratch_shapes=[pltpu.VMEM(shape, f32) for shape in shapes]
        + [
            pltpu.VMEM(totals.shape, bf16),
            pltpu.VMEM(block_out.shape, bf16), pltpu.VMEM(gtok.shape, f32),
            pltpu.VMEM((128, 128), f32), pltpu.VMEM((2, 8, 128), f32),
            pltpu.SemaphoreType.DMA((STREAMS + 2 + 2 * STREAMS + 14,)),
        ],
        compiler_params=pltpu.CompilerParams(vmem_limit_bytes=VMEM),
        name="finish",
    )(totals, piece, small, block_out, gtok)


def shards_any(
    tokens, norm1_gain, norm1_bias, qkv_weight, mix_pre, mix_post, proj_weight, proj_bias,
    norm2_gain, norm2_bias, fc1_weight, fc1_bias, conv_weight, fc2_weight, fc2_bias, cotangent,
):
    gather = lambda v, axis, dim: lax.all_gather(v, axis, axis=dim, tiled=True)
    both = jnp.concatenate([qkv_weight, proj_weight], axis=1)
    pair = lax.all_gather(gather(both, "dp", 0), "tensor", axis=0)
    columns = qkv_weight.shape[1]
    wqkv = jnp.concatenate([pair[0, :, :columns], pair[1, :, :columns]], axis=1)
    wproj = jnp.concatenate([pair[0, :, columns:], pair[1, :, columns:]], axis=1)
    fc1 = gather(fc1_weight, "tensor", 1)
    taps = jnp.concatenate([conv_weight, fc1_bias[None]], axis=0)
    taps = jnp.pad(gather(taps, "tensor", 1), ((0, TAPS - KS * KS - 1), (0, 0)))
    fc2 = gather(fc2_weight, "tensor", 0)
    block_out, gtok, gqkv, gproj, gfc1, gconv, gfc2, small = local_block(
        tokens, norm1_gain, norm1_bias, wqkv, mix_pre, mix_post, wproj, proj_bias, norm2_gain,
        norm2_bias, fc1, taps, fc2, fc2_bias, cotangent,
    )
    scatter = lambda v, axis, dim: lax.psum_scatter(v, axis, scatter_dimension=dim, tiled=True)
    gqkv = scatter(scatter(gqkv, "tensor", 1), "dp", 0)
    gproj = scatter(scatter(gproj, "tensor", 1), "dp", 0)
    gfc1 = lax.psum(scatter(gfc1, "tensor", 1), "dp")
    gfc2 = lax.psum(scatter(gfc2, "tensor", 0), "dp")
    gconv = lax.psum(scatter(gconv, "tensor", 1), "dp")
    small = lax.psum(small, ("dp", "tensor"))
    rows = jnp.concatenate([small[0:8], small[8:16], small[16:24]], axis=1)
    mixes = small[24, : 2 * HEADS * HEADS].reshape(2, HEADS, HEADS)
    return (
        block_out, gtok, rows[0], rows[1], gqkv, mixes[0] * 0.125, mixes[1], gproj, rows[2],
        rows[3], rows[4], gfc1, gconv[KS * KS], gconv[: KS * KS], gfc2, rows[5],
    )


def shards_sixteen(
    tokens, norm1_gain, norm1_bias, qkv_weight, mix_pre, mix_post, proj_weight, proj_bias,
    norm2_gain, norm2_bias, fc1_weight, fc1_bias, conv_weight, fc2_weight, fc2_bias, cotangent,
):
    turn = lambda v: jnp.transpose(v, (1, 0, 2))
    block_out, gtok, totals, piece, small = call_block(
        mix_pre, mix_post, turn(tokens), turn(cotangent), norm1_gain, norm1_bias, proj_bias, norm2_gain,
        norm2_bias, fc2_bias, qkv_weight, proj_weight, fc1_weight, conv_weight, fc1_bias,
        fc2_weight,
    )
    (
        gfc1, gb1, gconv, gfc2, gqkv, gproj, g1, b1, pb, g2, b2, fb, pre, post, block_out, gtok
    ) = call_finish(totals, piece, small, block_out, gtok, fc1_weight.shape[1])
    block_out, gtok = turn(block_out), turn(gtok)
    return (
        block_out, gtok, g1, b1, gqkv, pre, post, gproj, pb, g2, b2, gfc1, gb1, gconv, gfc2, fb
    )


def solution(mesh):
    spec = P(("dp", "tensor"), None, None)
    in_specs = (
        spec, P(), P(), P("dp", "tensor"), P(), P(), P("dp", "tensor"), P(), P(), P(),
        P(None, "tensor"), P("tensor"), P(None, "tensor"), P("tensor", None), P(), spec,
    )
    out_specs = (
        spec, spec, P(), P(), P("dp", "tensor"), P(), P(), P("dp", "tensor"), P(), P(), P(),
        P(None, "tensor"), P("tensor"), P(None, "tensor"), P("tensor", None), P(),
    )
    sixteen = mesh.shape["dp"] == 16 and mesh.shape["tensor"] == 2
    body = shards_sixteen if sixteen else shards_any
    return jax.shard_map(body, mesh=mesh, in_specs=in_specs, out_specs=out_specs, check_vma=False)
```

```python
import functools

import jax
import jax.numpy as jnp
import numpy as np
from jax import lax
from jax.experimental import pallas as pl
from jax.experimental.pallas import tpu as pltpu
from jax.sharding import PartitionSpec as P

HEADS = 6
HEAD_DIM = 64
KS = 7
GRID = 14
POINTS = 17
SEQ = 197
ROWS = 208
TAPS = 64
KEYS = 256
WIDTH = 384
HALF = 160
COEFS = 2 * HALF
CLASS_ROW = 145
CHUNK = 512
STREAM = 256
SMALL = 32
VMEM = 62 * 1024 * 1024

f32 = jnp.float32
bf16 = jnp.bfloat16


def fourier():
    pairs = [(0, 0)]
    for k in range(POINTS):
        for m in range(POINTS):
            other = ((-k) % POINTS, (-m) % POINTS)
            if (k, m) != (0, 0) and (k, m) < other:
                pairs.append((k, m))
    freq = np.array(pairs, np.float64)
    unit = 2.0 * np.pi / POINTS
    spots = np.array([(y, x) for y in range(GRID) for x in range(GRID)], np.float64)
    taps = np.array([(a - 3, c - 3) for a in range(KS) for c in range(KS)], np.float64)
    count = len(pairs)
    angle = unit * freq @ spots.T
    forward = np.zeros((COEFS, ROWS))
    forward[:count, 1:SEQ] = np.cos(angle)
    forward[HALF : HALF + count, 1:SEQ] = -np.sin(angle)
    forward[CLASS_ROW, 0] = 1.0
    weight = np.full((count, 1), 2.0)
    weight[0] = 1.0
    weight = weight / POINTS**2
    inverse = np.zeros((COEFS, ROWS))
    inverse[:count, 1:SEQ] = weight * np.cos(angle)
    inverse[HALF : HALF + count, 1:SEQ] = -weight * np.sin(angle)
    inverse[CLASS_ROW, 0] = 1.0
    turn = unit * freq @ taps.T
    kernel = np.zeros((COEFS, TAPS))
    kernel[:count, : KS * KS] = np.cos(turn)
    kernel[HALF : HALF + count, : KS * KS] = np.sin(turn)
    back = np.zeros((COEFS, TAPS))
    back[:count, : KS * KS] = weight * np.cos(turn)
    back[HALF : HALF + count, : KS * KS] = -weight * np.sin(turn)
    one = np.zeros((COEFS, 1))
    one[CLASS_ROW] = 1.0
    return forward, inverse.T, kernel, back.T, one


def split(matrix):
    high = np.asarray(matrix, np.float32).astype(bf16)
    low = (np.asarray(matrix, np.float32) - high.astype(np.float32)).astype(bf16)
    return high, low


def dot(a, b):
    return lax.dot_general(a, b, (((1,), (0,)), ((), ())), preferred_element_type=f32)


def dot_t(a, b):
    return lax.dot_general(a, b, (((1,), (1,)), ((), ())), preferred_element_type=f32)


def t_dot(a, b):
    return lax.dot_general(a, b, (((0,), (0,)), ((), ())), preferred_element_type=f32)


def centre(values):
    centred = values - jnp.mean(values, axis=-1, keepdims=True)
    spread = jnp.mean(centred * centred, axis=-1, keepdims=True)
    return centred, lax.rsqrt(spread + 1e-05)


def norm_back(centred, r, gain, grad):
    scaled = grad * gain
    moment = jnp.mean(scaled * centred, axis=-1, keepdims=True)
    back = r * (scaled - jnp.mean(scaled, axis=-1, keepdims=True) - centred * (r * r * moment))
    return back, grad * (centred * r)


def row(ref):
    return ref[...].reshape(1, ref.shape[0])


def add_rows(values):
    return jnp.sum(values, axis=0, keepdims=True)


def row_mask(shape):
    return lax.broadcasted_iota(jnp.int32, shape, 0) < SEQ


def attention_forward(
    pre, post, tok, wqkv, wproj, gain1, bias1, pbias, gain2, bias2,
    n1_out, packed_out, probs_out, attn_out, att_out, mid_out, n2_out, pad, score, keys,
):
    pad[SEQ - 5 :] = jnp.zeros((ROWS - SEQ + 5, WIDTH), f32)
    pad[:SEQ] = tok[0].astype(f32)
    inputs = pad[...]
    centred, r = centre(inputs)
    inside = row_mask((ROWS, WIDTH))
    n1 = jnp.where(inside, centred * r * row(gain1) + row(bias1), 0.0).astype(bf16)
    n1_out[0] = n1
    packed = dot(n1, wqkv[...]).astype(bf16)
    packed_out[0, :ROWS] = packed
    packed_out[0, ROWS:] = jnp.zeros((KEYS - ROWS, 3 * WIDTH), bf16)
    low_half = lax.broadcasted_iota(jnp.int32, (ROWS, 128), 1) < HEAD_DIM
    zero = jnp.zeros((ROWS, 128), bf16)
    for p in range(HEADS // 2):
        query = packed_out[0, :ROWS, 128 * p : 128 * p + 128]
        key = packed_out[0, :, WIDTH + 128 * p : WIDTH + 128 * p + 128]
        score[2 * p] = dot_t(jnp.where(low_half, query, zero), key)
        score[2 * p + 1] = dot_t(jnp.where(low_half, zero, query), key)
    valid = lax.broadcasted_iota(jnp.int32, (16, KEYS), 1) < SEQ

    def rows_step(step, carry):
        rows = pl.ds(pl.multiple_of(step * 16, 16), 16)
        scores = [score[h, rows, :] for h in range(HEADS)]
        probs = []
        for g in range(HEADS):
            mixed = scores[0] * (pre[g, 0] * 0.125)
            for h in range(1, HEADS):
                mixed = mixed + scores[h] * (pre[g, h] * 0.125)
            mixed = jnp.where(valid, mixed, -1e30)
            top = jnp.max(mixed, axis=-1, keepdims=True)
            raised = jnp.exp(mixed - top)
            prob = raised * (1.0 / jnp.sum(raised, axis=-1, keepdims=True))
            probs_out[0, g, rows, :] = prob
            probs.append(prob)
        for g in range(HEADS):
            mixed = probs[0] * post[g, 0]
            for h in range(1, HEADS):
                mixed = mixed + probs[h] * post[g, h]
            attn_out[0, g, rows, :] = mixed.astype(bf16)
        return carry

    lax.fori_loop(0, ROWS // 16, rows_step, 0)
    pieces = []
    for p in range(HEADS // 2):
        value = packed_out[0, :, 2 * WIDTH + 128 * p : 2 * WIDTH + 128 * p + 128]
        pieces.append(
            jnp.where(low_half, dot(attn_out[0, 2 * p], value), dot(attn_out[0, 2 * p + 1], value))
        )
    attended = jnp.concatenate(pieces, axis=1).astype(bf16)
    att_out[0] = attended
    middle = inputs + (dot(attended, wproj[...]) + row(pbias))
    mid_out[0] = middle
    centred, r = centre(middle)
    n2_out[0] = jnp.where(inside, centred * r * row(gain2) + row(bias2), 0.0).astype(bf16)


def gelu_parts(hidden):
    size = jnp.abs(hidden) * np.float32(np.sqrt(0.5))
    t = 1.0 / (1.0 + 0.3275911 * size)
    raised = jnp.exp(-(size * size))
    series = t * (
        0.254829592
        + t * (-0.284496736 + t * (1.421413741 + t * (-1.453152027 + t * 1.061405429)))
    )
    tail = 0.5 * series * raised
    cdf = jnp.where(hidden < 0.0, tail, 1.0 - tail)
    return hidden * cdf, cdf + hidden * (raised * np.float32(1.0 / np.sqrt(2.0 * np.pi)))


def mlp(
    n2, cot, mid, fc1, conv, fc2, fc2b, fwd, inv, kh, kl, bh, bl, one,
    block_out, gn2_out, gfc1_out, gconv_out, gfc2_out, gb2_out,
    cot_pad, pad, hid, grad, out_acc, conv_low, ghid_low,
):
    step = pl.program_id(0)
    images = n2.shape[0]

    @pl.when(step == 0)
    def _():
        total = jnp.zeros((1, WIDTH), f32)
        for b in range(images):
            pad[SEQ - 5 :] = jnp.zeros((ROWS - SEQ + 5, WIDTH), f32)
            pad[:SEQ] = cot[b].astype(f32)
            values = pad[...]
            total = total + add_rows(values)
            cot_pad[b * ROWS : (b + 1) * ROWS] = values.astype(bf16)
        gb2_out[...] = total

    w1 = fc1[...]
    w2 = fc2[...]
    taps = conv[...]
    turned = dot(kh[...], taps) + dot(kl[...], taps) + one[...]
    kr, ki = turned[:HALF], turned[HALF:]
    rows_all = n2[...].reshape(images * ROWS, WIDTH)
    hid[...] = dot(rows_all, w1) + taps.astype(f32)[KS * KS : KS * KS + 1]
    grad[...] = dot_t(cot_pad[...], w2)
    cross_r = jnp.zeros((HALF, CHUNK), f32)
    cross_i = jnp.zeros((HALF, CHUNK), f32)
    bias_sum = jnp.zeros((1, CHUNK), f32)
    for b in range(images):
        span = slice(b * ROWS, (b + 1) * ROWS)
        act, slope = gelu_parts(hid[span, :])
        x = dot(fwd[...], act.astype(bf16))
        y = dot(fwd[...], grad[span, :].astype(bf16))
        xr, xi = x[:HALF], x[HALF:]
        yr, yi = y[:HALF], y[HALF:]
        made = jnp.concatenate([xr * kr - xi * ki, xr * ki + xi * kr], axis=0).astype(bf16)
        back = jnp.concatenate([yr * kr + yi * ki, yi * kr - yr * ki], axis=0).astype(bf16)
        cross_r = cross_r + (xr * yr + xi * yi)
        cross_i = cross_i + (xi * yr - xr * yi)
        conv_low[span, :] = dot(inv[...], made).astype(bf16)
        ghid = (dot(inv[...], back) * slope).astype(bf16)
        bias_sum = bias_sum + add_rows(ghid.astype(f32))
        ghid_low[span, :] = ghid
    cross = jnp.concatenate([cross_r, cross_i], axis=0)
    high = cross.astype(bf16)
    low = (cross - high.astype(f32)).astype(bf16)
    gconv_out[...] = dot(bh[...], high) + dot(bl[...], high) + dot(bh[...], low)
    gconv_out[KS * KS : KS * KS + 1] = bias_sum
    convolved = conv_low[...]
    ghid_all = ghid_low[...]
    part = dot(convolved, w2).reshape(images, ROWS, WIDTH)
    part_grad = dot_t(ghid_all, w1).reshape(images, ROWS, WIDTH)
    gfc2_out[...] = t_dot(convolved, cot_pad[...])
    gfc1_out[...] = t_dot(rows_all, ghid_all)

    @pl.when(step == 0)
    def _():
        out_acc[...] = part
        gn2_out[...] = part_grad

    @pl.when(step > 0)
    def _():
        out_acc[...] += part
        gn2_out[...] += part_grad

    @pl.when(step == pl.num_programs(0) - 1)
    def _():
        for b in range(images):
            result = mid[b] + (out_acc[b] + row(fc2b))
            block_out[b] = result[:SEQ].astype(bf16)


def attention_backward(
    pre, post, tok, cot, n1, packed, probs, attn, att, mid, gn2, wqkv, wproj, gain1, gain2, gb2,
    gtok_out, gqkv_out, gproj_out, small_out,
    pad, score, weight, low, mix, rows_out, square,
):
    step = pl.program_id(0)

    @pl.when(step == 0)
    def _():
        gqkv_out[...] = jnp.zeros_like(gqkv_out)
        gproj_out[...] = jnp.zeros_like(gproj_out)
        rows_out[...] = jnp.zeros_like(rows_out)
        mix[...] = jnp.zeros_like(mix)

    pad[SEQ - 5 :] = jnp.zeros((ROWS - SEQ + 5, WIDTH), f32)
    pad[:SEQ] = cot[0].astype(f32)
    centred, r = centre(mid[0])
    grad = gn2[0]
    back, gain_rows = norm_back(centred, r, row(gain2), grad)
    rows_out[3:4] += add_rows(gain_rows)
    rows_out[4:5] += add_rows(grad)
    gmid = pad[...] + back
    gmid_low = gmid.astype(bf16)
    rows_out[2:3] += add_rows(gmid_low.astype(f32))
    gproj_out[...] += t_dot(att[0], gmid_low)
    gatt = dot_t(gmid_low, wproj[...]).astype(bf16)
    low_half = lax.broadcasted_iota(jnp.int32, (ROWS, 128), 1) < HEAD_DIM
    key_half = lax.broadcasted_iota(jnp.int32, (KEYS, 128), 1) < HEAD_DIM
    zero = jnp.zeros((ROWS, 128), bf16)
    for p in range(HEADS // 2):
        query = packed[0, :ROWS, 128 * p : 128 * p + 128]
        key = packed[0, :, WIDTH + 128 * p : WIDTH + 128 * p + 128]
        value = packed[0, :, 2 * WIDTH + 128 * p : 2 * WIDTH + 128 * p + 128]
        ahead = gatt[:, 128 * p : 128 * p + 128]
        score[2 * p] = dot_t(jnp.where(low_half, query, zero), key)
        score[2 * p + 1] = dot_t(jnp.where(low_half, zero, query), key)
        weight[2 * p] = dot_t(jnp.where(low_half, ahead, zero), value)
        weight[2 * p + 1] = dot_t(jnp.where(low_half, zero, ahead), value)

    def fold(values):
        values = values[:, :128] + values[:, 128:]
        return values[:8] + values[8:]

    def rows_step(index, carry):
        rows = pl.ds(pl.multiple_of(index * 16, 16), 16)
        weights = [weight[g, rows, :] for g in range(HEADS)]
        mixed = []
        for h in range(HEADS):
            prob = probs[0, h, rows, :]
            ahead = weights[0] * post[0, h]
            for g in range(1, HEADS):
                ahead = ahead + weights[g] * post[g, h]
            for g in range(HEADS):
                mix[HEADS * HEADS + g * HEADS + h] += fold(weights[g] * prob)
            inner = jnp.sum(prob * ahead, axis=-1, keepdims=True)
            mixed.append(prob * (ahead - inner))
        for h in range(HEADS):
            scores = score[h, rows, :]
            total = mixed[0] * pre[0, h]
            for g in range(1, HEADS):
                total = total + mixed[g] * pre[g, h]
            low[h, rows, :] = total.astype(bf16)
            for g in range(HEADS):
                mix[g * HEADS + h] += fold(mixed[g] * scores)
        return carry

    lax.fori_loop(0, ROWS // 16, rows_step, 0)
    queries, keys, values = [], [], []
    for p in range(HEADS // 2):
        query = packed[0, :ROWS, 128 * p : 128 * p + 128]
        key = packed[0, :, WIDTH + 128 * p : WIDTH + 128 * p + 128]
        ahead = gatt[:, 128 * p : 128 * p + 128]
        even, odd = low[2 * p], low[2 * p + 1]
        queries.append(jnp.where(low_half, dot(even, key), dot(odd, key)) * 0.125)
        keys.append(jnp.where(key_half, t_dot(even, query), t_dot(odd, query))[:ROWS] * 0.125)
        values.append(
            jnp.where(key_half, t_dot(attn[0, 2 * p], ahead), t_dot(attn[0, 2 * p + 1], ahead))[
                :ROWS
            ]
        )
    gpacked = jnp.concatenate(queries + keys + values, axis=1).astype(bf16)
    gqkv_out[...] += t_dot(n1[0], gpacked)
    gnormed = dot_t(gpacked, wqkv[...])
    pad[:SEQ] = tok[0].astype(f32)
    centred, r = centre(pad[...])
    back, gain_rows = norm_back(centred, r, row(gain1), gnormed)
    rows_out[0:1] += add_rows(gain_rows)
    rows_out[1:2] += add_rows(gnormed)
    gtok_out[0] = (gmid + back)[:SEQ]

    @pl.when(step == pl.num_programs(0) - 1)
    def _():
        rows_out[5:6] = gb2[...]
        for t in range(WIDTH // 128):
            small_out[8 * t : 8 * t + 8] = rows_out[:, 128 * t : 128 * t + 128]
        square[...] = jnp.zeros_like(square)
        square[: 2 * HEADS * HEADS] = jnp.sum(mix[...], axis=1)
        sums = add_rows(square[...].T)
        small_out[24:] = jnp.concatenate([sums, jnp.zeros((SMALL - 25, 128), f32)], axis=0)


def whole(shape):
    return pl.BlockSpec(shape, lambda *_: (0,) * len(shape))


def image(shape):
    return pl.BlockSpec((1,) + shape, lambda i: (i,) + (0,) * len(shape))


def params():
    return pltpu.CompilerParams(vmem_limit_bytes=VMEM, dimension_semantics=("arbitrary",))


def call_forward(tokens, wqkv, wproj, pre, post, gain1, bias1, pbias, gain2, bias2):
    images = tokens.shape[0]
    smem = pl.BlockSpec(memory_space=pltpu.SMEM)
    vector = whole((WIDTH,))
    return pl.pallas_call(
        attention_forward,
        grid=(images,),
        in_specs=[
            smem, smem, image((SEQ, WIDTH)), whole((WIDTH, 3 * WIDTH)), whole((WIDTH, WIDTH)),
            vector, vector, vector, vector, vector,
        ],
        out_specs=[
            image((ROWS, WIDTH)), image((KEYS, 3 * WIDTH)), image((HEADS, ROWS, KEYS)),
            image((HEADS, ROWS, KEYS)), image((ROWS, WIDTH)), image((ROWS, WIDTH)),
            image((ROWS, WIDTH)),
        ],
        out_shape=[
            jax.ShapeDtypeStruct((images, ROWS, WIDTH), bf16),
            jax.ShapeDtypeStruct((images, KEYS, 3 * WIDTH), bf16),
            jax.ShapeDtypeStruct((images, HEADS, ROWS, KEYS), f32),
            jax.ShapeDtypeStruct((images, HEADS, ROWS, KEYS), bf16),
            jax.ShapeDtypeStruct((images, ROWS, WIDTH), bf16),
            jax.ShapeDtypeStruct((images, ROWS, WIDTH), f32),
            jax.ShapeDtypeStruct((images, ROWS, WIDTH), bf16),
        ],
        scratch_shapes=[
            pltpu.VMEM((ROWS, WIDTH), f32),
            pltpu.VMEM((HEADS, ROWS, KEYS), f32),
            pltpu.VMEM((8, 128), f32),
        ],
        compiler_params=params(),
        name="attention_forward",
    )(pre, post, tokens, wqkv, wproj, gain1, bias1, pbias, gain2, bias2)


def call_mlp(n2, cotangent, middle, fc1, conv, fc2, fc2_bias):
    images = n2.shape[0]
    units = fc1.shape[1]
    steps = units // CHUNK
    forward, inverse, kernel, back, one = fourier()
    kernel_high, kernel_low = split(kernel)
    back_high, back_low = split(back)
    consts = [
        jnp.asarray(forward.astype(np.float32).astype(bf16)),
        jnp.asarray(inverse.astype(np.float32).astype(bf16)),
        jnp.asarray(kernel_high), jnp.asarray(kernel_low),
        jnp.asarray(back_high), jnp.asarray(back_low),
        jnp.asarray(one.astype(np.float32)),
    ]
    columns = lambda rows: pl.BlockSpec((rows, CHUNK), lambda i: (0, i))
    total = images * ROWS
    return pl.pallas_call(
        mlp,
        grid=(steps,),
        in_specs=[
            whole((images, ROWS, WIDTH)), whole((images, SEQ, WIDTH)), whole((images, ROWS, WIDTH)),
            columns(WIDTH), columns(TAPS),
            pl.BlockSpec((CHUNK, WIDTH), lambda i: (i, 0)), whole((WIDTH,)),
        ]
        + [whole(c.shape) for c in consts],
        out_specs=[
            whole((images, SEQ, WIDTH)), whole((images, ROWS, WIDTH)),
            columns(WIDTH), columns(TAPS),
            pl.BlockSpec((CHUNK, WIDTH), lambda i: (i, 0)), whole((1, WIDTH)),
        ],
        out_shape=[
            jax.ShapeDtypeStruct((images, SEQ, WIDTH), bf16),
            jax.ShapeDtypeStruct((images, ROWS, WIDTH), f32),
            jax.ShapeDtypeStruct((WIDTH, units), f32),
            jax.ShapeDtypeStruct((TAPS, units), f32),
            jax.ShapeDtypeStruct((units, WIDTH), f32),
            jax.ShapeDtypeStruct((1, WIDTH), f32),
        ],
        scratch_shapes=[
            pltpu.VMEM((total, WIDTH), bf16),
            pltpu.VMEM((ROWS, WIDTH), f32),
            pltpu.VMEM((total, CHUNK), f32),
            pltpu.VMEM((total, CHUNK), f32),
            pltpu.VMEM((images, ROWS, WIDTH), f32),
            pltpu.VMEM((total, CHUNK), bf16),
            pltpu.VMEM((total, CHUNK), bf16),
        ],
        compiler_params=params(),
        name="mlp",
    )(n2, cotangent, middle, fc1, conv, fc2, fc2_bias, *consts)


def call_backward(
    tokens, cotangent, n1, packed, probs, attn, att, mid, gn2, wqkv, wproj, pre, post, gain1, gain2, gb2
):
    images = tokens.shape[0]
    smem = pl.BlockSpec(memory_space=pltpu.SMEM)
    vector = whole((WIDTH,))
    return pl.pallas_call(
        attention_backward,
        grid=(images,),
        in_specs=[
            smem, smem, image((SEQ, WIDTH)), image((SEQ, WIDTH)), image((ROWS, WIDTH)),
            image((KEYS, 3 * WIDTH)), image((HEADS, ROWS, KEYS)), image((HEADS, ROWS, KEYS)),
            image((ROWS, WIDTH)), image((ROWS, WIDTH)), image((ROWS, WIDTH)),
            whole((WIDTH, 3 * WIDTH)), whole((WIDTH, WIDTH)), vector, vector,
            whole((1, WIDTH)),
        ],
        out_specs=[
            image((SEQ, WIDTH)), whole((WIDTH, 3 * WIDTH)), whole((WIDTH, WIDTH)),
            whole((SMALL, 128)),
        ],
        out_shape=[
            jax.ShapeDtypeStruct((images, SEQ, WIDTH), f32),
            jax.ShapeDtypeStruct((WIDTH, 3 * WIDTH), f32),
            jax.ShapeDtypeStruct((WIDTH, WIDTH), f32),
            jax.ShapeDtypeStruct((SMALL, 128), f32),
        ],
        scratch_shapes=[
            pltpu.VMEM((ROWS, WIDTH), f32),
            pltpu.VMEM((HEADS, ROWS, KEYS), f32),
            pltpu.VMEM((HEADS, ROWS, KEYS), f32),
            pltpu.VMEM((HEADS, ROWS, KEYS), bf16),
            pltpu.VMEM((2 * HEADS * HEADS, 8, 128), f32),
            pltpu.VMEM((8, WIDTH), f32),
            pltpu.VMEM((128, 128), f32),
        ],
        compiler_params=params(),
        name="attention_backward",
    )(
        pre, post, tokens, cotangent, n1, packed, probs, attn, att, mid, gn2, wqkv, wproj,
        gain1, gain2, gb2,
    )


def local_block(
    tokens, norm1_gain, norm1_bias, wqkv, mix_pre, mix_post, wproj, proj_bias, norm2_gain,
    norm2_bias, fc1, taps, fc2, fc2_bias, cotangent,
):
    n1, packed, probs, attn, att, mid, n2 = call_forward(
        tokens, wqkv, wproj, mix_pre, mix_post, norm1_gain, norm1_bias, proj_bias, norm2_gain,
        norm2_bias,
    )
    block_out, gn2, gfc1, gconv, gfc2, gb2 = call_mlp(n2, cotangent, mid, fc1, taps, fc2, fc2_bias)
    gtok, gqkv, gproj, small = call_backward(
        tokens, cotangent, n1, packed, probs, attn, att, mid, gn2, wqkv, wproj, mix_pre, mix_post,
        norm1_gain, norm2_gain, gb2,
    )
    return block_out, gtok, gqkv, gproj, gfc1, gconv, gfc2, small


SIDES = (8, 4, 2, 1)
DEPTH, PLANE = (0, 1), (2, 3)
ROUNDS = ((PLANE, DEPTH), (DEPTH, PLANE))
FLIPS = ((0, 1), (1, 0), (1, 1))
MESH_IDS = pl.DeviceIdType.MESH
PIECE = 144
PIECE_PARTS = ((0, 96), (96, 48))
BLOCK = 112
BLOCK_PARTS = ((0, 80), (80, 32))
STREAMS = 3
MLP_PLAN = {(1, 4): ((0, -1),), (3, 4): ((1, -1), (0, 0)), (5, 4): ((2, -1), (0, 1), (1, 0))}
BACK_PLAN = {
    (0, 3): ((0, 2), (1, 1)), (1, 1): ((2, 0),), (1, 2): ((1, 2),), (1, 3): ((2, 1),),
}
TAIL_PLAN = ()


class Place:
    def __init__(self):
        self.dp, self.core = lax.axis_index("dp"), lax.axis_index("tensor")
        self.bits = tuple(lax.rem(self.dp // stride, 2) for stride in SIDES)
        self.pair = (self.dp, 1 - self.core)

    def peer(self, axes, flip):
        dp = self.dp
        for axis, turn in zip(axes, flip):
            if turn:
                dp = dp + (1 - 2 * self.bits[axis]) * SIDES[axis]
        return dp, self.core

    def mine(self, axes):
        return {axis: self.bits[axis] for axis in axes}

    def theirs(self, axes, flip):
        return {
            axis: 1 - self.bits[axis] if turn else self.bits[axis] for axis, turn in zip(axes, flip)
        }

    def everyone(self):
        peers = [self.peer(axes, flip) for axes in (PLANE, DEPTH) for flip in FLIPS]
        return peers + [self.pair]


def greet(partners):
    barrier = pltpu.get_barrier_semaphore()
    for partner in partners:
        pl.semaphore_signal(barrier, inc=1, device_id=partner, device_id_type=MESH_IDS)
    return lambda: pl.semaphore_wait(barrier, len(partners))


def remote(src, dst, sems, index, device):
    return pltpu.make_async_remote_copy(
        src_ref=src, dst_ref=dst, send_sem=sems.at[(0,) + index], recv_sem=sems.at[(1,) + index],
        device_id=device, device_id_type=MESH_IDS,
    )


def region(fixed, rows):
    return tuple(fixed.get(axis, slice(None)) for axis in range(4)) + (rows,)


def index_of(d):
    return tuple((d // stride) % 2 for stride in SIDES)


class Sum:
    def __init__(self, acc, landing, sems, parts, where):
        self.acc, self.landing, self.sems = acc, landing, sems
        self.parts, self.where = parts, where

    def copy(self, part, turn, peer):
        rows, axes, flip = pl.ds(*self.parts[part]), ROUNDS[part][turn], FLIPS[peer]
        fixed = self.where.theirs(axes, flip)
        if turn == 0:
            dst = self.landing[0].at[peer, :, :, rows]
        else:
            fixed.update(self.where.mine(ROUNDS[part][0]))
            dst = self.landing[1].at[peer, rows]
        return remote(
            self.acc.at[region(fixed, rows)], dst, self.sems, (part, turn, peer),
            self.where.peer(axes, flip),
        )

    def start(self):
        for part in range(2):
            for peer in range(3):
                self.copy(part, 0, peer).start()

    def act(self, turn):
        for part in range(2):
            rows = pl.ds(*self.parts[part])
            first, second = ROUNDS[part]
            for peer in range(3):
                self.copy(part, turn, peer).wait_recv()
            for near in (0, 1) if turn == 0 else (None,):
                for far in (0, 1) if turn == 0 else (None,):
                    fixed = self.where.mine(first)
                    if turn == 0:
                        fixed.update({second[0]: near, second[1]: far})
                        came = [self.landing[0][peer, near, far, rows] for peer in range(3)]
                    else:
                        fixed.update(self.where.mine(second))
                        came = [self.landing[1][peer, rows] for peer in range(3)]
                    spot = region(fixed, rows)
                    total = self.acc[spot].astype(f32)
                    for values in came:
                        total = total + values.astype(f32)
                    self.acc[spot] = total.astype(bf16)
            if turn == 0:
                for peer in range(3):
                    self.copy(part, 1, peer).start()

    def finish(self):
        for part in range(2):
            for turn in range(2):
                for peer in range(3):
                    self.copy(part, turn, peer).wait_send()


class Gather:
    def __init__(self, full, sems, parts, where):
        self.full, self.sems, self.parts, self.where = full, sems, parts, where

    def spot(self, part, turn, flip):
        first, second = ROUNDS[part][::-1]
        if turn == 0:
            fixed = {**self.where.mine(second), **self.where.theirs(first, flip)}
        else:
            fixed = self.where.theirs(second, flip)
        return region(fixed, pl.ds(*self.parts[part]))

    def copy(self, part, turn, peer):
        axes, held = ROUNDS[part][::-1][turn], self.spot(part, turn, (0, 0))
        return remote(
            self.full.at[held], self.full.at[held], self.sems, (part, turn, peer),
            self.where.peer(axes, FLIPS[peer]),
        )

    def start(self):
        for part in range(2):
            for peer in range(3):
                self.copy(part, 0, peer).start()

    def act(self, turn, then=None):
        for part in range(2):
            for peer in range(3):
                self.copy(part, turn, peer).wait_recv()
            if turn == 0:
                for peer in range(3):
                    self.copy(part, 1, peer).start()
            if then is not None:
                for peer in range(3):
                    then(part, turn, peer)

    def finish(self):
        for part in range(2):
            for turn in range(2):
                for peer in range(3):
                    self.copy(part, turn, peer).wait_send()


def tiles(values):
    return jnp.concatenate(
        [values[:, 128 * t : 128 * t + 128] for t in range(values.shape[1] // 128)], axis=0
    )


def weave(*lists):
    steps = [((k + 0.5) / len(one), step) for one in lists for k, step in enumerate(one)]
    for _, step in sorted(steps, key=lambda item: item[0]):
        step()


def untiles(values, count):
    rows = values.shape[0] // count
    return jnp.concatenate([values[t * rows : (t + 1) * rows] for t in range(count)], axis=1)


def block_kernel(
    pre, post, tok, cot, gain1, bias1, pbias, gain2, bias2, fc2b,
    qkv, proj, fc1, conv, bias, fc2, fwd_in, inv_in, kh_in, kl_in, bh_in, bl_in, one,
    block_out, gtok_out, fulls_out, piece_out, small_out, *rest,
):
    (
        tok_held, cot_held, out_held, gtok_held, out_wide, fwd, inv, kh, kl, bh, bl,
        piece_full, piece_other, taps_pad, wqkv, wproj, fc1_blocks, fc2_full, conv_full,
        cot_pad, n1, packed, score, weight, probs, attn, att, mid, n2,
        turned, ghat, hid, hidden, slope, acted, weights, conv_low, ghid_low, gmid, gmid_low, gatt, low, gpacked, mix,
        rows_out, square, gqkv, gproj, small_sums, small_landed,
        streams_out, streams_came, streams_acc, streams_landing, gconv, made, ahead, behind, cross, att_bufs,
        local_sems, leave_sems, gather_sems, gather_pair_sems, stream_pair_sems, stream_sems, att_sems, att_pair_sems,
    ) = rest
    images = tok.shape[1]
    total = images * ROWS
    half = fc1.shape[1]
    where = Place()
    pair, core, mine = where.pair, where.core, where.bits
    met = greet(where.everyone())
    mine_start = pl.multiple_of(core * half, 128)
    cols, rows_of = pl.ds(mine_start, half), pl.ds(mine_start, half)
    span = lambda b: slice(b * ROWS, (b + 1) * ROWS)
    spans = [span(b) for b in range(images)]
    inside = row_mask((ROWS, WIDTH))
    fulls = [streams_came.at[s] for s in range(STREAMS)]
    sides = [(s, pl.ds(s * STREAM, STREAM)) for s in range(STREAMS)]
    local = [
        pltpu.make_async_copy(src, dst, local_sems.at[index])
        for index, (src, dst) in enumerate(
            (
                (tok, tok_held), (cot, cot_held), (fc2, fc2_full.at[rows_of]),
                (fwd_in, fwd), (kh_in, kh), (kl_in, kl),
                *((fc1.at[:, side], fc1_blocks.at[core * STREAMS + s]) for s, side in sides),
                (inv_in, inv), (bh_in, bh), (bl_in, bl),
            )
        )
    ]
    for copy in local:
        copy.start()

    both = jnp.concatenate([qkv[...].astype(f32), proj[...].astype(f32)], axis=1)
    piece_full[mine] = tiles(both).astype(bf16)
    taps_pad[...] = jnp.zeros(taps_pad.shape, f32)
    taps_pad[: KS * KS] = conv[...].astype(f32)
    taps_pad[KS * KS : KS * KS + 1] = bias[...].astype(f32).reshape(1, half)
    conv_full[:, cols] = taps_pad[...].astype(bf16)
    met()
    gather = Gather(piece_full, gather_sems, PIECE_PARTS, where)
    gather.start()
    weights_come = [
        remote(conv_full.at[:, cols], conv_full.at[:, cols], gather_pair_sems, (0,), pair),
        remote(fc2, fc2_full.at[rows_of], gather_pair_sems, (1,), pair),
        *(
            remote(
                fc1.at[:, side], fc1_blocks.at[core * STREAMS + s], gather_pair_sems, (2 + s,), pair
            )
            for s, side in sides
        ),
    ]
    forwards = [
        remote(
            piece_full.at[mine], piece_other.at[mine], gather_pair_sems, (2 + STREAMS,), pair
        )
    ]
    for copy in weights_come + forwards:
        copy.start()

    def forward(part, turn, peer):
        spot = gather.spot(part, turn, FLIPS[peer])
        copy = remote(
            piece_full.at[spot], piece_other.at[spot], gather_pair_sems,
            (3 + STREAMS + 6 * part + 3 * turn + peer,), pair,
        )
        copy.start()
        forwards.append(copy)

    cot_sum = jnp.zeros((1, WIDTH), f32)
    local[0].wait()
    local[1].wait()
    for source, ref in ((tok_held, mid), (cot_held, gmid)):
        flat = source[...].reshape(SEQ, images * WIDTH)
        for b in range(images):
            ref[b * ROWS + SEQ - 5 : (b + 1) * ROWS] = jnp.zeros((ROWS - SEQ + 5, WIDTH), f32)
            ref[b * ROWS : b * ROWS + SEQ] = flat[:, b * WIDTH : (b + 1) * WIDTH].astype(f32)
    for b in range(images):
        grads = gmid[spans[b], :]
        cot_sum = cot_sum + add_rows(grads)
        cot_pad[spans[b], :] = grads.astype(bf16)
    for b in range(images):
        centred, r = centre(mid[spans[b], :])
        n1[spans[b], :] = jnp.where(inside, centred * r * row(gain1) + row(bias1), 0.0).astype(bf16)

    def prepare(side, begin, end):
        def prepare_unit(s, carry):
            block = side * STREAMS + s
            units = pl.ds(pl.multiple_of(block * STREAM, STREAM), STREAM)
            taps = conv_full[:, units]
            turned[block] = dot(kh[...], taps) + dot(kl[...], taps) + one[...]
            grads = dot_t(cot_pad[...], fc2_full[units, :]).astype(bf16)
            for b in range(images):
                ghat[block, b] = dot(fwd[...], grads[spans[b]]).astype(bf16)
            return carry

        lax.fori_loop(begin, end, prepare_unit, 0)

    gather.act(0, forward)
    for copy in local[2:]:
        copy.wait()
    prepare(core, 0, STREAMS)
    for copy in weights_come:
        copy.wait_recv()
    prepare(1 - core, 0, STREAMS - 1)
    gather.act(1, forward)
    prepare(1 - core, STREAMS - 1, STREAMS)
    for copy in forwards:
        copy.wait_recv()
    width = qkv.shape[1]
    flip = core == 1
    for d in range(0, 16, 2):
        blocks = [
            jnp.concatenate([untiles(ref[index_of(e)].astype(f32), 6) for e in (d, d + 1)], axis=0)
            for ref in (piece_full, piece_other)
        ]
        first = jnp.where(flip, blocks[1], blocks[0])
        second = jnp.where(flip, blocks[0], blocks[1])
        rows = slice(24 * d, 24 * d + 48)
        wqkv[rows, :] = jnp.concatenate([first[:, :width], second[:, :width]], axis=1).astype(bf16)
        wproj[rows, :] = jnp.concatenate([first[:, width:], second[:, width:]], axis=1).astype(bf16)

    for n in range(0, 3 * WIDTH, WIDTH):
        gpacked[:, n : n + WIDTH] = dot(n1[...], wqkv[:, n : n + WIDTH]).astype(bf16)
    for b in range(images):
        packed[b % 2][b // 2, :ROWS] = gpacked[spans[b], :]
        packed[b % 2][b // 2, ROWS:] = jnp.zeros((KEYS - ROWS, 3 * WIDTH), bf16)
    low_half = lax.broadcasted_iota(jnp.int32, (ROWS, 128), 1) < HEAD_DIM
    key_half = lax.broadcasted_iota(jnp.int32, (KEYS, 128), 1) < HEAD_DIM
    zero = jnp.zeros((ROWS, 128), bf16)
    valid = lax.broadcasted_iota(jnp.int32, (16, KEYS), 1) < SEQ

    def section(q, side, which, pair_of_heads, count=KEYS):
        start = which * WIDTH + 128 * pair_of_heads
        return packed[side][q, :count, start : start + 128]

    def rows_at(q, side):
        return pl.ds(pl.multiple_of((2 * q + side) * ROWS, 16), ROWS)

    def skewed(q, stages, after=None):
        for beat in range(2 + max(depth for depth, _ in stages)):
            weave(
                *[
                    [functools.partial(step, q, beat - depth) for step in steps]
                    for depth, steps in stages
                    if 0 <= beat - depth < 2
                ]
            )
            if after is not None:
                after(beat)

    pairs = range(HEADS // 2)
    row_blocks = [slice(r, r + 16) for r in range(0, ROWS, 16)]

    def products(left, right, target, p):
        target[2 * p] = dot_t(jnp.where(low_half, left, zero), right)
        target[2 * p + 1] = dot_t(jnp.where(low_half, zero, left), right)

    def score_step(p, q, side):
        products(section(q, side, 0, p, ROWS), section(q, side, 1, p), score[side], p)

    def softmax_rows(rows, q, side):
        scores = [score[side][h, rows, :] for h in range(HEADS)]
        found = []
        for g in range(HEADS):
            mixed = scores[0] * (pre[g, 0] * 0.125)
            for h in range(1, HEADS):
                mixed = mixed + scores[h] * (pre[g, h] * 0.125)
            mixed = jnp.where(valid, mixed, -1e30)
            top = jnp.max(mixed, axis=-1, keepdims=True)
            raised = jnp.exp(mixed - top)
            prob = raised * (1.0 / jnp.sum(raised, axis=-1, keepdims=True))
            probs[side][q, g, rows, :] = prob
            found.append(prob)
        for g in range(HEADS):
            mixed = found[0] * post[g, 0]
            for h in range(1, HEADS):
                mixed = mixed + found[h] * post[g, h]
            attn[side][q, g, rows, :] = mixed.astype(bf16)

    def out_step(p, q, side):
        value = section(q, side, 2, p)
        even, odd = dot(attn[side][q, 2 * p], value), dot(attn[side][q, 2 * p + 1], value)
        att[rows_at(q, side), 128 * p : 128 * p + 128] = jnp.where(low_half, even, odd).astype(
            bf16
        )

    def each(function, items):
        return [functools.partial(function, item) for item in items]

    def attend(q, carry):
        skewed(
            q,
            (
                (0, each(score_step, pairs)), (1, each(softmax_rows, row_blocks)),
                (2, each(out_step, pairs)),
            ),
        )
        return carry

    lax.fori_loop(0, images // 2, attend, 0)
    hid[...] = dot(att[...], wproj[...])
    for b in range(images):
        middle = mid[spans[b], :] + (hid[spans[b], :] + row(pbias))
        mid[spans[b], :] = middle
        centred, r = centre(middle)
        n2[spans[b], :] = jnp.where(inside, centred * r * row(gain2) + row(bias2), 0.0).astype(bf16)

    def exchange_copy(s):
        return remote(streams_out.at[s], streams_came.at[s], stream_pair_sems, (s,), pair)

    sums = [
        Sum(
            streams_acc.at[s], [ref.at[s] for ref in streams_landing], stream_sems.at[s, 0],
            BLOCK_PARTS, where,
        )
        for s in range(STREAMS)
    ]
    gathers = [Gather(fulls[s], stream_sems.at[s, 1], BLOCK_PARTS, where) for s in range(STREAMS)]

    def act(s, step):
        if step < 0:
            sums[s].start()
        elif step < 2:
            sums[s].act(step)
            if step == 1:
                fulls[s][mine] = streams_acc[(s,) + mine]
                gathers[s].start()
        else:
            gathers[s].act(step - 2)

    def poll(plan, index, spot):
        for (turn, at), items in plan.items():
            if at == spot:

                @pl.when(index == turn)
                def _():
                    for item in items:
                        act(*item)

    def blocks():
        filters = tiles(gconv[...])
        empty = jnp.zeros((BLOCK - 104, 128), f32)
        for d in range(16):
            yield index_of(d), jnp.concatenate(
                [
                    tiles(gqkv[24 * d : 24 * d + 24, :STREAM]),
                    tiles(hid[16 * d : 16 * d + 16]),
                    filters[8 * d : 8 * d + 8],
                    empty,
                ],
                axis=0,
            )

    def mlp(i, carry):
        s, own = i // 2, lax.rem(i, 2)
        owner = (1 - core) * (1 - own) + core * own
        unit = owner * STREAMS + s
        units = pl.ds(pl.multiple_of(unit * STREAM, STREAM), STREAM)
        bias_row = conv_full[:, units].astype(f32)[KS * KS : KS * KS + 1]
        weights[...] = fc1_blocks[unit]
        sums_of = {"bias": jnp.zeros((8, STREAM), f32)}

        def first(b, start, count):
            rows = slice(b * ROWS + start, b * ROWS + start + count)
            hidden[b % 2][start : start + count] = dot(n2[rows, :], weights[...]) + bias_row

        def activate(b, start):
            rows = slice(start, start + 16)
            activated, slopes = gelu_parts(hidden[b % 2][rows])
            slope[b][rows] = slopes
            acted[b % 2][rows] = activated.astype(bf16)

        def transform(b, start, count):
            made[b % 2][start : start + count] = dot(
                fwd[start : start + count], acted[b % 2][...]
            )

        def multiply(b, start):
            real, imag = slice(start, start + 16), slice(HALF + start, HALF + start + 16)
            xr, xi = made[b % 2][real], made[b % 2][imag]
            yr, yi = ghat[unit, b, real].astype(f32), ghat[unit, b, imag].astype(f32)
            kr, ki = turned[unit, real], turned[unit, imag]
            ahead[b % 2][real] = (xr * kr - xi * ki).astype(bf16)
            ahead[b % 2][imag] = (xr * ki + xi * kr).astype(bf16)
            behind[b % 2][real] = (yr * kr + yi * ki).astype(bf16)
            behind[b % 2][imag] = (yi * kr - yr * ki).astype(bf16)
            cross_r, cross_i = xr * yr + xi * yi, xi * yr - xr * yi
            if b > 0:
                cross_r, cross_i = cross[real] + cross_r, cross[imag] + cross_i
            cross[real], cross[imag] = cross_r, cross_i

        def invert(b, start, count):
            near = slice(start, start + count)
            rows = slice(b * ROWS + start, b * ROWS + start + count)
            part = inv[near]
            conv_low[unit, rows] = dot(part, ahead[b % 2][...]).astype(bf16)
            ghid = (dot(part, behind[b % 2][...]) * slope[b][near]).astype(bf16)
            ghid_low[unit, rows] = ghid
            rounded = ghid.astype(f32)
            total = sums_of["bias"]
            for r in range(0, count, 8):
                total = total + rounded[r : r + 8]
            sums_of["bias"] = total

        stages = (
            lambda b: [functools.partial(first, b, 0, ROWS)],
            lambda b: [functools.partial(activate, b, start) for start in range(0, ROWS, 16)],
            lambda b: [
                functools.partial(transform, b, start, HALF) for start in (0, HALF)
            ],
            lambda b: [functools.partial(multiply, b, start) for start in range(0, HALF, 16)],
            lambda b: [functools.partial(invert, b, *block) for block in ((0, 112), (112, 96))],
        )
        for beat in range(images + len(stages) - 1):
            weave(
                *[
                    stage(beat - depth)
                    for depth, stage in enumerate(stages)
                    if 0 <= beat - depth < images
                ]
            )
        bias_sum = add_rows(sums_of["bias"])
        high = cross[...].astype(bf16)
        low_part = (cross[...] - high.astype(f32)).astype(bf16)
        last = lax.broadcasted_iota(jnp.int32, (TAPS, STREAM), 0) == KS * KS
        gconv[...] = jnp.where(
            last, bias_sum, dot(bh[...], high) + dot(bl[...], high) + dot(bh[...], low_part)
        )
        hid[:STREAM] = t_dot(conv_low[unit], cot_pad[...])
        gqkv[:, :STREAM] = t_dot(n2[...], ghid_low[unit])

        @pl.when(own == 0)
        def _():
            for index, values in blocks():
                streams_out[(s,) + index] = values.astype(bf16)
            exchange_copy(s).start()

        @pl.when(own == 1)
        def _():
            exchange_copy(s).wait_recv()
            for index, values in blocks():
                came = streams_came[(s,) + index].astype(f32)
                streams_acc[(s,) + index] = (values + came).astype(bf16)

        poll(MLP_PLAN, i, images)
        return carry

    lax.fori_loop(0, 2 * STREAMS, mlp, 0)

    every = range(2 * STREAMS)
    joined = lambda ref, *rows: jnp.concatenate([ref[(u,) + rows] for u in every], axis=1)
    for b in range(images):
        hid[spans[b], :] = dot_t(joined(ghid_low, spans[b]), joined(fc1_blocks))
    gain_sum = jnp.zeros((1, WIDTH), f32)
    bias_sum = jnp.zeros((1, WIDTH), f32)
    proj_sum = jnp.zeros((1, WIDTH), f32)
    for b in range(images):
        middle = mid[spans[b], :]
        centred, r = centre(middle)
        grad = hid[spans[b], :]
        back, gain_rows = norm_back(centred, r, row(gain2), grad)
        gain_sum = gain_sum + add_rows(gain_rows)
        bias_sum = bias_sum + add_rows(grad)
        whole_grad = gmid[spans[b], :] + back
        gmid[spans[b], :] = whole_grad
        rounded = whole_grad.astype(bf16)
        proj_sum = proj_sum + add_rows(rounded.astype(f32))
        gmid_low[spans[b], :] = rounded
    gatt[...] = dot_t(gmid_low[...], wproj[...]).astype(bf16)
    gproj[...] = t_dot(att[...], gmid_low[...])
    mix[...] = jnp.zeros_like(mix)

    def fold(values):
        values = values[:, :128] + values[:, 128:]
        return values[:8] + values[8:]

    def weight_step(p, q, side):
        ahead_p = gatt[rows_at(q, side), 128 * p : 128 * p + 128]
        products(ahead_p, section(q, side, 2, p), weight[side], p)

    def back_rows(rows, q, side):
        given = [weight[side][g, rows, :] for g in range(HEADS)]
        mixed = []
        for h in range(HEADS):
            prob = probs[side][q, h, rows, :]
            ahead_h = given[0] * post[0, h]
            for g in range(1, HEADS):
                ahead_h = ahead_h + given[g] * post[g, h]
            for g in range(HEADS):
                mix[HEADS * HEADS + g * HEADS + h] += fold(given[g] * prob)
            inner = jnp.sum(prob * ahead_h, axis=-1, keepdims=True)
            mixed.append(prob * (ahead_h - inner))
        for h in range(HEADS):
            scores = score[side][h, rows, :]
            total = mixed[0] * pre[0, h]
            for g in range(1, HEADS):
                total = total + mixed[g] * pre[g, h]
            low[side][h, rows, :] = total.astype(bf16)
            for g in range(HEADS):
                mix[g * HEADS + h] += fold(mixed[g] * scores)

    def value_step(p, q, side):
        rows, lanes = rows_at(q, side), 2 * WIDTH + 128 * p
        ahead_p = gatt[rows, 128 * p : 128 * p + 128]
        even, odd = t_dot(attn[side][q, 2 * p], ahead_p), t_dot(attn[side][q, 2 * p + 1], ahead_p)
        gpacked[rows, lanes : lanes + 128] = jnp.where(key_half, even, odd)[:ROWS].astype(bf16)

    def query_step(p, q, side):
        key = section(q, side, 1, p)
        even, odd = dot(low[side][2 * p], key), dot(low[side][2 * p + 1], key)
        gpacked[rows_at(q, side), 128 * p : 128 * p + 128] = (
            jnp.where(low_half, even, odd) * 0.125
        ).astype(bf16)

    def key_step(p, q, side):
        query, lanes = section(q, side, 0, p, ROWS), WIDTH + 128 * p
        even, odd = t_dot(low[side][2 * p], query), t_dot(low[side][2 * p + 1], query)
        gpacked[rows_at(q, side), lanes : lanes + 128] = (
            jnp.where(key_half, even, odd)[:ROWS] * 0.125
        ).astype(bf16)

    def back_couple(q, carry):
        skewed(
            q,
            (
                (0, each(score_step, pairs) + each(weight_step, pairs)),
                (1, each(back_rows, row_blocks)), (1, each(value_step, pairs)),
                (2, each(query_step, pairs) + each(key_step, pairs)),
            ),
            lambda beat: poll(BACK_PLAN, q, beat),
        )
        return carry

    lax.fori_loop(0, images // 2, back_couple, 0)
    for n in range(0, 3 * WIDTH, WIDTH):
        gqkv[:, n : n + WIDTH] = t_dot(n1[...], gpacked[:, n : n + WIDTH])

    width, proj_width = gqkv.shape[1] // 2, gproj.shape[1] // 2

    def pieces(side):
        for d in range(16):
            rows = slice(24 * d, 24 * d + 24)
            both = jnp.concatenate(
                [
                    gqkv[rows, side * width : (side + 1) * width],
                    gproj[rows, side * proj_width : (side + 1) * proj_width],
                ],
                axis=1,
            )
            yield index_of(d), tiles(both)

    gather.finish()
    for copy in forwards:
        copy.wait_send()
    for side in range(2):

        @pl.when(core == side)
        def _():
            for index, values in pieces(1 - side):
                piece_full[index] = values.astype(bf16)

    exchange = remote(piece_full, piece_other, att_pair_sems, (0,), pair)
    exchange.start()
    for b in range(images):
        hid[spans[b], :] = dot_t(gpacked[spans[b], :], wqkv[...])
    attention = Sum(att_bufs["acc"], att_bufs["landing"], att_sems, PIECE_PARTS, where)
    exchange.wait_recv()
    for side in range(2):

        @pl.when(core == side)
        def _():
            for index, values in pieces(side):
                came = piece_other[index].astype(f32)
                att_bufs["acc"][index] = (values + came).astype(bf16)

    attention.start()

    for item in TAIL_PLAN:
        act(*item)
    norm_gain = jnp.zeros((1, WIDTH), f32)
    norm_bias = jnp.zeros((1, WIDTH), f32)
    flat = tok_held[...].reshape(SEQ, images * WIDTH)
    for b in range(images):
        rows = slice(b * ROWS, b * ROWS + SEQ)
        centred, r = centre(flat[:, b * WIDTH : (b + 1) * WIDTH].astype(f32))
        grad = hid[rows, :]
        back, gain_rows = norm_back(centred, r, row(gain1), grad)
        norm_gain = norm_gain + add_rows(gain_rows)
        norm_bias = norm_bias + add_rows(grad)
        gtok_held[:, b, :] = gmid[rows, :] + back
    leaving = [pltpu.make_async_copy(gtok_held, gtok_out, leave_sems.at[1])]
    leaving[0].start()
    rows_out[...] = jnp.concatenate(
        [norm_gain, norm_bias, proj_sum, gain_sum, bias_sum, cot_sum, jnp.zeros((2, WIDTH), f32)],
        axis=0,
    )
    for t in range(WIDTH // 128):
        small_sums[0, 8 * t : 8 * t + 8] = rows_out[:, 128 * t : 128 * t + 128]
    square[...] = jnp.zeros_like(square)
    square[: 2 * HEADS * HEADS] = jnp.sum(mix[...], axis=1)
    line = add_rows(square[...].T)
    small_sums[0, 24:] = jnp.concatenate([line, jnp.zeros((SMALL - 25, 128), f32)], axis=0)

    def small_copy(turn, peer):
        if turn == 0:
            device = pair
        else:
            device = where.peer((PLANE, DEPTH)[turn - 1], FLIPS[peer])
        index = 0 if turn == 0 else 3 * turn - 2 + peer
        return remote(
            small_sums.at[turn], small_landed.at[index], att_pair_sems, (1 + index,), device
        )

    small_counts = (1, 3, 3)

    def small_start(turn):
        for peer in range(small_counts[turn]):
            small_copy(turn, peer).start()

    def small_take(turn):
        total = small_sums[turn]
        for peer in range(small_counts[turn]):
            small_copy(turn, peer).wait_recv()
            total = total + small_landed[0 if turn == 0 else 3 * turn - 2 + peer]
        return total

    def second_projection(b):
        second = dot(joined(conv_low, spans[b]), fc2_full[...])
        result = mid[spans[b], :] + (second + row(fc2b))
        out_wide[:, b, :] = result[:SEQ]

    small_start(0)
    for b in range(images // 2):
        second_projection(b)
    small_sums[1] = small_take(0)
    small_start(1)
    act(2, 2)
    attention.act(0)
    for b in range(images // 2, images):
        second_projection(b)
    out_held[...] = out_wide[...].astype(bf16)
    leaving.append(pltpu.make_async_copy(out_held, block_out, leave_sems.at[0]))
    leaving[1].start()
    small_sums[2] = small_take(1)
    small_start(2)
    for s in range(STREAMS):
        act(s, 3)
    leaving.append(pltpu.make_async_copy(streams_came, fulls_out, leave_sems.at[2]))
    leaving[2].start()
    small_out[...] = small_take(2)
    attention.act(1)
    piece_out[...] = att_bufs["acc"][mine]
    for copy in leaving:
        copy.wait()
    for copy in weights_come + [exchange]:
        copy.wait_send()
    for turn in range(3):
        for peer in range(small_counts[turn]):
            small_copy(turn, peer).wait_send()
    for s in range(STREAMS):
        exchange_copy(s).wait_send()
    attention.finish()
    for s in range(STREAMS):
        sums[s].finish()
        gathers[s].finish()


def call_block(
    pre, post, tok, cot, gain1, bias1, pbias, gain2, bias2, fc2b, qkv, proj, fc1, conv, bias, fc2
):
    images, half = tok.shape[1], fc1.shape[1]
    units, total = 2 * half, images * ROWS
    forward, inverse, kernel, back, one = fourier()
    kernel_high, kernel_low = split(kernel)
    back_high, back_low = split(back)
    consts = [
        jnp.asarray(forward.astype(np.float32).astype(bf16)),
        jnp.asarray(inverse.astype(np.float32).astype(bf16)),
        jnp.asarray(kernel_high), jnp.asarray(kernel_low),
        jnp.asarray(back_high), jnp.asarray(back_low),
        jnp.asarray(one.astype(np.float32)),
    ]
    vmem = pl.BlockSpec(memory_space=pltpu.VMEM)
    smem = pl.BlockSpec(memory_space=pltpu.SMEM)
    hbm = pl.BlockSpec(memory_space=pl.ANY)

    def bufs(rows):
        buffer = lambda free: pltpu.VMEM((2,) * free + (rows, 128), bf16)
        return {
            "acc": buffer(4),
            "landing": [
                pltpu.VMEM((3, 2, 2, rows, 128), bf16), pltpu.VMEM((3, rows, 128), bf16),
            ],
        }

    stacked = lambda free: pltpu.VMEM((STREAMS,) + (2,) * free + (BLOCK, 128), bf16)
    tall = lambda width, dtype: pltpu.VMEM((total, width), dtype)
    two = lambda shape, dtype, count=2: [pltpu.VMEM(shape, dtype) for _ in range(count)]
    scratch = dict(
        tok_held=pltpu.VMEM(tok.shape, bf16),
        cot_held=pltpu.VMEM(tok.shape, bf16),
        out_held=pltpu.VMEM(tok.shape, bf16),
        gtok_held=pltpu.VMEM(tok.shape, f32),
        out_wide=pltpu.VMEM(tok.shape, f32),
        **{
            name: pltpu.VMEM(value.shape, bf16)
            for name, value in zip(("fwd", "inv", "kh", "kl", "bh", "bl"), consts)
        },
        piece_full=pltpu.VMEM((2, 2, 2, 2, PIECE, 128), bf16),
        piece_other=pltpu.VMEM((2, 2, 2, 2, PIECE, 128), bf16),
        taps_pad=pltpu.VMEM((TAPS, half), f32),
        wqkv=pltpu.VMEM((WIDTH, 3 * WIDTH), bf16),
        wproj=pltpu.VMEM((WIDTH, WIDTH), bf16),
        fc1_blocks=pltpu.VMEM((2 * STREAMS, WIDTH, STREAM), bf16),
        fc2_full=pltpu.VMEM((units, WIDTH), bf16),
        conv_full=pltpu.VMEM((TAPS, units), bf16),
        cot_pad=tall(WIDTH, bf16),
        n1=tall(WIDTH, bf16),
        packed=two((images // 2, KEYS, 3 * WIDTH), bf16),
        score=two((HEADS, ROWS, KEYS), f32),
        weight=two((HEADS, ROWS, KEYS), f32),
        probs=two((images // 2, HEADS, ROWS, KEYS), f32),
        attn=two((images // 2, HEADS, ROWS, KEYS), bf16),
        att=tall(WIDTH, bf16),
        mid=tall(WIDTH, f32),
        n2=tall(WIDTH, bf16),
        turned=pltpu.VMEM((2 * STREAMS, COEFS, STREAM), f32),
        ghat=pltpu.VMEM((2 * STREAMS, images, COEFS, STREAM), bf16),
        hid=tall(WIDTH, f32),
        hidden=two((ROWS, STREAM), f32),
        slope=two((ROWS, STREAM), f32, images),
        acted=two((ROWS, STREAM), bf16),
        weights=pltpu.VMEM((WIDTH, STREAM), bf16),
        conv_low=pltpu.VMEM((2 * STREAMS, total, STREAM), bf16),
        ghid_low=pltpu.VMEM((2 * STREAMS, total, STREAM), bf16),
        gmid=tall(WIDTH, f32),
        gmid_low=tall(WIDTH, bf16),
        gatt=tall(WIDTH, bf16),
        low=two((HEADS, ROWS, KEYS), bf16),
        gpacked=tall(3 * WIDTH, bf16),
        mix=pltpu.VMEM((2 * HEADS * HEADS, 8, 128), f32),
        rows_out=pltpu.VMEM((8, WIDTH), f32),
        square=pltpu.VMEM((128, 128), f32),
        gqkv=pltpu.VMEM((WIDTH, 3 * WIDTH), f32),
        gproj=pltpu.VMEM((WIDTH, WIDTH), f32),
        small_sums=pltpu.VMEM((3, SMALL, 128), f32),
        small_landed=pltpu.VMEM((7, SMALL, 128), f32),
        streams_out=stacked(4),
        streams_came=stacked(4),
        streams_acc=stacked(4),
        streams_landing=[
            pltpu.VMEM((STREAMS, 3, 2, 2, BLOCK, 128), bf16),
            pltpu.VMEM((STREAMS, 3, BLOCK, 128), bf16),
        ],
        gconv=pltpu.VMEM((TAPS, STREAM), f32),
        made=two((COEFS, STREAM), f32),
        ahead=two((COEFS, STREAM), bf16),
        behind=two((COEFS, STREAM), bf16),
        cross=pltpu.VMEM((COEFS, STREAM), f32),
        att_bufs=bufs(PIECE),
        local_sems=pltpu.SemaphoreType.DMA((9 + STREAMS,)),
        leave_sems=pltpu.SemaphoreType.DMA((3,)),
        gather_sems=pltpu.SemaphoreType.DMA((2, 2, 2, 3)),
        gather_pair_sems=pltpu.SemaphoreType.DMA((2, 15 + STREAMS)),
        stream_pair_sems=pltpu.SemaphoreType.DMA((2, STREAMS)),
        stream_sems=pltpu.SemaphoreType.DMA((STREAMS, 2, 2, 2, 2, 3)),
        att_sems=pltpu.SemaphoreType.DMA((2, 2, 2, 3)),
        att_pair_sems=pltpu.SemaphoreType.DMA((2, 8)),
    )
    return pl.pallas_call(
        block_kernel,
        in_specs=[smem] * 2 + [hbm] * 2 + [vmem] * 8 + [hbm] + [vmem] * 2 + [hbm] * 7 + [vmem],
        out_specs=[hbm] * 3 + [vmem] * 2,
        out_shape=[
            jax.ShapeDtypeStruct(tok.shape, bf16),
            jax.ShapeDtypeStruct(tok.shape, f32),
        ]
        + [
            jax.ShapeDtypeStruct((STREAMS, 2, 2, 2, 2, BLOCK, 128), bf16),
            jax.ShapeDtypeStruct((PIECE, 128), bf16),
            jax.ShapeDtypeStruct((SMALL, 128), f32),
        ],
        scratch_shapes=list(scratch.values()),
        compiler_params=pltpu.CompilerParams(
            vmem_limit_bytes=VMEM, collective_id=0, has_side_effects=True
        ),
        name="block",
    )(
        pre, post, tok, cot, gain1, bias1, pbias, gain2, bias2, fc2b, qkv, proj, fc1, conv, bias,
        fc2, *consts,
    )


def finish_kernel(totals_in, piece, small, out_in, gtok_in, *rest):
    outs, rest = rest[:16], rest[16:]
    held, (totals, out_held, gtok_held, taps, mixes, sems) = rest[:14], rest[14:]
    gfc1, gb1, gconv, gfc2, gqkv, gproj, g1, b1, pb, g2, b2, fb, pre, post = held
    coming = [
        pltpu.make_async_copy(totals_in.at[s], totals.at[s], sems.at[s]) for s in range(STREAMS)
    ]
    coming += [
        pltpu.make_async_copy(gtok_in, gtok_held, sems.at[STREAMS]),
        pltpu.make_async_copy(out_in, out_held, sems.at[STREAMS + 1]),
    ]
    for copy in coming:
        copy.start()
    leaving = []

    def leave(src, dst):
        copy = pltpu.make_async_copy(src, dst, sems.at[STREAMS + 2 + len(leaving)])
        copy.start()
        leaving.append(copy)

    both = untiles(piece[...].astype(f32), 6)
    width = gqkv.shape[1]
    gqkv[...] = both[:, :width]
    gproj[...] = both[:, width:]
    rows = untiles(small[:24], 3)
    for index, ref in enumerate((g1, b1, pb, g2, b2, fb)):
        ref[...] = rows[index].reshape(ref.shape)
    line = small[24:25]
    for index, ref in enumerate((pre, post)):
        for g in range(HEADS):
            start = HEADS * HEADS * index + HEADS * g
            mixes[index, g : g + 1, :HEADS] = line[:, start : start + HEADS]
    pre[...] = mixes[0, :HEADS, :HEADS] * 0.125
    post[...] = mixes[1, :HEADS, :HEADS]
    for index in range(4, 14):
        leave(held[index], outs[index])
    for s in range(STREAMS):
        side = slice(s * STREAM, (s + 1) * STREAM)
        coming[s].wait()
        for d in range(16):
            block = totals[(s,) + index_of(d)].astype(f32)
            gfc1[24 * d : 24 * d + 24, side] = untiles(block[:48], 2)
            gfc2[s * STREAM + 16 * d : s * STREAM + 16 * d + 16, :] = untiles(block[48:96], 3)
            taps[8 * d : 8 * d + 8, :] = block[96:104]
        leave(gfc2.at[side], outs[3].at[side])
        leave(gfc1.at[:, side], outs[0].at[:, side])
        filters = untiles(taps[...], 2)
        gconv[:, side] = filters[: KS * KS]
        gb1[side] = filters[KS * KS]
        if s == 0:
            coming[STREAMS].wait()
            leave(gtok_held, outs[15])
            coming[STREAMS + 1].wait()
            leave(out_held, outs[14])
    leave(gconv, outs[2])
    leave(gb1, outs[1])
    for copy in leaving:
        copy.wait()


def call_finish(totals, piece, small, block_out, gtok, half):
    hbm = pl.BlockSpec(memory_space=pl.ANY)
    vmem = pl.BlockSpec(memory_space=pltpu.VMEM)
    shapes = [
        (WIDTH, half), (half,), (KS * KS, half), (half, WIDTH), (24, 3 * WIDTH // 2),
        (24, WIDTH // 2),
    ]
    shapes += [(WIDTH,)] * 6 + [(HEADS, HEADS)] * 2
    return pl.pallas_call(
        finish_kernel,
        in_specs=[hbm] + [vmem] * 2 + [hbm] * 2,
        out_specs=[hbm] * 16,
        out_shape=[jax.ShapeDtypeStruct(shape, f32) for shape in shapes]
        + [jax.ShapeDtypeStruct(v.shape, v.dtype) for v in (block_out, gtok)],
        scratch_shapes=[pltpu.VMEM(shape, f32) for shape in shapes]
        + [
            pltpu.VMEM(totals.shape, bf16),
            pltpu.VMEM(block_out.shape, bf16), pltpu.VMEM(gtok.shape, f32),
            pltpu.VMEM((128, 128), f32), pltpu.VMEM((2, 8, 128), f32),
            pltpu.SemaphoreType.DMA((STREAMS + 2 + 2 * STREAMS + 14,)),
        ],
        compiler_params=pltpu.CompilerParams(vmem_limit_bytes=VMEM),
        name="finish",
    )(totals, piece, small, block_out, gtok)


def shards_any(
    tokens, norm1_gain, norm1_bias, qkv_weight, mix_pre, mix_post, proj_weight, proj_bias,
    norm2_gain, norm2_bias, fc1_weight, fc1_bias, conv_weight, fc2_weight, fc2_bias, cotangent,
):
    gather = lambda v, axis, dim: lax.all_gather(v, axis, axis=dim, tiled=True)
    both = jnp.concatenate([qkv_weight, proj_weight], axis=1)
    pair = lax.all_gather(gather(both, "dp", 0), "tensor", axis=0)
    columns = qkv_weight.shape[1]
    wqkv = jnp.concatenate([pair[0, :, :columns], pair[1, :, :columns]], axis=1)
    wproj = jnp.concatenate([pair[0, :, columns:], pair[1, :, columns:]], axis=1)
    fc1 = gather(fc1_weight, "tensor", 1)
    taps = jnp.concatenate([conv_weight, fc1_bias[None]], axis=0)
    taps = jnp.pad(gather(taps, "tensor", 1), ((0, TAPS - KS * KS - 1), (0, 0)))
    fc2 = gather(fc2_weight, "tensor", 0)
    block_out, gtok, gqkv, gproj, gfc1, gconv, gfc2, small = local_block(
        tokens, norm1_gain, norm1_bias, wqkv, mix_pre, mix_post, wproj, proj_bias, norm2_gain,
        norm2_bias, fc1, taps, fc2, fc2_bias, cotangent,
    )
    scatter = lambda v, axis, dim: lax.psum_scatter(v, axis, scatter_dimension=dim, tiled=True)
    gqkv = scatter(scatter(gqkv, "tensor", 1), "dp", 0)
    gproj = scatter(scatter(gproj, "tensor", 1), "dp", 0)
    gfc1 = lax.psum(scatter(gfc1, "tensor", 1), "dp")
    gfc2 = lax.psum(scatter(gfc2, "tensor", 0), "dp")
    gconv = lax.psum(scatter(gconv, "tensor", 1), "dp")
    small = lax.psum(small, ("dp", "tensor"))
    rows = jnp.concatenate([small[0:8], small[8:16], small[16:24]], axis=1)
    mixes = small[24, : 2 * HEADS * HEADS].reshape(2, HEADS, HEADS)
    return (
        block_out, gtok, rows[0], rows[1], gqkv, mixes[0] * 0.125, mixes[1], gproj, rows[2],
        rows[3], rows[4], gfc1, gconv[KS * KS], gconv[: KS * KS], gfc2, rows[5],
    )


def shards_sixteen(
    tokens, norm1_gain, norm1_bias, qkv_weight, mix_pre, mix_post, proj_weight, proj_bias,
    norm2_gain, norm2_bias, fc1_weight, fc1_bias, conv_weight, fc2_weight, fc2_bias, cotangent,
):
    turn = lambda v: jnp.transpose(v, (1, 0, 2))
    block_out, gtok, totals, piece, small = call_block(
        mix_pre, mix_post, turn(tokens), turn(cotangent), norm1_gain, norm1_bias, proj_bias, norm2_gain,
        norm2_bias, fc2_bias, qkv_weight, proj_weight, fc1_weight, conv_weight, fc1_bias,
        fc2_weight,
    )
    (
        gfc1, gb1, gconv, gfc2, gqkv, gproj, g1, b1, pb, g2, b2, fb, pre, post, block_out, gtok
    ) = call_finish(totals, piece, small, block_out, gtok, fc1_weight.shape[1])
    block_out, gtok = turn(block_out), turn(gtok)
    return (
        block_out, gtok, g1, b1, gqkv, pre, post, gproj, pb, g2, b2, gfc1, gb1, gconv, gfc2, fb
    )


def solution(mesh):
    spec = P(("dp", "tensor"), None, None)
    in_specs = (
        spec, P(), P(), P("dp", "tensor"), P(), P(), P("dp", "tensor"), P(), P(), P(),
        P(None, "tensor"), P("tensor"), P(None, "tensor"), P("tensor", None), P(), spec,
    )
    out_specs = (
        spec, spec, P(), P(), P("dp", "tensor"), P(), P(), P("dp", "tensor"), P(), P(), P(),
        P(None, "tensor"), P("tensor"), P(None, "tensor"), P("tensor", None), P(),
    )
    sixteen = mesh.shape["dp"] == 16 and mesh.shape["tensor"] == 2
    body = shards_sixteen if sixteen else shards_any
    return jax.shard_map(body, mesh=mesh, in_specs=in_specs, out_specs=out_specs, check_vma=False)
```
